32 devices in a mesh: section: 2 (over z_hi), fsdp: 8 (over y, x, core), rep: 2 (over z_lo).
Axes of the slice: x: 2, y: 2, z: 4 (z_hi: 2, z_lo: 2; z = z_hi * 2 + z_lo), core: 2. Of those that a mesh axis runs over, the one named last changes fastest.
Arguments:
- section_inputs: bfloat16 [2, 2, 2, 1024, 2048], P('section', None, 'rep', 'fsdp'), may hold values from -6 to 6
- doc_lengths: int32 [2, 2, 3], P(None, 'rep'), may hold values from 1 to 1022, as said below
- mixer_gain: bfloat16 [2, 2048], P('section', 'fsdp'), may hold values from 0.25 to 1.75
- heads_weight: bfloat16 [2, 2048, 4096], P('section', 'fsdp'), may hold values from -0.125 to 0.125
- merge_weight: bfloat16 [2, 2048, 2048], P('section', 'fsdp'), may hold values from -0.5 to 0.5
- head_gain: bfloat16 [2, 256], P('section', 'fsdp'), may hold values from 0.25 to 1.75
- feed_gain: bfloat16 [2, 2048], P('section', 'fsdp'), may hold values from 0.25 to 1.75
- expand_weight: bfloat16 [2, 2048, 12288], P('section', 'fsdp'), may hold values from -0.125 to 0.125
- reduce_weight: bfloat16 [2, 6144, 2048], P('section', 'fsdp'), may hold values from -0.078125 to 0.078125
Outputs:
- section_outputs: float32 [2, 2, 2, 1024, 2048], P('section', None, 'rep', 'fsdp')
- grad_mixer_gain: float32 [2, 2048], P('section', 'fsdp')
- grad_heads_weight: float32 [2, 2048, 4096], P('section', 'fsdp')
- grad_merge_weight: float32 [2, 2048, 2048], P('section', 'fsdp')
- grad_head_gain: float32 [2, 256], P('section', 'fsdp')
- grad_feed_gain: float32 [2, 2048], P('section', 'fsdp')
- grad_expand_weight: float32 [2, 2048, 12288], P('section', 'fsdp')
- grad_reduce_weight: float32 [2, 6144, 2048], P('section', 'fsdp')
The draws below stay inside these ranges and needn't reach their ends.
Inputs may be any that keep to these rules, and one draw needn't show every extreme that they name: `doc_lengths`: the 3 lengths of each sequence are positive and sum to 1024.
All inputs are finite; a program needn't handle non-finite values.
Results may differ from the reference program's by a relative error of at most 0.025.
Values may be sent and summed in bfloat16 or wider, within the bound.
A program may use at most 448 MiB of HBM per device.

```python
import math
import jax
import jax.numpy as jnp
from jax import lax

D = 2048
FF = 6144
QUERY_HEADS = 16
KEY_VALUE_HEADS = 8
HEAD_SIZE = 128
MICRO = 2
DOCS = 3
ROWS = 128
LENGTH = 1024
SEQS = 2
QKV = 4096


def draw_doc_lengths(key, part):
    key = jax.random.fold_in(key, 11)
    short_key, pick_key = jax.random.split(key)
    short_docs = jax.random.randint(short_key, (MICRO, SEQS, DOCS), 1, max(ROWS // 2, 2))
    first_seq = (jnp.arange(MICRO)[:, None, None] == 0) & (jnp.arange(SEQS)[None, :, None] == 0)
    short_docs = jnp.where(first_seq, 1, short_docs)
    chosen = jax.random.randint(pick_key, (MICRO, SEQS, 1), 0, DOCS)
    is_long = jnp.arange(DOCS)[None, None, :] == chosen
    others = jnp.sum(jnp.where(is_long, 0, short_docs), axis=-1, keepdims=True)
    return jnp.where(is_long, LENGTH - others, short_docs).astype(jnp.int32)


def shard_levels(rng, dims, shards, low, top_value):
    factor_of, own = 1.0, jax.random.fold_in(rng, 6)
    for axis_at, shards_of in shards:
        steps = jnp.exp(jax.random.uniform(jax.random.fold_in(own, axis_at), (shards_of,), jnp.float32, low / len(shards), top_value / len(shards)))
        factor_of = factor_of * jnp.repeat(steps, dims[axis_at] // shards_of).reshape([-1 if axis == axis_at else 1 for axis in range(len(dims))])
    return factor_of


def noise(stream_key, extent, width, most, cuts=(), held_as=jnp.bfloat16):
    gain = shard_levels(stream_key, extent, cuts, -0.22, 0.18) if cuts else 1.0
    drawn = jax.random.normal(stream_key, extent, jnp.float32) * width * gain
    return jnp.minimum(jnp.maximum(drawn, -most), most).astype(held_as)


def setup_inputs(seed: int = 0) -> dict:
    arg_keys = jax.random.split(jax.random.key(seed), 10)
    section_inputs = noise(arg_keys[0], (2, MICRO, SEQS, LENGTH, D), 1.0, 6.0, ((0, 2), (2, 2), (3, 8)))
    doc_lengths = draw_doc_lengths(jax.random.fold_in(arg_keys[9], 71), 0)
    mixer_gain = jnp.clip(1.0 + 0.15 * jax.random.normal(arg_keys[2], (2, D), jnp.float32), 0.25, 1.75).astype(jnp.bfloat16)
    heads_weight = noise(arg_keys[3], (2, D, QKV), D ** -0.5, 0.125, ((0, 2), (1, 8)))
    merge_weight = noise(arg_keys[4], (2, QUERY_HEADS * HEAD_SIZE, D), (QUERY_HEADS * HEAD_SIZE // 16) ** -0.5, 0.5, ((0, 2), (1, 8)))
    head_gain = jnp.clip(1.0 + 0.15 * jax.random.normal(arg_keys[5], (2, 2 * HEAD_SIZE), jnp.float32), 0.25, 1.75).astype(jnp.bfloat16)
    feed_gain = jnp.clip(1.0 + 0.15 * jax.random.normal(arg_keys[6], (2, D), jnp.float32), 0.25, 1.75).astype(jnp.bfloat16)
    expand_weight = noise(arg_keys[7], (2, D, 2 * FF), D ** -0.5, 0.125, ((0, 2), (1, 8)))
    reduce_weight = noise(arg_keys[8], (2, FF, D), FF ** -0.5, 0.078125, ((0, 2), (1, 8)))
    return dict(section_inputs=section_inputs, doc_lengths=doc_lengths, mixer_gain=mixer_gain, heads_weight=heads_weight, merge_weight=merge_weight, head_gain=head_gain, feed_gain=feed_gain, expand_weight=expand_weight, reduce_weight=reduce_weight)


NORM_EPS = 1e-06
ROPE_BASE = 1000000.0
MASKED_SCORE = -1e+30
HIGHEST = lax.Precision.HIGHEST

@jax.custom_vjp
def lower_bound(v):
    return lax.optimization_barrier(v.astype(jnp.bfloat16)).astype(jnp.float32)

@jax.custom_vjp
def low_back(v):
    return v

def low_keep(v):
    return (lower_bound(v), None)

def low_pass(kept, grad):
    return (grad,)

def back_keep(v):
    return (v, None)

def back_low(kept, grad):
    return (lower_bound(grad),)
lower_bound.defvjp(low_keep, low_pass)
low_back.defvjp(back_keep, back_low)

def normed(values):
    return values * lax.rsqrt(lax.optimization_barrier(jnp.mean(values * values, axis=-1, keepdims=True)) + NORM_EPS)

def scaled(values, gain_row):
    return normed(values) * gain_row

def rotate(values, positions):
    half_width = values.shape[-1] // 2
    frequency = jnp.exp(jnp.arange(half_width, dtype=jnp.float32) * (-2.0 * math.log(ROPE_BASE) / values.shape[-1]))
    angles = positions.astype(jnp.float32)[:, None] * frequency[None, :]
    cosine = jnp.cos(angles)[:, None, :]
    sine_part = jnp.sin(angles)[:, None, :]
    lower_half = values[..., :half_width]
    upper_half = values[..., half_width:]
    return jnp.concatenate([lower_half * cosine - upper_half * sine_part, upper_half * cosine + lower_half * sine_part], axis=-1)

def places(doc_lengths, sequence_length):
    doc_ends = jnp.cumsum(doc_lengths).astype(jnp.int32)
    token_index = jnp.arange(sequence_length, dtype=jnp.int32)
    passed_ends = (token_index[:, None] >= doc_ends[None, :]).astype(jnp.int32)
    document_index = lax.optimization_barrier(jnp.sum(passed_ends, axis=1)).astype(jnp.int32)
    doc_start = lax.optimization_barrier(jnp.sum(passed_ends * doc_lengths[None, :], axis=1)).astype(jnp.int32)
    return (document_index, (token_index - doc_start).astype(jnp.int32))

def heads_of(projected_output, head_gain, positions):
    count_of_tokens = projected_output.shape[0]
    query_rows = projected_output[:, :QUERY_HEADS * HEAD_SIZE].reshape(count_of_tokens, QUERY_HEADS, HEAD_SIZE)
    heads_of_keys = projected_output[:, QUERY_HEADS * HEAD_SIZE:(QUERY_HEADS + KEY_VALUE_HEADS) * HEAD_SIZE].reshape(count_of_tokens, KEY_VALUE_HEADS, HEAD_SIZE)
    heads_of_values = projected_output[:, (QUERY_HEADS + KEY_VALUE_HEADS) * HEAD_SIZE:]
    return (rotate(scaled(query_rows, head_gain[:HEAD_SIZE]), positions), rotate(scaled(heads_of_keys, head_gain[HEAD_SIZE:]), positions), heads_of_values)

def gated_unit(joined):
    return jax.nn.silu(joined[:, :FF]) * joined[:, FF:]

def matmul(left_side, right_side):
    return jnp.dot(left_side, right_side, precision=HIGHEST, preferred_element_type=jnp.float32)

def attend_rows(query_rows, heads_of_keys, heads_of_values, document_index):
    sequence_length = query_rows.shape[0]
    block_row_list = min(512, sequence_length)
    token_index = jnp.arange(sequence_length, dtype=jnp.int32)
    grouped_heads = query_rows.reshape(sequence_length // block_row_list, block_row_list, KEY_VALUE_HEADS, QUERY_HEADS // KEY_VALUE_HEADS, HEAD_SIZE)
    doc_blocks = document_index.reshape(sequence_length // block_row_list, block_row_list)
    index_blocks = token_index.reshape(sequence_length // block_row_list, block_row_list)

    def one_block(entry):
        block_queries, block_docs, block_index = entry
        scores = jnp.einsum('rkgd,tkd->rkgt', block_queries, heads_of_keys, precision=HIGHEST) * HEAD_SIZE ** (-0.5)
        scores = low_back(scores)
        allowed = (block_docs[:, None] == document_index[None, :]) & (block_index[:, None] >= token_index[None, :])
        scores = jnp.where(allowed[:, None, None, :], scores, MASKED_SCORE)
        row_max = lax.optimization_barrier(jnp.max(scores, axis=-1, keepdims=True))
        exp_scores = jnp.exp(scores - row_max)
        attn_probs = lower_bound(exp_scores / lax.optimization_barrier(jnp.sum(exp_scores, axis=-1, keepdims=True)))
        return jnp.einsum('rkgt,tkd->rkgd', attn_probs, heads_of_values, precision=HIGHEST)
    heads_mixed = lax.map(jax.checkpoint(one_block), (grouped_heads, doc_blocks, index_blocks))
    return heads_mixed.reshape(sequence_length, QUERY_HEADS * HEAD_SIZE)

def decoder_layer(inputs, weights, document_index, positions):
    mixer_gain, heads_weight, merge_weight, head_gain, feed_gain, expand_weight, reduce_weight = weights
    sequence_length = inputs.shape[0]
    normal_a = lower_bound(scaled(inputs, mixer_gain))
    projected_output = low_back(matmul(normal_a, heads_weight))
    query_rows, heads_of_keys, heads_of_values = heads_of(projected_output, head_gain, positions)
    heads_mixed = attend_rows(lower_bound(query_rows), lower_bound(heads_of_keys), lower_bound(heads_of_values).reshape(sequence_length, KEY_VALUE_HEADS, HEAD_SIZE), document_index)
    heads_mixed = low_back(lower_bound(heads_mixed))
    middle = inputs + low_back(matmul(heads_mixed, merge_weight))
    normal_b = lower_bound(scaled(middle, feed_gain))
    joined = low_back(matmul(normal_b, expand_weight))
    hidden = lower_bound(gated_unit(joined))
    return middle + low_back(matmul(hidden, reduce_weight))

def reference(section_inputs, doc_lengths, mixer_gain, heads_weight, merge_weight, head_gain, feed_gain, expand_weight, reduce_weight):
    weights = tuple((entry.astype(jnp.float32) for entry in (mixer_gain, heads_weight, merge_weight, head_gain, feed_gain, expand_weight, reduce_weight)))
    inputs = section_inputs[0].astype(jnp.float32).reshape(MICRO * SEQS, LENGTH, D)
    cotangent = section_inputs[1].astype(jnp.float32).reshape(MICRO * SEQS, LENGTH, D)
    flat_lengths = doc_lengths.reshape(MICRO * SEQS, DOCS)

    def forward(layer_inputs, layer_weights):
        lower_layer = tuple((entry[0] for entry in layer_weights))
        upper_layer = tuple((entry[1] for entry in layer_weights))

        def one_sequence(unused_carry, entry):
            sequence, lengths_row = entry
            document_index, positions = places(lengths_row, LENGTH)
            handed = low_back(lower_bound(decoder_layer(sequence, lower_layer, document_index, positions)))
            return (unused_carry, decoder_layer(handed, upper_layer, document_index, positions))
        return lax.scan(one_sequence, jnp.zeros((), jnp.float32), (layer_inputs, flat_lengths))[1]
    outputs, pullback = jax.vjp(forward, inputs, weights)
    grad_inputs, grad_weights = pullback(cotangent)
    section_outputs = jnp.stack([grad_inputs, outputs]).reshape(2, MICRO, SEQS, LENGTH, D)
    return (section_outputs, grad_weights[0], grad_weights[1], grad_weights[2], grad_weights[3], grad_weights[4], grad_weights[5], grad_weights[6])
```

```python
import functools
import math

import jax
import jax.numpy as jnp
from jax import lax
from jax.experimental import pallas as pl
from jax.experimental.pallas import tpu as pltpu
from jax.sharding import PartitionSpec as P

FF = 6144
QUERY_HEADS = 16
KEY_VALUE_HEADS = 8
HEAD_SIZE = 128


NORM_EPS = 1e-06
ROPE_BASE = 1000000.0
MASKED_SCORE = -1e30
PLANE = 8


def from_behind(array, axis, by):
    count = lax.axis_size(axis)
    pairs = [(i, i + by) for i in range(count) if 0 <= i + by < count]
    return lax.ppermute(array, axis, pairs)


def normed(values):
    return values * lax.rsqrt(jnp.mean(values * values, axis=-1, keepdims=True) + NORM_EPS)


def scaled(values, gain_row):
    return normed(values) * gain_row


def rotate(values, positions):
    half_width = values.shape[-1] // 2
    frequency = jnp.exp(
        jnp.arange(half_width, dtype=jnp.float32) * (-2.0 * math.log(ROPE_BASE) / values.shape[-1])
    )
    angles = positions.astype(jnp.float32)[:, None] * frequency[None, :]
    cosine = jnp.cos(angles)[:, None, :]
    sine_part = jnp.sin(angles)[:, None, :]
    lower_half = values[..., :half_width]
    upper_half = values[..., half_width:]
    return jnp.concatenate(
        [
            lower_half * cosine - upper_half * sine_part,
            upper_half * cosine + lower_half * sine_part,
        ],
        axis=-1,
    )


def places(doc_lengths, sequence_length):
    doc_ends = jnp.cumsum(doc_lengths)
    token_index = jnp.arange(sequence_length, dtype=jnp.int32)
    passed_ends = (token_index[:, None] >= doc_ends[None, :]).astype(jnp.int32)
    document_index = jnp.sum(passed_ends, axis=1)
    doc_start = jnp.sum(passed_ends * doc_lengths[None, :], axis=1)
    return (document_index, token_index - doc_start)


def heads_of(projected_output, head_gain, positions):
    count_of_tokens = projected_output.shape[0]
    query_rows = projected_output[:, : QUERY_HEADS * HEAD_SIZE].reshape(
        count_of_tokens, QUERY_HEADS, HEAD_SIZE
    )
    heads_of_keys = projected_output[
        :, QUERY_HEADS * HEAD_SIZE : (QUERY_HEADS + KEY_VALUE_HEADS) * HEAD_SIZE
    ].reshape(count_of_tokens, KEY_VALUE_HEADS, HEAD_SIZE)
    heads_of_values = projected_output[:, (QUERY_HEADS + KEY_VALUE_HEADS) * HEAD_SIZE :]
    return (
        rotate(scaled(query_rows, head_gain[:HEAD_SIZE]), positions),
        rotate(scaled(heads_of_keys, head_gain[HEAD_SIZE:]), positions),
        heads_of_values,
    )


def gated_unit(joined):
    return jax.nn.silu(joined[:, :FF]) * joined[:, FF:]


def times_transposed(left_side, right_side):
    return lax.dot_general(
        left_side, right_side, (((1,), (1,)), ((), ())), preferred_element_type=jnp.float32
    )


def allowed_mask(doc_rows, row_start, document_index):
    row_index = row_start + jnp.arange(doc_rows.shape[0], dtype=jnp.int32)
    key_index = jnp.arange(document_index.shape[0], dtype=jnp.int32)
    return (doc_rows[:, None] == document_index[None, :]) & (
        row_index[:, None] >= key_index[None, :]
    )


def raw_scores(query_rows_second, rows_of_keys, allowed):
    grouped_heads = query_rows_second.reshape(
        query_rows_second.shape[0], KEY_VALUE_HEADS, QUERY_HEADS // KEY_VALUE_HEADS, HEAD_SIZE
    )
    heads_of_keys = rows_of_keys.reshape(rows_of_keys.shape[0], KEY_VALUE_HEADS, HEAD_SIZE)
    scores = jnp.einsum(
        "rkgd,tkd->rkgt", grouped_heads, heads_of_keys, preferred_element_type=jnp.float32
    ) * HEAD_SIZE ** (-0.5)
    return jnp.where(allowed[:, None, None, :], scores, MASKED_SCORE)


def attend_rows(query_rows_second, rows_of_keys, rows_of_values, allowed):
    scores = raw_scores(query_rows_second, rows_of_keys, allowed)
    row_max = jnp.max(scores, axis=-1, keepdims=True)
    exp_scores = jnp.exp(scores - row_max)
    row_totals = jnp.sum(exp_scores, axis=-1, keepdims=True)
    attn_probs = (exp_scores / row_totals).astype(jnp.bfloat16)
    heads_of_values = rows_of_values.reshape(rows_of_values.shape[0], KEY_VALUE_HEADS, HEAD_SIZE)
    heads_mixed = jnp.einsum(
        "rkgt,tkd->rkgd", attn_probs, heads_of_values, preferred_element_type=jnp.float32
    )
    return (
        heads_mixed.reshape(query_rows_second.shape[0], QUERY_HEADS * HEAD_SIZE),
        row_max + jnp.log(row_totals),
    )


def attend_back(
    query_rows_second, rows_of_keys, rows_of_values, allowed, log_totals, mixed_gradient_second
):
    count_of_rows = query_rows_second.shape[0]
    count_of_keys = rows_of_keys.shape[0]
    grouped_heads = query_rows_second.reshape(
        count_of_rows, KEY_VALUE_HEADS, QUERY_HEADS // KEY_VALUE_HEADS, HEAD_SIZE
    )
    heads_of_keys = rows_of_keys.reshape(count_of_keys, KEY_VALUE_HEADS, HEAD_SIZE)
    heads_of_values = rows_of_values.reshape(count_of_keys, KEY_VALUE_HEADS, HEAD_SIZE)
    heads_gradient = mixed_gradient_second.reshape(
        count_of_rows, KEY_VALUE_HEADS, QUERY_HEADS // KEY_VALUE_HEADS, HEAD_SIZE
    )
    attn_probs = jnp.exp(raw_scores(query_rows_second, rows_of_keys, allowed) - log_totals)
    grad_probs = jnp.einsum(
        "rkgd,tkd->rkgt", heads_gradient, heads_of_values, preferred_element_type=jnp.float32
    )
    grad_scores = (
        attn_probs * (grad_probs - jnp.sum(grad_probs * attn_probs, axis=-1, keepdims=True))
    ).astype(jnp.bfloat16)
    queries_gradient = jnp.einsum(
        "rkgt,tkd->rkgd", grad_scores, heads_of_keys, preferred_element_type=jnp.float32
    ) * HEAD_SIZE ** (-0.5)
    keys_gradient = jnp.einsum(
        "rkgt,rkgd->tkd", grad_scores, grouped_heads, preferred_element_type=jnp.float32
    ) * HEAD_SIZE ** (-0.5)
    values_gradient = jnp.einsum(
        "rkgt,rkgd->tkd",
        attn_probs.astype(jnp.bfloat16),
        heads_gradient,
        preferred_element_type=jnp.float32,
    )
    return (
        queries_gradient.reshape(count_of_rows, QUERY_HEADS, HEAD_SIZE),
        keys_gradient.reshape(count_of_keys, KEY_VALUE_HEADS * HEAD_SIZE),
        values_gradient.reshape(count_of_keys, KEY_VALUE_HEADS * HEAD_SIZE),
    )


def layer_forward(inputs, layer_full, positions, allowed):
    mixer_gain, heads_weight, merge_weight, head_gain, feed_gain, expand_weight, reduce_weight = (
        layer_full
    )
    count_of_rows = inputs.shape[0]
    normal_a = scaled(inputs, mixer_gain).astype(jnp.bfloat16)
    projected_output = jnp.dot(normal_a, heads_weight, preferred_element_type=jnp.float32)
    query_rows, heads_of_keys, heads_of_values = heads_of(projected_output, head_gain, positions)
    rows_of_keys, rows_of_values = (
        lax.all_gather(
            heads_of_keys.reshape(count_of_rows, KEY_VALUE_HEADS * HEAD_SIZE).astype(jnp.bfloat16),
            "fsdp",
            axis=0,
            tiled=True,
        ),
        lax.all_gather(heads_of_values.astype(jnp.bfloat16), "fsdp", axis=0, tiled=True),
    )
    heads_mixed, log_totals = attend_rows(
        query_rows.astype(jnp.bfloat16), rows_of_keys, rows_of_values, allowed
    )
    mixed_b = heads_mixed.astype(jnp.bfloat16)
    middle = inputs + jnp.dot(mixed_b, merge_weight, preferred_element_type=jnp.float32)
    normal_b = scaled(middle, feed_gain).astype(jnp.bfloat16)
    joined = jnp.dot(normal_b, expand_weight, preferred_element_type=jnp.float32)
    hidden = gated_unit(joined).astype(jnp.bfloat16)
    result = middle + jnp.dot(hidden, reduce_weight, preferred_element_type=jnp.float32)
    return (
        result,
        (
            inputs,
            normal_a,
            projected_output,
            rows_of_keys,
            rows_of_values,
            log_totals,
            mixed_b,
            middle,
            normal_b,
            joined,
            hidden,
        ),
    )


def layer_backward(upstream, layer_full, saved, positions, allowed):
    mixer_gain, heads_weight, merge_weight, head_gain, feed_gain, expand_weight, reduce_weight = (
        layer_full
    )
    (
        inputs,
        normal_a,
        projected_output,
        rows_of_keys,
        rows_of_values,
        log_totals,
        mixed_b,
        middle,
        normal_b,
        joined,
        hidden,
    ) = saved
    count_of_rows = inputs.shape[0]
    upstream_b = upstream.astype(jnp.bfloat16)
    grad_hidden = times_transposed(upstream_b, reduce_weight)
    unused_joined, gated_back = jax.vjp(gated_unit, joined)
    grad_joined = gated_back(grad_hidden)[0].astype(jnp.bfloat16)
    unused_feed, feed_back = jax.vjp(scaled, middle, feed_gain)
    grad_middle_part, grad_feed = feed_back(times_transposed(grad_joined, expand_weight))
    grad_middle = upstream + grad_middle_part
    grad_middle_b = grad_middle.astype(jnp.bfloat16)
    grad_mixed = times_transposed(grad_middle_b, merge_weight).astype(jnp.bfloat16)
    head_values, heads_back = jax.vjp(
        lambda projected_rows, gain_rows: heads_of(projected_rows, gain_rows, positions),
        projected_output,
        head_gain,
    )
    queries_gradient, grad_keys_all, grad_values_all = attend_back(
        head_values[0].astype(jnp.bfloat16),
        rows_of_keys,
        rows_of_values,
        allowed,
        log_totals,
        grad_mixed,
    )
    keys_gradient, values_gradient = (
        lax.psum_scatter(
            grad_keys_all.astype(jnp.bfloat16), "fsdp", scatter_dimension=0, tiled=True
        ).astype(jnp.float32),
        lax.psum_scatter(
            grad_values_all.astype(jnp.bfloat16), "fsdp", scatter_dimension=0, tiled=True
        ).astype(jnp.float32),
    )
    grad_projected, grad_head = heads_back(
        (
            queries_gradient,
            keys_gradient.reshape(count_of_rows, KEY_VALUE_HEADS, HEAD_SIZE),
            values_gradient,
        )
    )
    grad_projected_b = grad_projected.astype(jnp.bfloat16)
    unused_mixer, mixer_back = jax.vjp(scaled, inputs, mixer_gain)
    grad_inputs_part, grad_mixer = mixer_back(times_transposed(grad_projected_b, heads_weight))
    operands = (
        normal_a,
        grad_projected_b,
        mixed_b,
        grad_middle_b,
        normal_b,
        grad_joined,
        hidden,
        upstream_b,
    )
    return (grad_middle + grad_inputs_part, operands, (grad_mixer, grad_feed, grad_head))


def product_term(left_side, right_side):
    return lax.dot_general(
        left_side, right_side, (((0,), (0,)), ((), ())), preferred_element_type=jnp.float32
    )


def reduce_grads(operands, gain_terms):
    (
        normal_a,
        grad_projected_b,
        mixed_b,
        grad_middle_b,
        normal_b,
        grad_joined,
        hidden,
        upstream_b,
    ) = operands
    heads_gradient = lax.psum_scatter(
        product_term(normal_a, grad_projected_b).astype(jnp.bfloat16),
        "fsdp",
        scatter_dimension=0,
        tiled=True,
    )
    grad_merge = lax.psum_scatter(
        product_term(mixed_b, grad_middle_b).astype(jnp.bfloat16),
        "fsdp",
        scatter_dimension=0,
        tiled=True,
    )
    grad_expand = lax.psum_scatter(
        product_term(normal_b, grad_joined).astype(jnp.bfloat16),
        "fsdp",
        scatter_dimension=0,
        tiled=True,
    )
    grad_reduce = lax.psum_scatter(
        product_term(hidden, upstream_b).astype(jnp.bfloat16),
        "fsdp",
        scatter_dimension=0,
        tiled=True,
    )
    grad_mixer, grad_feed, grad_head = (
        lax.psum_scatter(gain_terms[0], "fsdp", scatter_dimension=0, tiled=True),
        lax.psum_scatter(gain_terms[1], "fsdp", scatter_dimension=0, tiled=True),
        lax.psum_scatter(gain_terms[2], "fsdp", scatter_dimension=0, tiled=True),
    )
    return (
        lax.psum(grad_mixer.astype(jnp.bfloat16), "rep").astype(jnp.float32),
        lax.psum(heads_gradient, "rep").astype(jnp.float32),
        lax.psum(grad_merge, "rep").astype(jnp.float32),
        lax.psum(grad_head.astype(jnp.bfloat16), "rep").astype(jnp.float32),
        lax.psum(grad_feed.astype(jnp.bfloat16), "rep").astype(jnp.float32),
        lax.psum(grad_expand, "rep").astype(jnp.float32),
        lax.psum(grad_reduce, "rep").astype(jnp.float32),
    )


def body(
    section_inputs,
    doc_lengths,
    mixer_gain,
    heads_weight,
    merge_weight,
    head_gain,
    feed_gain,
    expand_weight,
    reduce_weight,
):
    section_index = lax.axis_index("section")
    head_section = section_index == 0
    shard_index = lax.axis_index("fsdp")
    count_of_rows = section_inputs.shape[3]
    sequence_length = count_of_rows * lax.axis_size("fsdp")
    own_rows = section_inputs[0, :, 0]
    micro_count = own_rows.shape[0]
    mixer_part = (
        lax.all_gather(mixer_gain, "fsdp", axis=1, tiled=True),
        lax.all_gather(heads_weight, "fsdp", axis=1, tiled=True),
        lax.all_gather(merge_weight, "fsdp", axis=1, tiled=True),
        lax.all_gather(head_gain, "fsdp", axis=1, tiled=True),
    )
    feed_part = (
        lax.all_gather(feed_gain, "fsdp", axis=1, tiled=True),
        lax.all_gather(expand_weight, "fsdp", axis=1, tiled=True),
        lax.all_gather(reduce_weight, "fsdp", axis=1, tiled=True),
    )
    layer_full = (
        mixer_part[0][0].astype(jnp.float32),
        mixer_part[1][0],
        mixer_part[2][0],
        mixer_part[3][0].astype(jnp.float32),
        feed_part[0][0].astype(jnp.float32),
        feed_part[1][0],
        feed_part[2][0],
    )

    def layout(micro_slot):
        document_index, positions = places(doc_lengths[micro_slot, 0], sequence_length)
        row_start = shard_index * count_of_rows
        doc_rows = lax.dynamic_slice_in_dim(document_index, row_start, count_of_rows)
        own_positions = lax.dynamic_slice_in_dim(positions, row_start, count_of_rows)
        return (own_positions, allowed_mask(doc_rows, row_start, document_index))

    results = jnp.zeros((micro_count, count_of_rows, own_rows.shape[2]), jnp.float32)
    saved_acts = None
    arrived = jnp.zeros((count_of_rows, own_rows.shape[2]), jnp.bfloat16)
    for step_index in range(micro_count + 1):
        slot_raw = step_index - section_index
        is_live = (slot_raw >= 0) & (slot_raw < micro_count)
        micro_slot = jnp.clip(slot_raw, 0, micro_count - 1)
        inputs = jnp.where(
            head_section, own_rows[min(step_index, micro_count - 1)], arrived
        ).astype(jnp.float32)
        positions, allowed = layout(micro_slot)
        result, saved = layer_forward(inputs, layer_full, positions, allowed)
        if saved_acts is None:
            saved_acts = tuple(
                (jnp.zeros((micro_count,) + current.shape, current.dtype) for current in saved)
            )
        saved_acts = tuple(
            (
                jnp.where(is_live, buffer.at[micro_slot].set(current), buffer)
                for buffer, current in zip(saved_acts, saved)
            )
        )
        results = jnp.where(
            is_live & jnp.logical_not(head_section), results.at[micro_slot].set(result), results
        )
        if step_index < micro_count:
            arrived = from_behind(result.astype(jnp.bfloat16), "section", 1)
    gradients = None
    stashed = None
    gain_sums = None
    from_next = jnp.zeros((count_of_rows, own_rows.shape[2]), jnp.bfloat16)
    for step_index in range(micro_count + 1):
        slot_raw = step_index - 1 + section_index
        is_live = (slot_raw >= 0) & (slot_raw < micro_count)
        micro_slot = jnp.clip(slot_raw, 0, micro_count - 1)
        upstream = jnp.where(
            head_section, from_next, own_rows[min(step_index, micro_count - 1)]
        ).astype(jnp.float32)
        upstream = jnp.where(is_live, upstream, 0.0)
        positions, allowed = layout(micro_slot)
        saved = tuple((buffer[micro_slot] for buffer in saved_acts))
        grad_inputs, operands, gain_terms = layer_backward(
            upstream, layer_full, saved, positions, allowed
        )
        results = jnp.where(
            is_live & head_section, results.at[micro_slot].set(grad_inputs), results
        )
        if step_index < micro_count:
            from_next = from_behind(grad_inputs.astype(jnp.bfloat16), "section", -1)
        if stashed is None:
            stashed = tuple(
                (jnp.zeros((micro_count,) + current.shape, current.dtype) for current in operands)
            )
            gain_sums = tuple((jnp.zeros_like(current) for current in gain_terms))
        stashed = tuple(
            (
                jnp.where(is_live, buffer.at[micro_slot].set(current), buffer)
                for buffer, current in zip(stashed, operands)
            )
        )
        gain_sums = tuple(
            (total_so_far + current for total_so_far, current in zip(gain_sums, gain_terms))
        )
    merged = tuple(
        (buffer.reshape((micro_count * count_of_rows,) + buffer.shape[2:]) for buffer in stashed)
    )
    gradients = reduce_grads(merged, gain_sums)
    grad_mixer, heads_gradient, grad_merge, grad_head, grad_feed, grad_expand, grad_reduce = (
        gradients
    )
    return (
        results[None, :, None],
        grad_mixer[None],
        heads_gradient[None],
        grad_merge[None],
        grad_head[None],
        grad_feed[None],
        grad_expand[None],
        grad_reduce[None],
    )


MESH = pl.DeviceIdType.MESH
MERGED = QUERY_HEADS // KEY_VALUE_HEADS * HEAD_SIZE
JOINT = MERGED + 2 * HEAD_SIZE
VMEM_BYTES = 63 * 2**20


def mm(left, right):
    return jnp.dot(left, right, preferred_element_type=jnp.float32)


def mm_t(left, right):
    return lax.dot_general(
        left, right, (((1,), (1,)), ((), ())), preferred_element_type=jnp.float32
    )


def t_mm(left, right):
    return lax.dot_general(
        left, right, (((0,), (0,)), ((), ())), preferred_element_type=jnp.float32
    )


def remote(src, dst, send, recv, device):
    return pltpu.make_async_remote_copy(
        src_ref=src,
        dst_ref=dst,
        send_sem=send,
        recv_sem=recv,
        device_id=device,
        device_id_type=MESH,
    )


class Place:
    def __init__(self):
        self.index = lax.axis_index("fsdp")
        self.core = lax.rem(self.index, 2)
        self.chip = lax.div(self.index, 2)
        self.x = lax.rem(self.chip, 2)
        self.y = lax.div(self.chip, 2)
        self.x_peer = {"fsdp": self.index + 2 - 4 * self.x}
        self.y_peer = {"fsdp": self.index + 4 - 8 * self.y}
        self.core_peer = {"fsdp": self.index + 1 - 2 * self.core}
        self.section = lax.axis_index("section")
        self.section_peer = {"section": 1 - self.section}

    def chip_at(self, rel):
        x, y = self.x, self.y
        if rel in (1, 3):
            x = 1 - x
        if rel in (2, 3):
            y = 1 - y
        return 2 * y + x

    def greet(self):
        barrier = pltpu.get_barrier_semaphore()
        peers = (self.x_peer, self.y_peer, self.core_peer, self.section_peer)
        for peer in peers:
            pl.semaphore_signal(barrier, inc=1, device_id=peer, device_id_type=MESH)
        pl.semaphore_wait(barrier, len(peers))


class Gather:
    def __init__(self, place, full, send, recv, rows):
        half = rows // 2

        def span(rel, part=None):
            first = (2 * place.chip_at(rel) + place.core) * rows
            if part is None:
                return pl.ds(pl.multiple_of(first, rows), rows)
            return pl.ds(pl.multiple_of(first + part * half, half), half)

        def copy(at, piece, peer):
            block = full.at[piece]
            return remote(block, block, send.at[at], recv.at[at], peer)

        self.copies = [
            copy(0, span(0, 1), place.x_peer),
            copy(1, span(0, 0), place.x_peer),
            copy(2, span(0, 0), place.y_peer),
            copy(3, span(0, 1), place.y_peer),
            copy(4, span(0), place.core_peer),
            copy(5, span(1, 1), place.y_peer),
            copy(6, span(2, 0), place.x_peer),
            copy(7, span(1), place.core_peer),
            copy(8, span(2), place.core_peer),
            copy(9, span(3), place.core_peer),
        ]

    def start(self):
        for at in (0, 2, 4, 1, 3):
            self.copies[at].start()

    def relay(self):
        self.copies[0].wait_recv()
        self.copies[5].start()
        self.copies[2].wait_recv()
        self.copies[6].start()

    def near(self):
        self.copies[1].wait_recv()
        self.copies[7].start()
        self.copies[3].wait_recv()
        self.copies[8].start()

    def far(self):
        self.copies[5].wait_recv()
        self.copies[6].wait_recv()
        self.copies[9].start()

    def wait(self, at):
        self.copies[at].wait_recv()

    def finish(self):
        for entry in self.copies:
            entry.wait_send()

    def over_blocks(self, block):
        self.start()
        self.wait(4)
        block(0)
        self.relay()
        self.near()
        self.wait(7)
        block(1)
        self.wait(8)
        block(2)
        self.far()
        self.wait(9)
        block(3)


class Scatter:
    def __init__(self, place, held, to_core, from_core, to_x, to_y, from_x, from_y, send, recv, rows):
        self.place, self.held, self.to_core, self.from_core = place, held, to_core, from_core
        self.to_x, self.to_y, self.from_x, self.from_y = to_x, to_y, from_x, from_y
        self.rows, self.half = rows, rows // 2

        def copy(at, src, dst, peer):
            return remote(src, dst, send.at[at], recv.at[at], peer)

        self.copies = [
            copy(rel, to_core.at[rel], from_core.at[rel], place.core_peer) for rel in range(4)
        ] + [
            copy(4, to_x.at[0], from_x.at[0], place.x_peer),
            copy(5, to_y.at[0], from_y.at[0], place.y_peer),
            copy(6, to_x.at[1], from_x.at[1], place.x_peer),
            copy(7, to_y.at[1], from_y.at[1], place.y_peer),
            copy(8, to_y.at[2], from_y.at[2], place.y_peer),
            copy(9, to_x.at[2], from_x.at[2], place.x_peer),
        ]

    def put(self, rel, product, width):
        step, rows, mine = 512, self.rows, self.place.core == 0

        @pl.loop(0, width // step)
        def _(at):
            columns = pl.ds(pl.multiple_of(at * step, step), step)
            value = product(columns)
            low, high = value[:rows], value[rows:]
            self.held[rel, :, columns] = jnp.where(mine, low, high)
            self.to_core[rel, :, columns] = jnp.where(mine, high, low).astype(jnp.bfloat16)

        self.copies[rel].start()

    def pair(self, rel):
        self.copies[rel].wait_recv()
        half, held = self.half, self.held

        @pl.loop(0, self.rows // 16)
        def _(at):
            span = pl.ds(pl.multiple_of(at * 16, 16), 16)
            held[rel, span, :] += self.from_core[rel, span, :].astype(jnp.float32)

        if rel == 3:
            self.to_x[0] = held[3, :half].astype(jnp.bfloat16)
            self.copies[4].start()
            self.to_y[0] = held[3, half:].astype(jnp.bfloat16)
            self.copies[5].start()
        if rel == 1:
            self.to_x[1] = held[1, :half].astype(jnp.bfloat16)
            self.copies[6].start()
        if rel == 2:
            self.to_y[1] = held[2, half:].astype(jnp.bfloat16)
            self.copies[7].start()

    def relay(self):
        half, held = self.half, self.held
        self.copies[4].wait_recv()
        self.to_y[2] = (held[2, :half] + self.from_x[0].astype(jnp.float32)).astype(jnp.bfloat16)
        self.copies[8].start()
        self.copies[5].wait_recv()
        self.to_x[2] = (held[1, half:] + self.from_y[0].astype(jnp.float32)).astype(jnp.bfloat16)
        self.copies[9].start()

    def total(self, add):
        for at in (6, 7, 8, 9):
            self.copies[at].wait_recv()
        count = self.half // 16

        @pl.loop(0, count)
        def _(at):
            span = pl.ds(pl.multiple_of(at * 16, 16), 16)
            low = self.held[0, span, :] + self.from_x[1, span, :].astype(jnp.float32)
            add(span, low + self.from_y[2, span, :].astype(jnp.float32))

        @pl.loop(0, count)
        def _(at):
            span = pl.ds(pl.multiple_of(at * 16, 16), 16)
            below = pl.ds(pl.multiple_of(self.half + at * 16, 16), 16)
            high = self.held[0, below, :] + self.from_y[1, span, :].astype(jnp.float32)
            add(below, high + self.from_x[2, span, :].astype(jnp.float32))

        for entry in self.copies:
            entry.wait_send()


def by_rows(count, body):
    @pl.loop(0, count // 16)
    def _(at):
        body(pl.ds(pl.multiple_of(at * 16, 16), 16))


def inverse_size(values):
    return lax.rsqrt(jnp.mean(values * values, axis=-1, keepdims=True) + NORM_EPS)


def norm_back(values, gain, upstream):
    size = inverse_size(values)
    scaled_up = upstream * gain
    back = size * scaled_up - values * (
        size * size * size * jnp.mean(values * scaled_up, axis=-1, keepdims=True)
    )
    return back, upstream * values * size


def turn(values, cosine, sine):
    return values * cosine + pltpu.roll(values, HEAD_SIZE // 2, 1) * sine


def turn_back(values, cosine, sine):
    return values * cosine + pltpu.roll(values * sine, HEAD_SIZE // 2, 1)


def probabilities(queries, keys, first_keys, first_row):
    scores = mm_t(queries, keys) * HEAD_SIZE ** (-0.5)
    key_index = lax.broadcasted_iota(jnp.int32, scores.shape, 1)
    row_index = first_row + lax.broadcasted_iota(jnp.int32, scores.shape, 0)
    allowed = (key_index >= first_keys) & (key_index <= row_index)
    scores = jnp.where(allowed, scores, MASKED_SCORE)
    powers = jnp.exp(scores - jnp.max(scores, axis=-1, keepdims=True))
    return powers / jnp.sum(powers, axis=-1, keepdims=True)


def forward_kernel(
    rows,
    own_ref,
    gains_ref,
    head_gain_ref,
    cos_ref,
    sin_ref,
    first_ref,
    heads_w,
    merge_w,
    expand_w,
    reduce_w,
    out_results,
    out_inputs,
    out_normal_a,
    out_projected,
    out_heads,
    out_mixed,
    out_middle,
    out_normal_b,
    out_joined,
    out_hidden,
    wh,
    wm,
    we,
    wr,
    current,
    arrived,
    full_a,
    full_b,
    cosine,
    sine,
    first_key,
    projected,
    heads,
    mixed,
    joined,
    hidden,
    held,
    to_core,
    core_a,
    core_b,
    to_x,
    to_y,
    x_a,
    y_a,
    x_b,
    y_b,
    middle,
    result,
    result_b,
    load_sem,
    save_sem,
    table_sem,
    hand_send,
    hand_recv,
    ga_send,
    ga_recv,
    sa_send,
    sa_recv,
    gb_send,
    gb_recv,
    sb_send,
    sb_recv,
):
    place = Place()
    micro_count = own_ref.shape[0]
    chip_rows = 2 * rows
    width = current.shape[1]
    hidden_width = wr.shape[0]
    loads = [
        pltpu.make_async_copy(src, dst, load_sem.at[at])
        for at, (src, dst) in enumerate(
            ((heads_w, wh), (merge_w, wm), (expand_w, we), (reduce_w, wr))
        )
    ]
    for load in loads:
        load.start()
    place.greet()
    head = place.section == 0
    own_rows = pl.ds(pl.multiple_of(place.index * rows, rows), rows)

    def block_rows(rel):
        return pl.ds(pl.multiple_of(place.chip_at(rel) * chip_rows, chip_rows), chip_rows)

    def hand(step):
        return remote(
            result_b, arrived.at[step], hand_send.at[step], hand_recv.at[step], place.section_peer
        )

    @pl.loop(0, micro_count + 1)
    def _(step):
        slot = jnp.clip(step - place.section, 0, micro_count - 1)
        tables = [
            pltpu.make_async_copy(src.at[slot], dst, table_sem.at[at])
            for at, (src, dst) in enumerate(
                ((cos_ref, cosine), (sin_ref, sine), (first_ref, first_key))
            )
        ]
        for table in tables:
            table.start()

        @pl.when(head)
        def _():
            current[...] = own_ref[slot]

        @pl.when(jnp.logical_not(head) & (step == 0))
        def _():
            current[...] = jnp.zeros_like(current)

        @pl.when(jnp.logical_not(head) & (step > 0))
        def _():
            hand(step - 1).wait_recv()
            current[...] = arrived[step - 1]

        def save(at, src, dst):
            copy = pltpu.make_async_copy(src, dst.at[slot], save_sem.at[at])
            copy.start()
            return copy

        saves = [save(0, current, out_inputs)]

        def enter(span):
            values = current[span, :].astype(jnp.float32)
            base = pl.multiple_of(place.index * rows + span.start, 16)
            full_a[pl.ds(base, 16), :] = (
                values * inverse_size(values) * gains_ref[0:1, :]
            ).astype(jnp.bfloat16)

        by_rows(rows, enter)
        for table in tables:
            table.wait()

        @pl.when(step == 0)
        def _():
            loads[0].wait()

        gather = Gather(place, full_a, ga_send, ga_recv, rows)

        def heads_block(rel):
            span = block_rows(rel)
            values = mm(full_a[span, :], wh[...])
            projected[span, :] = values
            for at in range(3):
                columns = pl.ds(at * HEAD_SIZE, HEAD_SIZE)
                one = values[:, at * HEAD_SIZE : (at + 1) * HEAD_SIZE]
                gain = head_gain_ref[0:1, :] if at < 2 else head_gain_ref[1:2, :]
                heads[span, columns] = turn(
                    one * inverse_size(one) * gain, cosine[span, :], sine[span, :]
                ).astype(jnp.bfloat16)
            heads[span, 3 * HEAD_SIZE :] = values[:, 3 * HEAD_SIZE :].astype(jnp.bfloat16)

        gather.over_blocks(heads_block)
        saves += [
            save(1, full_a, out_normal_a),
            save(2, projected, out_projected),
            save(3, heads, out_heads),
        ]

        @pl.when(step == 0)
        def _():
            loads[1].wait()

        scatter = Scatter(
            place, held, to_core, core_a, to_x, to_y, x_a, y_a, sa_send, sa_recv, rows
        )

        def attend_block(rel):
            first_row = place.chip_at(rel) * chip_rows
            span = block_rows(rel)
            for at in range(2):
                columns = pl.ds(at * HEAD_SIZE, HEAD_SIZE)
                probs = probabilities(
                    heads[span, columns],
                    heads[:, 2 * HEAD_SIZE : 3 * HEAD_SIZE],
                    first_key[span, :],
                    first_row,
                )
                mixed[span, columns] = mm(
                    probs.astype(jnp.bfloat16), heads[:, 3 * HEAD_SIZE :]
                ).astype(jnp.bfloat16)
            scatter.put(rel, lambda columns: mm(mixed[span, :], wm[:, columns]), width)

        attend_block(3)
        attend_block(2)
        scatter.pair(3)
        attend_block(1)
        scatter.pair(2)
        attend_block(0)
        scatter.pair(1)
        saves.append(save(4, mixed, out_mixed))
        scatter.relay()
        scatter.pair(0)

        def residual(span, value):
            values = value + current[span, :].astype(jnp.float32)
            middle[span, :] = values
            base = pl.multiple_of(place.index * rows + span.start, 16)
            full_b[pl.ds(base, 16), :] = (
                values * inverse_size(values) * gains_ref[1:2, :]
            ).astype(jnp.bfloat16)

        scatter.total(residual)
        gather.finish()
        saves.append(save(5, middle, out_middle))
        for copy in saves[:5]:
            copy.wait()

        @pl.when(step == 0)
        def _():
            loads[2].wait()
            loads[3].wait()

        gather_b = Gather(place, full_b, gb_send, gb_recv, rows)
        scatter_b = Scatter(
            place, held, to_core, core_b, to_x, to_y, x_b, y_b, sb_send, sb_recv, rows
        )

        joined_copies = {}

        def feed_block(rel):
            span = block_rows(rel)
            stage = joined.at[rel % 2]
            if rel >= 2:
                joined_copies[rel - 2].wait()

            @pl.loop(0, hidden_width // 256)
            def _(at):
                columns = pl.ds(pl.multiple_of(at * 256, 256), 256)
                later = pl.ds(pl.multiple_of(hidden_width + at * 256, 256), 256)
                gate = mm(full_b[span, :], we[:, columns])
                up = mm(full_b[span, :], we[:, later])
                stage[:, columns] = gate
                stage[:, later] = up
                hidden[span, columns] = (gate * jax.nn.sigmoid(gate) * up).astype(jnp.bfloat16)

            copy = pltpu.make_async_copy(stage, out_joined.at[slot, span], save_sem.at[8 + rel % 2])
            copy.start()
            joined_copies[rel] = copy
            scatter_b.put(rel, lambda columns: mm(hidden[span, :], wr[:, columns]), width)
            if rel >= 1:
                scatter_b.pair(rel - 1)

        gather_b.over_blocks(feed_block)
        later_saves = [save(6, full_b, out_normal_b), save(7, hidden, out_hidden)]
        scatter_b.pair(3)
        scatter_b.relay()

        @pl.when(head & (step > 0))
        def _():
            hand(step - 1).wait_send()

        def finish(span, value):
            values = value + middle[span, :]
            result[span, :] = values
            result_b[span, :] = values.astype(jnp.bfloat16)

        scatter_b.total(finish)

        @pl.when(head & (step < micro_count))
        def _():
            hand(step).start()

        final = save(0, result, out_results)
        gather_b.finish()
        for copy in [saves[5]] + later_saves + [joined_copies[2], joined_copies[3], final]:
            copy.wait()


def backward_kernel(
    rows,
    own_ref,
    gains_ref,
    head_gain_ref,
    cos_ref,
    sin_ref,
    first_ref,
    heads_w,
    merge_w,
    expand_w,
    reduce_w,
    in_inputs,
    in_projected,
    in_heads,
    in_middle,
    in_joined,
    out_results,
    out_upstream,
    out_grad_joined,
    out_grad_middle,
    out_grad_projected,
    out_gains,
    out_head_gain,
    wh,
    wm,
    we,
    wr,
    arrived,
    current,
    full_a,
    full_b,
    cosine,
    sine,
    first_key,
    projected,
    heads,
    grad_mixed,
    grad_queries,
    grad_keys,
    grad_values,
    grad_projected,
    joined,
    grad_joined,
    held,
    to_core,
    core_a,
    core_b,
    to_x,
    to_y,
    x_a,
    y_a,
    x_b,
    y_b,
    middle,
    inputs,
    result,
    load_sem,
    save_sem,
    table_sem,
    joined_sem,
    hand_send,
    hand_recv,
    ga_send,
    ga_recv,
    sa_send,
    sa_recv,
    gb_send,
    gb_recv,
    sb_send,
    sb_recv,
):
    place = Place()
    micro_count = own_ref.shape[0]
    chip_rows = 2 * rows
    width = current.shape[1]
    hidden_width = wr.shape[0]
    length = full_a.shape[0]
    loads = [
        pltpu.make_async_copy(src, dst, load_sem.at[at])
        for at, (src, dst) in enumerate(
            ((reduce_w, wr), (expand_w, we), (merge_w, wm), (heads_w, wh))
        )
    ]
    for load in loads:
        load.start()
    place.greet()
    head = place.section == 0
    own_rows = pl.ds(pl.multiple_of(place.index * rows, rows), rows)

    def block_rows(rel):
        return pl.ds(pl.multiple_of(place.chip_at(rel) * chip_rows, chip_rows), chip_rows)

    def hand(step):
        return remote(
            current, arrived.at[step], hand_send.at[step], hand_recv.at[step], place.section_peer
        )

    @pl.loop(0, micro_count + 1)
    def _(step):
        slot = jnp.clip(step - 1 + place.section, 0, micro_count - 1)
        tables = [
            pltpu.make_async_copy(src.at[slot], dst, table_sem.at[at])
            for at, (src, dst) in enumerate(
                (
                    (in_middle, middle),
                    (cos_ref, cosine),
                    (sin_ref, sine),
                    (first_ref, first_key),
                    (in_projected, projected),
                    (in_heads, heads),
                    (in_inputs, inputs),
                )
            )
        ]
        for table in tables:
            table.start()

        def joined_load(rel):
            return pltpu.make_async_copy(
                in_joined.at[slot, block_rows(rel)], joined.at[rel % 2], joined_sem.at[rel % 2]
            )

        joined_load(0).start()
        joined_load(1).start()

        @pl.when(jnp.logical_not(head) & (step > 0))
        def _():
            hand(step - 1).wait_send()

        @pl.when(jnp.logical_not(head))
        def _():
            current[...] = own_ref[slot]

        @pl.when(head & (step == 0))
        def _():
            current[...] = jnp.zeros_like(current)

        @pl.when(head & (step > 0))
        def _():
            hand(step - 1).wait_recv()
            current[...] = arrived[step - 1]

        full_a[own_rows, :] = current[...]

        def save(at, src, dst):
            copy = pltpu.make_async_copy(src, dst.at[slot], save_sem.at[at])
            copy.start()
            return copy

        @pl.when(step == 0)
        def _():
            loads[0].wait()
            loads[1].wait()

        gather = Gather(place, full_a, ga_send, ga_recv, rows)
        scatter = Scatter(
            place, held, to_core, core_a, to_x, to_y, x_a, y_a, sa_send, sa_recv, rows
        )
        grad_copies = {}

        def feed_block(rel):
            span = block_rows(rel)
            stage, out = joined.at[rel % 2], grad_joined.at[rel % 2]
            joined_load(rel).wait()
            if rel >= 2:
                grad_copies[rel - 2].wait()

            @pl.loop(0, hidden_width // 256)
            def _(at):
                columns = pl.ds(pl.multiple_of(at * 256, 256), 256)
                later = pl.ds(pl.multiple_of(hidden_width + at * 256, 256), 256)
                grad = mm_t(full_a[span, :], wr[columns, :])
                gate, up = stage[:, columns], stage[:, later]
                sigmoid = jax.nn.sigmoid(gate)
                unit = gate * sigmoid
                out[:, columns] = (grad * up * (sigmoid + unit * (1.0 - sigmoid))).astype(
                    jnp.bfloat16
                )
                out[:, later] = (grad * unit).astype(jnp.bfloat16)

            if rel < 2:
                joined_load(rel + 2).start()
            copy = pltpu.make_async_copy(
                out, out_grad_joined.at[slot, span], save_sem.at[8 + rel % 2]
            )
            copy.start()
            grad_copies[rel] = copy
            scatter.put(rel, lambda columns: mm_t(out[...], we[columns, :]), width)
            if rel >= 1:
                scatter.pair(rel - 1)

        gather.over_blocks(feed_block)
        upstream_save = save(0, full_a, out_upstream)
        scatter.pair(3)
        scatter.relay()
        for table in tables:
            table.wait()
        out_gains[slot, 1:2, :] = jnp.zeros((1, width), jnp.float32)

        def feed_norm(span, value):
            back, gain_term = norm_back(middle[span, :], gains_ref[1:2, :], value)
            out_gains[slot, 1:2, :] += jnp.sum(gain_term, axis=0, keepdims=True)
            total = back + current[span, :].astype(jnp.float32)
            result[span, :] = total
            base = pl.multiple_of(place.index * rows + span.start, 16)
            full_b[pl.ds(base, 16), :] = total.astype(jnp.bfloat16)

        scatter.total(feed_norm)
        gather.finish()
        for copy in (upstream_save, grad_copies[2], grad_copies[3]):
            copy.wait()

        @pl.when(step == 0)
        def _():
            loads[2].wait()
            loads[3].wait()

        gather_b = Gather(place, full_b, gb_send, gb_recv, rows)
        scatter_b = Scatter(
            place, held, to_core, core_b, to_x, to_y, x_b, y_b, sb_send, sb_recv, rows
        )

        def mixed_block(rel):
            span = block_rows(rel)
            grad_mixed[span, :] = mm_t(full_b[span, :], wm[...]).astype(jnp.bfloat16)

        gather_b.over_blocks(mixed_block)
        middle_save = save(1, full_b, out_grad_middle)
        grad_keys[...] = jnp.zeros_like(grad_keys)
        grad_values[...] = jnp.zeros_like(grad_values)

        for block in range(length // chip_rows):
            span = pl.ds(block * chip_rows, chip_rows)
            seen = (block + 1) * chip_rows
            keys = heads[:seen, 2 * HEAD_SIZE : 3 * HEAD_SIZE]
            values = heads[:seen, 3 * HEAD_SIZE :]
            for at in range(2):
                columns = pl.ds(at * HEAD_SIZE, HEAD_SIZE)
                queries = heads[span, columns]
                grad = grad_mixed[span, columns]
                probs = probabilities(queries, keys, first_key[span, :], block * chip_rows)
                grad_probs = mm_t(grad, values)
                grad_scores = (
                    probs * (grad_probs - jnp.sum(probs * grad_probs, axis=-1, keepdims=True))
                ).astype(jnp.bfloat16)
                grad_queries[span, columns] = mm(grad_scores, keys) * HEAD_SIZE ** (-0.5)
                grad_keys[:seen, :] += t_mm(grad_scores, queries) * HEAD_SIZE ** (-0.5)
                grad_values[:seen, :] += t_mm(probs.astype(jnp.bfloat16), grad)

        out_head_gain[slot] = jnp.zeros_like(out_head_gain[slot])

        def project_block(rel):
            span = block_rows(rel)
            for at in range(3):
                columns = pl.ds(at * HEAD_SIZE, HEAD_SIZE)
                which = 0 if at < 2 else 1
                upstream = grad_queries[span, columns] if at < 2 else grad_keys[span, :]
                back, gain_term = norm_back(
                    projected[span, columns],
                    head_gain_ref[which : which + 1, :],
                    turn_back(upstream, cosine[span, :], sine[span, :]),
                )
                out_head_gain[slot, which : which + 1, :] += jnp.sum(
                    gain_term, axis=0, keepdims=True
                )
                grad_projected[span, columns] = back.astype(jnp.bfloat16)
            grad_projected[span, 3 * HEAD_SIZE :] = grad_values[span, :].astype(jnp.bfloat16)
            scatter_b.put(rel, lambda columns: mm_t(grad_projected[span, :], wh[columns, :]), width)

        project_block(3)
        project_block(2)
        scatter_b.pair(3)
        project_block(1)
        scatter_b.pair(2)
        project_block(0)
        scatter_b.pair(1)
        projected_save = save(2, grad_projected, out_grad_projected)
        scatter_b.relay()
        scatter_b.pair(0)
        out_gains[slot, 0:1, :] = jnp.zeros((1, width), jnp.float32)

        def mixer_norm(span, value):
            back, gain_term = norm_back(
                inputs[span, :].astype(jnp.float32), gains_ref[0:1, :], value
            )
            out_gains[slot, 0:1, :] += jnp.sum(gain_term, axis=0, keepdims=True)
            total = back + result[span, :]
            result[span, :] = total
            current[span, :] = total.astype(jnp.bfloat16)

        scatter_b.total(mixer_norm)

        @pl.when(jnp.logical_not(head) & (step < micro_count))
        def _():
            hand(step).start()

        final = save(3, result, out_results)
        gather_b.finish()
        for copy in (middle_save, projected_save, final):
            copy.wait()


def sems(*counts):
    return [pltpu.SemaphoreType.DMA((count,)) for count in counts]


def vmem(*shapes):
    return [pltpu.VMEM(shape, dtype) for *shape, dtype in shapes]


def any_spec():
    return pl.BlockSpec(memory_space=pl.ANY)


def vmem_spec():
    return pl.BlockSpec(memory_space=pltpu.VMEM)


def exchange_buffers(rows, width):
    half, b16 = rows // 2, jnp.bfloat16
    return vmem(
        (4, rows, width, jnp.float32),
        (4, rows, width, b16),
        (4, rows, width, b16),
        (4, rows, width, b16),
        *(((3, half, width, b16),) * 6),
    )


def run_forward(own, gains, head_gain, cosine, sine, first_key, weights):
    micro, rows, width = own.shape
    length = cosine.shape[1]
    hidden_width = weights[3].shape[0]
    f32, b16 = jnp.float32, jnp.bfloat16
    shape = jax.ShapeDtypeStruct
    return pl.pallas_call(
        functools.partial(forward_kernel, rows),
        out_shape=(
            shape((micro, rows, width), f32),
            shape((micro, rows, width), b16),
            shape((micro, length, width), b16),
            shape((micro, length, JOINT), f32),
            shape((micro, length, JOINT), b16),
            shape((micro, length, MERGED), b16),
            shape((micro, rows, width), f32),
            shape((micro, length, width), b16),
            shape((micro, length, 2 * hidden_width), f32),
            shape((micro, length, hidden_width), b16),
        ),
        in_specs=[vmem_spec()] * 3 + [any_spec()] * 7,
        out_specs=(any_spec(),) * 10,
        scratch_shapes=vmem(
            (width, JOINT, b16),
            (MERGED, width, b16),
            (width, 2 * hidden_width, b16),
            (hidden_width, width, b16),
            (rows, width, b16),
            (micro, rows, width, b16),
            (length, width, b16),
            (length, width, b16),
            (length, HEAD_SIZE, f32),
            (length, HEAD_SIZE, f32),
            (length, 1, jnp.int32),
            (length, JOINT, f32),
            (length, JOINT, b16),
            (length, MERGED, b16),
            (2, 2 * rows, 2 * hidden_width, f32),
            (length, hidden_width, b16),
        )
        + exchange_buffers(rows, width)
        + vmem((rows, width, f32), (rows, width, f32), (rows, width, b16))
        + sems(4, 10, 3, micro, micro, *((10,) * 8)),
        compiler_params=pltpu.CompilerParams(
            collective_id=1, has_side_effects=True, vmem_limit_bytes=VMEM_BYTES
        ),
    )(own, gains, head_gain, cosine, sine, first_key, *weights)


def run_backward(own, gains, head_gain, cosine, sine, first_key, weights, saved):
    micro, rows, width = own.shape
    length = cosine.shape[1]
    hidden_width = weights[3].shape[0]
    f32, b16 = jnp.float32, jnp.bfloat16
    shape = jax.ShapeDtypeStruct
    return pl.pallas_call(
        functools.partial(backward_kernel, rows),
        out_shape=(
            shape((micro, rows, width), f32),
            shape((micro, length, width), b16),
            shape((micro, length, 2 * hidden_width), b16),
            shape((micro, length, width), b16),
            shape((micro, length, JOINT), b16),
            shape((micro, 2, width), f32),
            shape((micro, 2, HEAD_SIZE), f32),
        ),
        in_specs=[vmem_spec()] * 3 + [any_spec()] * 12,
        out_specs=(any_spec(),) * 5 + (vmem_spec(),) * 2,
        scratch_shapes=vmem(
            (width, JOINT, b16),
            (MERGED, width, b16),
            (width, 2 * hidden_width, b16),
            (hidden_width, width, b16),
            (micro, rows, width, b16),
            (rows, width, b16),
            (length, width, b16),
            (length, width, b16),
            (length, HEAD_SIZE, f32),
            (length, HEAD_SIZE, f32),
            (length, 1, jnp.int32),
            (length, JOINT, f32),
            (length, JOINT, b16),
            (length, MERGED, b16),
            (length, MERGED, f32),
            (length, HEAD_SIZE, f32),
            (length, HEAD_SIZE, f32),
            (length, JOINT, b16),
            (2, 2 * rows, 2 * hidden_width, f32),
            (2, 2 * rows, 2 * hidden_width, b16),
        )
        + exchange_buffers(rows, width)
        + vmem((rows, width, f32), (rows, width, b16), (rows, width, f32))
        + sems(4, 10, 7, 2, micro, micro, *((10,) * 8)),
        compiler_params=pltpu.CompilerParams(
            collective_id=2, has_side_effects=True, vmem_limit_bytes=VMEM_BYTES
        ),
    )(own, gains, head_gain, cosine, sine, first_key, *weights, *saved)


def position_tables(lengths, length):
    document_index, positions = places(lengths, length)
    half_width = HEAD_SIZE // 2
    frequency = jnp.exp(
        jnp.arange(half_width, dtype=jnp.float32) * (-2.0 * math.log(ROPE_BASE) / HEAD_SIZE)
    )
    angles = positions.astype(jnp.float32)[:, None] * frequency[None, :]
    cosine, sine = jnp.cos(angles), jnp.sin(angles)
    first_key = jnp.arange(length, dtype=jnp.int32) - positions
    return (
        jnp.concatenate([cosine, cosine], axis=-1),
        jnp.concatenate([-sine, sine], axis=-1),
        first_key[:, None],
    )


def tensor_parallel_body(
    section_inputs,
    doc_lengths,
    mixer_gain,
    heads_weight,
    merge_weight,
    head_gain,
    feed_gain,
    expand_weight,
    reduce_weight,
):
    shards = lax.axis_size("fsdp")
    own = section_inputs[0, :, 0]
    micro, rows, width = own.shape
    length = rows * shards
    depth = heads_weight.shape[1]
    hidden_width = reduce_weight.shape[1]
    query_width = QUERY_HEADS * HEAD_SIZE

    def by_shard(weight, parts):
        return weight.reshape(weight.shape[0], parts, shards, -1).swapaxes(0, 2)

    heads_parts = heads_weight[0]
    pieces = jnp.concatenate(
        [
            heads_parts[:, :query_width].reshape(depth, shards, MERGED),
            heads_parts[:, query_width : query_width + shards * HEAD_SIZE].reshape(
                depth, shards, HEAD_SIZE
            ),
            heads_parts[:, query_width + shards * HEAD_SIZE :].reshape(depth, shards, HEAD_SIZE),
        ],
        axis=-1,
    ).swapaxes(0, 1)
    expand_pieces = (
        expand_weight[0]
        .reshape(depth, 2, shards, hidden_width)
        .transpose(2, 0, 1, 3)
        .reshape(shards, depth, 2 * hidden_width)
    )
    heads_full = lax.all_to_all(pieces, "fsdp", 0, 0, tiled=True).reshape(width, JOINT)
    expand_full = lax.all_to_all(expand_pieces, "fsdp", 0, 0, tiled=True).reshape(
        width, 2 * hidden_width
    )
    weights = (heads_full, merge_weight[0], expand_full, reduce_weight[0])
    all_gains = lax.all_gather(
        jnp.concatenate([mixer_gain[0], feed_gain[0], head_gain[0]]), "fsdp", axis=0
    ).astype(jnp.float32)
    gains = jnp.stack(
        [all_gains[:, :depth].reshape(-1), all_gains[:, depth : 2 * depth].reshape(-1)]
    )
    head_gains = all_gains[:, 2 * depth :].reshape(2, HEAD_SIZE)
    tables = [position_tables(doc_lengths[at, 0], length) for at in range(micro)]
    cosine, sine, first_key = (jnp.stack(entry) for entry in zip(*tables))

    (
        results,
        inputs,
        normal_a,
        projected,
        heads,
        mixed,
        middle,
        normal_b,
        joined,
        hidden,
    ) = run_forward(own, gains, head_gains, cosine, sine, first_key, weights)
    grad_results, upstream, grad_joined, grad_middle, grad_projected, gain_terms, head_terms = (
        run_backward(
            own,
            gains,
            head_gains,
            cosine,
            sine,
            first_key,
            weights,
            (inputs, projected, heads, middle, joined),
        )
    )

    def product(left, right):
        return product_term(
            left.reshape(micro * length, -1), right.reshape(micro * length, -1)
        ).astype(jnp.bfloat16)

    def with_replica(term):
        other = lax.ppermute(term, "rep", [(0, 1), (1, 0)])
        return term.astype(jnp.float32) + other.astype(jnp.float32)

    def to_owners(term):
        return lax.all_to_all(term.reshape(shards, depth, -1), "fsdp", 0, 0, tiled=True)

    grad_reduce = with_replica(product(hidden, upstream))
    expand_term = to_owners(product(normal_b, grad_joined))
    grad_expand = with_replica(
        expand_term.reshape(shards, depth, 2, hidden_width)
        .transpose(1, 2, 0, 3)
        .reshape(depth, 2 * shards * hidden_width)
    )
    grad_merge = with_replica(product(mixed, grad_middle))
    heads_term = to_owners(product(normal_a, grad_projected)).swapaxes(0, 1)
    grad_heads = with_replica(
        jnp.concatenate(
            [
                heads_term[:, :, :MERGED].reshape(depth, -1),
                heads_term[:, :, MERGED : MERGED + HEAD_SIZE].reshape(depth, -1),
                heads_term[:, :, MERGED + HEAD_SIZE :].reshape(depth, -1),
            ],
            axis=-1,
        )
    )
    terms = jnp.concatenate(
        [jnp.sum(gain_terms, axis=0).reshape(-1), jnp.sum(head_terms, axis=0).reshape(-1)]
    )
    sums = lax.psum(terms, ("fsdp", "rep"))
    index = lax.axis_index("fsdp")

    def own_part(first, count):
        return lax.dynamic_slice_in_dim(sums, first + index * count, count)[None]

    head_count = head_gain.shape[1]
    return (
        jnp.where(lax.axis_index("section") == 0, grad_results, results)[None, :, None],
        own_part(0, depth),
        grad_heads[None],
        grad_merge[None],
        own_part(2 * width, head_count),
        own_part(width, depth),
        grad_expand[None],
        grad_reduce[None],
    )


def solution(mesh):
    plane = mesh.shape["fsdp"] == PLANE
    return jax.shard_map(
        tensor_parallel_body if plane else body,
        mesh=mesh,
        in_specs=(
            P("section", None, "rep", "fsdp", None),
            P(None, "rep", None),
            P("section", "fsdp"),
            P("section", "fsdp", None),
            P("section", "fsdp", None),
            P("section", "fsdp"),
            P("section", "fsdp"),
            P("section", "fsdp", None),
            P("section", "fsdp", None),
        ),
        out_specs=(
            P("section", None, "rep", "fsdp", None),
            P("section", "fsdp"),
            P("section", "fsdp", None),
            P("section", "fsdp", None),
            P("section", "fsdp"),
            P("section", "fsdp"),
            P("section", "fsdp", None),
            P("section", "fsdp", None),
        ),
        check_vma=False,
    )
```

```python
import functools
import math

import jax
import jax.numpy as jnp
from jax import lax
from jax.experimental import pallas as pl
from jax.experimental.pallas import tpu as pltpu
from jax.sharding import PartitionSpec as P

FF = 6144
QUERY_HEADS = 16
KEY_VALUE_HEADS = 8
HEAD_SIZE = 128


NORM_EPS = 1e-06
ROPE_BASE = 1000000.0
MASKED_SCORE = -1e30
PLANE = 8


def from_behind(array, axis, by):
    count = lax.axis_size(axis)
    pairs = [(i, i + by) for i in range(count) if 0 <= i + by < count]
    return lax.ppermute(array, axis, pairs)


def normed(values):
    return values * lax.rsqrt(jnp.mean(values * values, axis=-1, keepdims=True) + NORM_EPS)


def scaled(values, gain_row):
    return normed(values) * gain_row


def rotate(values, positions):
    half_width = values.shape[-1] // 2
    frequency = jnp.exp(
        jnp.arange(half_width, dtype=jnp.float32) * (-2.0 * math.log(ROPE_BASE) / values.shape[-1])
    )
    angles = positions.astype(jnp.float32)[:, None] * frequency[None, :]
    cosine = jnp.cos(angles)[:, None, :]
    sine_part = jnp.sin(angles)[:, None, :]
    lower_half = values[..., :half_width]
    upper_half = values[..., half_width:]
    return jnp.concatenate(
        [
            lower_half * cosine - upper_half * sine_part,
            upper_half * cosine + lower_half * sine_part,
        ],
        axis=-1,
    )


def places(doc_lengths, sequence_length):
    doc_ends = jnp.cumsum(doc_lengths)
    token_index = jnp.arange(sequence_length, dtype=jnp.int32)
    passed_ends = (token_index[:, None] >= doc_ends[None, :]).astype(jnp.int32)
    document_index = jnp.sum(passed_ends, axis=1)
    doc_start = jnp.sum(passed_ends * doc_lengths[None, :], axis=1)
    return (document_index, token_index - doc_start)


def heads_of(projected_output, head_gain, positions):
    count_of_tokens = projected_output.shape[0]
    query_rows = projected_output[:, : QUERY_HEADS * HEAD_SIZE].reshape(
        count_of_tokens, QUERY_HEADS, HEAD_SIZE
    )
    heads_of_keys = projected_output[
        :, QUERY_HEADS * HEAD_SIZE : (QUERY_HEADS + KEY_VALUE_HEADS) * HEAD_SIZE
    ].reshape(count_of_tokens, KEY_VALUE_HEADS, HEAD_SIZE)
    heads_of_values = projected_output[:, (QUERY_HEADS + KEY_VALUE_HEADS) * HEAD_SIZE :]
    return (
        rotate(scaled(query_rows, head_gain[:HEAD_SIZE]), positions),
        rotate(scaled(heads_of_keys, head_gain[HEAD_SIZE:]), positions),
        heads_of_values,
    )


def gated_unit(joined):
    return jax.nn.silu(joined[:, :FF]) * joined[:, FF:]


def times_transposed(left_side, right_side):
    return lax.dot_general(
        left_side, right_side, (((1,), (1,)), ((), ())), preferred_element_type=jnp.float32
    )


def allowed_mask(doc_rows, row_start, document_index):
    row_index = row_start + jnp.arange(doc_rows.shape[0], dtype=jnp.int32)
    key_index = jnp.arange(document_index.shape[0], dtype=jnp.int32)
    return (doc_rows[:, None] == document_index[None, :]) & (
        row_index[:, None] >= key_index[None, :]
    )


def raw_scores(query_rows_second, rows_of_keys, allowed):
    grouped_heads = query_rows_second.reshape(
        query_rows_second.shape[0], KEY_VALUE_HEADS, QUERY_HEADS // KEY_VALUE_HEADS, HEAD_SIZE
    )
    heads_of_keys = rows_of_keys.reshape(rows_of_keys.shape[0], KEY_VALUE_HEADS, HEAD_SIZE)
    scores = jnp.einsum(
        "rkgd,tkd->rkgt", grouped_heads, heads_of_keys, preferred_element_type=jnp.float32
    ) * HEAD_SIZE ** (-0.5)
    return jnp.where(allowed[:, None, None, :], scores, MASKED_SCORE)


def attend_rows(query_rows_second, rows_of_keys, rows_of_values, allowed):
    scores = raw_scores(query_rows_second, rows_of_keys, allowed)
    row_max = jnp.max(scores, axis=-1, keepdims=True)
    exp_scores = jnp.exp(scores - row_max)
    row_totals = jnp.sum(exp_scores, axis=-1, keepdims=True)
    attn_probs = (exp_scores / row_totals).astype(jnp.bfloat16)
    heads_of_values = rows_of_values.reshape(rows_of_values.shape[0], KEY_VALUE_HEADS, HEAD_SIZE)
    heads_mixed = jnp.einsum(
        "rkgt,tkd->rkgd", attn_probs, heads_of_values, preferred_element_type=jnp.float32
    )
    return (
        heads_mixed.reshape(query_rows_second.shape[0], QUERY_HEADS * HEAD_SIZE),
        row_max + jnp.log(row_totals),
    )


def attend_back(
    query_rows_second, rows_of_keys, rows_of_values, allowed, log_totals, mixed_gradient_second
):
    count_of_rows = query_rows_second.shape[0]
    count_of_keys = rows_of_keys.shape[0]
    grouped_heads = query_rows_second.reshape(
        count_of_rows, KEY_VALUE_HEADS, QUERY_HEADS // KEY_VALUE_HEADS, HEAD_SIZE
    )
    heads_of_keys = rows_of_keys.reshape(count_of_keys, KEY_VALUE_HEADS, HEAD_SIZE)
    heads_of_values = rows_of_values.reshape(count_of_keys, KEY_VALUE_HEADS, HEAD_SIZE)
    heads_gradient = mixed_gradient_second.reshape(
        count_of_rows, KEY_VALUE_HEADS, QUERY_HEADS // KEY_VALUE_HEADS, HEAD_SIZE
    )
    attn_probs = jnp.exp(raw_scores(query_rows_second, rows_of_keys, allowed) - log_totals)
    grad_probs = jnp.einsum(
        "rkgd,tkd->rkgt", heads_gradient, heads_of_values, preferred_element_type=jnp.float32
    )
    grad_scores = (
        attn_probs * (grad_probs - jnp.sum(grad_probs * attn_probs, axis=-1, keepdims=True))
    ).astype(jnp.bfloat16)
    queries_gradient = jnp.einsum(
        "rkgt,tkd->rkgd", grad_scores, heads_of_keys, preferred_element_type=jnp.float32
    ) * HEAD_SIZE ** (-0.5)
    keys_gradient = jnp.einsum(
        "rkgt,rkgd->tkd", grad_scores, grouped_heads, preferred_element_type=jnp.float32
    ) * HEAD_SIZE ** (-0.5)
    values_gradient = jnp.einsum(
        "rkgt,rkgd->tkd",
        attn_probs.astype(jnp.bfloat16),
        heads_gradient,
        preferred_element_type=jnp.float32,
    )
    return (
        queries_gradient.reshape(count_of_rows, QUERY_HEADS, HEAD_SIZE),
        keys_gradient.reshape(count_of_keys, KEY_VALUE_HEADS * HEAD_SIZE),
        values_gradient.reshape(count_of_keys, KEY_VALUE_HEADS * HEAD_SIZE),
    )


def layer_forward(inputs, layer_full, positions, allowed):
    mixer_gain, heads_weight, merge_weight, head_gain, feed_gain, expand_weight, reduce_weight = (
        layer_full
    )
    count_of_rows = inputs.shape[0]
    normal_a = scaled(inputs, mixer_gain).astype(jnp.bfloat16)
    projected_output = jnp.dot(normal_a, heads_weight, preferred_element_type=jnp.float32)
    query_rows, heads_of_keys, heads_of_values = heads_of(projected_output, head_gain, positions)
    rows_of_keys, rows_of_values = (
        lax.all_gather(
            heads_of_keys.reshape(count_of_rows, KEY_VALUE_HEADS * HEAD_SIZE).astype(jnp.bfloat16),
            "fsdp",
            axis=0,
            tiled=True,
        ),
        lax.all_gather(heads_of_values.astype(jnp.bfloat16), "fsdp", axis=0, tiled=True),
    )
    heads_mixed, log_totals = attend_rows(
        query_rows.astype(jnp.bfloat16), rows_of_keys, rows_of_values, allowed
    )
    mixed_b = heads_mixed.astype(jnp.bfloat16)
    middle = inputs + jnp.dot(mixed_b, merge_weight, preferred_element_type=jnp.float32)
    normal_b = scaled(middle, feed_gain).astype(jnp.bfloat16)
    joined = jnp.dot(normal_b, expand_weight, preferred_element_type=jnp.float32)
    hidden = gated_unit(joined).astype(jnp.bfloat16)
    result = middle + jnp.dot(hidden, reduce_weight, preferred_element_type=jnp.float32)
    return (
        result,
        (
            inputs,
            normal_a,
            projected_output,
            rows_of_keys,
            rows_of_values,
            log_totals,
            mixed_b,
            middle,
            normal_b,
            joined,
            hidden,
        ),
    )


def layer_backward(upstream, layer_full, saved, positions, allowed):
    mixer_gain, heads_weight, merge_weight, head_gain, feed_gain, expand_weight, reduce_weight = (
        layer_full
    )
    (
        inputs,
        normal_a,
        projected_output,
        rows_of_keys,
        rows_of_values,
        log_totals,
        mixed_b,
        middle,
        normal_b,
        joined,
        hidden,
    ) = saved
    count_of_rows = inputs.shape[0]
    upstream_b = upstream.astype(jnp.bfloat16)
    grad_hidden = times_transposed(upstream_b, reduce_weight)
    unused_joined, gated_back = jax.vjp(gated_unit, joined)
    grad_joined = gated_back(grad_hidden)[0].astype(jnp.bfloat16)
    unused_feed, feed_back = jax.vjp(scaled, middle, feed_gain)
    grad_middle_part, grad_feed = feed_back(times_transposed(grad_joined, expand_weight))
    grad_middle = upstream + grad_middle_part
    grad_middle_b = grad_middle.astype(jnp.bfloat16)
    grad_mixed = times_transposed(grad_middle_b, merge_weight).astype(jnp.bfloat16)
    head_values, heads_back = jax.vjp(
        lambda projected_rows, gain_rows: heads_of(projected_rows, gain_rows, positions),
        projected_output,
        head_gain,
    )
    queries_gradient, grad_keys_all, grad_values_all = attend_back(
        head_values[0].astype(jnp.bfloat16),
        rows_of_keys,
        rows_of_values,
        allowed,
        log_totals,
        grad_mixed,
    )
    keys_gradient, values_gradient = (
        lax.psum_scatter(
            grad_keys_all.astype(jnp.bfloat16), "fsdp", scatter_dimension=0, tiled=True
        ).astype(jnp.float32),
        lax.psum_scatter(
            grad_values_all.astype(jnp.bfloat16), "fsdp", scatter_dimension=0, tiled=True
        ).astype(jnp.float32),
    )
    grad_projected, grad_head = heads_back(
        (
            queries_gradient,
            keys_gradient.reshape(count_of_rows, KEY_VALUE_HEADS, HEAD_SIZE),
            values_gradient,
        )
    )
    grad_projected_b = grad_projected.astype(jnp.bfloat16)
    unused_mixer, mixer_back = jax.vjp(scaled, inputs, mixer_gain)
    grad_inputs_part, grad_mixer = mixer_back(times_transposed(grad_projected_b, heads_weight))
    operands = (
        normal_a,
        grad_projected_b,
        mixed_b,
        grad_middle_b,
        normal_b,
        grad_joined,
        hidden,
        upstream_b,
    )
    return (grad_middle + grad_inputs_part, operands, (grad_mixer, grad_feed, grad_head))


def product_term(left_side, right_side):
    return lax.dot_general(
        left_side, right_side, (((0,), (0,)), ((), ())), preferred_element_type=jnp.float32
    )


def reduce_grads(operands, gain_terms):
    (
        normal_a,
        grad_projected_b,
        mixed_b,
        grad_middle_b,
        normal_b,
        grad_joined,
        hidden,
        upstream_b,
    ) = operands
    heads_gradient = lax.psum_scatter(
        product_term(normal_a, grad_projected_b).astype(jnp.bfloat16),
        "fsdp",
        scatter_dimension=0,
        tiled=True,
    )
    grad_merge = lax.psum_scatter(
        product_term(mixed_b, grad_middle_b).astype(jnp.bfloat16),
        "fsdp",
        scatter_dimension=0,
        tiled=True,
    )
    grad_expand = lax.psum_scatter(
        product_term(normal_b, grad_joined).astype(jnp.bfloat16),
        "fsdp",
        scatter_dimension=0,
        tiled=True,
    )
    grad_reduce = lax.psum_scatter(
        product_term(hidden, upstream_b).astype(jnp.bfloat16),
        "fsdp",
        scatter_dimension=0,
        tiled=True,
    )
    grad_mixer, grad_feed, grad_head = (
        lax.psum_scatter(gain_terms[0], "fsdp", scatter_dimension=0, tiled=True),
        lax.psum_scatter(gain_terms[1], "fsdp", scatter_dimension=0, tiled=True),
        lax.psum_scatter(gain_terms[2], "fsdp", scatter_dimension=0, tiled=True),
    )
    return (
        lax.psum(grad_mixer.astype(jnp.bfloat16), "rep").astype(jnp.float32),
        lax.psum(heads_gradient, "rep").astype(jnp.float32),
        lax.psum(grad_merge, "rep").astype(jnp.float32),
        lax.psum(grad_head.astype(jnp.bfloat16), "rep").astype(jnp.float32),
        lax.psum(grad_feed.astype(jnp.bfloat16), "rep").astype(jnp.float32),
        lax.psum(grad_expand, "rep").astype(jnp.float32),
        lax.psum(grad_reduce, "rep").astype(jnp.float32),
    )


def body(
    section_inputs,
    doc_lengths,
    mixer_gain,
    heads_weight,
    merge_weight,
    head_gain,
    feed_gain,
    expand_weight,
    reduce_weight,
):
    section_index = lax.axis_index("section")
    head_section = section_index == 0
    shard_index = lax.axis_index("fsdp")
    count_of_rows = section_inputs.shape[3]
    sequence_length = count_of_rows * lax.axis_size("fsdp")
    own_rows = section_inputs[0, :, 0]
    micro_count = own_rows.shape[0]
    mixer_part = (
        lax.all_gather(mixer_gain, "fsdp", axis=1, tiled=True),
        lax.all_gather(heads_weight, "fsdp", axis=1, tiled=True),
        lax.all_gather(merge_weight, "fsdp", axis=1, tiled=True),
        lax.all_gather(head_gain, "fsdp", axis=1, tiled=True),
    )
    feed_part = (
        lax.all_gather(feed_gain, "fsdp", axis=1, tiled=True),
        lax.all_gather(expand_weight, "fsdp", axis=1, tiled=True),
        lax.all_gather(reduce_weight, "fsdp", axis=1, tiled=True),
    )
    layer_full = (
        mixer_part[0][0].astype(jnp.float32),
        mixer_part[1][0],
        mixer_part[2][0],
        mixer_part[3][0].astype(jnp.float32),
        feed_part[0][0].astype(jnp.float32),
        feed_part[1][0],
        feed_part[2][0],
    )

    def layout(micro_slot):
        document_index, positions = places(doc_lengths[micro_slot, 0], sequence_length)
        row_start = shard_index * count_of_rows
        doc_rows = lax.dynamic_slice_in_dim(document_index, row_start, count_of_rows)
        own_positions = lax.dynamic_slice_in_dim(positions, row_start, count_of_rows)
        return (own_positions, allowed_mask(doc_rows, row_start, document_index))

    results = jnp.zeros((micro_count, count_of_rows, own_rows.shape[2]), jnp.float32)
    saved_acts = None
    arrived = jnp.zeros((count_of_rows, own_rows.shape[2]), jnp.bfloat16)
    for step_index in range(micro_count + 1):
        slot_raw = step_index - section_index
        is_live = (slot_raw >= 0) & (slot_raw < micro_count)
        micro_slot = jnp.clip(slot_raw, 0, micro_count - 1)
        inputs = jnp.where(
            head_section, own_rows[min(step_index, micro_count - 1)], arrived
        ).astype(jnp.float32)
        positions, allowed = layout(micro_slot)
        result, saved = layer_forward(inputs, layer_full, positions, allowed)
        if saved_acts is None:
            saved_acts = tuple(
                (jnp.zeros((micro_count,) + current.shape, current.dtype) for current in saved)
            )
        saved_acts = tuple(
            (
                jnp.where(is_live, buffer.at[micro_slot].set(current), buffer)
                for buffer, current in zip(saved_acts, saved)
            )
        )
        results = jnp.where(
            is_live & jnp.logical_not(head_section), results.at[micro_slot].set(result), results
        )
        if step_index < micro_count:
            arrived = from_behind(result.astype(jnp.bfloat16), "section", 1)
    gradients = None
    stashed = None
    gain_sums = None
    from_next = jnp.zeros((count_of_rows, own_rows.shape[2]), jnp.bfloat16)
    for step_index in range(micro_count + 1):
        slot_raw = step_index - 1 + section_index
        is_live = (slot_raw >= 0) & (slot_raw < micro_count)
        micro_slot = jnp.clip(slot_raw, 0, micro_count - 1)
        upstream = jnp.where(
            head_section, from_next, own_rows[min(step_index, micro_count - 1)]
        ).astype(jnp.float32)
        upstream = jnp.where(is_live, upstream, 0.0)
        positions, allowed = layout(micro_slot)
        saved = tuple((buffer[micro_slot] for buffer in saved_acts))
        grad_inputs, operands, gain_terms = layer_backward(
            upstream, layer_full, saved, positions, allowed
        )
        results = jnp.where(
            is_live & head_section, results.at[micro_slot].set(grad_inputs), results
        )
        if step_index < micro_count:
            from_next = from_behind(grad_inputs.astype(jnp.bfloat16), "section", -1)
        if stashed is None:
            stashed = tuple(
                (jnp.zeros((micro_count,) + current.shape, current.dtype) for current in operands)
            )
            gain_sums = tuple((jnp.zeros_like(current) for current in gain_terms))
        stashed = tuple(
            (
                jnp.where(is_live, buffer.at[micro_slot].set(current), buffer)
                for buffer, current in zip(stashed, operands)
            )
        )
        gain_sums = tuple(
            (total_so_far + current for total_so_far, current in zip(gain_sums, gain_terms))
        )
    merged = tuple(
        (buffer.reshape((micro_count * count_of_rows,) + buffer.shape[2:]) for buffer in stashed)
    )
    gradients = reduce_grads(merged, gain_sums)
    grad_mixer, heads_gradient, grad_merge, grad_head, grad_feed, grad_expand, grad_reduce = (
        gradients
    )
    return (
        results[None, :, None],
        grad_mixer[None],
        heads_gradient[None],
        grad_merge[None],
        grad_head[None],
        grad_feed[None],
        grad_expand[None],
        grad_reduce[None],
    )


MESH = pl.DeviceIdType.MESH
MERGED = QUERY_HEADS // KEY_VALUE_HEADS * HEAD_SIZE
JOINT = MERGED + 2 * HEAD_SIZE
VMEM_BYTES = 63 * 2**20


def mm(left, right):
    return jnp.dot(left, right, preferred_element_type=jnp.float32)


def mm_t(left, right):
    return lax.dot_general(
        left, right, (((1,), (1,)), ((), ())), preferred_element_type=jnp.float32
    )


def t_mm(left, right):
    return lax.dot_general(
        left, right, (((0,), (0,)), ((), ())), preferred_element_type=jnp.float32
    )


def remote(src, dst, send, recv, device):
    return pltpu.make_async_remote_copy(
        src_ref=src,
        dst_ref=dst,
        send_sem=send,
        recv_sem=recv,
        device_id=device,
        device_id_type=MESH,
    )


class Place:
    def __init__(self):
        self.index = lax.axis_index("fsdp")
        self.core = lax.rem(self.index, 2)
        self.chip = lax.div(self.index, 2)
        self.x = lax.rem(self.chip, 2)
        self.y = lax.div(self.chip, 2)
        self.x_peer = {"fsdp": self.index + 2 - 4 * self.x}
        self.y_peer = {"fsdp": self.index + 4 - 8 * self.y}
        self.core_peer = {"fsdp": self.index + 1 - 2 * self.core}
        self.section = lax.axis_index("section")
        self.section_peer = {"section": 1 - self.section}
        self.rep_peer = {"rep": 1 - lax.axis_index("rep")}

    def chip_at(self, rel):
        x, y = self.x, self.y
        if rel in (1, 3):
            x = 1 - x
        if rel in (2, 3):
            y = 1 - y
        return 2 * y + x

    def others(self):
        order = ((3, 0), (3, 1), (1, 0), (1, 1), (2, 0), (2, 1), (0, 1), (0, 0))
        return [
            (at, 2 * self.chip_at(rel) + (1 - self.core if other else self.core))
            for at, (rel, other) in enumerate(order)
        ]

    def greet(self, peers):
        barrier = pltpu.get_barrier_semaphore()
        for peer in peers:
            pl.semaphore_signal(barrier, inc=1, device_id=peer, device_id_type=MESH)
        pl.semaphore_wait(barrier, len(peers))


class Gather:
    def __init__(self, place, full, send, recv, rows):
        half = rows // 2

        def span(rel, part=None):
            first = (2 * place.chip_at(rel) + place.core) * rows
            if part is None:
                return pl.ds(pl.multiple_of(first, rows), rows)
            return pl.ds(pl.multiple_of(first + part * half, half), half)

        def copy(at, piece, peer):
            block = full.at[piece]
            return remote(block, block, send.at[at], recv.at[at], peer)

        self.copies = [
            copy(0, span(0, 1), place.x_peer),
            copy(1, span(0, 0), place.x_peer),
            copy(2, span(0, 0), place.y_peer),
            copy(3, span(0, 1), place.y_peer),
            copy(4, span(0), place.core_peer),
            copy(5, span(1, 1), place.y_peer),
            copy(6, span(2, 0), place.x_peer),
            copy(7, span(1), place.core_peer),
            copy(8, span(2), place.core_peer),
            copy(9, span(3), place.core_peer),
        ]

    def start(self):
        for at in (0, 2, 4, 1, 3):
            self.copies[at].start()

    def relay(self):
        self.copies[0].wait_recv()
        self.copies[5].start()
        self.copies[2].wait_recv()
        self.copies[6].start()

    def near(self):
        self.copies[1].wait_recv()
        self.copies[7].start()
        self.copies[3].wait_recv()
        self.copies[8].start()

    def far(self):
        self.copies[5].wait_recv()
        self.copies[6].wait_recv()
        self.copies[9].start()

    def wait(self, at):
        self.copies[at].wait_recv()

    def finish(self):
        for entry in self.copies:
            entry.wait_send()

    def over_blocks(self, block):
        self.start()
        self.wait(4)
        block(0)
        self.relay()
        self.near()
        self.wait(7)
        block(1)
        self.wait(8)
        block(2)
        self.far()
        self.wait(9)
        block(3)


class Scatter:
    def __init__(self, place, held, to_core, from_core, to_x, to_y, from_x, from_y, send, recv, rows):
        self.place, self.held, self.to_core, self.from_core = place, held, to_core, from_core
        self.to_x, self.to_y, self.from_x, self.from_y = to_x, to_y, from_x, from_y
        self.rows, self.half = rows, rows // 2

        def copy(at, src, dst, peer):
            return remote(src, dst, send.at[at], recv.at[at], peer)

        self.copies = [
            copy(rel, to_core.at[rel], from_core.at[rel], place.core_peer) for rel in range(4)
        ] + [
            copy(4, to_x.at[0], from_x.at[0], place.x_peer),
            copy(5, to_y.at[0], from_y.at[0], place.y_peer),
            copy(6, to_x.at[1], from_x.at[1], place.x_peer),
            copy(7, to_y.at[1], from_y.at[1], place.y_peer),
            copy(8, to_y.at[2], from_y.at[2], place.y_peer),
            copy(9, to_x.at[2], from_x.at[2], place.x_peer),
        ]

    def put(self, rel, product, width):
        step, rows, mine = 512, self.rows, self.place.core == 0

        @pl.loop(0, width // step)
        def _(at):
            columns = pl.ds(pl.multiple_of(at * step, step), step)
            value = product(columns)
            low, high = value[:rows], value[rows:]
            self.held[rel, :, columns] = jnp.where(mine, low, high)
            self.to_core[rel, :, columns] = jnp.where(mine, high, low).astype(jnp.bfloat16)

        self.copies[rel].start()

    def pair(self, rel):
        self.copies[rel].wait_recv()
        half, held = self.half, self.held

        @pl.loop(0, self.rows // 16)
        def _(at):
            span = pl.ds(pl.multiple_of(at * 16, 16), 16)
            held[rel, span, :] += self.from_core[rel, span, :].astype(jnp.float32)

        if rel == 3:
            self.to_x[0] = held[3, :half].astype(jnp.bfloat16)
            self.copies[4].start()
            self.to_y[0] = held[3, half:].astype(jnp.bfloat16)
            self.copies[5].start()
        if rel == 1:
            self.to_x[1] = held[1, :half].astype(jnp.bfloat16)
            self.copies[6].start()
        if rel == 2:
            self.to_y[1] = held[2, half:].astype(jnp.bfloat16)
            self.copies[7].start()

    def relay(self):
        half, held = self.half, self.held
        self.copies[4].wait_recv()
        self.to_y[2] = (held[2, :half] + self.from_x[0].astype(jnp.float32)).astype(jnp.bfloat16)
        self.copies[8].start()
        self.copies[5].wait_recv()
        self.to_x[2] = (held[1, half:] + self.from_y[0].astype(jnp.float32)).astype(jnp.bfloat16)
        self.copies[9].start()

    def total(self, add):
        for at in (6, 7, 8, 9):
            self.copies[at].wait_recv()
        count = self.half // 16

        @pl.loop(0, count)
        def _(at):
            span = pl.ds(pl.multiple_of(at * 16, 16), 16)
            low = self.held[0, span, :] + self.from_x[1, span, :].astype(jnp.float32)
            add(span, low + self.from_y[2, span, :].astype(jnp.float32))

        @pl.loop(0, count)
        def _(at):
            span = pl.ds(pl.multiple_of(at * 16, 16), 16)
            below = pl.ds(pl.multiple_of(self.half + at * 16, 16), 16)
            high = self.held[0, below, :] + self.from_y[1, span, :].astype(jnp.float32)
            add(below, high + self.from_x[2, span, :].astype(jnp.float32))

        for entry in self.copies:
            entry.wait_send()


def by_rows(count, body):
    @pl.loop(0, count // 16)
    def _(at):
        body(pl.ds(pl.multiple_of(at * 16, 16), 16))


def inverse_size(values):
    return lax.rsqrt(jnp.mean(values * values, axis=-1, keepdims=True) + NORM_EPS)


def norm_back(values, gain, upstream):
    size = inverse_size(values)
    scaled_up = upstream * gain
    back = size * scaled_up - values * (
        size * size * size * jnp.mean(values * scaled_up, axis=-1, keepdims=True)
    )
    return back, upstream * values * size


def turn(values, cosine, sine):
    return values * cosine + pltpu.roll(values, HEAD_SIZE // 2, 1) * sine


def turn_back(values, cosine, sine):
    return values * cosine + pltpu.roll(values * sine, HEAD_SIZE // 2, 1)


def probabilities(queries, keys, first_keys, first_row):
    scores = mm_t(queries, keys) * HEAD_SIZE ** (-0.5)
    key_index = lax.broadcasted_iota(jnp.int32, scores.shape, 1)
    row_index = first_row + lax.broadcasted_iota(jnp.int32, scores.shape, 0)
    allowed = (key_index >= first_keys) & (key_index <= row_index)
    scores = jnp.where(allowed, scores, MASKED_SCORE)
    powers = jnp.exp(scores - jnp.max(scores, axis=-1, keepdims=True))
    return powers / jnp.sum(powers, axis=-1, keepdims=True)


def forward_kernel(
    rows,
    own_ref,
    gain_ref,
    cos_ref,
    sin_ref,
    first_ref,
    heads_w,
    merge_w,
    expand_w,
    reduce_w,
    out_results,
    out_inputs,
    out_normal_a,
    out_projected,
    out_heads,
    out_mixed,
    out_middle,
    out_normal_b,
    out_joined,
    out_hidden,
    out_heads_w,
    out_expand_w,
    gains_ref,
    head_gain_ref,
    all_gains,
    wh,
    wm,
    we,
    wr,
    current,
    arrived,
    full_a,
    full_b,
    cosine,
    sine,
    first_key,
    projected,
    heads,
    mixed,
    joined,
    hidden,
    held,
    to_core,
    core_a,
    core_b,
    to_x,
    to_y,
    x_a,
    y_a,
    x_b,
    y_b,
    middle,
    result,
    result_b,
    load_sem,
    spread_send,
    spread_recv,
    save_sem,
    table_sem,
    hand_send,
    hand_recv,
    ga_send,
    ga_recv,
    sa_send,
    sa_recv,
    gb_send,
    gb_recv,
    sb_send,
    sb_recv,
):
    place = Place()
    micro_count = own_ref.shape[0]
    chip_rows = 2 * rows
    width = current.shape[1]
    hidden_width = wr.shape[0]
    depth = heads_w.shape[0]
    query_width, key_width = QUERY_HEADS * HEAD_SIZE, KEY_VALUE_HEADS * HEAD_SIZE
    loads = [
        pltpu.make_async_copy(src, dst, load_sem.at[at])
        for at, (src, dst) in enumerate(((merge_w, wm), (reduce_w, wr)))
    ]
    for load in loads:
        load.start()
    shard_rows = pl.ds(pl.multiple_of(place.index * depth, depth), depth)

    def spread(at, device, piece, src, dst):
        if at < 7:
            return remote(
                src, dst, spread_send.at[piece, at], spread_recv.at[piece, at], {"fsdp": device}
            )
        return pltpu.make_async_copy(src, dst, load_sem.at[2 + piece])

    def columns_of(first, device, count):
        return pl.ds(pl.multiple_of(first + device * count, 128), count)

    gain_copies = [
        spread(at, device, 0, gain_ref, all_gains.at[place.index])
        for at, device in place.others()
    ]
    heads_copies, expand_copies = [], []
    for at, device in place.others():
        for piece, first, count, into in (
            (1, 0, MERGED, 0),
            (2, query_width, HEAD_SIZE, MERGED),
            (3, query_width + key_width, HEAD_SIZE, MERGED + HEAD_SIZE),
        ):
            src = heads_w.at[:, columns_of(first, device, count)]
            heads_copies.append(
                spread(at, device, piece, src, wh.at[shard_rows, pl.ds(into, count)])
            )
        for piece in range(2):
            src = expand_w.at[:, columns_of(piece * FF, device, hidden_width)]
            expand_copies.append(
                spread(
                    at,
                    device,
                    4 + piece,
                    src,
                    we.at[shard_rows, pl.ds(piece * hidden_width, hidden_width)],
                )
            )

    def arrive(copies, pieces):
        for at, copy in enumerate(copies):
            if at // pieces < 7:
                copy.wait_recv()
            else:
                copy.wait()

    heads_out = pltpu.make_async_copy(wh, out_heads_w, load_sem.at[8])
    expand_out = pltpu.make_async_copy(we, out_expand_w, load_sem.at[9])
    place.greet([{"fsdp": device} for _, device in place.others()[:7]] + [place.section_peer])
    for copy in gain_copies + heads_copies:
        copy.start()
    arrive(gain_copies, 1)
    for shard in range(PLANE):
        part = slice(shard * depth, (shard + 1) * depth)
        gains_ref[0:1, part] = all_gains[shard][:, :depth]
        gains_ref[1:2, part] = all_gains[shard][:, depth : 2 * depth]
    per_row = PLANE // 2
    count = 2 * HEAD_SIZE // PLANE
    for row in range(2):
        head_gain_ref[row : row + 1, :] = jnp.concatenate(
            [
                all_gains[row * per_row + at][:, 2 * depth : 2 * depth + count]
                for at in range(per_row)
            ],
            axis=1,
        )
    head = place.section == 0
    def hand(step):
        return remote(
            result_b, arrived.at[step], hand_send.at[step], hand_recv.at[step], place.section_peer
        )

    @pl.loop(0, micro_count + 1)
    def _(step):
        slot = jnp.clip(step - place.section, 0, micro_count - 1)
        tables = [
            pltpu.make_async_copy(src.at[slot], dst, table_sem.at[at])
            for at, (src, dst) in enumerate(
                ((cos_ref, cosine), (sin_ref, sine), (first_ref, first_key))
            )
        ]
        for table in tables:
            table.start()

        @pl.when(head)
        def _():
            current[...] = own_ref[slot]

        @pl.when(jnp.logical_not(head) & (step == 0))
        def _():
            current[...] = jnp.zeros_like(current)

        @pl.when(jnp.logical_not(head) & (step > 0))
        def _():
            hand(step - 1).wait_recv()
            current[...] = arrived[step - 1]

        def save(at, src, dst):
            copy = pltpu.make_async_copy(src, dst.at[slot], save_sem.at[at])
            copy.start()
            return copy

        saves = [save(0, current, out_inputs)]

        def enter(span):
            values = current[span, :].astype(jnp.float32)
            base = pl.multiple_of(place.index * rows + span.start, 16)
            full_a[pl.ds(base, 16), :] = (
                values * inverse_size(values) * gains_ref[0:1, :]
            ).astype(jnp.bfloat16)

        by_rows(rows, enter)
        for table in tables:
            table.wait()

        gather = Gather(place, full_a, ga_send, ga_recv, rows)

        def heads_block(rel):
            span = block_rows(place, rel, rows)
            if rel == 0:

                @pl.when(step == 0)
                def _():
                    arrive(heads_copies, 3)
                    heads_out.start()

            values = mm(full_a[span, :], wh[...])
            projected[span, :] = values
            for at in range(3):
                columns = pl.ds(at * HEAD_SIZE, HEAD_SIZE)
                one = values[:, at * HEAD_SIZE : (at + 1) * HEAD_SIZE]
                gain = head_gain_ref[0:1, :] if at < 2 else head_gain_ref[1:2, :]
                heads[span, columns] = turn(
                    one * inverse_size(one) * gain, cosine[span, :], sine[span, :]
                ).astype(jnp.bfloat16)
            heads[span, 3 * HEAD_SIZE :] = values[:, 3 * HEAD_SIZE :].astype(jnp.bfloat16)

        gather.over_blocks(heads_block)
        saves += [
            save(1, full_a, out_normal_a),
            save(2, projected, out_projected),
            save(3, heads, out_heads),
        ]

        @pl.when(step == 0)
        def _():
            for copy in expand_copies:
                copy.start()
            loads[0].wait()

        scatter = Scatter(
            place, held, to_core, core_a, to_x, to_y, x_a, y_a, sa_send, sa_recv, rows
        )

        def attend_block(rel):
            first_row = place.chip_at(rel) * chip_rows
            span = block_rows(place, rel, rows)
            for at in range(2):
                columns = pl.ds(at * HEAD_SIZE, HEAD_SIZE)
                probs = probabilities(
                    heads[span, columns],
                    heads[:, 2 * HEAD_SIZE : 3 * HEAD_SIZE],
                    first_key[span, :],
                    first_row,
                )
                mixed[span, columns] = mm(
                    probs.astype(jnp.bfloat16), heads[:, 3 * HEAD_SIZE :]
                ).astype(jnp.bfloat16)
            scatter.put(rel, lambda columns: mm(mixed[span, :], wm[:, columns]), width)

        attend_block(3)
        attend_block(2)
        scatter.pair(3)
        attend_block(1)
        scatter.pair(2)
        attend_block(0)
        scatter.pair(1)
        saves.append(save(4, mixed, out_mixed))
        scatter.relay()
        scatter.pair(0)

        def residual(span, value):
            values = value + current[span, :].astype(jnp.float32)
            middle[span, :] = values
            base = pl.multiple_of(place.index * rows + span.start, 16)
            full_b[pl.ds(base, 16), :] = (
                values * inverse_size(values) * gains_ref[1:2, :]
            ).astype(jnp.bfloat16)

        scatter.total(residual)
        gather.finish()
        saves.append(save(5, middle, out_middle))
        for copy in saves[:5]:
            copy.wait()

        @pl.when(step == 0)
        def _():
            arrive(expand_copies, 2)
            expand_out.start()
            loads[1].wait()

        gather_b = Gather(place, full_b, gb_send, gb_recv, rows)
        scatter_b = Scatter(
            place, held, to_core, core_b, to_x, to_y, x_b, y_b, sb_send, sb_recv, rows
        )

        joined_copies = {}

        def feed_block(rel):
            span = block_rows(place, rel, rows)
            stage = joined.at[rel % 2]
            if rel >= 2:
                joined_copies[rel - 2].wait()

            @pl.loop(0, hidden_width // 256)
            def _(at):
                columns = pl.ds(pl.multiple_of(at * 256, 256), 256)
                later = pl.ds(pl.multiple_of(hidden_width + at * 256, 256), 256)
                gate = mm(full_b[span, :], we[:, columns])
                up = mm(full_b[span, :], we[:, later])
                stage[:, columns] = gate
                stage[:, later] = up
                hidden[span, columns] = (gate * jax.nn.sigmoid(gate) * up).astype(jnp.bfloat16)

            copy = pltpu.make_async_copy(stage, out_joined.at[slot, span], save_sem.at[8 + rel % 2])
            copy.start()
            joined_copies[rel] = copy
            scatter_b.put(rel, lambda columns: mm(hidden[span, :], wr[:, columns]), width)
            if rel >= 1:
                scatter_b.pair(rel - 1)

        gather_b.over_blocks(feed_block)
        later_saves = [save(6, full_b, out_normal_b), save(7, hidden, out_hidden)]
        scatter_b.pair(3)
        scatter_b.relay()

        @pl.when(head & (step > 0))
        def _():
            hand(step - 1).wait_send()

        def finish(span, value):
            values = value + middle[span, :]
            result[span, :] = values
            result_b[span, :] = values.astype(jnp.bfloat16)

        scatter_b.total(finish)

        @pl.when(head & (step < micro_count))
        def _():
            hand(step).start()

        final = save(0, result, out_results)
        gather_b.finish()
        for copy in [saves[5]] + later_saves + [joined_copies[2], joined_copies[3], final]:
            copy.wait()

    heads_out.wait()
    expand_out.wait()
    for pieces, copies in ((1, gain_copies), (3, heads_copies), (2, expand_copies)):
        for copy in copies[: 7 * pieces]:
            copy.wait_send()


def backward_kernel(
    rows,
    own_ref,
    gains_ref,
    head_gain_ref,
    cos_ref,
    sin_ref,
    first_ref,
    heads_w,
    merge_w,
    expand_w,
    reduce_w,
    in_inputs,
    in_projected,
    in_heads,
    in_middle,
    in_joined,
    out_results,
    out_upstream,
    out_grad_joined,
    out_grad_middle,
    out_grad_projected,
    out_gains,
    out_head_gain,
    wh,
    wm,
    we,
    wr,
    arrived,
    current,
    full_a,
    full_b,
    cosine,
    sine,
    first_key,
    projected,
    heads,
    grad_mixed,
    grad_queries,
    grad_keys,
    grad_values,
    grad_projected,
    joined,
    grad_joined,
    held,
    to_core,
    core_a,
    core_b,
    to_x,
    to_y,
    x_a,
    y_a,
    x_b,
    y_b,
    middle,
    inputs,
    result,
    load_sem,
    save_sem,
    table_sem,
    joined_sem,
    hand_send,
    hand_recv,
    ga_send,
    ga_recv,
    sa_send,
    sa_recv,
    gb_send,
    gb_recv,
    sb_send,
    sb_recv,
):
    place = Place()
    micro_count = own_ref.shape[0]
    chip_rows = 2 * rows
    width = current.shape[1]
    hidden_width = wr.shape[0]
    loads = [
        pltpu.make_async_copy(src, dst, load_sem.at[at])
        for at, (src, dst) in enumerate(
            ((reduce_w, wr), (expand_w, we), (merge_w, wm), (heads_w, wh))
        )
    ]
    for load in loads:
        load.start()
    place.greet((place.x_peer, place.y_peer, place.core_peer, place.section_peer))
    head = place.section == 0
    own_rows = pl.ds(pl.multiple_of(place.index * rows, rows), rows)

    def hand(step):
        return remote(
            current, arrived.at[step], hand_send.at[step], hand_recv.at[step], place.section_peer
        )

    @pl.loop(0, micro_count + 1)
    def _(step):
        slot = jnp.clip(step - 1 + place.section, 0, micro_count - 1)
        tables = [
            pltpu.make_async_copy(src.at[slot], dst, table_sem.at[at])
            for at, (src, dst) in enumerate(
                (
                    (in_middle, middle),
                    (cos_ref, cosine),
                    (sin_ref, sine),
                    (first_ref, first_key),
                    (in_projected, projected),
                    (in_heads, heads),
                    (in_inputs, inputs),
                )
            )
        ]
        for table in tables:
            table.start()

        def joined_load(rel):
            return pltpu.make_async_copy(
                in_joined.at[slot, block_rows(place, rel, rows)], joined.at[rel % 2], joined_sem.at[rel % 2]
            )

        joined_load(0).start()
        joined_load(1).start()

        @pl.when(jnp.logical_not(head) & (step > 0))
        def _():
            hand(step - 1).wait_send()

        @pl.when(jnp.logical_not(head))
        def _():
            current[...] = own_ref[slot]

        @pl.when(head & (step == 0))
        def _():
            current[...] = jnp.zeros_like(current)

        @pl.when(head & (step > 0))
        def _():
            hand(step - 1).wait_recv()
            current[...] = arrived[step - 1]

        full_a[own_rows, :] = current[...]

        def save(at, src, dst):
            copy = pltpu.make_async_copy(src, dst.at[slot], save_sem.at[at])
            copy.start()
            return copy

        @pl.when(step == 0)
        def _():
            loads[0].wait()
            loads[1].wait()

        gather = Gather(place, full_a, ga_send, ga_recv, rows)
        scatter = Scatter(
            place, held, to_core, core_a, to_x, to_y, x_a, y_a, sa_send, sa_recv, rows
        )
        grad_copies = {}

        def feed_block(rel):
            span = block_rows(place, rel, rows)
            stage, out = joined.at[rel % 2], grad_joined.at[rel % 2]
            joined_load(rel).wait()
            if rel >= 2:
                grad_copies[rel - 2].wait()

            @pl.loop(0, hidden_width // 256)
            def _(at):
                columns = pl.ds(pl.multiple_of(at * 256, 256), 256)
                later = pl.ds(pl.multiple_of(hidden_width + at * 256, 256), 256)
                grad = mm_t(full_a[span, :], wr[columns, :])
                gate, up = stage[:, columns], stage[:, later]
                sigmoid = jax.nn.sigmoid(gate)
                unit = gate * sigmoid
                out[:, columns] = (grad * up * (sigmoid + unit * (1.0 - sigmoid))).astype(
                    jnp.bfloat16
                )
                out[:, later] = (grad * unit).astype(jnp.bfloat16)

            if rel < 2:
                joined_load(rel + 2).start()
            copy = pltpu.make_async_copy(
                out, out_grad_joined.at[slot, span], save_sem.at[8 + rel % 2]
            )
            copy.start()
            grad_copies[rel] = copy
            scatter.put(rel, lambda columns: mm_t(out[...], we[columns, :]), width)
            if rel >= 1:
                scatter.pair(rel - 1)

        gather.over_blocks(feed_block)
        upstream_save = save(0, full_a, out_upstream)
        scatter.pair(3)
        scatter.relay()
        for table in tables:
            table.wait()
        out_gains[slot, 1:2, :] = jnp.zeros((1, width), jnp.float32)

        def feed_norm(span, value):
            back, gain_term = norm_back(middle[span, :], gains_ref[1:2, :], value)
            out_gains[slot, 1:2, :] += jnp.sum(gain_term, axis=0, keepdims=True)
            total = back + current[span, :].astype(jnp.float32)
            result[span, :] = total
            base = pl.multiple_of(place.index * rows + span.start, 16)
            full_b[pl.ds(base, 16), :] = total.astype(jnp.bfloat16)

        scatter.total(feed_norm)
        gather.finish()
        for copy in (upstream_save, grad_copies[2], grad_copies[3]):
            copy.wait()

        @pl.when(step == 0)
        def _():
            loads[2].wait()
            loads[3].wait()

        save_result = save(3, result, out_results)

        @pl.when(step < micro_count)
        def _():
            save_result.wait()
            gather_b = Gather(place, full_b, gb_send, gb_recv, rows)
            scatter_b = Scatter(
                place, held, to_core, core_b, to_x, to_y, x_b, y_b, sb_send, sb_recv, rows
            )

            def mixed_block(rel):
                span = block_rows(place, rel, rows)
                grad_mixed[span, :] = mm_t(full_b[span, :], wm[...]).astype(jnp.bfloat16)

            gather_b.over_blocks(mixed_block)
            middle_save = save(1, full_b, out_grad_middle)
            attention_back(
                heads, grad_mixed, first_key, grad_queries, grad_keys, grad_values, 2 * rows
            )
            project_back(
                place,
                scatter_b,
                projected,
                head_gain_ref,
                cosine,
                sine,
                grad_queries,
                grad_keys,
                grad_values,
                grad_projected,
                out_head_gain.at[slot],
                wh,
                rows,
            )
            projected_save = save(2, grad_projected, out_grad_projected)
            scatter_b.relay()
            scatter_b.pair(0)
            input_back(scatter_b, inputs, gains_ref, out_gains.at[slot], result, current)

            @pl.when(jnp.logical_not(head))
            def _():
                hand(step).start()

            final = save(3, result, out_results)
            gather_b.finish()
            for copy in (middle_save, projected_save, final):
                copy.wait()

        @pl.when(step == micro_count)
        def _():
            save_result.wait()


def block_rows(place, rel, rows):
    return pl.ds(pl.multiple_of(place.chip_at(rel) * 2 * rows, 2 * rows), 2 * rows)


def attention_back(
    heads, grad_mixed, first_key, grad_queries, grad_keys, grad_values, chip_rows
):
    grad_keys[...] = jnp.zeros_like(grad_keys)
    grad_values[...] = jnp.zeros_like(grad_values)
    for block in range(heads.shape[0] // chip_rows):
        span = pl.ds(block * chip_rows, chip_rows)
        seen = (block + 1) * chip_rows
        keys = heads[:seen, 2 * HEAD_SIZE : 3 * HEAD_SIZE]
        values = heads[:seen, 3 * HEAD_SIZE :]
        for at in range(2):
            columns = pl.ds(at * HEAD_SIZE, HEAD_SIZE)
            queries = heads[span, columns]
            grad = grad_mixed[span, columns]
            probs = probabilities(queries, keys, first_key[span, :], block * chip_rows)
            grad_probs = mm_t(grad, values)
            grad_scores = (
                probs * (grad_probs - jnp.sum(probs * grad_probs, axis=-1, keepdims=True))
            ).astype(jnp.bfloat16)
            grad_queries[span, columns] = mm(grad_scores, keys) * HEAD_SIZE ** (-0.5)
            grad_keys[:seen, :] += t_mm(grad_scores, queries) * HEAD_SIZE ** (-0.5)
            grad_values[:seen, :] += t_mm(probs.astype(jnp.bfloat16), grad)


def project_back(
    place,
    scatter,
    projected,
    head_gain_ref,
    cosine,
    sine,
    grad_queries,
    grad_keys,
    grad_values,
    grad_projected,
    out_head_gain,
    wh,
    rows,
):
    out_head_gain[...] = jnp.zeros_like(out_head_gain)

    def project_block(rel):
        span = block_rows(place, rel, rows)
        for at in range(3):
            columns = pl.ds(at * HEAD_SIZE, HEAD_SIZE)
            which = 0 if at < 2 else 1
            upstream = grad_queries[span, columns] if at < 2 else grad_keys[span, :]
            back, gain_term = norm_back(
                projected[span, columns],
                head_gain_ref[which : which + 1, :],
                turn_back(upstream, cosine[span, :], sine[span, :]),
            )
            out_head_gain[which : which + 1, :] += jnp.sum(gain_term, axis=0, keepdims=True)
            grad_projected[span, columns] = back.astype(jnp.bfloat16)
        grad_projected[span, 3 * HEAD_SIZE :] = grad_values[span, :].astype(jnp.bfloat16)
        scatter.put(rel, lambda columns: mm_t(grad_projected[span, :], wh[columns, :]), wh.shape[0])

    project_block(3)
    project_block(2)
    scatter.pair(3)
    project_block(1)
    scatter.pair(2)
    project_block(0)
    scatter.pair(1)


def input_back(scatter, inputs, gains_ref, out_gains, result, result_b):
    out_gains[0:1, :] = jnp.zeros_like(out_gains[0:1, :])

    def mixer_norm(span, value):
        back, gain_term = norm_back(inputs[span, :].astype(jnp.float32), gains_ref[0:1, :], value)
        out_gains[0:1, :] += jnp.sum(gain_term, axis=0, keepdims=True)
        total = back + result[span, :]
        result[span, :] = total
        if result_b is not None:
            result_b[span, :] = total.astype(jnp.bfloat16)

    scatter.total(mixer_norm)


def gradient_kernel(
    rows,
    gains_ref,
    head_gain_ref,
    cos_ref,
    sin_ref,
    first_ref,
    heads_w,
    merge_w,
    in_inputs,
    in_projected,
    in_heads,
    in_result,
    hidden_all,
    upstream_all,
    normal_b_all,
    grad_joined_all,
    mixed_all,
    grad_middle_all,
    normal_a_all,
    grad_projected_all,
    out_result,
    own_heads,
    other_heads,
    own_merge,
    other_merge,
    own_expand,
    other_expand,
    own_reduce,
    other_reduce,
    out_gains,
    out_head_gain,
    wh,
    wm,
    full,
    cosine,
    sine,
    first_key,
    projected,
    heads,
    grad_mixed,
    grad_queries,
    grad_keys,
    grad_values,
    grad_projected,
    held,
    to_core,
    from_core,
    to_x,
    to_y,
    from_x,
    from_y,
    inputs,
    result,
    tiles,
    turned,
    wide,
    narrow,
    first_projected,
    expand_blocks,
    reduce_block,
    load_sem,
    tile_sem,
    save_sem,
    g_send,
    g_recv,
    s_send,
    s_recv,
    spread_send,
    spread_recv,
    rep_send,
    rep_recv,
):
    place = Place()
    length, width = full.shape
    depth = wm.shape[0]
    hidden_width = reduce_block.shape[0]
    last = in_inputs.shape[0] - 1
    tokens = wide.shape[0]
    query_width, key_width = QUERY_HEADS * HEAD_SIZE, KEY_VALUE_HEADS * HEAD_SIZE

    def load(at, src, dst):
        copy = pltpu.make_async_copy(src, dst, load_sem.at[at])
        copy.start()
        return copy

    result_load = load(0, in_result.at[last], result)
    wide_load = load(1, upstream_all, wide)
    others = place.others()
    jobs = (
        [(hidden_all, at) for at in range(hidden_width // depth)]
        + [(normal_b_all, device) for _, device in others]
        + [(mixed_all, 0)]
        + [(normal_a_all, device) for _, device in others]
    )

    def tile_load(job):
        source, at = jobs[job]
        columns = pl.ds(pl.multiple_of(at * depth, depth), depth)
        return pltpu.make_async_copy(
            source.at[:, columns], tiles.at[job % 2], tile_sem.at[job % 2]
        )

    def take(job):
        tile_load(job).wait()

        @pl.loop(0, tokens // 256)
        def _(at):
            span = pl.ds(pl.multiple_of(at * 256, 256), 256)
            turned[:, span] = tiles[job % 2, span, :].T

        if job + 2 < len(jobs):
            tile_load(job + 2).start()

    tile_load(0).start()
    tile_load(1).start()
    narrow_load = load(2, grad_joined_all, narrow)
    loads = [
        load(at + 3, src, dst)
        for at, (src, dst) in enumerate(
            (
                (merge_w, wm),
                (heads_w, wh),
                (cos_ref.at[last], cosine),
                (sin_ref.at[last], sine),
                (first_ref.at[last], first_key),
                (in_projected.at[last], projected),
                (in_heads.at[last], heads),
                (in_inputs.at[last], inputs),
                (grad_projected_all.at[0], first_projected),
            )
        )
    ]
    place.greet([{"fsdp": device} for _, device in others[:7]] + [place.rep_peer])

    def rep_copy(at, src, dst):
        return remote(src, dst, rep_send.at[at], rep_recv.at[at], place.rep_peer)

    def spread(at, device, piece, src, dst):
        if at < 7:
            return remote(
                src, dst, spread_send.at[piece, at], spread_recv.at[piece, at], {"fsdp": device}
            )
        return pltpu.make_async_copy(src, dst, save_sem.at[4 + piece])

    def columns_of(first, device, count):
        return pl.ds(pl.multiple_of(first + device * count, 128), count)

    result_load.wait()

    def enter(span):
        base = pl.multiple_of(place.index * rows + span.start, 16)
        full[pl.ds(base, 16), :] = result[span, :].astype(jnp.bfloat16)

    by_rows(rows, enter)
    gather = Gather(place, full, g_send, g_recv, rows)
    gather.start()

    wide_load.wait()
    own_saves, rep_copies = [], []
    for at in range(hidden_width // depth):
        take(at)
        span = pl.ds(at * depth, depth)

        @pl.loop(0, width // 512)
        def _(chunk):
            columns = pl.ds(pl.multiple_of(chunk * 512, 512), 512)
            reduce_block[span, columns] = mm(turned[...], wide[:, columns]).astype(jnp.bfloat16)

        copy = rep_copy(at, reduce_block.at[span], other_reduce.at[span])
        copy.start()
        rep_copies.append(copy)
        copy = pltpu.make_async_copy(reduce_block.at[span], own_reduce.at[span], save_sem.at[at])
        copy.start()
        own_saves.append(copy)
        if at == 0:
            gather.relay()
            gather.near()
    gather.far()
    middle_load = load(12, grad_middle_all.at[0], wide.at[pl.ds(0, length)])
    narrow_load.wait()
    job = hidden_width // depth
    expand_copies, expand_reps = [], []
    for at, device in others:
        take(job)
        job += 1

        @pl.loop(0, narrow.shape[1] // 512)
        def _(chunk):
            columns = pl.ds(pl.multiple_of(chunk * 512, 512), 512)
            expand_blocks[at, :, columns] = mm(turned[...], narrow[:, columns]).astype(
                jnp.bfloat16
            )

        for piece in range(2):
            src = expand_blocks.at[at, :, pl.ds(piece * hidden_width, hidden_width)]
            first = piece * FF
            copy = spread(
                at,
                device,
                piece,
                src,
                own_expand.at[:, columns_of(first, place.index, hidden_width)],
            )
            copy.start()
            expand_copies.append(copy)
            theirs = columns_of(first, device, hidden_width)
            expand_reps.append(
                rep_copy(
                    4 + 2 * at + piece,
                    own_expand.at[:, theirs] if at < 7 else src,
                    other_expand.at[:, theirs],
                )
            )
    for copy in expand_reps[14:]:
        copy.start()
    for copy in loads:
        copy.wait()
    for rel, at in ((0, 4), (1, 7), (2, 8), (3, 9)):
        gather.wait(at)
        span = block_rows(place, rel, rows)
        grad_mixed[span, :] = mm_t(full[span, :], wm[...]).astype(jnp.bfloat16)
    attention_back(heads, grad_mixed, first_key, grad_queries, grad_keys, grad_values, 2 * rows)
    scatter = Scatter(
        place, held, to_core, from_core, to_x, to_y, from_x, from_y, s_send, s_recv, rows
    )
    project_back(
        place,
        scatter,
        projected,
        head_gain_ref,
        cosine,
        sine,
        grad_queries,
        grad_keys,
        grad_values,
        grad_projected,
        out_head_gain,
        wh,
        rows,
    )
    scatter.relay()
    scatter.pair(0)
    input_back(scatter, inputs, gains_ref, out_gains, result, None)
    result_save = pltpu.make_async_copy(result, out_result, save_sem.at[9])
    result_save.start()

    for at in range(14):
        expand_copies[at].wait_recv()
        expand_reps[at].start()

    middle_load.wait()
    take(job)
    job += 1

    @pl.loop(0, width // 512)
    def _(chunk):
        columns = pl.ds(pl.multiple_of(chunk * 512, 512), 512)
        value = mm(turned[:, :length], wide[:length, columns])
        value += mm(turned[:, length:], full[:, columns])
        wm[:, columns] = value.astype(jnp.bfloat16)

    merge_rep = rep_copy(3, wm, other_merge)
    merge_rep.start()
    merge_save = pltpu.make_async_copy(wm, own_merge, save_sem.at[3])
    merge_save.start()
    heads_copies = []
    for at, device in others:
        take(job)
        job += 1
        value = mm(turned[:, :length], first_projected[...])
        value += mm(turned[:, length:], grad_projected[...])
        block = pl.ds(at * depth, depth)
        wh[block, :] = value.astype(jnp.bfloat16)
        for piece, first, count, start in (
            (2, 0, MERGED, 0),
            (3, query_width, HEAD_SIZE, MERGED),
            (4, query_width + key_width, HEAD_SIZE, MERGED + HEAD_SIZE),
        ):
            copy = spread(
                at,
                device,
                piece,
                wh.at[block, pl.ds(start, count)],
                own_heads.at[:, columns_of(first, place.index, count)],
            )
            copy.start()
            heads_copies.append(copy)
    for copy in heads_copies[:21]:
        copy.wait_recv()
    for copy in heads_copies[21:]:
        copy.wait()
    heads_rep = rep_copy(20, own_heads, other_heads)
    heads_rep.start()
    gather.finish()
    for copy in expand_copies[14:] + own_saves + [result_save, merge_save]:
        copy.wait()
    for copy in expand_copies[:14] + heads_copies[:21]:
        copy.wait_send()
    for copy in rep_copies + expand_reps + [merge_rep, heads_rep]:
        copy.wait()


def sems(*counts):
    return [pltpu.SemaphoreType.DMA((count,)) for count in counts]


def vmem(*shapes):
    return [pltpu.VMEM(shape, dtype) for *shape, dtype in shapes]


def any_spec():
    return pl.BlockSpec(memory_space=pl.ANY)


def vmem_spec():
    return pl.BlockSpec(memory_space=pltpu.VMEM)


def exchange_buffers(rows, width):
    half, b16 = rows // 2, jnp.bfloat16
    return vmem(
        (4, rows, width, jnp.float32),
        (4, rows, width, b16),
        (4, rows, width, b16),
        (4, rows, width, b16),
        *(((3, half, width, b16),) * 6),
    )


def run_forward(own, gain_row, cosine, sine, first_key, weights):
    micro, rows, width = own.shape
    length = cosine.shape[1]
    hidden_width = weights[3].shape[0]
    f32, b16 = jnp.float32, jnp.bfloat16
    shape = jax.ShapeDtypeStruct
    return pl.pallas_call(
        functools.partial(forward_kernel, rows),
        out_shape=(
            shape((micro, rows, width), f32),
            shape((micro, rows, width), b16),
            shape((micro, length, width), b16),
            shape((micro, length, JOINT), f32),
            shape((micro, length, JOINT), b16),
            shape((micro, length, MERGED), b16),
            shape((micro, rows, width), f32),
            shape((micro, length, width), b16),
            shape((micro, length, 2 * hidden_width), f32),
            shape((micro, length, hidden_width), b16),
            shape((width, JOINT), b16),
            shape((width, 2 * hidden_width), b16),
            shape((2, width), f32),
            shape((2, HEAD_SIZE), f32),
        ),
        in_specs=[vmem_spec()] * 2 + [any_spec()] * 7,
        out_specs=(any_spec(),) * 12 + (vmem_spec(),) * 2,
        scratch_shapes=vmem(
            (PLANE, *gain_row.shape, f32),
            (width, JOINT, b16),
            (MERGED, width, b16),
            (width, 2 * hidden_width, b16),
            (hidden_width, width, b16),
            (rows, width, b16),
            (micro, rows, width, b16),
            (length, width, b16),
            (length, width, b16),
            (length, HEAD_SIZE, f32),
            (length, HEAD_SIZE, f32),
            (length, 1, jnp.int32),
            (length, JOINT, f32),
            (length, JOINT, b16),
            (length, MERGED, b16),
            (2, 2 * rows, 2 * hidden_width, f32),
            (length, hidden_width, b16),
        )
        + exchange_buffers(rows, width)
        + vmem((rows, width, f32), (rows, width, f32), (rows, width, b16))
        + sems(10)
        + [pltpu.SemaphoreType.DMA((6, PLANE - 1))] * 2
        + sems(10, 3, micro, micro, *((10,) * 8)),
        compiler_params=pltpu.CompilerParams(
            collective_id=1, has_side_effects=True, vmem_limit_bytes=VMEM_BYTES
        ),
    )(own, gain_row, cosine, sine, first_key, *weights)


def run_backward(own, gains, head_gain, cosine, sine, first_key, weights, saved):
    micro, rows, width = own.shape
    length = cosine.shape[1]
    hidden_width = weights[3].shape[0]
    f32, b16 = jnp.float32, jnp.bfloat16
    shape = jax.ShapeDtypeStruct
    return pl.pallas_call(
        functools.partial(backward_kernel, rows),
        out_shape=(
            shape((micro, rows, width), f32),
            shape((micro, length, width), b16),
            shape((micro, length, 2 * hidden_width), b16),
            shape((micro, length, width), b16),
            shape((micro, length, JOINT), b16),
            shape((micro, 2, width), f32),
            shape((micro, 2, HEAD_SIZE), f32),
        ),
        in_specs=[vmem_spec()] * 3 + [any_spec()] * 12,
        out_specs=(any_spec(),) * 5 + (vmem_spec(),) * 2,
        scratch_shapes=vmem(
            (width, JOINT, b16),
            (MERGED, width, b16),
            (width, 2 * hidden_width, b16),
            (hidden_width, width, b16),
            (micro, rows, width, b16),
            (rows, width, b16),
            (length, width, b16),
            (length, width, b16),
            (length, HEAD_SIZE, f32),
            (length, HEAD_SIZE, f32),
            (length, 1, jnp.int32),
            (length, JOINT, f32),
            (length, JOINT, b16),
            (length, MERGED, b16),
            (length, MERGED, f32),
            (length, HEAD_SIZE, f32),
            (length, HEAD_SIZE, f32),
            (length, JOINT, b16),
            (2, 2 * rows, 2 * hidden_width, f32),
            (2, 2 * rows, 2 * hidden_width, b16),
        )
        + exchange_buffers(rows, width)
        + vmem((rows, width, f32), (rows, width, b16), (rows, width, f32))
        + sems(4, 10, 7, 2, micro, micro, *((10,) * 8)),
        compiler_params=pltpu.CompilerParams(
            collective_id=2, has_side_effects=True, vmem_limit_bytes=VMEM_BYTES
        ),
    )(own, gains, head_gain, cosine, sine, first_key, *weights, *saved)


def run_gradients(gains, head_gain, cosine, sine, first_key, weights, saved, operands):
    micro, rows, width = saved[0].shape
    length = cosine.shape[1]
    hidden_width = operands[0].shape[1]
    depth = weights[1].shape[0]
    f32, b16 = jnp.float32, jnp.bfloat16
    shape = jax.ShapeDtypeStruct
    terms = ((depth, PLANE * JOINT), (depth, width), (depth, 2 * FF), (hidden_width, width))
    return pl.pallas_call(
        functools.partial(gradient_kernel, rows),
        out_shape=(shape((rows, width), f32),)
        + tuple(shape(term, b16) for term in terms for _ in range(2))
        + (shape((1, width), f32), shape((2, HEAD_SIZE), f32)),
        in_specs=[vmem_spec()] * 2 + [any_spec()] * 17,
        out_specs=(any_spec(),) * 9 + (vmem_spec(),) * 2,
        scratch_shapes=vmem(
            (width, JOINT, b16),
            (MERGED, width, b16),
            (length, width, b16),
            (length, HEAD_SIZE, f32),
            (length, HEAD_SIZE, f32),
            (length, 1, jnp.int32),
            (length, JOINT, f32),
            (length, JOINT, b16),
            (length, MERGED, b16),
            (length, MERGED, f32),
            (length, HEAD_SIZE, f32),
            (length, HEAD_SIZE, f32),
            (length, JOINT, b16),
            (4, rows, width, f32),
            (4, rows, width, b16),
            (4, rows, width, b16),
            *(((3, rows // 2, width, b16),) * 4),
            (rows, width, b16),
            (rows, width, f32),
            (2, micro * length, depth, b16),
            (depth, micro * length, b16),
            (micro * length, width, b16),
            (micro * length, 2 * hidden_width, b16),
            (length, JOINT, b16),
            (PLANE, depth, 2 * hidden_width, b16),
            (hidden_width, width, b16),
        )
        + sems(13, 2, 10, *((10,) * 4))
        + [pltpu.SemaphoreType.DMA((5, PLANE - 1))] * 2
        + sems(21, 21),
        compiler_params=pltpu.CompilerParams(
            collective_id=3, has_side_effects=True, vmem_limit_bytes=VMEM_BYTES
        ),
    )(gains, head_gain, cosine, sine, first_key, *weights, *saved, *operands)


def position_tables(lengths, length):
    document_index, positions = places(lengths, length)
    half_width = HEAD_SIZE // 2
    frequency = jnp.exp(
        jnp.arange(half_width, dtype=jnp.float32) * (-2.0 * math.log(ROPE_BASE) / HEAD_SIZE)
    )
    angles = positions.astype(jnp.float32)[:, None] * frequency[None, :]
    cosine, sine = jnp.cos(angles), jnp.sin(angles)
    first_key = jnp.arange(length, dtype=jnp.int32) - positions
    return (
        jnp.concatenate([cosine, cosine], axis=-1),
        jnp.concatenate([-sine, sine], axis=-1),
        first_key[:, None],
    )


def tensor_parallel_body(
    section_inputs,
    doc_lengths,
    mixer_gain,
    heads_weight,
    merge_weight,
    head_gain,
    feed_gain,
    expand_weight,
    reduce_weight,
):
    shards = lax.axis_size("fsdp")
    own = section_inputs[0, :, 0]
    micro, rows, width = own.shape
    length = rows * shards
    depth = heads_weight.shape[1]
    hidden_width = reduce_weight.shape[1]
    query_width = QUERY_HEADS * HEAD_SIZE

    gain_row = jnp.concatenate([mixer_gain[0], feed_gain[0], head_gain[0]]).astype(jnp.float32)
    gain_row = jnp.pad(gain_row, (0, -gain_row.shape[0] % 128))[None]
    tables = [position_tables(doc_lengths[at, 0], length) for at in range(micro)]
    cosine, sine, first_key = (jnp.stack(entry) for entry in zip(*tables))

    (
        results,
        inputs,
        normal_a,
        projected,
        heads,
        mixed,
        middle,
        normal_b,
        joined,
        hidden,
        heads_full,
        expand_full,
        gains,
        head_gains,
    ) = run_forward(
        own,
        gain_row,
        cosine,
        sine,
        first_key,
        (heads_weight[0], merge_weight[0], expand_weight[0], reduce_weight[0]),
    )
    grad_results, upstream, grad_joined, grad_middle, grad_projected, gain_terms, head_terms = (
        run_backward(
            own,
            gains,
            head_gains,
            cosine,
            sine,
            first_key,
            (heads_full, merge_weight[0], expand_full, reduce_weight[0]),
            (inputs, projected, heads, middle, joined),
        )
    )

    def flat(array):
        return array.reshape(micro * length, -1)

    last_result, *terms, mixer_term, head_term = run_gradients(
        gains,
        head_gains,
        cosine,
        sine,
        first_key,
        (heads_full, merge_weight[0]),
        (inputs, projected, heads, grad_results),
        (
            flat(hidden),
            flat(upstream),
            flat(normal_b),
            flat(grad_joined),
            flat(mixed),
            grad_middle,
            flat(normal_a),
            grad_projected,
        ),
    )
    grad_heads, grad_merge, grad_expand, grad_reduce = (
        (terms[at].astype(jnp.float32) + terms[at + 1].astype(jnp.float32))[None]
        for at in range(0, 8, 2)
    )
    mixer_term = mixer_term[0] + jnp.sum(gain_terms[:-1, 0], axis=0)
    head_term = head_term + jnp.sum(head_terms[:-1], axis=0)
    sums = lax.psum(
        jnp.concatenate([mixer_term, jnp.sum(gain_terms[:, 1], axis=0), head_term.reshape(-1)]),
        ("fsdp", "rep"),
    )
    index = lax.axis_index("fsdp")

    def own_part(first, count):
        return lax.dynamic_slice_in_dim(sums, first + index * count, count)[None]

    head_count = head_gain.shape[1]
    grad_results = jnp.concatenate([grad_results[:-1], last_result[None]])
    return (
        jnp.where(lax.axis_index("section") == 0, grad_results, results)[None, :, None],
        own_part(0, depth),
        grad_heads,
        grad_merge,
        own_part(2 * width, head_count),
        own_part(width, depth),
        grad_expand,
        grad_reduce,
    )


def solution(mesh):
    plane = mesh.shape["fsdp"] == PLANE
    return jax.shard_map(
        tensor_parallel_body if plane else body,
        mesh=mesh,
        in_specs=(
            P("section", None, "rep", "fsdp", None),
            P(None, "rep", None),
            P("section", "fsdp"),
            P("section", "fsdp", None),
            P("section", "fsdp", None),
            P("section", "fsdp"),
            P("section", "fsdp"),
            P("section", "fsdp", None),
            P("section", "fsdp", None),
        ),
        out_specs=(
            P("section", None, "rep", "fsdp", None),
            P("section", "fsdp"),
            P("section", "fsdp", None),
            P("section", "fsdp", None),
            P("section", "fsdp"),
            P("section", "fsdp"),
            P("section", "fsdp", None),
            P("section", "fsdp", None),
        ),
        check_vma=False,
    )
```

```python
import functools
import math
import types
import typing

import jax
import jax.numpy as jnp
from jax import lax
from jax.experimental import pallas as pl
from jax.experimental.pallas import tpu as pltpu
from jax.sharding import PartitionSpec as P

FF = 6144
QUERY_HEADS = 16
KEY_VALUE_HEADS = 8
HEAD_SIZE = 128


NORM_EPS = 1e-06
ROPE_BASE = 1000000.0
MASKED_SCORE = -1e30
PLANE = 8


def from_behind(array, axis, by):
    count = lax.axis_size(axis)
    pairs = [(i, i + by) for i in range(count) if 0 <= i + by < count]
    return lax.ppermute(array, axis, pairs)


def normed(values):
    return values * lax.rsqrt(jnp.mean(values * values, axis=-1, keepdims=True) + NORM_EPS)


def scaled(values, gain_row):
    return normed(values) * gain_row


def rotate(values, positions):
    half_width = values.shape[-1] // 2
    frequency = jnp.exp(
        jnp.arange(half_width, dtype=jnp.float32) * (-2.0 * math.log(ROPE_BASE) / values.shape[-1])
    )
    angles = positions.astype(jnp.float32)[:, None] * frequency[None, :]
    cosine = jnp.cos(angles)[:, None, :]
    sine_part = jnp.sin(angles)[:, None, :]
    lower_half = values[..., :half_width]
    upper_half = values[..., half_width:]
    return jnp.concatenate(
        [
            lower_half * cosine - upper_half * sine_part,
            upper_half * cosine + lower_half * sine_part,
        ],
        axis=-1,
    )


def places(doc_lengths, sequence_length):
    doc_ends = jnp.cumsum(doc_lengths)
    token_index = jnp.arange(sequence_length, dtype=jnp.int32)
    passed_ends = (token_index[:, None] >= doc_ends[None, :]).astype(jnp.int32)
    document_index = jnp.sum(passed_ends, axis=1)
    doc_start = jnp.sum(passed_ends * doc_lengths[None, :], axis=1)
    return (document_index, token_index - doc_start)


def heads_of(projected_output, head_gain, positions):
    count_of_tokens = projected_output.shape[0]
    query_rows = projected_output[:, : QUERY_HEADS * HEAD_SIZE].reshape(
        count_of_tokens, QUERY_HEADS, HEAD_SIZE
    )
    heads_of_keys = projected_output[
        :, QUERY_HEADS * HEAD_SIZE : (QUERY_HEADS + KEY_VALUE_HEADS) * HEAD_SIZE
    ].reshape(count_of_tokens, KEY_VALUE_HEADS, HEAD_SIZE)
    heads_of_values = projected_output[:, (QUERY_HEADS + KEY_VALUE_HEADS) * HEAD_SIZE :]
    return (
        rotate(scaled(query_rows, head_gain[:HEAD_SIZE]), positions),
        rotate(scaled(heads_of_keys, head_gain[HEAD_SIZE:]), positions),
        heads_of_values,
    )


def gated_unit(joined):
    return jax.nn.silu(joined[:, :FF]) * joined[:, FF:]


def times_transposed(left_side, right_side):
    return lax.dot_general(
        left_side, right_side, (((1,), (1,)), ((), ())), preferred_element_type=jnp.float32
    )


def allowed_mask(doc_rows, row_start, document_index):
    row_index = row_start + jnp.arange(doc_rows.shape[0], dtype=jnp.int32)
    key_index = jnp.arange(document_index.shape[0], dtype=jnp.int32)
    return (doc_rows[:, None] == document_index[None, :]) & (
        row_index[:, None] >= key_index[None, :]
    )


def raw_scores(query_rows_second, rows_of_keys, allowed):
    grouped_heads = query_rows_second.reshape(
        query_rows_second.shape[0], KEY_VALUE_HEADS, QUERY_HEADS // KEY_VALUE_HEADS, HEAD_SIZE
    )
    heads_of_keys = rows_of_keys.reshape(rows_of_keys.shape[0], KEY_VALUE_HEADS, HEAD_SIZE)
    scores = jnp.einsum(
        "rkgd,tkd->rkgt", grouped_heads, heads_of_keys, preferred_element_type=jnp.float32
    ) * HEAD_SIZE ** (-0.5)
    return jnp.where(allowed[:, None, None, :], scores, MASKED_SCORE)


def attend_rows(query_rows_second, rows_of_keys, rows_of_values, allowed):
    scores = raw_scores(query_rows_second, rows_of_keys, allowed)
    row_max = jnp.max(scores, axis=-1, keepdims=True)
    exp_scores = jnp.exp(scores - row_max)
    row_totals = jnp.sum(exp_scores, axis=-1, keepdims=True)
    attn_probs = (exp_scores / row_totals).astype(jnp.bfloat16)
    heads_of_values = rows_of_values.reshape(rows_of_values.shape[0], KEY_VALUE_HEADS, HEAD_SIZE)
    heads_mixed = jnp.einsum(
        "rkgt,tkd->rkgd", attn_probs, heads_of_values, preferred_element_type=jnp.float32
    )
    return (
        heads_mixed.reshape(query_rows_second.shape[0], QUERY_HEADS * HEAD_SIZE),
        row_max + jnp.log(row_totals),
    )


def attend_back(
    query_rows_second, rows_of_keys, rows_of_values, allowed, log_totals, mixed_gradient_second
):
    count_of_rows = query_rows_second.shape[0]
    count_of_keys = rows_of_keys.shape[0]
    grouped_heads = query_rows_second.reshape(
        count_of_rows, KEY_VALUE_HEADS, QUERY_HEADS // KEY_VALUE_HEADS, HEAD_SIZE
    )
    heads_of_keys = rows_of_keys.reshape(count_of_keys, KEY_VALUE_HEADS, HEAD_SIZE)
    heads_of_values = rows_of_values.reshape(count_of_keys, KEY_VALUE_HEADS, HEAD_SIZE)
    heads_gradient = mixed_gradient_second.reshape(
        count_of_rows, KEY_VALUE_HEADS, QUERY_HEADS // KEY_VALUE_HEADS, HEAD_SIZE
    )
    attn_probs = jnp.exp(raw_scores(query_rows_second, rows_of_keys, allowed) - log_totals)
    grad_probs = jnp.einsum(
        "rkgd,tkd->rkgt", heads_gradient, heads_of_values, preferred_element_type=jnp.float32
    )
    grad_scores = (
        attn_probs * (grad_probs - jnp.sum(grad_probs * attn_probs, axis=-1, keepdims=True))
    ).astype(jnp.bfloat16)
    queries_gradient = jnp.einsum(
        "rkgt,tkd->rkgd", grad_scores, heads_of_keys, preferred_element_type=jnp.float32
    ) * HEAD_SIZE ** (-0.5)
    keys_gradient = jnp.einsum(
        "rkgt,rkgd->tkd", grad_scores, grouped_heads, preferred_element_type=jnp.float32
    ) * HEAD_SIZE ** (-0.5)
    values_gradient = jnp.einsum(
        "rkgt,rkgd->tkd",
        attn_probs.astype(jnp.bfloat16),
        heads_gradient,
        preferred_element_type=jnp.float32,
    )
    return (
        queries_gradient.reshape(count_of_rows, QUERY_HEADS, HEAD_SIZE),
        keys_gradient.reshape(count_of_keys, KEY_VALUE_HEADS * HEAD_SIZE),
        values_gradient.reshape(count_of_keys, KEY_VALUE_HEADS * HEAD_SIZE),
    )


def layer_forward(inputs, layer_full, positions, allowed):
    mixer_gain, heads_weight, merge_weight, head_gain, feed_gain, expand_weight, reduce_weight = (
        layer_full
    )
    count_of_rows = inputs.shape[0]
    normal_a = scaled(inputs, mixer_gain).astype(jnp.bfloat16)
    projected_output = jnp.dot(normal_a, heads_weight, preferred_element_type=jnp.float32)
    query_rows, heads_of_keys, heads_of_values = heads_of(projected_output, head_gain, positions)
    rows_of_keys, rows_of_values = (
        lax.all_gather(
            heads_of_keys.reshape(count_of_rows, KEY_VALUE_HEADS * HEAD_SIZE).astype(jnp.bfloat16),
            "fsdp",
            axis=0,
            tiled=True,
        ),
        lax.all_gather(heads_of_values.astype(jnp.bfloat16), "fsdp", axis=0, tiled=True),
    )
    heads_mixed, log_totals = attend_rows(
        query_rows.astype(jnp.bfloat16), rows_of_keys, rows_of_values, allowed
    )
    mixed_b = heads_mixed.astype(jnp.bfloat16)
    middle = inputs + jnp.dot(mixed_b, merge_weight, preferred_element_type=jnp.float32)
    normal_b = scaled(middle, feed_gain).astype(jnp.bfloat16)
    joined = jnp.dot(normal_b, expand_weight, preferred_element_type=jnp.float32)
    hidden = gated_unit(joined).astype(jnp.bfloat16)
    result = middle + jnp.dot(hidden, reduce_weight, preferred_element_type=jnp.float32)
    return (
        result,
        (
            inputs,
            normal_a,
            projected_output,
            rows_of_keys,
            rows_of_values,
            log_totals,
            mixed_b,
            middle,
            normal_b,
            joined,
            hidden,
        ),
    )


def layer_backward(upstream, layer_full, saved, positions, allowed):
    mixer_gain, heads_weight, merge_weight, head_gain, feed_gain, expand_weight, reduce_weight = (
        layer_full
    )
    (
        inputs,
        normal_a,
        projected_output,
        rows_of_keys,
        rows_of_values,
        log_totals,
        mixed_b,
        middle,
        normal_b,
        joined,
        hidden,
    ) = saved
    count_of_rows = inputs.shape[0]
    upstream_b = upstream.astype(jnp.bfloat16)
    grad_hidden = times_transposed(upstream_b, reduce_weight)
    unused_joined, gated_back = jax.vjp(gated_unit, joined)
    grad_joined = gated_back(grad_hidden)[0].astype(jnp.bfloat16)
    unused_feed, feed_back = jax.vjp(scaled, middle, feed_gain)
    grad_middle_part, grad_feed = feed_back(times_transposed(grad_joined, expand_weight))
    grad_middle = upstream + grad_middle_part
    grad_middle_b = grad_middle.astype(jnp.bfloat16)
    grad_mixed = times_transposed(grad_middle_b, merge_weight).astype(jnp.bfloat16)
    head_values, heads_back = jax.vjp(
        lambda projected_rows, gain_rows: heads_of(projected_rows, gain_rows, positions),
        projected_output,
        head_gain,
    )
    queries_gradient, grad_keys_all, grad_values_all = attend_back(
        head_values[0].astype(jnp.bfloat16),
        rows_of_keys,
        rows_of_values,
        allowed,
        log_totals,
        grad_mixed,
    )
    keys_gradient, values_gradient = (
        lax.psum_scatter(
            grad_keys_all.astype(jnp.bfloat16), "fsdp", scatter_dimension=0, tiled=True
        ).astype(jnp.float32),
        lax.psum_scatter(
            grad_values_all.astype(jnp.bfloat16), "fsdp", scatter_dimension=0, tiled=True
        ).astype(jnp.float32),
    )
    grad_projected, grad_head = heads_back(
        (
            queries_gradient,
            keys_gradient.reshape(count_of_rows, KEY_VALUE_HEADS, HEAD_SIZE),
            values_gradient,
        )
    )
    grad_projected_b = grad_projected.astype(jnp.bfloat16)
    unused_mixer, mixer_back = jax.vjp(scaled, inputs, mixer_gain)
    grad_inputs_part, grad_mixer = mixer_back(times_transposed(grad_projected_b, heads_weight))
    operands = (
        normal_a,
        grad_projected_b,
        mixed_b,
        grad_middle_b,
        normal_b,
        grad_joined,
        hidden,
        upstream_b,
    )
    return (grad_middle + grad_inputs_part, operands, (grad_mixer, grad_feed, grad_head))


def product_term(left_side, right_side):
    return lax.dot_general(
        left_side, right_side, (((0,), (0,)), ((), ())), preferred_element_type=jnp.float32
    )


def reduce_grads(operands, gain_terms):
    (
        normal_a,
        grad_projected_b,
        mixed_b,
        grad_middle_b,
        normal_b,
        grad_joined,
        hidden,
        upstream_b,
    ) = operands
    heads_gradient = lax.psum_scatter(
        product_term(normal_a, grad_projected_b).astype(jnp.bfloat16),
        "fsdp",
        scatter_dimension=0,
        tiled=True,
    )
    grad_merge = lax.psum_scatter(
        product_term(mixed_b, grad_middle_b).astype(jnp.bfloat16),
        "fsdp",
        scatter_dimension=0,
        tiled=True,
    )
    grad_expand = lax.psum_scatter(
        product_term(normal_b, grad_joined).astype(jnp.bfloat16),
        "fsdp",
        scatter_dimension=0,
        tiled=True,
    )
    grad_reduce = lax.psum_scatter(
        product_term(hidden, upstream_b).astype(jnp.bfloat16),
        "fsdp",
        scatter_dimension=0,
        tiled=True,
    )
    grad_mixer, grad_feed, grad_head = (
        lax.psum_scatter(gain_terms[0], "fsdp", scatter_dimension=0, tiled=True),
        lax.psum_scatter(gain_terms[1], "fsdp", scatter_dimension=0, tiled=True),
        lax.psum_scatter(gain_terms[2], "fsdp", scatter_dimension=0, tiled=True),
    )
    return (
        lax.psum(grad_mixer.astype(jnp.bfloat16), "rep").astype(jnp.float32),
        lax.psum(heads_gradient, "rep").astype(jnp.float32),
        lax.psum(grad_merge, "rep").astype(jnp.float32),
        lax.psum(grad_head.astype(jnp.bfloat16), "rep").astype(jnp.float32),
        lax.psum(grad_feed.astype(jnp.bfloat16), "rep").astype(jnp.float32),
        lax.psum(grad_expand, "rep").astype(jnp.float32),
        lax.psum(grad_reduce, "rep").astype(jnp.float32),
    )


def body(
    section_inputs,
    doc_lengths,
    mixer_gain,
    heads_weight,
    merge_weight,
    head_gain,
    feed_gain,
    expand_weight,
    reduce_weight,
):
    section_index = lax.axis_index("section")
    head_section = section_index == 0
    shard_index = lax.axis_index("fsdp")
    count_of_rows = section_inputs.shape[3]
    sequence_length = count_of_rows * lax.axis_size("fsdp")
    own_rows = section_inputs[0, :, 0]
    micro_count = own_rows.shape[0]
    mixer_part = (
        lax.all_gather(mixer_gain, "fsdp", axis=1, tiled=True),
        lax.all_gather(heads_weight, "fsdp", axis=1, tiled=True),
        lax.all_gather(merge_weight, "fsdp", axis=1, tiled=True),
        lax.all_gather(head_gain, "fsdp", axis=1, tiled=True),
    )
    feed_part = (
        lax.all_gather(feed_gain, "fsdp", axis=1, tiled=True),
        lax.all_gather(expand_weight, "fsdp", axis=1, tiled=True),
        lax.all_gather(reduce_weight, "fsdp", axis=1, tiled=True),
    )
    layer_full = (
        mixer_part[0][0].astype(jnp.float32),
        mixer_part[1][0],
        mixer_part[2][0],
        mixer_part[3][0].astype(jnp.float32),
        feed_part[0][0].astype(jnp.float32),
        feed_part[1][0],
        feed_part[2][0],
    )

    def layout(micro_slot):
        document_index, positions = places(doc_lengths[micro_slot, 0], sequence_length)
        row_start = shard_index * count_of_rows
        doc_rows = lax.dynamic_slice_in_dim(document_index, row_start, count_of_rows)
        own_positions = lax.dynamic_slice_in_dim(positions, row_start, count_of_rows)
        return (own_positions, allowed_mask(doc_rows, row_start, document_index))

    results = jnp.zeros((micro_count, count_of_rows, own_rows.shape[2]), jnp.float32)
    saved_acts = None
    arrived = jnp.zeros((count_of_rows, own_rows.shape[2]), jnp.bfloat16)
    for step_index in range(micro_count + 1):
        slot_raw = step_index - section_index
        is_live = (slot_raw >= 0) & (slot_raw < micro_count)
        micro_slot = jnp.clip(slot_raw, 0, micro_count - 1)
        inputs = jnp.where(
            head_section, own_rows[min(step_index, micro_count - 1)], arrived
        ).astype(jnp.float32)
        positions, allowed = layout(micro_slot)
        result, saved = layer_forward(inputs, layer_full, positions, allowed)
        if saved_acts is None:
            saved_acts = tuple(
                (jnp.zeros((micro_count,) + current.shape, current.dtype) for current in saved)
            )
        saved_acts = tuple(
            (
                jnp.where(is_live, buffer.at[micro_slot].set(current), buffer)
                for buffer, current in zip(saved_acts, saved)
            )
        )
        results = jnp.where(
            is_live & jnp.logical_not(head_section), results.at[micro_slot].set(result), results
        )
        if step_index < micro_count:
            arrived = from_behind(result.astype(jnp.bfloat16), "section", 1)
    gradients = None
    stashed = None
    gain_sums = None
    from_next = jnp.zeros((count_of_rows, own_rows.shape[2]), jnp.bfloat16)
    for step_index in range(micro_count + 1):
        slot_raw = step_index - 1 + section_index
        is_live = (slot_raw >= 0) & (slot_raw < micro_count)
        micro_slot = jnp.clip(slot_raw, 0, micro_count - 1)
        upstream = jnp.where(
            head_section, from_next, own_rows[min(step_index, micro_count - 1)]
        ).astype(jnp.float32)
        upstream = jnp.where(is_live, upstream, 0.0)
        positions, allowed = layout(micro_slot)
        saved = tuple((buffer[micro_slot] for buffer in saved_acts))
        grad_inputs, operands, gain_terms = layer_backward(
            upstream, layer_full, saved, positions, allowed
        )
        results = jnp.where(
            is_live & head_section, results.at[micro_slot].set(grad_inputs), results
        )
        if step_index < micro_count:
            from_next = from_behind(grad_inputs.astype(jnp.bfloat16), "section", -1)
        if stashed is None:
            stashed = tuple(
                (jnp.zeros((micro_count,) + current.shape, current.dtype) for current in operands)
            )
            gain_sums = tuple((jnp.zeros_like(current) for current in gain_terms))
        stashed = tuple(
            (
                jnp.where(is_live, buffer.at[micro_slot].set(current), buffer)
                for buffer, current in zip(stashed, operands)
            )
        )
        gain_sums = tuple(
            (total_so_far + current for total_so_far, current in zip(gain_sums, gain_terms))
        )
    merged = tuple(
        (buffer.reshape((micro_count * count_of_rows,) + buffer.shape[2:]) for buffer in stashed)
    )
    gradients = reduce_grads(merged, gain_sums)
    grad_mixer, heads_gradient, grad_merge, grad_head, grad_feed, grad_expand, grad_reduce = (
        gradients
    )
    return (
        results[None, :, None],
        grad_mixer[None],
        heads_gradient[None],
        grad_merge[None],
        grad_head[None],
        grad_feed[None],
        grad_expand[None],
        grad_reduce[None],
    )


MESH = pl.DeviceIdType.MESH
MERGED = QUERY_HEADS // KEY_VALUE_HEADS * HEAD_SIZE
JOINT = MERGED + 2 * HEAD_SIZE
VMEM_BYTES = 63 * 2**20


def mm(left, right):
    return jnp.dot(left, right, preferred_element_type=jnp.float32)


def mm_t(left, right):
    return lax.dot_general(
        left, right, (((1,), (1,)), ((), ())), preferred_element_type=jnp.float32
    )


def t_mm(left, right):
    return lax.dot_general(
        left, right, (((0,), (0,)), ((), ())), preferred_element_type=jnp.float32
    )


def remote(src, dst, send, recv, device):
    return pltpu.make_async_remote_copy(
        src_ref=src,
        dst_ref=dst,
        send_sem=send,
        recv_sem=recv,
        device_id=device,
        device_id_type=MESH,
    )


class Place:
    def __init__(self):
        self.index = lax.axis_index("fsdp")
        self.core = lax.rem(self.index, 2)
        self.chip = lax.div(self.index, 2)
        self.x = lax.rem(self.chip, 2)
        self.y = lax.div(self.chip, 2)
        self.x_peer = {"fsdp": self.index + 2 - 4 * self.x}
        self.y_peer = {"fsdp": self.index + 4 - 8 * self.y}
        self.core_peer = {"fsdp": self.index + 1 - 2 * self.core}
        self.section = lax.axis_index("section")
        self.section_peer = {"section": 1 - self.section}
        self.replica = lax.axis_index("rep")
        self.rep_peer = {"rep": 1 - self.replica}

    def chip_at(self, rel):
        x, y = self.x, self.y
        if rel in (1, 3):
            x = 1 - x
        if rel in (2, 3):
            y = 1 - y
        return 2 * y + x

    def others(self):
        order = ((3, 0), (3, 1), (1, 0), (1, 1), (2, 0), (2, 1), (0, 1), (0, 0))
        return [
            (at, 2 * self.chip_at(rel) + (1 - self.core if other else self.core))
            for at, (rel, other) in enumerate(order)
        ]

    def greet(self, peers):
        barrier = pltpu.get_barrier_semaphore()
        for peer in peers:
            pl.semaphore_signal(barrier, inc=1, device_id=peer, device_id_type=MESH)
        pl.semaphore_wait(barrier, len(peers))


class Gather:
    def __init__(self, place, full, send, recv, rows):
        half = rows // 2

        def span(rel, part=None):
            first = (2 * place.chip_at(rel) + place.core) * rows
            if part is None:
                return pl.ds(pl.multiple_of(first, rows), rows)
            return pl.ds(pl.multiple_of(first + part * half, half), half)

        def copy(at, piece, peer):
            block = full.at[piece]
            return remote(block, block, send.at[at], recv.at[at], peer)

        self.copies = [
            copy(0, span(0, 1), place.x_peer),
            copy(1, span(0, 0), place.x_peer),
            copy(2, span(0, 0), place.y_peer),
            copy(3, span(0, 1), place.y_peer),
            copy(4, span(0), place.core_peer),
            copy(5, span(1, 1), place.y_peer),
            copy(6, span(2, 0), place.x_peer),
            copy(7, span(1), place.core_peer),
            copy(8, span(2), place.core_peer),
            copy(9, span(3), place.core_peer),
        ]

    def start(self):
        for at in (0, 2, 4, 1, 3):
            self.copies[at].start()

    def relay(self):
        self.copies[0].wait_recv()
        self.copies[5].start()
        self.copies[2].wait_recv()
        self.copies[6].start()

    def near(self):
        self.copies[1].wait_recv()
        self.copies[7].start()
        self.copies[3].wait_recv()
        self.copies[8].start()

    def far(self):
        self.copies[5].wait_recv()
        self.copies[6].wait_recv()
        self.copies[9].start()

    def wait(self, at):
        self.copies[at].wait_recv()

    def finish(self):
        for entry in self.copies:
            entry.wait_send()

    def over_blocks(self, block, between=lambda: None, early=lambda at: None):
        self.start()
        early(0)
        self.wait(4)
        block(0)
        early(1)
        self.relay()
        early(2)
        self.near()
        self.wait(7)
        block(1)
        early(3)
        self.wait(8)
        block(2)
        early(4)
        between()
        self.far()
        self.wait(9)
        block(3)


class Scatter:
    def __init__(self, place, held, to_core, from_core, to_x, to_y, from_x, from_y, send, recv, rows):
        self.place, self.held, self.to_core, self.from_core = place, held, to_core, from_core
        self.to_x, self.to_y, self.from_x, self.from_y = to_x, to_y, from_x, from_y
        self.rows, self.half = rows, rows // 2

        def copy(at, src, dst, peer):
            return remote(src, dst, send.at[at], recv.at[at], peer)

        self.copies = [
            copy(rel, to_core.at[rel], from_core.at[rel], place.core_peer) for rel in range(4)
        ] + [
            copy(4, to_x.at[0], from_x.at[0], place.x_peer),
            copy(5, to_y.at[0], from_y.at[0], place.y_peer),
            copy(6, to_x.at[1], from_x.at[1], place.x_peer),
            copy(7, to_y.at[1], from_y.at[1], place.y_peer),
            copy(8, to_y.at[2], from_y.at[2], place.y_peer),
            copy(9, to_x.at[2], from_x.at[2], place.x_peer),
        ]

    def put(self, rel, product, width):
        step, rows, mine = 512, self.rows, self.place.core == 0

        @pl.loop(0, width // step)
        def _(at):
            columns = pl.ds(pl.multiple_of(at * step, step), step)
            value = product(columns)
            low, high = value[:rows], value[rows:]
            self.held[rel, :, columns] = jnp.where(mine, low, high)
            self.to_core[rel, :, columns] = jnp.where(mine, high, low).astype(jnp.bfloat16)

        self.copies[rel].start()

    def pair(self, rel):
        self.copies[rel].wait_recv()
        half, held = self.half, self.held

        @pl.loop(0, self.rows // 16)
        def _(at):
            span = pl.ds(pl.multiple_of(at * 16, 16), 16)
            held[rel, span, :] += self.from_core[rel, span, :].astype(jnp.float32)

        if rel == 3:
            self.to_x[0] = held[3, :half].astype(jnp.bfloat16)
            self.copies[4].start()
            self.to_y[0] = held[3, half:].astype(jnp.bfloat16)
            self.copies[5].start()
        if rel == 1:
            self.to_x[1] = held[1, :half].astype(jnp.bfloat16)
            self.copies[6].start()
        if rel == 2:
            self.to_y[1] = held[2, half:].astype(jnp.bfloat16)
            self.copies[7].start()

    def relay(self):
        half, held = self.half, self.held
        self.copies[4].wait_recv()
        self.to_y[2] = (held[2, :half] + self.from_x[0].astype(jnp.float32)).astype(jnp.bfloat16)
        self.copies[8].start()
        self.copies[5].wait_recv()
        self.to_x[2] = (held[1, half:] + self.from_y[0].astype(jnp.float32)).astype(jnp.bfloat16)
        self.copies[9].start()

    def total(self, add):
        for at in (6, 7, 8, 9):
            self.copies[at].wait_recv()
        count = self.half // 16

        @pl.loop(0, count)
        def _(at):
            span = pl.ds(pl.multiple_of(at * 16, 16), 16)
            low = self.held[0, span, :] + self.from_x[1, span, :].astype(jnp.float32)
            add(span, low + self.from_y[2, span, :].astype(jnp.float32))

        @pl.loop(0, count)
        def _(at):
            span = pl.ds(pl.multiple_of(at * 16, 16), 16)
            below = pl.ds(pl.multiple_of(self.half + at * 16, 16), 16)
            high = self.held[0, below, :] + self.from_y[1, span, :].astype(jnp.float32)
            add(below, high + self.from_x[2, span, :].astype(jnp.float32))

        for entry in self.copies:
            entry.wait_send()


def by_rows(count, body):
    @pl.loop(0, count // 16)
    def _(at):
        body(pl.ds(pl.multiple_of(at * 16, 16), 16))


def inverse_size(values):
    return lax.rsqrt(jnp.mean(values * values, axis=-1, keepdims=True) + NORM_EPS)


def norm_back(values, gain, upstream):
    size = inverse_size(values)
    scaled_up = upstream * gain
    back = size * scaled_up - values * (
        size * size * size * jnp.mean(values * scaled_up, axis=-1, keepdims=True)
    )
    return back, upstream * values * size


def turn(values, cosine, sine):
    return values * cosine + pltpu.roll(values, HEAD_SIZE // 2, 1) * sine


def turn_back(values, cosine, sine):
    return values * cosine + pltpu.roll(values * sine, HEAD_SIZE // 2, 1)


def probabilities(queries, keys, first_keys, first_row):
    scores = mm_t(queries, keys) * HEAD_SIZE ** (-0.5)
    key_index = lax.broadcasted_iota(jnp.int32, scores.shape, 1)
    row_index = first_row + lax.broadcasted_iota(jnp.int32, scores.shape, 0)
    allowed = (key_index >= first_keys) & (key_index <= row_index)
    scores = jnp.where(allowed, scores, MASKED_SCORE)
    powers = jnp.exp(scores - jnp.max(scores, axis=-1, keepdims=True))
    return powers / jnp.sum(powers, axis=-1, keepdims=True)


def block_rows(place, rel, rows):
    return pl.ds(pl.multiple_of(place.chip_at(rel) * 2 * rows, 2 * rows), 2 * rows)


def shard_columns(first, device, count):
    return pl.ds(pl.multiple_of(first + device * count, 128), count)


def layer_forward_step(place, rows, refs, buffers, slot, step, hooks):
    (wh, wm, we, wr), gains_ref, head_gain_ref = refs.weights, refs.gains, refs.head_gain
    current, middle, result, result_b = (
        buffers.current,
        buffers.middle,
        buffers.result,
        buffers.result_b,
    )
    full_a, full_b = buffers.full_a, buffers.full_b
    projected, heads, mixed = buffers.projected, buffers.heads, buffers.mixed
    joined, hidden = buffers.joined, buffers.hidden
    chip_rows, width, hidden_width = 2 * rows, current.shape[1], wr.shape[0]
    save_sem = buffers.save_sem
    tables = [
        pltpu.make_async_copy(src.at[slot], dst, buffers.table_sem.at[at])
        for at, (src, dst) in enumerate(zip(refs.tables, buffers.tables))
    ]
    cosine, sine, first_key = buffers.tables
    for table in tables:
        table.start()

    def save(at, src, dst):
        copy = pltpu.make_async_copy(src, dst.at[slot], save_sem.at[at])
        copy.start()
        return copy

    saves = [save(0, current, refs.inputs)]

    def enter(span):
        values = current[span, :].astype(jnp.float32)
        base = pl.multiple_of(place.index * rows + span.start, 16)
        full_a[pl.ds(base, 16), :] = (
            values * inverse_size(values) * gains_ref[0:1, :]
        ).astype(jnp.bfloat16)

    by_rows(rows, enter)
    for table in tables:
        table.wait()
    gather = Gather(place, full_a, *buffers.gather_a, rows)

    def heads_block(rel):
        span = block_rows(place, rel, rows)
        if rel == 0:
            hooks.heads()
        values = mm(full_a[span, :], wh[...])
        projected[span, :] = values
        for at in range(3):
            columns = pl.ds(at * HEAD_SIZE, HEAD_SIZE)
            one = values[:, at * HEAD_SIZE : (at + 1) * HEAD_SIZE]
            gain = head_gain_ref[0:1, :] if at < 2 else head_gain_ref[1:2, :]
            heads[span, columns] = turn(
                one * inverse_size(one) * gain, cosine[span, :], sine[span, :]
            ).astype(jnp.bfloat16)
        heads[span, 3 * HEAD_SIZE :] = values[:, 3 * HEAD_SIZE :].astype(jnp.bfloat16)

    gather.over_blocks(heads_block)
    hooks.service()
    saves += [
        save(1, full_a, refs.normal_a),
        save(2, projected, refs.projected),
        save(3, heads, refs.heads),
    ]
    scatter = Scatter(place, *buffers.scatter, *buffers.scatter_a, rows)

    def attend_block(rel):
        first_row = place.chip_at(rel) * chip_rows
        span = block_rows(place, rel, rows)
        for at in range(2):
            columns = pl.ds(at * HEAD_SIZE, HEAD_SIZE)
            probs = probabilities(
                heads[span, columns],
                heads[:, 2 * HEAD_SIZE : 3 * HEAD_SIZE],
                first_key[span, :],
                first_row,
            )
            mixed[span, columns] = mm(
                probs.astype(jnp.bfloat16), heads[:, 3 * HEAD_SIZE :]
            ).astype(jnp.bfloat16)
        scatter.put(rel, lambda columns: mm(mixed[span, :], wm[:, columns]), width)

    attend_block(3)
    scatter.pair(3)
    attend_block(2)
    scatter.pair(2)
    attend_block(1)
    scatter.pair(1)
    attend_block(0)
    saves.append(save(4, mixed, refs.mixed))
    scatter.relay()
    scatter.pair(0)

    def residual(span, value):
        values = value + current[span, :].astype(jnp.float32)
        middle[span, :] = values
        base = pl.multiple_of(place.index * rows + span.start, 16)
        full_b[pl.ds(base, 16), :] = (
            values * inverse_size(values) * gains_ref[1:2, :]
        ).astype(jnp.bfloat16)

    scatter.total(residual)
    gather.finish()
    saves.append(save(5, middle, refs.middle))
    for copy in saves[:5]:
        copy.wait()
    gather_b = Gather(place, full_b, *buffers.gather_b, rows)
    scatter_b = Scatter(place, *buffers.scatter, *buffers.scatter_b, rows)
    joined_copies = {}

    def feed_block(rel):
        span = block_rows(place, rel, rows)
        stage = joined.at[rel % 2]
        if rel == 0:
            hooks.feed()
        if rel >= 2:
            joined_copies[rel - 2].wait()

        @pl.loop(0, hidden_width // 256)
        def _(at):
            columns = pl.ds(pl.multiple_of(at * 256, 256), 256)
            later = pl.ds(pl.multiple_of(hidden_width + at * 256, 256), 256)
            gate = mm(full_b[span, :], we[:, columns])
            up = mm(full_b[span, :], we[:, later])
            stage[:, columns] = gate
            stage[:, later] = up
            hidden[span, columns] = (gate * jax.nn.sigmoid(gate) * up).astype(jnp.bfloat16)

        copy = pltpu.make_async_copy(
            stage, refs.joined.at[slot, span], save_sem.at[8 + rel % 2]
        )
        copy.start()
        joined_copies[rel] = copy
        scatter_b.put(rel, lambda columns: mm(hidden[span, :], wr[:, columns]), width)
        if rel in (1, 2):
            scatter_b.pair(rel - 1)

    gather_b.over_blocks(feed_block, lambda: scatter_b.pair(2))
    later_saves = [save(6, full_b, refs.normal_b), save(7, hidden, refs.hidden)]
    scatter_b.pair(3)
    scatter_b.relay()
    hooks.finish()

    def finish(span, value):
        values = value + middle[span, :]
        result[span, :] = values
        result_b[span, :] = values.astype(jnp.bfloat16)

    scatter_b.total(finish)
    hooks.hand()
    gather_b.finish()
    for copy in [saves[5]] + later_saves + [joined_copies[2], joined_copies[3]]:
        copy.wait()
    hooks.after()


def feed_back(place, rows, gather, scatter, full, weights, joined, joined_load, out_of, done):
    wm, we, wr = weights
    hidden_width, width = wr.shape

    def feed_block(rel):
        span = block_rows(place, rel, rows)
        stage, out = joined.at[rel % 2], out_of(rel)
        joined_load(rel).wait()

        @pl.loop(0, hidden_width // 256)
        def _(at):
            columns = pl.ds(pl.multiple_of(at * 256, 256), 256)
            later = pl.ds(pl.multiple_of(hidden_width + at * 256, 256), 256)
            grad = mm_t(full[span, :], wr[columns, :])
            gate, up = stage[:, columns], stage[:, later]
            sigmoid = jax.nn.sigmoid(gate)
            unit = gate * sigmoid
            out[:, columns] = (grad * up * (sigmoid + unit * (1.0 - sigmoid))).astype(jnp.bfloat16)
            out[:, later] = (grad * unit).astype(jnp.bfloat16)

        if rel < 2:
            joined_load(rel + 2).start()
        done(rel, out)
        scatter.put(rel, lambda columns: mm_t(out[...], we[columns, :]), width)
        if rel in (1, 2):
            scatter.pair(rel - 1)

    gather.over_blocks(feed_block, lambda: scatter.pair(2))
    scatter.pair(3)


def feed_input_back(place, rows, scatter, middle, gains_ref, out_gains, current, result, full_b):
    out_gains[1:2, :] = jnp.zeros_like(out_gains[1:2, :])

    def feed_norm(span, value):
        back, gain_term = norm_back(middle[span, :], gains_ref[1:2, :], value)
        out_gains[1:2, :] += jnp.sum(gain_term, axis=0, keepdims=True)
        total = back + current[span, :].astype(jnp.float32)
        result[span, :] = total
        base = pl.multiple_of(place.index * rows + span.start, 16)
        full_b[pl.ds(base, 16), :] = total.astype(jnp.bfloat16)

    scatter.total(feed_norm)


def attention_back(
    heads, grad_mixed, first_key, grad_queries, grad_keys, grad_values, chip_rows
):
    grad_keys[...] = jnp.zeros_like(grad_keys)
    grad_values[...] = jnp.zeros_like(grad_values)
    for block in range(heads.shape[0] // chip_rows):
        span = pl.ds(block * chip_rows, chip_rows)
        seen = (block + 1) * chip_rows
        keys = heads[:seen, 2 * HEAD_SIZE : 3 * HEAD_SIZE]
        values = heads[:seen, 3 * HEAD_SIZE :]
        for at in range(2):
            columns = pl.ds(at * HEAD_SIZE, HEAD_SIZE)
            queries = heads[span, columns]
            grad = grad_mixed[span, columns]
            probs = probabilities(queries, keys, first_key[span, :], block * chip_rows)
            grad_probs = mm_t(grad, values)
            grad_scores = (
                probs * (grad_probs - jnp.sum(probs * grad_probs, axis=-1, keepdims=True))
            ).astype(jnp.bfloat16)
            grad_queries[span, columns] = mm(grad_scores, keys) * HEAD_SIZE ** (-0.5)
            grad_keys[:seen, :] += t_mm(grad_scores, queries) * HEAD_SIZE ** (-0.5)
            grad_values[:seen, :] += t_mm(probs.astype(jnp.bfloat16), grad)


def project_back(
    place, rows, scatter, buffers, head_gain_ref, out_head_gain, wh
):
    projected, grad_projected = buffers.projected, buffers.grad_projected
    grad_queries, grad_keys, grad_values = buffers.attention_grads
    cosine, sine, _ = buffers.tables
    out_head_gain[...] = jnp.zeros_like(out_head_gain)

    def project_block(rel):
        span = block_rows(place, rel, rows)
        for at in range(3):
            columns = pl.ds(at * HEAD_SIZE, HEAD_SIZE)
            which = 0 if at < 2 else 1
            upstream = grad_queries[span, columns] if at < 2 else grad_keys[span, :]
            back, gain_term = norm_back(
                projected[span, columns],
                head_gain_ref[which : which + 1, :],
                turn_back(upstream, cosine[span, :], sine[span, :]),
            )
            out_head_gain[which : which + 1, :] += jnp.sum(gain_term, axis=0, keepdims=True)
            grad_projected[span, columns] = back.astype(jnp.bfloat16)
        grad_projected[span, 3 * HEAD_SIZE :] = grad_values[span, :].astype(jnp.bfloat16)
        scatter.put(rel, lambda columns: mm_t(grad_projected[span, :], wh[columns, :]), wh.shape[0])

    project_block(3)
    scatter.pair(3)
    project_block(2)
    scatter.pair(2)
    project_block(1)
    scatter.pair(1)
    project_block(0)


def input_back(scatter, inputs, gains_ref, out_gains, result, result_b):
    out_gains[0:1, :] = jnp.zeros_like(out_gains[0:1, :])

    def mixer_norm(span, value):
        back, gain_term = norm_back(inputs[span, :].astype(jnp.float32), gains_ref[0:1, :], value)
        out_gains[0:1, :] += jnp.sum(gain_term, axis=0, keepdims=True)
        total = back + result[span, :]
        result[span, :] = total
        if result_b is not None:
            result_b[span, :] = total.astype(jnp.bfloat16)

    scatter.total(mixer_norm)


def layer_backward_step(place, rows, refs, buffers, slot, hooks):
    (wh, wm, we, wr), gains_ref = refs.weights, refs.gains
    current, middle, result, result_b, inputs = (
        buffers.current,
        buffers.middle,
        buffers.result,
        buffers.result_b,
        buffers.inputs,
    )
    full_a, full_b, joined = buffers.full_a, buffers.full_b, buffers.joined
    save_sem, grad_joined = buffers.save_sem, buffers.grad_joined
    tables = [
        pltpu.make_async_copy(src.at[slot], dst, buffers.table_sem.at[at])
        for at, (src, dst) in enumerate(
            [
                *zip(refs.tables, buffers.tables),
                (refs.middle, middle),
                (refs.projected, buffers.projected),
                (refs.heads, buffers.heads),
                (refs.inputs, inputs),
            ]
        )
    ]
    for table in tables:
        table.start()

    def joined_load(rel):
        return pltpu.make_async_copy(
            refs.joined.at[slot, block_rows(place, rel, rows)],
            joined.at[rel % 2],
            buffers.joined_sem.at[rel % 2],
        )

    joined_load(0).start()
    joined_load(1).start()
    own_rows = pl.ds(pl.multiple_of(place.index * rows, rows), rows)
    full_a[own_rows, :] = current[...]

    def save(at, src, dst):
        copy = pltpu.make_async_copy(src, dst.at[slot], save_sem.at[at])
        copy.start()
        return copy

    gather = Gather(place, full_a, *buffers.gather_a, rows)
    scatter = Scatter(place, *buffers.scatter, *buffers.scatter_a, rows)
    def out_of(rel):
        return grad_joined.at[block_rows(place, rel, rows)]

    feed_back(
        place,
        rows,
        gather,
        scatter,
        full_a,
        (wm, we, wr),
        joined,
        joined_load,
        out_of,
        lambda rel, out: None,
    )
    upstream_save = save(0, full_a, refs.upstream)
    scatter.relay()
    for table in tables:
        table.wait()
    out_gains = refs.out_gains.at[slot]
    feed_input_back(place, rows, scatter, middle, gains_ref, out_gains, current, result, full_b)
    gather.finish()
    upstream_save.wait()
    gather_b = Gather(place, full_b, *buffers.gather_b, rows)
    scatter_b = Scatter(place, *buffers.scatter, *buffers.scatter_b, rows)
    grad_mixed = buffers.mixed

    def mixed_block(rel):
        span = block_rows(place, rel, rows)
        grad_mixed[span, :] = mm_t(full_b[span, :], wm[...]).astype(jnp.bfloat16)

    gather_b.over_blocks(mixed_block, early=hooks.early)
    middle_save = save(1, full_b, refs.grad_middle)
    attention_back(
        buffers.heads,
        grad_mixed,
        buffers.tables[2],
        *buffers.attention_grads,
        2 * rows,
    )
    project_back(
        place, rows, scatter_b, buffers, refs.head_gain, refs.out_head_gain.at[slot], wh
    )
    projected_save = save(2, buffers.grad_projected, refs.grad_projected)
    hooks.early(5)
    scatter_b.relay()
    scatter_b.pair(0)
    hooks.finish()
    input_back(scatter_b, inputs, gains_ref, out_gains, result, result_b)
    hooks.hand()
    gather_b.finish()
    for copy in (middle_save, projected_save):
        copy.wait()


class Saved(typing.NamedTuple):
    inputs: typing.Any
    normal_a: typing.Any
    projected: typing.Any
    heads: typing.Any
    mixed: typing.Any
    middle: typing.Any
    normal_b: typing.Any
    joined: typing.Any
    hidden: typing.Any
    upstream: typing.Any
    grad_middle: typing.Any
    grad_projected: typing.Any


class Layers(typing.NamedTuple):
    rows: typing.Any
    saved: Saved
    handed: typing.Any
    own_first: typing.Any
    other_first: typing.Any
    other_normal: typing.Any
    heads_w: typing.Any
    expand_w: typing.Any
    gains: typing.Any
    head_gain: typing.Any
    gain_terms: typing.Any
    head_terms: typing.Any


class LayerBuffers(typing.NamedTuple):
    current: typing.Any
    inputs: typing.Any
    middle: typing.Any
    result: typing.Any
    result_b: typing.Any
    full_a: typing.Any
    full_b: typing.Any
    projected: typing.Any
    heads: typing.Any
    mixed: typing.Any
    joined: typing.Any
    hidden: typing.Any
    grad_joined: typing.Any
    grad_projected: typing.Any


class GradientBuffers(typing.NamedTuple):
    current: typing.Any
    inputs: typing.Any
    result: typing.Any
    full_a: typing.Any
    full_b: typing.Any
    projected: typing.Any
    heads: typing.Any
    mixed: typing.Any
    joined: typing.Any
    grad_projected: typing.Any


def layers_kernel(rows, *refs):
    refs = list(refs)

    def some(count):
        taken = refs[:count]
        del refs[:count]
        return taken

    own_ref, gain_ref = some(2)
    table_refs = some(3)
    heads_w, merge_w, expand_w, reduce_w = some(4)
    (out_rows,) = some(1)
    saved = types.SimpleNamespace(**Saved(*some(12))._asdict())
    out_handed, own_first, other_first, other_normal = some(4)
    out_heads_w, out_expand_w = some(2)
    gains_ref, head_gain_ref, out_gains, out_head_gain = some(4)
    all_gains, wh, wm, we, wr, arrived = some(6)
    buffers = types.SimpleNamespace(**LayerBuffers(*some(14))._asdict())
    buffers.tables = some(3)
    buffers.attention_grads = some(3)
    buffers.scatter = some(7)
    first_tiles, first_turned, first_stage = some(3)
    load_sem, spread_send, spread_recv = some(3)
    share_send, share_recv = some(2)
    tile_sem, first_sem, first_send, first_recv, normal_send, normal_recv = some(6)
    buffers.save_sem, buffers.table_sem, buffers.joined_sem = some(3)
    hand_send, hand_recv, out_sem = some(3)
    buffers.gather_a, buffers.scatter_a = some(2), some(2)
    buffers.gather_b, buffers.scatter_b = some(2), some(2)
    saved.weights, saved.tables = (wh, wm, we, wr), table_refs
    saved.gains, saved.head_gain = gains_ref, head_gain_ref
    saved.out_gains, saved.out_head_gain = out_gains, out_head_gain
    place = Place()
    head = place.section == 0
    rest = jnp.logical_not(head)
    hidden_width = wr.shape[0]
    depth = heads_w.shape[0]
    query_width, key_width = QUERY_HEADS * HEAD_SIZE, KEY_VALUE_HEADS * HEAD_SIZE
    loads = [
        pltpu.make_async_copy(src, dst, load_sem.at[at])
        for at, (src, dst) in enumerate(((merge_w, wm), (reduce_w, wr)))
    ]
    for load in loads:
        load.start()
    shard_rows = pl.ds(pl.multiple_of(place.index * depth, depth), depth)

    def spread(at, device, piece, src, dst):
        if at < 7:
            return remote(
                src, dst, spread_send.at[piece, at], spread_recv.at[piece, at], {"fsdp": device}
            )
        return pltpu.make_async_copy(src, dst, load_sem.at[2 + piece])

    gain_copies = [
        spread(at, device, 0, gain_ref, all_gains.at[place.index])
        for at, device in place.others()
    ]
    heads_copies, expand_copies = [], []
    for at, device in place.others():
        for piece, first, count, into in (
            (1, 0, MERGED, 0),
            (2, query_width, HEAD_SIZE, MERGED),
            (3, query_width + key_width, HEAD_SIZE, MERGED + HEAD_SIZE),
        ):
            src = heads_w.at[:, shard_columns(first, device, count)]
            heads_copies.append(
                spread(at, device, piece, src, wh.at[shard_rows, pl.ds(into, count)])
            )
        for piece in range(2):
            src = expand_w.at[:, shard_columns(piece * FF, device, hidden_width)]
            dst = we.at[shard_rows, pl.ds(piece * hidden_width, hidden_width)]
            expand_copies.append(spread(at, device, 4 + piece, src, dst))

    def arrive(copies, pieces):
        for copy in copies[:-pieces]:
            copy.wait_recv()
        for copy in copies[-pieces:]:
            copy.wait()

    heads_out = pltpu.make_async_copy(wh, out_heads_w, load_sem.at[8])
    expand_out = pltpu.make_async_copy(we, out_expand_w, load_sem.at[9])

    def share(at, device, kind, weight):
        block = weight.at[pl.ds(pl.multiple_of(device * depth, depth), depth)]
        return remote(
            block, block, share_send.at[kind, at], share_recv.at[kind, at], place.rep_peer
        )

    def start_all(copies, pieces, shared, first=0, last=PLANE):
        for at, device in place.others()[first:last]:
            mine = copies[at * pieces : (at + 1) * pieces]

            def begin():
                for copy in mine:
                    copy.start()

            if at < shared:
                pl.when(place.replica == at % 2)(begin)
            else:
                begin()

    def pass_on(copies, pieces, kind, weight, first, last):
        for at, device in place.others()[first:last]:
            mine = copies[at * pieces : (at + 1) * pieces]

            @pl.when(place.replica == at % 2)
            def _():
                for copy in mine:
                    copy.wait_recv()
                share(at, device, kind, weight).start()

    def take_shared(kind, weight, shared):
        for at, device in place.others()[:shared]:

            @pl.when(place.replica != at % 2)
            def _():
                share(at, device, kind, weight).wait_recv()

    def sent(copies, pieces, kind, weight, shared):
        for at, device in place.others()[:7]:
            mine = copies[at * pieces : (at + 1) * pieces]

            def settle():
                for copy in mine:
                    copy.wait_send()
                if at < shared:
                    share(at, device, kind, weight).wait_send()

            if at < shared:
                pl.when(place.replica == at % 2)(settle)
            else:
                settle()

    place.greet(
        [{"fsdp": device} for _, device in place.others()[:7]]
        + [place.section_peer, place.rep_peer]
    )
    for copy in gain_copies:
        copy.start()
    start_all(heads_copies, 3, 2)

    arrive(gain_copies, 1)
    for shard in range(PLANE):
        part = slice(shard * depth, (shard + 1) * depth)
        gains_ref[0:1, part] = all_gains[shard][:, :depth]
        gains_ref[1:2, part] = all_gains[shard][:, depth : 2 * depth]
    per_row = PLANE // 2
    count = 2 * HEAD_SIZE // PLANE
    for row in range(2):
        head_gain_ref[row : row + 1, :] = jnp.concatenate(
            [
                all_gains[row * per_row + at][:, 2 * depth : 2 * depth + count]
                for at in range(per_row)
            ],
            axis=1,
        )

    current, result, result_b = buffers.current, buffers.result, buffers.result_b
    length = buffers.full_a.shape[0]

    def tile_rows(at):
        return pl.ds(at * depth, depth)

    def first_tile(at):
        return pltpu.make_async_copy(
            saved.normal_b.at[0, :, tile_rows(at)], first_tiles.at[at % 2], tile_sem.at[at % 2]
        )

    def first_save(at):
        return pltpu.make_async_copy(
            first_stage.at[at % 2], own_first.at[tile_rows(at)], first_sem.at[at % 2]
        )

    def first_copy(at):
        block = tile_rows(at)
        return remote(
            own_first.at[block],
            other_first.at[block],
            first_send.at[at],
            first_recv.at[at],
            place.rep_peer,
        )

    def early_tile(at):
        first_tile(at).wait()

        @pl.loop(0, length // 256)
        def _(chunk):
            span = pl.ds(pl.multiple_of(chunk * 256, 256), 256)
            first_turned[:, span] = first_tiles[at % 2, span, :].T

        if at + 2 < PLANE:
            first_tile(at + 2).start()

        @pl.loop(0, 2 * hidden_width // 512)
        def _(chunk):
            columns = pl.ds(pl.multiple_of(chunk * 512, 512), 512)
            first_stage[at % 2, :, columns] = mm(
                first_turned[...], buffers.grad_joined[:, columns]
            ).astype(jnp.bfloat16)

        first_save(at).start()
        if at:
            first_save(at - 1).wait()
            pl.when(head)(first_copy(at - 1).start)
        if at == PLANE - 1:
            first_save(at).wait()
            pl.when(head)(first_copy(at).start)

    half = length // 2
    half_rows = pl.ds(pl.multiple_of(place.core * half, half), half)
    normal_copy = remote(
        saved.normal_b.at[1, half_rows],
        other_normal.at[half_rows],
        normal_send.at[0],
        normal_recv.at[0],
        place.rep_peer,
    )
    normal_pass = remote(
        other_normal.at[half_rows],
        other_normal.at[half_rows],
        normal_send.at[1],
        normal_recv.at[1],
        place.core_peer,
    )

    def hand(slot):
        return remote(
            result_b, arrived.at[slot], hand_send.at[slot], hand_recv.at[slot], place.section_peer
        )

    def rows_copy(slot):
        return pltpu.make_async_copy(result, out_rows.at[slot], out_sem.at[0])

    def save_rows(slot):
        copy = rows_copy(slot)
        copy.start()
        copy.wait()

    def heads_ready():
        pass_on(heads_copies, 3, 0, wh, 0, 2)
        arrive(heads_copies[6:], 3)
        take_shared(0, wh, 2)
        heads_out.start()
        start_all(expand_copies, 2, 2, 0, 2)

    def expand_service():
        pass_on(expand_copies, 2, 1, we, 0, 2)
        start_all(expand_copies, 2, 2, 2)

    def feed_ready():
        arrive(expand_copies[4:], 2)
        take_shared(1, we, 2)
        expand_out.start()

    @pl.when(rest)
    def _():
        heads_ready()
        expand_service()
        feed_ready()

    for load in loads:
        load.wait()

    @pl.loop(0, 5)
    def _(step):
        forward = (head & (step <= 1)) | (rest & ((step == 1) | (step == 3)))
        backward = (step == 4) | (rest & (step == 2))

        @pl.when(forward)
        def _():
            slot = jnp.where(head, step, lax.div(step - 1, 2))

            @pl.when(head)
            def _():
                current[...] = own_ref[slot]

            @pl.when(rest)
            def _():
                hand(slot).wait_recv()
                current[...] = arrived[slot]

            def first(body):
                return lambda: pl.when(head & (slot == 0))(body)


            def finish():
                @pl.when(slot == 1)
                def _():
                    hand(0).wait_send()

            def handing():
                @pl.when(head)
                def _():
                    hand(slot).start()

                @pl.when(rest)
                def _():
                    save_rows(slot)

            def after():
                pl.when(slot == 1)(normal_copy.start)

            layer_forward_step(
                place,
                rows,
                saved,
                buffers,
                slot,
                step,
                types.SimpleNamespace(
                    heads=first(heads_ready),
                    feed=first(feed_ready),
                    service=first(expand_service),
                    finish=finish,
                    hand=handing,
                    after=after,
                ),
            )

        @pl.when(backward)
        def _():
            slot = jnp.where(head, 0, lax.div(step - 2, 2))

            @pl.when(head)
            def _():
                hand(0).wait_recv()
                current[...] = arrived[0]

            @pl.when(rest)
            def _():
                current[...] = own_ref[slot]

            def finish():
                @pl.when(head)
                def _():
                    hand(1).wait_send()

            def handing():
                @pl.when(rest)
                def _():
                    hand(slot).start()

                @pl.when(rest & (slot == 0))
                def _():
                    for at in range(PLANE):
                        first_copy(at).start()

                @pl.when(head)
                def _():
                    rows_copy(slot).start()

            def early(at):
                groups = ((), (0, 1, 2), (3,), (4,), (5, 6), (7,))

                @pl.when(slot == 0)
                def _():
                    if at == 0:
                        first_tile(0).start()
                        first_tile(1).start()
                    for tile in groups[at]:
                        early_tile(tile)

            hooks = types.SimpleNamespace(finish=finish, hand=handing, early=early)
            layer_backward_step(place, rows, saved, buffers, slot, hooks)

    @pl.when(head)
    def _():
        hand(1).wait_recv()
        current[...] = arrived[1]

    @pl.when(rest)
    def _():
        hand(1).wait_send()
        current[...] = own_ref[1]

    handed = pltpu.make_async_copy(current, out_handed, out_sem.at[1])
    handed.start()
    normal_copy.wait_recv()
    normal_pass.start()
    heads_out.wait()
    expand_out.wait()
    for copy in gain_copies[:7]:
        copy.wait_send()
    sent(heads_copies, 3, 0, wh, 2)
    sent(expand_copies, 2, 1, we, 2)
    for at in range(PLANE):
        first_copy(at).wait()
    normal_copy.wait_send()
    normal_pass.wait()
    handed.wait()
    pl.when(head)(lambda: rows_copy(0).wait())


def gradient_kernel(rows, *refs):
    refs = list(refs)

    def some(count):
        taken = refs[:count]
        del refs[:count]
        return taken

    gains_ref, head_gain_ref, first_gains, first_head_gain = some(4)
    table_refs = some(3)
    heads_w, merge_w, expand_w, reduce_w = some(4)
    in_handed, in_inputs, in_projected, in_heads, in_middle, in_joined = some(6)
    hidden_all, upstream_all, normal_b_all, other_normal = some(4)
    mixed_all, grad_middle_all, normal_a_all, grad_projected_all = some(4)
    own_first, other_first = some(2)
    (out_result,) = some(1)
    own_heads, other_heads, own_merge, other_merge = some(4)
    own_expand, own_reduce, other_reduce = some(3)
    (out_gain,) = some(1)
    wh, wm, we, wr = some(4)
    buffers = types.SimpleNamespace(**GradientBuffers(*some(10))._asdict())
    buffers.tables = some(3)
    buffers.attention_grads = some(3)
    buffers.scatter = some(7)
    tiles, turned, wide, narrow, first_projected = some(5)
    gains, head_gain, gain_out, gain_in, gain_sum, gain_other = some(6)
    load_sem, tile_sem, joined_sem, save_sem = some(4)
    buffers.gather_a, buffers.scatter_a = some(2), some(2)
    buffers.gather_b, buffers.scatter_b = some(2), some(2)
    spread_send, spread_recv, rep_send, rep_recv = some(4)
    current, inputs, result = buffers.current, buffers.inputs, buffers.result
    full_a, full_b, grad_mixed = buffers.full_a, buffers.full_b, buffers.mixed
    joined, grad_projected = buffers.joined, buffers.grad_projected

    place = Place()
    length, width = full_a.shape
    depth = wm.shape[0]
    hidden_width = wr.shape[0]
    last = in_inputs.shape[0] - 1
    tokens = narrow.shape[0]
    query_width, key_width = QUERY_HEADS * HEAD_SIZE, KEY_VALUE_HEADS * HEAD_SIZE
    others = place.others()

    def load(at, src, dst):
        copy = pltpu.make_async_copy(src, dst, load_sem.at[at])
        copy.start()
        return copy

    upstream_load = load(0, in_handed, current)
    reduce_load = load(1, reduce_w, wr)

    def joined_load(rel):
        return pltpu.make_async_copy(
            in_joined.at[last, block_rows(place, rel, rows)],
            joined.at[rel % 2],
            joined_sem.at[rel % 2],
        )

    joined_load(0).start()
    joined_load(1).start()
    expand_load = load(2, expand_w, we)
    middle_load = load(3, in_middle.at[last], result)
    wide_load = load(4, upstream_all.at[0], wide)
    plain = [(hidden_all, at) for at in range(hidden_width // depth)] + [(mixed_all, 0)]
    plain += [(normal_a_all, device) for _, device in others]
    job_count = len(plain) + len(others)

    def token_rows(replica):
        return pl.ds(pl.multiple_of(replica * length, length), length)

    def tile_loads(job):
        source, at = plain[job] if job < len(plain) else (None, others[job - len(plain)][1])
        columns = pl.ds(pl.multiple_of(at * depth, depth), depth)
        if source is not None:
            return [
                pltpu.make_async_copy(
                    source.at[:, columns], tiles.at[job % 2], tile_sem.at[job % 2, 0]
                )
            ]
        parts = (
            (normal_b_all.at[last, :, columns], place.replica),
            (other_normal.at[:, columns], 1 - place.replica),
        )
        return [
            pltpu.make_async_copy(
                src, tiles.at[job % 2, token_rows(replica)], tile_sem.at[job % 2, part]
            )
            for part, (src, replica) in enumerate(parts)
        ]

    def tile_start(job):
        for copy in tile_loads(job):
            copy.start()

    def take(job):
        for copy in tile_loads(job):
            copy.wait()

        @pl.loop(0, tokens // 256)
        def _(at):
            span = pl.ds(pl.multiple_of(at * 256, 256), 256)
            turned[:, span] = tiles[job % 2, span, :].T

        if job + 2 < job_count:
            tile_start(job + 2)

    tile_start(0)
    tile_start(1)
    projected_load = load(5, grad_projected_all.at[0], first_projected)
    loads = [
        load(at + 6, src, dst)
        for at, (src, dst) in enumerate(
            [(merge_w, wm), (heads_w, wh)]
            + [(src.at[last], dst) for src, dst in zip(table_refs, buffers.tables)]
            + [
                (in_projected.at[last], buffers.projected),
                (in_heads.at[last], buffers.heads),
                (in_inputs.at[last], inputs),
            ]
        )
    ]
    place.greet([{"fsdp": device} for _, device in others[:7]] + [place.rep_peer])

    def rep_copy(at, src, dst):
        return remote(src, dst, rep_send.at[at], rep_recv.at[at], place.rep_peer)

    def spread(at, device, piece, src, dst):
        if at < 7:
            return remote(
                src, dst, spread_send.at[piece, at], spread_recv.at[piece, at], {"fsdp": device}
            )
        return pltpu.make_async_copy(src, dst, save_sem.at[4 + piece])

    upstream_load.wait()
    own_rows = pl.ds(pl.multiple_of(place.index * rows, rows), rows)
    full_a[own_rows, :] = current[...]
    reduce_load.wait()
    expand_load.wait()
    gather = Gather(place, full_a, *buffers.gather_a, rows)
    scatter = Scatter(place, *buffers.scatter, *buffers.scatter_a, rows)

    joined_reps = []

    def out_of(rel):
        first = place.replica * length + place.chip_at(rel) * 2 * rows
        return narrow.at[pl.ds(pl.multiple_of(first, 2 * rows), 2 * rows)]

    def done(rel, out):
        copy = rep_copy(4 + rel, out, out)
        copy.start()
        joined_reps.append(copy)

    feed_back(
        place,
        rows,
        gather,
        scatter,
        full_a,
        (wm, we, wr),
        joined,
        joined_load,
        out_of,
        done,
    )
    wide_load.wait()
    own_saves, rep_copies = [], []
    for at in range(hidden_width // depth):
        take(at)
        span = pl.ds(at * depth, depth)

        @pl.loop(0, width // 512)
        def _(chunk):
            columns = pl.ds(pl.multiple_of(chunk * 512, 512), 512)
            value = mm(turned[:, :length], wide[:, columns])
            value += mm(turned[:, length:], full_a[:, columns])
            wr[span, columns] = value.astype(jnp.bfloat16)

        copy = rep_copy(at, wr.at[span], other_reduce.at[span])
        copy.start()
        rep_copies.append(copy)
        copy = pltpu.make_async_copy(wr.at[span], own_reduce.at[span], save_sem.at[at])
        copy.start()
        own_saves.append(copy)
        if at == 1:
            scatter.relay()
    grad_middle_load = load(4, grad_middle_all.at[0], wide)
    middle_load.wait()
    feed_input_back(place, rows, scatter, result, gains_ref, gains, current, result, full_b)
    gather.finish()
    gather_b = Gather(place, full_b, *buffers.gather_b, rows)
    scatter_b = Scatter(place, *buffers.scatter, *buffers.scatter_b, rows)
    gather_b.start()
    for copy in loads:
        copy.wait()
    gather_b.relay()
    gather_b.near()
    gather_b.far()
    for rel, at in ((0, 4), (1, 7), (2, 8), (3, 9)):
        gather_b.wait(at)
        span = block_rows(place, rel, rows)
        grad_mixed[span, :] = mm_t(full_b[span, :], wm[...]).astype(jnp.bfloat16)
    attention_back(
        buffers.heads,
        grad_mixed,
        buffers.tables[2],
        *buffers.attention_grads,
        2 * rows,
    )
    project_back(place, rows, scatter_b, buffers, head_gain_ref, head_gain, wh)
    job = hidden_width // depth
    grad_middle_load.wait()
    take(job)
    job += 1

    @pl.loop(0, width // 512)
    def _(chunk):
        columns = pl.ds(pl.multiple_of(chunk * 512, 512), 512)
        value = mm(turned[:, :length], wide[:, columns])
        value += mm(turned[:, length:], full_b[:, columns])
        wm[:, columns] = value.astype(jnp.bfloat16)

    merge_rep = rep_copy(3, wm, other_merge)
    merge_rep.start()
    merge_save = pltpu.make_async_copy(wm, own_merge, save_sem.at[3])
    merge_save.start()
    scatter_b.relay()
    scatter_b.pair(0)
    input_back(scatter_b, inputs, gains_ref, gains, result, None)
    result_save = pltpu.make_async_copy(result, out_result, save_sem.at[10])
    result_save.start()

    gain_copies = []
    gains[...] += first_gains[0]
    head_gain[...] += first_head_gain[0]
    per_row = PLANE // 2
    count = 2 * HEAD_SIZE // PLANE
    for shard in range(PLANE):
        part = slice(shard * depth, (shard + 1) * depth)
        lanes = slice(shard % per_row * count, (shard % per_row + 1) * count)
        row = shard // per_row
        gain_out[shard] = jnp.zeros_like(gain_out[shard])
        gain_out[shard, :, :depth] = gains[0:1, part]
        gain_out[shard, :, depth : 2 * depth] = gains[1:2, part]
        gain_out[shard, :, 2 * depth : 2 * depth + count] = head_gain[row : row + 1, lanes]
    for at, device in others:
        copy = spread(at, device, 5, gain_out.at[device], gain_in.at[place.index])
        copy.start()
        gain_copies.append(copy)

    projected_load.wait()
    heads_copies = []
    for at, device in others:
        take(job)
        job += 1
        value = mm(turned[:, :length], first_projected[...])
        value += mm(turned[:, length:], grad_projected[...])
        block = pl.ds(at * depth, depth)
        wh[block, :] = value.astype(jnp.bfloat16)
        for piece, first, count, start in (
            (2, 0, MERGED, 0),
            (3, query_width, HEAD_SIZE, MERGED),
            (4, query_width + key_width, HEAD_SIZE, MERGED + HEAD_SIZE),
        ):
            copy = spread(
                at,
                device,
                piece,
                wh.at[block, pl.ds(start, count)],
                own_heads.at[:, shard_columns(first, place.index, count)],
            )
            copy.start()
            heads_copies.append(copy)
    def first_loads(at, device):
        block = pl.ds(pl.multiple_of(device * depth, depth), depth)
        return [
            pltpu.make_async_copy(
                src.at[block],
                wide.at[
                    pl.ds((2 * (at % 2) + part) * depth, depth), pl.ds(0, 2 * hidden_width)
                ],
                load_sem.at[14 + 2 * (at % 2) + part],
            )
            for part, src in enumerate((own_first, other_first))
        ]

    for at, device in others[:2]:
        for copy in first_loads(at, device):
            copy.start()
    for copy in joined_reps:
        copy.wait_recv()
    expand_copies = []
    for at, device in others:
        take(job)
        job += 1
        block = pl.ds(at * depth, depth)
        for copy in first_loads(at, device):
            copy.wait()
        mine = pl.ds(2 * (at % 2) * depth, depth)
        theirs = pl.ds((2 * (at % 2) + 1) * depth, depth)

        @pl.loop(0, narrow.shape[1] // 512)
        def _(chunk):
            columns = pl.ds(pl.multiple_of(chunk * 512, 512), 512)
            value = wide[mine, columns].astype(jnp.float32)
            value += wide[theirs, columns].astype(jnp.float32)
            value += mm(turned[...], narrow[:, columns])
            we[block, columns] = value.astype(jnp.bfloat16)

        if at + 2 < PLANE:
            for copy in first_loads(*others[at + 2]):
                copy.start()
        for piece in range(2):
            copy = spread(
                at,
                device,
                piece,
                we.at[block, pl.ds(piece * hidden_width, hidden_width)],
                own_expand.at[:, shard_columns(piece * FF, place.index, hidden_width)],
            )
            copy.start()
            expand_copies.append(copy)
        if at == 3:
            for copy in heads_copies[:21]:
                copy.wait_recv()
            for copy in heads_copies[21:]:
                copy.wait()
            heads_rep = rep_copy(8, own_heads, other_heads)
            heads_rep.start()
            for copy in gain_copies[:7]:
                copy.wait_recv()
            gain_copies[7].wait()
            total = gain_in[0]
            for shard in range(1, PLANE):
                total += gain_in[shard]
            gain_sum[...] = total
            gain_rep = rep_copy(9, gain_sum, gain_other)
            gain_rep.start()
    gain_rep.wait()
    out_gain[...] = gain_sum[...] + gain_other[...]
    gather_b.finish()
    for copy in expand_copies[:14]:
        copy.wait_recv()
    for copy in expand_copies[14:] + own_saves + [result_save, merge_save]:
        copy.wait()
    for copy in expand_copies[:14] + heads_copies[:21] + gain_copies[:7] + joined_reps:
        copy.wait_send()
    for copy in rep_copies + [merge_rep, heads_rep]:
        copy.wait()


def sems(*counts):
    return [pltpu.SemaphoreType.DMA((count,)) for count in counts]


def vmem(*shapes):
    return [pltpu.VMEM(shape, dtype) for *shape, dtype in shapes]


def any_specs(count):
    return [pl.BlockSpec(memory_space=pl.ANY)] * count


def vmem_specs(count):
    return [pl.BlockSpec(memory_space=pltpu.VMEM)] * count


def kernel_params(collective_id):
    return pltpu.CompilerParams(
        collective_id=collective_id, has_side_effects=True, vmem_limit_bytes=VMEM_BYTES
    )


def weight_buffers(width, hidden_width):
    b16 = jnp.bfloat16
    return vmem(
        (width, JOINT, b16),
        (MERGED, width, b16),
        (width, 2 * hidden_width, b16),
        (hidden_width, width, b16),
    )


def table_buffers(length):
    return vmem(
        (length, HEAD_SIZE, jnp.float32),
        (length, HEAD_SIZE, jnp.float32),
        (length, 1, jnp.int32),
    )


def attention_buffers(length):
    return vmem(
        (length, MERGED, jnp.float32),
        (length, HEAD_SIZE, jnp.float32),
        (length, HEAD_SIZE, jnp.float32),
    )


def scatter_buffers(rows, width):
    half, b16 = rows // 2, jnp.bfloat16
    return vmem(
        (4, rows, width, jnp.float32),
        (4, rows, width, b16),
        (4, rows, width, b16),
        *(((3, half, width, b16),) * 4),
    )


def run_layers(own, gain_row, tables, weights):
    micro, rows, width = own.shape
    length = tables[0].shape[1]
    hidden_width, depth = weights[3].shape[0], weights[0].shape[0]
    f32, b16 = jnp.float32, jnp.bfloat16
    shape = jax.ShapeDtypeStruct
    stashes = (
        (rows, width, b16),
        (length, width, b16),
        (length, JOINT, f32),
        (length, JOINT, b16),
        (length, MERGED, b16),
        (rows, width, f32),
        (length, width, b16),
        (length, 2 * hidden_width, f32),
        (length, hidden_width, b16),
        (length, width, b16),
        (length, width, b16),
        (length, JOINT, b16),
    )
    out = pl.pallas_call(
        functools.partial(layers_kernel, rows),
        out_shape=(
            shape((micro, rows, width), f32),
            *(shape((micro, *size), dtype) for *size, dtype in stashes),
            shape((rows, width), b16),
            shape((width, 2 * hidden_width), b16),
            shape((width, 2 * hidden_width), b16),
            shape((length, width), b16),
            shape((width, JOINT), b16),
            shape((width, 2 * hidden_width), b16),
            shape((2, width), f32),
            shape((2, HEAD_SIZE), f32),
            shape((micro, 2, width), f32),
            shape((micro, 2, HEAD_SIZE), f32),
        ),
        in_specs=vmem_specs(2) + any_specs(7),
        out_specs=any_specs(19) + vmem_specs(4),
        scratch_shapes=vmem((PLANE, *gain_row.shape, f32))
        + weight_buffers(width, hidden_width)
        + vmem(
            (micro, rows, width, b16),
            (rows, width, b16),
            (rows, width, b16),
            (rows, width, f32),
            (rows, width, f32),
            (rows, width, b16),
            (length, width, b16),
            (length, width, b16),
            (length, JOINT, f32),
            (length, JOINT, b16),
            (length, MERGED, b16),
            (2, 2 * rows, 2 * hidden_width, f32),
            (length, hidden_width, b16),
            (length, 2 * hidden_width, b16),
            (length, JOINT, b16),
        )
        + table_buffers(length)
        + attention_buffers(length)
        + scatter_buffers(rows, width)
        + vmem(
            (2, length, depth, b16),
            (depth, length, b16),
            (2, depth, 2 * hidden_width, b16),
        )
        + sems(10)
        + [pltpu.SemaphoreType.DMA((6, PLANE - 1))] * 2
        + [pltpu.SemaphoreType.DMA((2, 2))] * 2
        + sems(2, 2, PLANE, PLANE, 2, 2)
        + sems(10, 7, 2, micro, micro, 2, *((10,) * 8)),
        compiler_params=kernel_params(1),
    )(own, gain_row, *tables, *weights)
    return Layers(out[0], Saved(*out[1:13]), *out[13:])


def run_gradients(layers, tables, merge_w, reduce_w):
    saved = layers.saved
    micro, rows, width = saved.inputs.shape
    length = tables[0].shape[1]
    hidden_width, depth = reduce_w.shape[0], merge_w.shape[0]
    f32, b16 = jnp.float32, jnp.bfloat16
    shape = jax.ShapeDtypeStruct
    heads_term, merge_term = (depth, PLANE * JOINT), (depth, width)
    expand_term, reduce_term = (depth, 2 * FF), (hidden_width, width)
    terms = (heads_term,) * 2 + (merge_term,) * 2 + (expand_term,) + (reduce_term,) * 2
    gain_width = -(-(2 * depth + 2 * HEAD_SIZE // PLANE) // 128) * 128

    def flat(array):
        return array.reshape(micro * length, -1)

    return pl.pallas_call(
        functools.partial(gradient_kernel, rows),
        out_shape=(shape((rows, width), f32),)
        + tuple(shape(term, b16) for term in terms)
        + (shape((1, gain_width), f32),),
        in_specs=vmem_specs(4) + any_specs(23),
        out_specs=any_specs(8) + vmem_specs(1),
        scratch_shapes=weight_buffers(width, hidden_width)
        + vmem(
            (rows, width, b16),
            (rows, width, b16),
            (rows, width, f32),
            (length, width, b16),
            (length, width, b16),
            (length, JOINT, f32),
            (length, JOINT, b16),
            (length, MERGED, b16),
            (2, 2 * rows, 2 * hidden_width, f32),
            (length, JOINT, b16),
        )
        + table_buffers(length)
        + attention_buffers(length)
        + scatter_buffers(rows, width)
        + vmem(
            (2, micro * length, depth, b16),
            (depth, micro * length, b16),
            (length, width, b16),
            (2 * length, 2 * hidden_width, b16),
            (length, JOINT, b16),
            (2, width, f32),
            (2, HEAD_SIZE, f32),
            (PLANE, 1, gain_width, f32),
            (PLANE, 1, gain_width, f32),
            (1, gain_width, f32),
            (1, gain_width, f32),
        )
        + sems(18)
        + [pltpu.SemaphoreType.DMA((2, 2))]
        + sems(2, 11, *((10,) * 8))
        + [pltpu.SemaphoreType.DMA((6, PLANE - 1))] * 2
        + sems(10, 10),
        compiler_params=kernel_params(2),
    )(
        layers.gains,
        layers.head_gain,
        layers.gain_terms,
        layers.head_terms,
        *tables,
        layers.heads_w,
        merge_w,
        layers.expand_w,
        reduce_w,
        layers.handed,
        saved.inputs,
        saved.projected,
        saved.heads,
        saved.middle,
        saved.joined,
        flat(saved.hidden),
        saved.upstream,
        saved.normal_b,
        layers.other_normal,
        flat(saved.mixed),
        saved.grad_middle,
        flat(saved.normal_a),
        saved.grad_projected,
        layers.own_first,
        layers.other_first,
    )


def position_tables(lengths, length):
    document_index, positions = places(lengths, length)
    half_width = HEAD_SIZE // 2
    frequency = jnp.exp(
        jnp.arange(half_width, dtype=jnp.float32) * (-2.0 * math.log(ROPE_BASE) / HEAD_SIZE)
    )
    angles = positions.astype(jnp.float32)[:, None] * frequency[None, :]
    cosine, sine = jnp.cos(angles), jnp.sin(angles)
    first_key = jnp.arange(length, dtype=jnp.int32) - positions
    return (
        jnp.concatenate([cosine, cosine], axis=-1),
        jnp.concatenate([-sine, sine], axis=-1),
        first_key[:, None],
    )


def tensor_parallel_body(
    section_inputs,
    doc_lengths,
    mixer_gain,
    heads_weight,
    merge_weight,
    head_gain,
    feed_gain,
    expand_weight,
    reduce_weight,
):
    shards = lax.axis_size("fsdp")
    own = section_inputs[0, :, 0]
    micro, rows, width = own.shape
    length = rows * shards
    depth = heads_weight.shape[1]
    hidden_width = reduce_weight.shape[1]
    query_width = QUERY_HEADS * HEAD_SIZE

    gain_row = jnp.concatenate([mixer_gain[0], feed_gain[0], head_gain[0]]).astype(jnp.float32)
    gain_row = jnp.pad(gain_row, (0, -gain_row.shape[0] % 128))[None]
    tables = [position_tables(doc_lengths[at, 0], length) for at in range(micro)]
    cosine, sine, first_key = (jnp.stack(entry) for entry in zip(*tables))

    table_rows = (cosine, sine, first_key)
    layers = run_layers(
        own,
        gain_row,
        table_rows,
        (heads_weight[0], merge_weight[0], expand_weight[0], reduce_weight[0]),
    )
    last_rows, *terms, gain_sums = run_gradients(
        layers, table_rows, merge_weight[0], reduce_weight[0]
    )
    grad_expand = terms.pop(4).astype(jnp.float32)[None]
    grad_heads, grad_merge, grad_reduce = (
        (terms[at].astype(jnp.float32) + terms[at + 1].astype(jnp.float32))[None]
        for at in range(0, 6, 2)
    )
    head_count = head_gain.shape[1]
    head = lax.axis_index("section") == 0
    last_rows = jnp.where(head, last_rows, layers.rows[-1])
    return (
        jnp.concatenate([layers.rows[:-1], last_rows[None]])[None, :, None],
        gain_sums[:, :depth],
        grad_heads,
        grad_merge,
        gain_sums[:, 2 * depth : 2 * depth + head_count],
        gain_sums[:, depth : 2 * depth],
        grad_expand,
        grad_reduce,
    )


def solution(mesh):
    plane = mesh.shape["fsdp"] == PLANE
    return jax.shard_map(
        tensor_parallel_body if plane else body,
        mesh=mesh,
        in_specs=(
            P("section", None, "rep", "fsdp", None),
            P(None, "rep", None),
            P("section", "fsdp"),
            P("section", "fsdp", None),
            P("section", "fsdp", None),
            P("section", "fsdp"),
            P("section", "fsdp"),
            P("section", "fsdp", None),
            P("section", "fsdp", None),
        ),
        out_specs=(
            P("section", None, "rep", "fsdp", None),
            P("section", "fsdp"),
            P("section", "fsdp", None),
            P("section", "fsdp", None),
            P("section", "fsdp"),
            P("section", "fsdp"),
            P("section", "fsdp", None),
            P("section", "fsdp", None),
        ),
        check_vma=False,
    )
```

```python
import functools
import math
import types
import typing

import jax
import jax.numpy as jnp
from jax import lax
from jax.experimental import pallas as pl
from jax.experimental.pallas import tpu as pltpu
from jax.sharding import PartitionSpec as P

FF = 6144
QUERY_HEADS = 16
KEY_VALUE_HEADS = 8
HEAD_SIZE = 128


NORM_EPS = 1e-06
ROPE_BASE = 1000000.0
MASKED_SCORE = -1e30
PLANE = 8


def from_behind(array, axis, by):
    count = lax.axis_size(axis)
    pairs = [(i, i + by) for i in range(count) if 0 <= i + by < count]
    return lax.ppermute(array, axis, pairs)


def normed(values):
    return values * lax.rsqrt(jnp.mean(values * values, axis=-1, keepdims=True) + NORM_EPS)


def scaled(values, gain_row):
    return normed(values) * gain_row


def rotate(values, positions):
    half_width = values.shape[-1] // 2
    frequency = jnp.exp(
        jnp.arange(half_width, dtype=jnp.float32) * (-2.0 * math.log(ROPE_BASE) / values.shape[-1])
    )
    angles = positions.astype(jnp.float32)[:, None] * frequency[None, :]
    cosine = jnp.cos(angles)[:, None, :]
    sine_part = jnp.sin(angles)[:, None, :]
    lower_half = values[..., :half_width]
    upper_half = values[..., half_width:]
    return jnp.concatenate(
        [
            lower_half * cosine - upper_half * sine_part,
            upper_half * cosine + lower_half * sine_part,
        ],
        axis=-1,
    )


def places(doc_lengths, sequence_length):
    doc_ends = jnp.cumsum(doc_lengths)
    token_index = jnp.arange(sequence_length, dtype=jnp.int32)
    passed_ends = (token_index[:, None] >= doc_ends[None, :]).astype(jnp.int32)
    document_index = jnp.sum(passed_ends, axis=1)
    doc_start = jnp.sum(passed_ends * doc_lengths[None, :], axis=1)
    return (document_index, token_index - doc_start)


def heads_of(projected_output, head_gain, positions):
    count_of_tokens = projected_output.shape[0]
    query_rows = projected_output[:, : QUERY_HEADS * HEAD_SIZE].reshape(
        count_of_tokens, QUERY_HEADS, HEAD_SIZE
    )
    heads_of_keys = projected_output[
        :, QUERY_HEADS * HEAD_SIZE : (QUERY_HEADS + KEY_VALUE_HEADS) * HEAD_SIZE
    ].reshape(count_of_tokens, KEY_VALUE_HEADS, HEAD_SIZE)
    heads_of_values = projected_output[:, (QUERY_HEADS + KEY_VALUE_HEADS) * HEAD_SIZE :]
    return (
        rotate(scaled(query_rows, head_gain[:HEAD_SIZE]), positions),
        rotate(scaled(heads_of_keys, head_gain[HEAD_SIZE:]), positions),
        heads_of_values,
    )


def gated_unit(joined):
    return jax.nn.silu(joined[:, :FF]) * joined[:, FF:]


def times_transposed(left_side, right_side):
    return lax.dot_general(
        left_side, right_side, (((1,), (1,)), ((), ())), preferred_element_type=jnp.float32
    )


def allowed_mask(doc_rows, row_start, document_index):
    row_index = row_start + jnp.arange(doc_rows.shape[0], dtype=jnp.int32)
    key_index = jnp.arange(document_index.shape[0], dtype=jnp.int32)
    return (doc_rows[:, None] == document_index[None, :]) & (
        row_index[:, None] >= key_index[None, :]
    )


def raw_scores(query_rows_second, rows_of_keys, allowed):
    grouped_heads = query_rows_second.reshape(
        query_rows_second.shape[0], KEY_VALUE_HEADS, QUERY_HEADS // KEY_VALUE_HEADS, HEAD_SIZE
    )
    heads_of_keys = rows_of_keys.reshape(rows_of_keys.shape[0], KEY_VALUE_HEADS, HEAD_SIZE)
    scores = jnp.einsum(
        "rkgd,tkd->rkgt", grouped_heads, heads_of_keys, preferred_element_type=jnp.float32
    ) * HEAD_SIZE ** (-0.5)
    return jnp.where(allowed[:, None, None, :], scores, MASKED_SCORE)


def attend_rows(query_rows_second, rows_of_keys, rows_of_values, allowed):
    scores = raw_scores(query_rows_second, rows_of_keys, allowed)
    row_max = jnp.max(scores, axis=-1, keepdims=True)
    exp_scores = jnp.exp(scores - row_max)
    row_totals = jnp.sum(exp_scores, axis=-1, keepdims=True)
    attn_probs = (exp_scores / row_totals).astype(jnp.bfloat16)
    heads_of_values = rows_of_values.reshape(rows_of_values.shape[0], KEY_VALUE_HEADS, HEAD_SIZE)
    heads_mixed = jnp.einsum(
        "rkgt,tkd->rkgd", attn_probs, heads_of_values, preferred_element_type=jnp.float32
    )
    return (
        heads_mixed.reshape(query_rows_second.shape[0], QUERY_HEADS * HEAD_SIZE),
        row_max + jnp.log(row_totals),
    )


def attend_back(
    query_rows_second, rows_of_keys, rows_of_values, allowed, log_totals, mixed_gradient_second
):
    count_of_rows = query_rows_second.shape[0]
    count_of_keys = rows_of_keys.shape[0]
    grouped_heads = query_rows_second.reshape(
        count_of_rows, KEY_VALUE_HEADS, QUERY_HEADS // KEY_VALUE_HEADS, HEAD_SIZE
    )
    heads_of_keys = rows_of_keys.reshape(count_of_keys, KEY_VALUE_HEADS, HEAD_SIZE)
    heads_of_values = rows_of_values.reshape(count_of_keys, KEY_VALUE_HEADS, HEAD_SIZE)
    heads_gradient = mixed_gradient_second.reshape(
        count_of_rows, KEY_VALUE_HEADS, QUERY_HEADS // KEY_VALUE_HEADS, HEAD_SIZE
    )
    attn_probs = jnp.exp(raw_scores(query_rows_second, rows_of_keys, allowed) - log_totals)
    grad_probs = jnp.einsum(
        "rkgd,tkd->rkgt", heads_gradient, heads_of_values, preferred_element_type=jnp.float32
    )
    grad_scores = (
        attn_probs * (grad_probs - jnp.sum(grad_probs * attn_probs, axis=-1, keepdims=True))
    ).astype(jnp.bfloat16)
    queries_gradient = jnp.einsum(
        "rkgt,tkd->rkgd", grad_scores, heads_of_keys, preferred_element_type=jnp.float32
    ) * HEAD_SIZE ** (-0.5)
    keys_gradient = jnp.einsum(
        "rkgt,rkgd->tkd", grad_scores, grouped_heads, preferred_element_type=jnp.float32
    ) * HEAD_SIZE ** (-0.5)
    values_gradient = jnp.einsum(
        "rkgt,rkgd->tkd",
        attn_probs.astype(jnp.bfloat16),
        heads_gradient,
        preferred_element_type=jnp.float32,
    )
    return (
        queries_gradient.reshape(count_of_rows, QUERY_HEADS, HEAD_SIZE),
        keys_gradient.reshape(count_of_keys, KEY_VALUE_HEADS * HEAD_SIZE),
        values_gradient.reshape(count_of_keys, KEY_VALUE_HEADS * HEAD_SIZE),
    )


def layer_forward(inputs, layer_full, positions, allowed):
    mixer_gain, heads_weight, merge_weight, head_gain, feed_gain, expand_weight, reduce_weight = (
        layer_full
    )
    count_of_rows = inputs.shape[0]
    normal_a = scaled(inputs, mixer_gain).astype(jnp.bfloat16)
    projected_output = jnp.dot(normal_a, heads_weight, preferred_element_type=jnp.float32)
    query_rows, heads_of_keys, heads_of_values = heads_of(projected_output, head_gain, positions)
    rows_of_keys, rows_of_values = (
        lax.all_gather(
            heads_of_keys.reshape(count_of_rows, KEY_VALUE_HEADS * HEAD_SIZE).astype(jnp.bfloat16),
            "fsdp",
            axis=0,
            tiled=True,
        ),
        lax.all_gather(heads_of_values.astype(jnp.bfloat16), "fsdp", axis=0, tiled=True),
    )
    heads_mixed, log_totals = attend_rows(
        query_rows.astype(jnp.bfloat16), rows_of_keys, rows_of_values, allowed
    )
    mixed_b = heads_mixed.astype(jnp.bfloat16)
    middle = inputs + jnp.dot(mixed_b, merge_weight, preferred_element_type=jnp.float32)
    normal_b = scaled(middle, feed_gain).astype(jnp.bfloat16)
    joined = jnp.dot(normal_b, expand_weight, preferred_element_type=jnp.float32)
    hidden = gated_unit(joined).astype(jnp.bfloat16)
    result = middle + jnp.dot(hidden, reduce_weight, preferred_element_type=jnp.float32)
    return (
        result,
        (
            inputs,
            normal_a,
            projected_output,
            rows_of_keys,
            rows_of_values,
            log_totals,
            mixed_b,
            middle,
            normal_b,
            joined,
            hidden,
        ),
    )


def layer_backward(upstream, layer_full, saved, positions, allowed):
    mixer_gain, heads_weight, merge_weight, head_gain, feed_gain, expand_weight, reduce_weight = (
        layer_full
    )
    (
        inputs,
        normal_a,
        projected_output,
        rows_of_keys,
        rows_of_values,
        log_totals,
        mixed_b,
        middle,
        normal_b,
        joined,
        hidden,
    ) = saved
    count_of_rows = inputs.shape[0]
    upstream_b = upstream.astype(jnp.bfloat16)
    grad_hidden = times_transposed(upstream_b, reduce_weight)
    unused_joined, gated_back = jax.vjp(gated_unit, joined)
    grad_joined = gated_back(grad_hidden)[0].astype(jnp.bfloat16)
    unused_feed, feed_back = jax.vjp(scaled, middle, feed_gain)
    grad_middle_part, grad_feed = feed_back(times_transposed(grad_joined, expand_weight))
    grad_middle = upstream + grad_middle_part
    grad_middle_b = grad_middle.astype(jnp.bfloat16)
    grad_mixed = times_transposed(grad_middle_b, merge_weight).astype(jnp.bfloat16)
    head_values, heads_back = jax.vjp(
        lambda projected_rows, gain_rows: heads_of(projected_rows, gain_rows, positions),
        projected_output,
        head_gain,
    )
    queries_gradient, grad_keys_all, grad_values_all = attend_back(
        head_values[0].astype(jnp.bfloat16),
        rows_of_keys,
        rows_of_values,
        allowed,
        log_totals,
        grad_mixed,
    )
    keys_gradient, values_gradient = (
        lax.psum_scatter(
            grad_keys_all.astype(jnp.bfloat16), "fsdp", scatter_dimension=0, tiled=True
        ).astype(jnp.float32),
        lax.psum_scatter(
            grad_values_all.astype(jnp.bfloat16), "fsdp", scatter_dimension=0, tiled=True
        ).astype(jnp.float32),
    )
    grad_projected, grad_head = heads_back(
        (
            queries_gradient,
            keys_gradient.reshape(count_of_rows, KEY_VALUE_HEADS, HEAD_SIZE),
            values_gradient,
        )
    )
    grad_projected_b = grad_projected.astype(jnp.bfloat16)
    unused_mixer, mixer_back = jax.vjp(scaled, inputs, mixer_gain)
    grad_inputs_part, grad_mixer = mixer_back(times_transposed(grad_projected_b, heads_weight))
    operands = (
        normal_a,
        grad_projected_b,
        mixed_b,
        grad_middle_b,
        normal_b,
        grad_joined,
        hidden,
        upstream_b,
    )
    return (grad_middle + grad_inputs_part, operands, (grad_mixer, grad_feed, grad_head))


def product_term(left_side, right_side):
    return lax.dot_general(
        left_side, right_side, (((0,), (0,)), ((), ())), preferred_element_type=jnp.float32
    )


def reduce_grads(operands, gain_terms):
    (
        normal_a,
        grad_projected_b,
        mixed_b,
        grad_middle_b,
        normal_b,
        grad_joined,
        hidden,
        upstream_b,
    ) = operands
    heads_gradient = lax.psum_scatter(
        product_term(normal_a, grad_projected_b).astype(jnp.bfloat16),
        "fsdp",
        scatter_dimension=0,
        tiled=True,
    )
    grad_merge = lax.psum_scatter(
        product_term(mixed_b, grad_middle_b).astype(jnp.bfloat16),
        "fsdp",
        scatter_dimension=0,
        tiled=True,
    )
    grad_expand = lax.psum_scatter(
        product_term(normal_b, grad_joined).astype(jnp.bfloat16),
        "fsdp",
        scatter_dimension=0,
        tiled=True,
    )
    grad_reduce = lax.psum_scatter(
        product_term(hidden, upstream_b).astype(jnp.bfloat16),
        "fsdp",
        scatter_dimension=0,
        tiled=True,
    )
    grad_mixer, grad_feed, grad_head = (
        lax.psum_scatter(gain_terms[0], "fsdp", scatter_dimension=0, tiled=True),
        lax.psum_scatter(gain_terms[1], "fsdp", scatter_dimension=0, tiled=True),
        lax.psum_scatter(gain_terms[2], "fsdp", scatter_dimension=0, tiled=True),
    )
    return (
        lax.psum(grad_mixer.astype(jnp.bfloat16), "rep").astype(jnp.float32),
        lax.psum(heads_gradient, "rep").astype(jnp.float32),
        lax.psum(grad_merge, "rep").astype(jnp.float32),
        lax.psum(grad_head.astype(jnp.bfloat16), "rep").astype(jnp.float32),
        lax.psum(grad_feed.astype(jnp.bfloat16), "rep").astype(jnp.float32),
        lax.psum(grad_expand, "rep").astype(jnp.float32),
        lax.psum(grad_reduce, "rep").astype(jnp.float32),
    )


def body(
    section_inputs,
    doc_lengths,
    mixer_gain,
    heads_weight,
    merge_weight,
    head_gain,
    feed_gain,
    expand_weight,
    reduce_weight,
):
    section_index = lax.axis_index("section")
    head_section = section_index == 0
    shard_index = lax.axis_index("fsdp")
    count_of_rows = section_inputs.shape[3]
    sequence_length = count_of_rows * lax.axis_size("fsdp")
    own_rows = section_inputs[0, :, 0]
    micro_count = own_rows.shape[0]
    mixer_part = (
        lax.all_gather(mixer_gain, "fsdp", axis=1, tiled=True),
        lax.all_gather(heads_weight, "fsdp", axis=1, tiled=True),
        lax.all_gather(merge_weight, "fsdp", axis=1, tiled=True),
        lax.all_gather(head_gain, "fsdp", axis=1, tiled=True),
    )
    feed_part = (
        lax.all_gather(feed_gain, "fsdp", axis=1, tiled=True),
        lax.all_gather(expand_weight, "fsdp", axis=1, tiled=True),
        lax.all_gather(reduce_weight, "fsdp", axis=1, tiled=True),
    )
    layer_full = (
        mixer_part[0][0].astype(jnp.float32),
        mixer_part[1][0],
        mixer_part[2][0],
        mixer_part[3][0].astype(jnp.float32),
        feed_part[0][0].astype(jnp.float32),
        feed_part[1][0],
        feed_part[2][0],
    )

    def layout(micro_slot):
        document_index, positions = places(doc_lengths[micro_slot, 0], sequence_length)
        row_start = shard_index * count_of_rows
        doc_rows = lax.dynamic_slice_in_dim(document_index, row_start, count_of_rows)
        own_positions = lax.dynamic_slice_in_dim(positions, row_start, count_of_rows)
        return (own_positions, allowed_mask(doc_rows, row_start, document_index))

    results = jnp.zeros((micro_count, count_of_rows, own_rows.shape[2]), jnp.float32)
    saved_acts = None
    arrived = jnp.zeros((count_of_rows, own_rows.shape[2]), jnp.bfloat16)
    for step_index in range(micro_count + 1):
        slot_raw = step_index - section_index
        is_live = (slot_raw >= 0) & (slot_raw < micro_count)
        micro_slot = jnp.clip(slot_raw, 0, micro_count - 1)
        inputs = jnp.where(
            head_section, own_rows[min(step_index, micro_count - 1)], arrived
        ).astype(jnp.float32)
        positions, allowed = layout(micro_slot)
        result, saved = layer_forward(inputs, layer_full, positions, allowed)
        if saved_acts is None:
            saved_acts = tuple(
                (jnp.zeros((micro_count,) + current.shape, current.dtype) for current in saved)
            )
        saved_acts = tuple(
            (
                jnp.where(is_live, buffer.at[micro_slot].set(current), buffer)
                for buffer, current in zip(saved_acts, saved)
            )
        )
        results = jnp.where(
            is_live & jnp.logical_not(head_section), results.at[micro_slot].set(result), results
        )
        if step_index < micro_count:
            arrived = from_behind(result.astype(jnp.bfloat16), "section", 1)
    gradients = None
    stashed = None
    gain_sums = None
    from_next = jnp.zeros((count_of_rows, own_rows.shape[2]), jnp.bfloat16)
    for step_index in range(micro_count + 1):
        slot_raw = step_index - 1 + section_index
        is_live = (slot_raw >= 0) & (slot_raw < micro_count)
        micro_slot = jnp.clip(slot_raw, 0, micro_count - 1)
        upstream = jnp.where(
            head_section, from_next, own_rows[min(step_index, micro_count - 1)]
        ).astype(jnp.float32)
        upstream = jnp.where(is_live, upstream, 0.0)
        positions, allowed = layout(micro_slot)
        saved = tuple((buffer[micro_slot] for buffer in saved_acts))
        grad_inputs, operands, gain_terms = layer_backward(
            upstream, layer_full, saved, positions, allowed
        )
        results = jnp.where(
            is_live & head_section, results.at[micro_slot].set(grad_inputs), results
        )
        if step_index < micro_count:
            from_next = from_behind(grad_inputs.astype(jnp.bfloat16), "section", -1)
        if stashed is None:
            stashed = tuple(
                (jnp.zeros((micro_count,) + current.shape, current.dtype) for current in operands)
            )
            gain_sums = tuple((jnp.zeros_like(current) for current in gain_terms))
        stashed = tuple(
            (
                jnp.where(is_live, buffer.at[micro_slot].set(current), buffer)
                for buffer, current in zip(stashed, operands)
            )
        )
        gain_sums = tuple(
            (total_so_far + current for total_so_far, current in zip(gain_sums, gain_terms))
        )
    merged = tuple(
        (buffer.reshape((micro_count * count_of_rows,) + buffer.shape[2:]) for buffer in stashed)
    )
    gradients = reduce_grads(merged, gain_sums)
    grad_mixer, heads_gradient, grad_merge, grad_head, grad_feed, grad_expand, grad_reduce = (
        gradients
    )
    return (
        results[None, :, None],
        grad_mixer[None],
        heads_gradient[None],
        grad_merge[None],
        grad_head[None],
        grad_feed[None],
        grad_expand[None],
        grad_reduce[None],
    )


MESH = pl.DeviceIdType.MESH
MERGED = QUERY_HEADS // KEY_VALUE_HEADS * HEAD_SIZE
JOINT = MERGED + 2 * HEAD_SIZE
VMEM_BYTES = 63 * 2**20


def mm(left, right):
    return jnp.dot(left, right, preferred_element_type=jnp.float32)


def mm_t(left, right):
    return lax.dot_general(
        left, right, (((1,), (1,)), ((), ())), preferred_element_type=jnp.float32
    )


def t_mm(left, right):
    return lax.dot_general(
        left, right, (((0,), (0,)), ((), ())), preferred_element_type=jnp.float32
    )


def remote(src, dst, send, recv, device):
    return pltpu.make_async_remote_copy(
        src_ref=src,
        dst_ref=dst,
        send_sem=send,
        recv_sem=recv,
        device_id=device,
        device_id_type=MESH,
    )


class Place:
    def __init__(self):
        self.index = lax.axis_index("fsdp")
        self.core = lax.rem(self.index, 2)
        self.chip = lax.div(self.index, 2)
        self.x = lax.rem(self.chip, 2)
        self.y = lax.div(self.chip, 2)
        self.x_peer = {"fsdp": self.index + 2 - 4 * self.x}
        self.y_peer = {"fsdp": self.index + 4 - 8 * self.y}
        self.core_peer = {"fsdp": self.index + 1 - 2 * self.core}
        self.section = lax.axis_index("section")
        self.section_peer = {"section": 1 - self.section}
        self.replica = lax.axis_index("rep")
        self.rep_peer = {"rep": 1 - self.replica}

    def chip_at(self, rel):
        x, y = self.x, self.y
        if rel in (1, 3):
            x = 1 - x
        if rel in (2, 3):
            y = 1 - y
        return 2 * y + x

    def others(self):
        order = ((3, 0), (3, 1), (1, 0), (1, 1), (2, 0), (2, 1), (0, 1), (0, 0))
        return [
            (at, 2 * self.chip_at(rel) + (1 - self.core if other else self.core))
            for at, (rel, other) in enumerate(order)
        ]

    def greet(self, peers):
        barrier = pltpu.get_barrier_semaphore()
        for peer in peers:
            pl.semaphore_signal(barrier, inc=1, device_id=peer, device_id_type=MESH)
        pl.semaphore_wait(barrier, len(peers))


class Gather:
    def __init__(self, place, full, send, recv, rows):
        half = rows // 2

        def span(rel, part=None):
            first = (2 * place.chip_at(rel) + place.core) * rows
            if part is None:
                return pl.ds(pl.multiple_of(first, rows), rows)
            return pl.ds(pl.multiple_of(first + part * half, half), half)

        def copy(at, piece, peer):
            block = full.at[piece]
            return remote(block, block, send.at[at], recv.at[at], peer)

        self.copies = [
            copy(0, span(0, 1), place.x_peer),
            copy(1, span(0, 0), place.x_peer),
            copy(2, span(0, 0), place.y_peer),
            copy(3, span(0, 1), place.y_peer),
            copy(4, span(0), place.core_peer),
            copy(5, span(1, 1), place.y_peer),
            copy(6, span(2, 0), place.x_peer),
            copy(7, span(1), place.core_peer),
            copy(8, span(2), place.core_peer),
            copy(9, span(3), place.core_peer),
        ]

    def start(self):
        for at in (0, 2, 4, 1, 3):
            self.copies[at].start()

    def relay(self):
        self.copies[0].wait_recv()
        self.copies[5].start()
        self.copies[2].wait_recv()
        self.copies[6].start()

    def near(self):
        self.copies[1].wait_recv()
        self.copies[7].start()
        self.copies[3].wait_recv()
        self.copies[8].start()

    def far(self):
        self.copies[5].wait_recv()
        self.copies[6].wait_recv()
        self.copies[9].start()

    def wait(self, at):
        self.copies[at].wait_recv()

    def finish(self):
        for entry in self.copies:
            entry.wait_send()

    def over_blocks(self, block, between=lambda: None, early=lambda at: None):
        self.start()
        early(0)
        self.wait(4)
        block(0)
        early(1)
        self.relay()
        early(2)
        self.near()
        self.wait(7)
        block(1)
        early(3)
        self.wait(8)
        block(2)
        early(4)
        between()
        self.far()
        self.wait(9)
        block(3)


class Scatter:
    def __init__(self, place, held, to_core, from_core, to_x, to_y, from_x, from_y, send, recv, rows):
        self.place, self.held, self.to_core, self.from_core = place, held, to_core, from_core
        self.to_x, self.to_y, self.from_x, self.from_y = to_x, to_y, from_x, from_y
        self.rows, self.half = rows, rows // 2

        def copy(at, src, dst, peer):
            return remote(src, dst, send.at[at], recv.at[at], peer)

        self.copies = [
            copy(rel, to_core.at[rel], from_core.at[rel], place.core_peer) for rel in range(4)
        ] + [
            copy(4, to_x.at[0], from_x.at[0], place.x_peer),
            copy(5, to_y.at[0], from_y.at[0], place.y_peer),
            copy(6, to_x.at[1], from_x.at[1], place.x_peer),
            copy(7, to_y.at[1], from_y.at[1], place.y_peer),
            copy(8, to_y.at[2], from_y.at[2], place.y_peer),
            copy(9, to_x.at[2], from_x.at[2], place.x_peer),
        ]

    def put(self, rel, product, width):
        step, rows, mine = 512, self.rows, self.place.core == 0

        @pl.loop(0, width // step)
        def _(at):
            columns = pl.ds(pl.multiple_of(at * step, step), step)
            value = product(columns)
            low, high = value[:rows], value[rows:]
            self.held[rel, :, columns] = jnp.where(mine, low, high)
            self.to_core[rel, :, columns] = jnp.where(mine, high, low).astype(jnp.bfloat16)

        self.copies[rel].start()

    def pair(self, rel):
        self.copies[rel].wait_recv()
        half, held = self.half, self.held

        @pl.loop(0, self.rows // 16)
        def _(at):
            span = pl.ds(pl.multiple_of(at * 16, 16), 16)
            held[rel, span, :] += self.from_core[rel, span, :].astype(jnp.float32)

        if rel == 3:
            self.to_x[0] = held[3, :half].astype(jnp.bfloat16)
            self.copies[4].start()
            self.to_y[0] = held[3, half:].astype(jnp.bfloat16)
            self.copies[5].start()
        if rel == 1:
            self.to_x[1] = held[1, :half].astype(jnp.bfloat16)
            self.copies[6].start()
        if rel == 2:
            self.to_y[1] = held[2, half:].astype(jnp.bfloat16)
            self.copies[7].start()

    def relay(self):
        half, held = self.half, self.held
        self.copies[4].wait_recv()
        self.to_y[2] = (held[2, :half] + self.from_x[0].astype(jnp.float32)).astype(jnp.bfloat16)
        self.copies[8].start()
        self.copies[5].wait_recv()
        self.to_x[2] = (held[1, half:] + self.from_y[0].astype(jnp.float32)).astype(jnp.bfloat16)
        self.copies[9].start()

    def total(self, add):
        for at in (6, 7, 8, 9):
            self.copies[at].wait_recv()
        count = self.half // 16

        @pl.loop(0, count)
        def _(at):
            span = pl.ds(pl.multiple_of(at * 16, 16), 16)
            low = self.held[0, span, :] + self.from_x[1, span, :].astype(jnp.float32)
            add(span, low + self.from_y[2, span, :].astype(jnp.float32))

        @pl.loop(0, count)
        def _(at):
            span = pl.ds(pl.multiple_of(at * 16, 16), 16)
            below = pl.ds(pl.multiple_of(self.half + at * 16, 16), 16)
            high = self.held[0, below, :] + self.from_y[1, span, :].astype(jnp.float32)
            add(below, high + self.from_x[2, span, :].astype(jnp.float32))

        for entry in self.copies:
            entry.wait_send()


def turn_tile(tile, turned, first, last):
    for at in range(last - first):
        span = pl.ds(pl.multiple_of((first + at) * 256, 256), 256)
        turned[:, span] = tile[span, :].T


def product_and_turn(width, product, tile, turned):
    step, quarter = width // 4, turned.shape[1] // 1024

    @pl.loop(0, 4)
    def _(chunk):
        product(pl.ds(pl.multiple_of(chunk * step, 128), step))
        for at in range(quarter):
            span = pl.ds(pl.multiple_of((chunk * quarter + at) * 256, 256), 256)
            turned[:, span] = tile[span, :].T


def by_rows(count, body):
    @pl.loop(0, count // 16)
    def _(at):
        body(pl.ds(pl.multiple_of(at * 16, 16), 16))


def inverse_size(values):
    return lax.rsqrt(jnp.mean(values * values, axis=-1, keepdims=True) + NORM_EPS)


def norm_back(values, gain, upstream):
    size = inverse_size(values)
    scaled_up = upstream * gain
    back = size * scaled_up - values * (
        size * size * size * jnp.mean(values * scaled_up, axis=-1, keepdims=True)
    )
    return back, upstream * values * size


def turn(values, cosine, sine):
    return values * cosine + pltpu.roll(values, HEAD_SIZE // 2, 1) * sine


def turn_back(values, cosine, sine):
    return values * cosine + pltpu.roll(values * sine, HEAD_SIZE // 2, 1)


def probabilities(queries, keys, first_keys, first_row):
    scores = mm_t(queries, keys) * HEAD_SIZE ** (-0.5)
    key_index = lax.broadcasted_iota(jnp.int32, scores.shape, 1)
    row_index = first_row + lax.broadcasted_iota(jnp.int32, scores.shape, 0)
    allowed = (key_index >= first_keys) & (key_index <= row_index)
    scores = jnp.where(allowed, scores, MASKED_SCORE)
    powers = jnp.exp(scores - jnp.max(scores, axis=-1, keepdims=True))
    return powers / jnp.sum(powers, axis=-1, keepdims=True)


def block_rows(place, rel, rows):
    return pl.ds(pl.multiple_of(place.chip_at(rel) * 2 * rows, 2 * rows), 2 * rows)


def shard_columns(first, device, count):
    return pl.ds(pl.multiple_of(first + device * count, 128), count)


def layer_forward_step(place, rows, refs, buffers, slot, step, hooks):
    (wh, wm, we, wr), gains_ref, head_gain_ref = refs.weights, refs.gains, refs.head_gain
    current, middle, result, result_b = (
        buffers.current,
        buffers.middle,
        buffers.result,
        buffers.result_b,
    )
    full_a, full_b = buffers.full_a, buffers.full_b
    projected, heads, mixed = buffers.projected, buffers.heads, buffers.mixed
    joined = buffers.joined
    chip_rows, width, hidden_width = 2 * rows, current.shape[1], wr.shape[0]
    save_sem = buffers.save_sem
    tables = [
        pltpu.make_async_copy(src.at[slot], dst, buffers.table_sem.at[at])
        for at, (src, dst) in enumerate(zip(refs.tables, buffers.tables))
    ]
    cosine, sine, first_key = buffers.tables
    for table in tables:
        table.start()

    def save(at, src, dst):
        copy = pltpu.make_async_copy(src, dst.at[slot], save_sem.at[at])
        copy.start()
        return copy

    saves = [save(0, current, refs.inputs)]

    def enter(span):
        values = current[span, :].astype(jnp.float32)
        base = pl.multiple_of(place.index * rows + span.start, 16)
        full_a[pl.ds(base, 16), :] = (
            values * inverse_size(values) * gains_ref[0:1, :]
        ).astype(jnp.bfloat16)

    by_rows(rows, enter)
    for table in tables:
        table.wait()
    gather = Gather(place, full_a, *buffers.gather_a, rows)

    def heads_block(rel):
        span = block_rows(place, rel, rows)
        if rel == 0:
            hooks.heads()
        values = mm(full_a[span, :], wh[...])
        projected[span, :] = values
        for at in range(3):
            columns = pl.ds(at * HEAD_SIZE, HEAD_SIZE)
            one = values[:, at * HEAD_SIZE : (at + 1) * HEAD_SIZE]
            gain = head_gain_ref[0:1, :] if at < 2 else head_gain_ref[1:2, :]
            heads[span, columns] = turn(
                one * inverse_size(one) * gain, cosine[span, :], sine[span, :]
            ).astype(jnp.bfloat16)
        heads[span, 3 * HEAD_SIZE :] = values[:, 3 * HEAD_SIZE :].astype(jnp.bfloat16)

    gather.over_blocks(heads_block)
    hooks.service()
    saves += [
        save(1, full_a, refs.normal_a),
        save(2, projected, refs.projected),
        save(3, heads, refs.heads),
    ]
    scatter = Scatter(place, *buffers.scatter, *buffers.scatter_a, rows)

    def attend_block(rel):
        first_row = place.chip_at(rel) * chip_rows
        span = block_rows(place, rel, rows)
        for at in range(2):
            columns = pl.ds(at * HEAD_SIZE, HEAD_SIZE)
            probs = probabilities(
                heads[span, columns],
                heads[:, 2 * HEAD_SIZE : 3 * HEAD_SIZE],
                first_key[span, :],
                first_row,
            )
            mixed[span, columns] = mm(
                probs.astype(jnp.bfloat16), heads[:, 3 * HEAD_SIZE :]
            ).astype(jnp.bfloat16)
        scatter.put(rel, lambda columns: mm(mixed[span, :], wm[:, columns]), width)

    attend_block(3)
    scatter.pair(3)
    attend_block(2)
    scatter.pair(2)
    attend_block(1)
    scatter.pair(1)
    attend_block(0)
    saves.append(save(4, mixed, refs.mixed))
    scatter.relay()
    scatter.pair(0)

    def residual(span, value):
        values = value + current[span, :].astype(jnp.float32)
        middle[span, :] = values
        base = pl.multiple_of(place.index * rows + span.start, 16)
        full_b[pl.ds(base, 16), :] = (
            values * inverse_size(values) * gains_ref[1:2, :]
        ).astype(jnp.bfloat16)

    scatter.total(residual)
    gather.finish()
    saves.append(save(5, middle, refs.middle))
    for copy in saves[:5]:
        copy.wait()
    gather_b = Gather(place, full_b, *buffers.gather_b, rows)
    scatter_b = Scatter(place, *buffers.scatter, *buffers.scatter_b, rows)
    joined_copies, hidden_copies = {}, []

    def feed_block(rel):
        span = block_rows(place, rel, rows)
        stage = joined.at[rel % 2]
        hidden = buffers.blocks.at[rel // 2, :, pl.ds(rel % 2 * hidden_width, hidden_width)]
        if rel == 0:
            hooks.feed()
        if rel >= 2:
            joined_copies[rel - 2].wait()

        @pl.loop(0, hidden_width // 256)
        def _(at):
            columns = pl.ds(pl.multiple_of(at * 256, 256), 256)
            later = pl.ds(pl.multiple_of(hidden_width + at * 256, 256), 256)
            gate = mm(full_b[span, :], we[:, columns])
            up = mm(full_b[span, :], we[:, later])
            stage[:, columns] = gate
            stage[:, later] = up
            hidden[:, columns] = (gate * jax.nn.sigmoid(gate) * up).astype(jnp.bfloat16)

        copy = pltpu.make_async_copy(
            stage, refs.joined.at[slot, span], save_sem.at[8 + rel % 2]
        )
        copy.start()
        joined_copies[rel] = copy
        copy = pltpu.make_async_copy(
            hidden, refs.hidden.at[slot, span], buffers.hidden_sem.at[rel]
        )
        copy.start()
        hidden_copies.append(copy)
        scatter_b.put(rel, lambda columns: mm(hidden[...], wr[:, columns]), width)
        if rel in (1, 2):
            scatter_b.pair(rel - 1)

    gather_b.over_blocks(feed_block, lambda: scatter_b.pair(2))
    later_saves = [save(6, full_b, refs.normal_b)] + hidden_copies
    scatter_b.pair(3)
    scatter_b.relay()
    hooks.finish()
    saves[5].wait()

    def finish(span, value):
        values = value + middle[span, :]
        result[span, :] = values
        result_b[span, :] = values.astype(jnp.bfloat16)

    scatter_b.total(finish)
    hooks.hand()
    gather_b.finish()
    for copy in later_saves + [joined_copies[2], joined_copies[3]]:
        copy.wait()
    hooks.after()


def feed_back(place, rows, gather, scatter, full, weights, joined, joined_load, out_of, done):
    wm, we, wr = weights
    hidden_width, width = wr.shape

    def feed_block(rel):
        span = block_rows(place, rel, rows)
        stage, out = joined.at[rel % 2], out_of(rel)
        joined_load(rel).wait()

        @pl.loop(0, hidden_width // 256)
        def _(at):
            columns = pl.ds(pl.multiple_of(at * 256, 256), 256)
            later = pl.ds(pl.multiple_of(hidden_width + at * 256, 256), 256)
            grad = mm_t(full[span, :], wr[columns, :])
            gate, up = stage[:, columns], stage[:, later]
            sigmoid = jax.nn.sigmoid(gate)
            unit = gate * sigmoid
            out[:, columns] = (grad * up * (sigmoid + unit * (1.0 - sigmoid))).astype(jnp.bfloat16)
            out[:, later] = (grad * unit).astype(jnp.bfloat16)

        if rel < 2:
            joined_load(rel + 2).start()
        done(rel, out)
        scatter.put(rel, lambda columns: mm_t(out[...], we[columns, :]), width)
        if rel in (1, 2):
            scatter.pair(rel - 1)

    gather.over_blocks(feed_block, lambda: scatter.pair(2))
    scatter.pair(3)


def feed_input_back(place, rows, scatter, middle, gains_ref, out_gains, current, result, full_b):
    out_gains[1:2, :] = jnp.zeros_like(out_gains[1:2, :])

    def feed_norm(span, value):
        back, gain_term = norm_back(middle[span, :], gains_ref[1:2, :], value)
        out_gains[1:2, :] += jnp.sum(gain_term, axis=0, keepdims=True)
        total = back + current[span, :].astype(jnp.float32)
        result[span, :] = total
        base = pl.multiple_of(place.index * rows + span.start, 16)
        full_b[pl.ds(base, 16), :] = total.astype(jnp.bfloat16)

    scatter.total(feed_norm)


def kept_probs(held, joined, at, block, chip_rows):
    rows, seen = chip_rows // 2, (block + 1) * chip_rows
    if at == 0:
        first, columns = ((2, 2 * chip_rows), (2, 0), (0, 4 * chip_rows), (0, 0))[block]
        return held.at[pl.ds(first, 2), pl.ds(0, rows), pl.ds(columns, seen)]
    first, columns = ((1, 3 * chip_rows), (0, 4 * chip_rows), (1, 0), (0, 0))[block]
    return joined.at[first, pl.ds(0, chip_rows), pl.ds(columns, seen)]


def attention_probs(held, joined, heads, first_key, chip_rows):
    for block in range(heads.shape[0] // chip_rows):
        span = pl.ds(block * chip_rows, chip_rows)
        seen = (block + 1) * chip_rows
        keys = heads[:seen, 2 * HEAD_SIZE : 3 * HEAD_SIZE]
        for at in range(2):
            queries = heads[span, pl.ds(at * HEAD_SIZE, HEAD_SIZE)]
            probs = probabilities(queries, keys, first_key[span, :], block * chip_rows)
            kept = kept_probs(held, joined, at, block, chip_rows)
            kept[...] = probs.reshape(kept.shape)


def attention_back(
    held, joined, heads, grad_mixed, grad_queries, grad_keys, grad_values, chip_rows
):
    grad_keys[...] = jnp.zeros_like(grad_keys)
    grad_values[...] = jnp.zeros_like(grad_values)
    for block in range(heads.shape[0] // chip_rows):
        span = pl.ds(block * chip_rows, chip_rows)
        seen = (block + 1) * chip_rows
        keys = heads[:seen, 2 * HEAD_SIZE : 3 * HEAD_SIZE]
        values = heads[:seen, 3 * HEAD_SIZE :]
        for at in range(2):
            columns = pl.ds(at * HEAD_SIZE, HEAD_SIZE)
            queries = heads[span, columns]
            grad = grad_mixed[span, columns]
            probs = kept_probs(held, joined, at, block, chip_rows)[...]
            probs = probs.reshape(chip_rows, seen)
            grad_probs = mm_t(grad, values)
            grad_scores = (
                probs * (grad_probs - jnp.sum(probs * grad_probs, axis=-1, keepdims=True))
            ).astype(jnp.bfloat16)
            grad_queries[span, columns] = mm(grad_scores, keys) * HEAD_SIZE ** (-0.5)
            grad_keys[:seen, :] += t_mm(grad_scores, queries) * HEAD_SIZE ** (-0.5)
            grad_values[:seen, :] += t_mm(probs.astype(jnp.bfloat16), grad)


def project_back(
    place, rows, scatter, buffers, head_gain_ref, out_head_gain, wh
):
    projected, grad_projected = buffers.projected, buffers.grad_projected
    grad_queries, grad_keys, grad_values = buffers.attention_grads
    cosine, sine, _ = buffers.tables
    out_head_gain[...] = jnp.zeros_like(out_head_gain)

    def project_block(rel):
        span = block_rows(place, rel, rows)
        for at in range(3):
            columns = pl.ds(at * HEAD_SIZE, HEAD_SIZE)
            which = 0 if at < 2 else 1
            upstream = grad_queries[span, columns] if at < 2 else grad_keys[span, :]
            back, gain_term = norm_back(
                projected[span, columns],
                head_gain_ref[which : which + 1, :],
                turn_back(upstream, cosine[span, :], sine[span, :]),
            )
            out_head_gain[which : which + 1, :] += jnp.sum(gain_term, axis=0, keepdims=True)
            grad_projected[span, columns] = back.astype(jnp.bfloat16)
        grad_projected[span, 3 * HEAD_SIZE :] = grad_values[span, :].astype(jnp.bfloat16)
        scatter.put(rel, lambda columns: mm_t(grad_projected[span, :], wh[columns, :]), wh.shape[0])

    project_block(3)
    scatter.pair(3)
    project_block(2)
    scatter.pair(2)
    project_block(1)
    scatter.pair(1)
    project_block(0)


def input_back(scatter, inputs, gains_ref, out_gains, result, result_b):
    out_gains[0:1, :] = jnp.zeros_like(out_gains[0:1, :])

    def mixer_norm(span, value):
        back, gain_term = norm_back(inputs[span, :].astype(jnp.float32), gains_ref[0:1, :], value)
        out_gains[0:1, :] += jnp.sum(gain_term, axis=0, keepdims=True)
        total = back + result[span, :]
        result[span, :] = total
        if result_b is not None:
            result_b[span, :] = total.astype(jnp.bfloat16)

    scatter.total(mixer_norm)


def layer_backward_step(place, rows, refs, buffers, slot, hooks):
    (wh, wm, we, wr), gains_ref = refs.weights, refs.gains
    current, middle, result, result_b, inputs = (
        buffers.current,
        buffers.middle,
        buffers.result,
        buffers.result_b,
        buffers.inputs,
    )
    full_a, full_b, joined = buffers.full_a, buffers.full_b, buffers.joined
    save_sem, grad_joined = buffers.save_sem, buffers.grad_joined
    tables = [
        pltpu.make_async_copy(src.at[slot], dst, buffers.table_sem.at[at])
        for at, (src, dst) in enumerate(
            [
                *zip(refs.tables, buffers.tables),
                (refs.middle, middle),
                (refs.projected, buffers.projected),
                (refs.heads, buffers.heads),
                (refs.inputs, inputs),
            ]
        )
    ]
    for table in tables:
        table.start()

    def joined_load(rel):
        return pltpu.make_async_copy(
            refs.joined.at[slot, block_rows(place, rel, rows)],
            joined.at[rel % 2],
            buffers.joined_sem.at[rel % 2],
        )

    joined_load(0).start()
    joined_load(1).start()
    own_rows = pl.ds(pl.multiple_of(place.index * rows, rows), rows)
    full_a[own_rows, :] = current[...]

    def save(at, src, dst):
        copy = pltpu.make_async_copy(src, dst.at[slot], save_sem.at[at])
        copy.start()
        return copy

    gather = Gather(place, full_a, *buffers.gather_a, rows)
    scatter = Scatter(place, *buffers.scatter, *buffers.scatter_a, rows)
    length = full_a.shape[0]

    def out_of(rel):
        first = place.replica * length + place.chip_at(rel) * 2 * rows
        return grad_joined.at[pl.ds(pl.multiple_of(first, 2 * rows), 2 * rows)]

    feed_back(
        place,
        rows,
        gather,
        scatter,
        full_a,
        (wm, we, wr),
        joined,
        joined_load,
        out_of,
        hooks.done,
    )
    upstream_save = save(0, full_a, refs.upstream)
    scatter.relay()
    for table in tables:
        table.wait()
    out_gains = refs.out_gains.at[slot]
    feed_input_back(place, rows, scatter, middle, gains_ref, out_gains, current, result, full_b)
    gather.finish()
    upstream_save.wait()
    for rel in range(4):
        hooks.settled(rel, out_of(rel))
    gather_b = Gather(place, full_b, *buffers.gather_b, rows)
    scatter_b = Scatter(place, *buffers.scatter, *buffers.scatter_b, rows)
    grad_mixed = buffers.mixed

    def mixed_block(rel):
        span = block_rows(place, rel, rows)
        grad_mixed[span, :] = mm_t(full_b[span, :], wm[...]).astype(jnp.bfloat16)

    held, heads = buffers.scatter[0], buffers.heads

    def early(at):
        hooks.early(at)
        if at == 0:
            attention_probs(held, joined, heads, buffers.tables[2], 2 * rows)

    gather_b.over_blocks(mixed_block, early=early)
    middle_save = save(1, full_b, refs.grad_middle)
    attention_back(held, joined, heads, grad_mixed, *buffers.attention_grads, 2 * rows)
    project_back(
        place, rows, scatter_b, buffers, refs.head_gain, refs.out_head_gain.at[slot], wh
    )
    projected_save = save(2, buffers.grad_projected, refs.grad_projected)
    hooks.early(5)
    scatter_b.relay()
    scatter_b.pair(0)
    hooks.early(6)
    hooks.finish()
    input_back(scatter_b, inputs, gains_ref, out_gains, result, result_b)
    hooks.hand()
    gather_b.finish()
    for copy in (middle_save, projected_save):
        copy.wait()


class Saved(typing.NamedTuple):
    inputs: typing.Any
    normal_a: typing.Any
    projected: typing.Any
    heads: typing.Any
    mixed: typing.Any
    middle: typing.Any
    normal_b: typing.Any
    joined: typing.Any
    hidden: typing.Any
    upstream: typing.Any
    grad_middle: typing.Any
    grad_projected: typing.Any


class Layers(typing.NamedTuple):
    rows: typing.Any
    saved: Saved
    handed: typing.Any
    own_joined: typing.Any
    other_joined: typing.Any
    first_sum: typing.Any
    other_normal: typing.Any
    heads_w: typing.Any
    expand_w: typing.Any
    gains: typing.Any
    head_gain: typing.Any
    gain_terms: typing.Any
    head_terms: typing.Any


class LayerBuffers(typing.NamedTuple):
    current: typing.Any
    inputs: typing.Any
    result: typing.Any
    result_b: typing.Any
    full_a: typing.Any
    full_b: typing.Any
    projected: typing.Any
    heads: typing.Any
    mixed: typing.Any
    joined: typing.Any
    grad_joined: typing.Any
    grad_projected: typing.Any


class GradientBuffers(typing.NamedTuple):
    current: typing.Any
    inputs: typing.Any
    result: typing.Any
    full_a: typing.Any
    full_b: typing.Any
    projected: typing.Any
    heads: typing.Any
    mixed: typing.Any
    joined: typing.Any
    grad_projected: typing.Any


def layers_kernel(rows, *refs):
    refs = list(refs)

    def some(count):
        taken = refs[:count]
        del refs[:count]
        return taken

    own_ref, gain_ref = some(2)
    table_refs = some(3)
    heads_w, merge_w, expand_w, reduce_w = some(4)
    (out_rows,) = some(1)
    saved = types.SimpleNamespace(**Saved(*some(12))._asdict())
    out_handed, own_joined, other_joined, first_sum, other_normal = some(5)
    out_heads_w, out_expand_w = some(2)
    gains_ref, head_gain_ref, out_gains, out_head_gain = some(4)
    all_gains, wh, wm, we, wr, arrived = some(6)
    buffers = types.SimpleNamespace(**LayerBuffers(*some(12))._asdict())
    buffers.middle = buffers.result
    buffers.tables = some(3)
    buffers.attention_grads = some(3)
    buffers.scatter = some(7)
    first_tiles, first_turned, first_stage = some(3)
    buffers.blocks = first_stage
    load_sem, spread_send, spread_recv = some(3)
    share_send, share_recv = some(2)
    tile_sem, first_sem, first_send, first_recv, normal_send, normal_recv = some(6)
    buffers.save_sem, buffers.table_sem, buffers.joined_sem, buffers.hidden_sem = some(4)
    hand_send, hand_recv, out_sem = some(3)
    buffers.gather_a, buffers.scatter_a = some(2), some(2)
    buffers.gather_b, buffers.scatter_b = some(2), some(2)
    saved.weights, saved.tables = (wh, wm, we, wr), table_refs
    saved.gains, saved.head_gain = gains_ref, head_gain_ref
    saved.out_gains, saved.out_head_gain = out_gains, out_head_gain
    place = Place()
    head = place.section == 0
    rest = jnp.logical_not(head)
    hidden_width = wr.shape[0]
    depth = heads_w.shape[0]
    query_width, key_width = QUERY_HEADS * HEAD_SIZE, KEY_VALUE_HEADS * HEAD_SIZE
    loads = [
        pltpu.make_async_copy(src, dst, load_sem.at[at])
        for at, (src, dst) in enumerate(((merge_w, wm), (reduce_w, wr)))
    ]
    for load in loads:
        load.start()
    shard_rows = pl.ds(pl.multiple_of(place.index * depth, depth), depth)

    def spread(at, device, piece, src, dst):
        if at < 7:
            return remote(
                src, dst, spread_send.at[piece, at], spread_recv.at[piece, at], {"fsdp": device}
            )
        return pltpu.make_async_copy(src, dst, load_sem.at[2 + piece])

    gain_copies = [
        spread(at, device, 0, gain_ref, all_gains.at[place.index])
        for at, device in place.others()
    ]
    heads_copies, expand_copies = [], []
    for at, device in place.others():
        for piece, first, count, into in (
            (1, 0, MERGED, 0),
            (2, query_width, HEAD_SIZE, MERGED),
            (3, query_width + key_width, HEAD_SIZE, MERGED + HEAD_SIZE),
        ):
            src = heads_w.at[:, shard_columns(first, device, count)]
            heads_copies.append(
                spread(at, device, piece, src, wh.at[shard_rows, pl.ds(into, count)])
            )
        for piece in range(2):
            src = expand_w.at[:, shard_columns(piece * FF, device, hidden_width)]
            dst = we.at[shard_rows, pl.ds(piece * hidden_width, hidden_width)]
            expand_copies.append(spread(at, device, 4 + piece, src, dst))

    def arrive(copies, pieces):
        for copy in copies[:-pieces]:
            copy.wait_recv()
        for copy in copies[-pieces:]:
            copy.wait()

    heads_out = pltpu.make_async_copy(wh, out_heads_w, load_sem.at[8])
    expand_out = pltpu.make_async_copy(we, out_expand_w, load_sem.at[9])

    def share(at, device, kind, weight):
        block = weight.at[pl.ds(pl.multiple_of(device * depth, depth), depth)]
        return remote(
            block, block, share_send.at[kind, at], share_recv.at[kind, at], place.rep_peer
        )

    def start_all(copies, pieces, shared, first=0, last=PLANE):
        for at, device in place.others()[first:last]:
            mine = copies[at * pieces : (at + 1) * pieces]

            def begin():
                for copy in mine:
                    copy.start()

            if at < shared:
                pl.when(place.replica == at % 2)(begin)
            else:
                begin()

    def pass_on(copies, pieces, kind, weight, first, last):
        for at, device in place.others()[first:last]:
            mine = copies[at * pieces : (at + 1) * pieces]

            @pl.when(place.replica == at % 2)
            def _():
                for copy in mine:
                    copy.wait_recv()
                share(at, device, kind, weight).start()

    def take_shared(kind, weight, shared):
        for at, device in place.others()[:shared]:

            @pl.when(place.replica != at % 2)
            def _():
                share(at, device, kind, weight).wait_recv()

    def sent(copies, pieces, kind, weight, shared):
        for at, device in place.others()[:7]:
            mine = copies[at * pieces : (at + 1) * pieces]

            def settle():
                for copy in mine:
                    copy.wait_send()
                if at < shared:
                    share(at, device, kind, weight).wait_send()

            if at < shared:
                pl.when(place.replica == at % 2)(settle)
            else:
                settle()

    place.greet(
        [{"fsdp": device} for _, device in place.others()[:7]]
        + [place.section_peer, place.rep_peer]
    )
    for copy in gain_copies:
        copy.start()
    start_all(heads_copies, 3, 2)

    arrive(gain_copies, 1)
    for shard in range(PLANE):
        part = slice(shard * depth, (shard + 1) * depth)
        gains_ref[0:1, part] = all_gains[shard][:, :depth]
        gains_ref[1:2, part] = all_gains[shard][:, depth : 2 * depth]
    per_row = PLANE // 2
    count = 2 * HEAD_SIZE // PLANE
    for row in range(2):
        head_gain_ref[row : row + 1, :] = jnp.concatenate(
            [
                all_gains[row * per_row + at][:, 2 * depth : 2 * depth + count]
                for at in range(per_row)
            ],
            axis=1,
        )

    current, result, result_b = buffers.current, buffers.result, buffers.result_b
    length = buffers.full_a.shape[0]

    def joined_save(rel, out):
        return pltpu.make_async_copy(
            out, own_joined.at[block_rows(place, rel, rows)], first_sem.at[rel]
        )

    def joined_copy(rel, out):
        return remote(
            out,
            other_joined.at[block_rows(place, rel, rows)],
            first_send.at[rel],
            first_recv.at[rel],
            place.rep_peer,
        )

    def saved_block(rel):
        return own_joined.at[block_rows(place, rel, rows)]

    half = length // 2
    half_rows = pl.ds(pl.multiple_of(place.core * half, half), half)

    def normal_copy(slot):
        return remote(
            saved.normal_b.at[slot, half_rows],
            other_normal.at[slot, half_rows],
            normal_send.at[slot],
            normal_recv.at[slot],
            place.rep_peer,
        )

    def normal_pass(slot):
        block = other_normal.at[slot, half_rows]
        return remote(
            block, block, normal_send.at[2 + slot], normal_recv.at[2 + slot], place.core_peer
        )

    def token_rows(replica):
        return pl.ds(pl.multiple_of(replica * length, length), length)

    def first_loads(at):
        columns = pl.ds(pl.multiple_of(at * depth, depth), depth)
        parts = (
            (saved.normal_b.at[0, :, columns], place.replica),
            (other_normal.at[0, :, columns], 1 - place.replica),
        )
        into = lax.rem(at, 2)
        return [
            pltpu.make_async_copy(
                src, first_tiles.at[into, token_rows(replica)], tile_sem.at[into, part]
            )
            for part, (src, replica) in enumerate(parts)
        ]

    def first_save(at):
        rows_at = pl.ds(pl.multiple_of(at * depth, depth), depth)
        return pltpu.make_async_copy(
            first_stage.at[lax.rem(at, 2)], first_sum.at[rows_at], first_sem.at[lax.rem(at, 2)]
        )

    def whole_load(part):
        src, replica = ((own_joined, place.replica), (other_joined, 1 - place.replica))[part]
        return pltpu.make_async_copy(
            src, buffers.grad_joined.at[token_rows(replica)], first_sem.at[2 + part]
        )

    def first_begin():
        normal_copy(0).wait_recv()
        normal_pass(0).start()
        for rel in range(4):
            joined_copy(rel, saved_block(rel)).wait()
        for part in range(2):
            whole_load(part).start()
        normal_pass(0).wait_recv()
        for at in range(2):
            for copy in first_loads(jnp.int32(at)):
                copy.start()

    def first_turn():
        for part in range(2):
            whole_load(part).wait()
        for copy in first_loads(jnp.int32(0)):
            copy.wait()
        turn_tile(first_tiles.at[0], first_turned.at[0], 0, 2 * length // 256)
        for copy in first_loads(jnp.int32(2)):
            copy.start()

    def first_job(at):
        into, later = lax.rem(at, 2), lax.rem(at + 1, 2)

        @pl.when(at + 1 < PLANE)
        def _():
            for copy in first_loads(at + 1):
                copy.wait()

        @pl.when(at >= 2)
        def _():
            first_save(at - 2).wait()

        def product(columns):
            first_stage[into, :, columns] = mm(
                first_turned[into], buffers.grad_joined[:, columns]
            ).astype(jnp.bfloat16)

        product_and_turn(
            2 * hidden_width, product, first_tiles.at[later], first_turned.at[later]
        )
        first_save(at).start()

        @pl.when(at + 3 < PLANE)
        def _():
            for copy in first_loads(at + 3):
                copy.start()

    def first_jobs(first, last):
        @pl.loop(first, last)
        def _(at):
            first_job(at)

    def first_end():
        for at in (PLANE - 2, PLANE - 1):
            first_save(jnp.int32(at)).wait()

    def hand(slot):
        return remote(
            result_b, arrived.at[slot], hand_send.at[slot], hand_recv.at[slot], place.section_peer
        )

    def rows_copy(slot):
        return pltpu.make_async_copy(result, out_rows.at[slot], out_sem.at[0])

    def save_rows(slot):
        copy = rows_copy(slot)
        copy.start()
        copy.wait()

    def heads_ready():
        pass_on(heads_copies, 3, 0, wh, 0, 2)
        arrive(heads_copies[6:], 3)
        take_shared(0, wh, 2)
        heads_out.start()
        start_all(expand_copies, 2, 2, 0, 2)

    def expand_service():
        pass_on(expand_copies, 2, 1, we, 0, 2)
        start_all(expand_copies, 2, 2, 2)

    def feed_ready():
        arrive(expand_copies[4:], 2)
        take_shared(1, we, 2)
        expand_out.start()

    @pl.when(rest)
    def _():
        heads_ready()
        expand_service()
        feed_ready()

    for load in loads:
        load.wait()

    @pl.loop(0, 5)
    def _(step):
        forward = (head & (step <= 1)) | (rest & ((step == 1) | (step == 3)))
        backward = (step == 4) | (rest & (step == 2))

        @pl.when(forward)
        def _():
            slot = jnp.where(head, step, lax.div(step - 1, 2))

            @pl.when(head)
            def _():
                current[...] = own_ref[slot]

            @pl.when(rest)
            def _():
                hand(slot).wait_recv()
                current[...] = arrived[slot]

            def first(body):
                return lambda: pl.when(head & (slot == 0))(body)


            def finish():
                @pl.when(slot == 1)
                def _():
                    hand(0).wait_send()

            def handing():
                @pl.when(head)
                def _():
                    hand(slot).start()

                @pl.when(rest)
                def _():
                    save_rows(slot)

            def after():
                normal_copy(slot).start()

            layer_forward_step(
                place,
                rows,
                saved,
                buffers,
                slot,
                step,
                types.SimpleNamespace(
                    heads=first(heads_ready),
                    feed=first(feed_ready),
                    service=first(expand_service),
                    finish=finish,
                    hand=handing,
                    after=after,
                ),
            )

        @pl.when(backward)
        def _():
            slot = jnp.where(head, 0, lax.div(step - 2, 2))

            @pl.when(head)
            def _():
                hand(0).wait_recv()
                current[...] = arrived[0]

            @pl.when(rest)
            def _():
                current[...] = own_ref[slot]

            def finish():
                @pl.when(head)
                def _():
                    hand(1).wait_send()

            def handing():
                @pl.when(rest)
                def _():
                    hand(slot).start()

                @pl.when(rest & (slot == 0))
                def _():
                    for rel in range(4):
                        joined_copy(rel, saved_block(rel)).start()

                @pl.when(head)
                def _():
                    rows_copy(slot).start()

            def done(rel, out):
                @pl.when(slot == 0)
                def _():
                    joined_save(rel, out).start()

                @pl.when(head)
                def _():
                    joined_copy(rel, out).start()

            def settled(rel, out):
                pl.when(slot == 0)(lambda: joined_save(rel, out).wait())

            def early(at):
                @pl.when(rest & (slot == 1))
                def _():
                    if at == 0:
                        first_begin()
                    elif at == 2:
                        first_turn()
                    elif at == 3:
                        first_jobs(0, 2)
                    elif at == 6:
                        first_jobs(2, 5)

            hooks = types.SimpleNamespace(
                finish=finish, hand=handing, done=done, settled=settled, early=early
            )
            layer_backward_step(place, rows, saved, buffers, slot, hooks)

    @pl.when(head)
    def _():
        first_begin()
        first_turn()
        first_jobs(0, 5)

    first_jobs(5, PLANE)

    first_end()
    normal_copy(1).wait_recv()
    normal_pass(1).start()

    @pl.when(head)
    def _():
        hand(1).wait_recv()
        current[...] = arrived[1]

    @pl.when(rest)
    def _():
        hand(1).wait_send()
        current[...] = own_ref[1]

    handed = pltpu.make_async_copy(current, out_handed, out_sem.at[1])
    handed.start()
    normal_pass(1).wait_recv()
    heads_out.wait()
    expand_out.wait()
    for copy in gain_copies[:7]:
        copy.wait_send()
    sent(heads_copies, 3, 0, wh, 2)
    sent(expand_copies, 2, 1, we, 2)
    for slot in range(2):
        normal_copy(slot).wait_send()
        normal_pass(slot).wait_send()
    handed.wait()
    pl.when(head)(lambda: rows_copy(0).wait())


def gradient_kernel(rows, *refs):
    refs = list(refs)

    def some(count):
        taken = refs[:count]
        del refs[:count]
        return taken

    gains_ref, head_gain_ref, first_gains, first_head_gain = some(4)
    table_refs = some(3)
    heads_w, merge_w, expand_w, reduce_w = some(4)
    in_handed, in_inputs, in_projected, in_heads, in_middle, in_joined = some(6)
    hidden_all, upstream_all, normal_b_all, other_normal = some(4)
    mixed_all, grad_middle_all, normal_a_all, grad_projected_all = some(4)
    first_sum, out_result = some(2)
    own_heads, other_heads, own_merge, other_merge = some(4)
    own_expand, own_reduce, other_reduce = some(3)
    (out_gain,) = some(1)
    wh, wm, we, wr = some(4)
    buffers = types.SimpleNamespace(**GradientBuffers(*some(10))._asdict())
    buffers.tables = some(3)
    buffers.attention_grads = some(3)
    buffers.scatter = some(7)
    tiles, turned, wide, narrow, first_projected = some(5)
    gains, head_gain, gain_out, gain_in, gain_sum, gain_other = some(6)
    load_sem, tile_sem, joined_sem, save_sem = some(4)
    buffers.gather_a, buffers.scatter_a = some(2), some(2)
    buffers.gather_b, buffers.scatter_b = some(2), some(2)
    spread_send, spread_recv, rep_send, rep_recv = some(4)
    current, inputs, result = buffers.current, buffers.inputs, buffers.result
    full_a, full_b, grad_mixed = buffers.full_a, buffers.full_b, buffers.mixed
    joined, grad_projected = buffers.joined, buffers.grad_projected

    place = Place()
    length, width = full_a.shape
    depth = wm.shape[0]
    hidden_width = wr.shape[0]
    last = in_inputs.shape[0] - 1
    tokens = narrow.shape[0]
    query_width, key_width = QUERY_HEADS * HEAD_SIZE, KEY_VALUE_HEADS * HEAD_SIZE
    others = place.others()

    def load(at, src, dst):
        copy = pltpu.make_async_copy(src, dst, load_sem.at[at])
        copy.start()
        return copy

    upstream_load = load(0, in_handed, current)
    reduce_load = load(1, reduce_w, wr)

    def joined_load(rel):
        return pltpu.make_async_copy(
            in_joined.at[last, block_rows(place, rel, rows)],
            joined.at[rel % 2],
            joined_sem.at[rel % 2],
        )

    joined_load(0).start()
    joined_load(1).start()
    expand_load = load(2, expand_w, we)
    middle_load = load(3, in_middle.at[last], result)
    wide_load = load(4, upstream_all.at[0], wide)
    plain = [(hidden_all, at) for at in range(hidden_width // depth)] + [(mixed_all, 0)]
    plain += [(normal_a_all, device) for _, device in others]
    job_count = len(plain) + len(others)

    def token_rows(replica):
        return pl.ds(pl.multiple_of(replica * length, length), length)

    def tile_loads(job):
        source, at = plain[job] if job < len(plain) else (None, others[job - len(plain)][1])
        columns = pl.ds(pl.multiple_of(at * depth, depth), depth)
        if source is not None:
            return [
                pltpu.make_async_copy(
                    source.at[:, columns], tiles.at[job % 2], tile_sem.at[job % 2, 0]
                )
            ]
        parts = (
            (normal_b_all.at[last, :, columns], place.replica),
            (other_normal.at[last, :, columns], 1 - place.replica),
        )
        return [
            pltpu.make_async_copy(
                src, tiles.at[job % 2, token_rows(replica)], tile_sem.at[job % 2, part]
            )
            for part, (src, replica) in enumerate(parts)
        ]

    def tile_start(job):
        for copy in tile_loads(job):
            copy.start()

    def run_job(job, width, product):
        now, later = turned.at[job % 2], (job + 1) % 2
        if job + 1 < job_count:
            for copy in tile_loads(job + 1):
                copy.wait()
        product_and_turn(
            width, lambda columns: product(now, columns), tiles.at[later], turned.at[later]
        )
        if job + 3 < job_count:
            tile_start(job + 3)

    tile_start(0)
    tile_start(1)
    projected_load = load(5, grad_projected_all.at[0], first_projected)
    loads = [
        load(at + 6, src, dst)
        for at, (src, dst) in enumerate(
            [(merge_w, wm), (heads_w, wh)]
            + [(src.at[last], dst) for src, dst in zip(table_refs, buffers.tables)]
            + [
                (in_projected.at[last], buffers.projected),
                (in_heads.at[last], buffers.heads),
                (in_inputs.at[last], inputs),
            ]
        )
    ]
    place.greet([{"fsdp": device} for _, device in others[:7]] + [place.rep_peer])

    def rep_copy(at, src, dst):
        return remote(src, dst, rep_send.at[at], rep_recv.at[at], place.rep_peer)

    def spread(at, device, piece, src, dst):
        if at < 7:
            return remote(
                src, dst, spread_send.at[piece, at], spread_recv.at[piece, at], {"fsdp": device}
            )
        return pltpu.make_async_copy(src, dst, save_sem.at[4 + piece])

    upstream_load.wait()
    own_rows = pl.ds(pl.multiple_of(place.index * rows, rows), rows)
    full_a[own_rows, :] = current[...]
    gather = Gather(place, full_a, *buffers.gather_a, rows)
    scatter = Scatter(place, *buffers.scatter, *buffers.scatter_a, rows)

    joined_reps = []

    def out_of(rel):
        if rel == 0:
            reduce_load.wait()
            expand_load.wait()
        first = place.replica * length + place.chip_at(rel) * 2 * rows
        return narrow.at[pl.ds(pl.multiple_of(first, 2 * rows), 2 * rows)]

    def done(rel, out):
        copy = rep_copy(4 + rel, out, out)
        copy.start()
        joined_reps.append(copy)

    feed_back(
        place,
        rows,
        gather,
        scatter,
        full_a,
        (wm, we, wr),
        joined,
        joined_load,
        out_of,
        done,
    )
    wide_load.wait()
    for copy in tile_loads(0):
        copy.wait()
    turn_tile(tiles.at[0], turned.at[0], 0, tokens // 256)
    tile_start(2)
    own_saves, rep_copies = [], []
    for at in range(hidden_width // depth):
        span = pl.ds(at * depth, depth)

        def product(tile, columns):
            value = mm(tile[:, :length], wide[:, columns])
            value += mm(tile[:, length:], full_a[:, columns])
            wr[span, columns] = value.astype(jnp.bfloat16)

        run_job(at, width, product)
        copy = rep_copy(at, wr.at[span], other_reduce.at[span])
        copy.start()
        rep_copies.append(copy)
        copy = pltpu.make_async_copy(wr.at[span], own_reduce.at[span], save_sem.at[at])
        copy.start()
        own_saves.append(copy)
        if at == 1:
            scatter.relay()
    grad_middle_load = load(4, grad_middle_all.at[0], wide)
    middle_load.wait()
    feed_input_back(place, rows, scatter, result, gains_ref, gains, current, result, full_b)
    gather.finish()
    gather_b = Gather(place, full_b, *buffers.gather_b, rows)
    scatter_b = Scatter(place, *buffers.scatter, *buffers.scatter_b, rows)
    gather_b.start()
    for copy in loads:
        copy.wait()
    held = buffers.scatter[0]
    attention_probs(held, joined, buffers.heads, buffers.tables[2], 2 * rows)
    gather_b.relay()
    gather_b.near()
    gather_b.far()
    for rel, at in ((0, 4), (1, 7), (2, 8), (3, 9)):
        gather_b.wait(at)
        span = block_rows(place, rel, rows)
        grad_mixed[span, :] = mm_t(full_b[span, :], wm[...]).astype(jnp.bfloat16)
    attention_back(
        held, joined, buffers.heads, grad_mixed, *buffers.attention_grads, 2 * rows
    )
    project_back(place, rows, scatter_b, buffers, head_gain_ref, head_gain, wh)
    job = hidden_width // depth
    grad_middle_load.wait()

    def merge_product(tile, columns):
        value = mm(tile[:, :length], wide[:, columns])
        value += mm(tile[:, length:], full_b[:, columns])
        wm[:, columns] = value.astype(jnp.bfloat16)

    run_job(job, width, merge_product)
    job += 1
    merge_rep = rep_copy(3, wm, other_merge)
    merge_rep.start()
    merge_save = pltpu.make_async_copy(wm, own_merge, save_sem.at[3])
    merge_save.start()
    projected_load.wait()
    heads_copies = []
    for at, device in others:
        block = pl.ds(at * depth, depth)

        def product(tile, columns):
            value = mm(tile[:, :length], first_projected[:, columns])
            value += mm(tile[:, length:], grad_projected[:, columns])
            wh[block, columns] = value.astype(jnp.bfloat16)

        run_job(job, JOINT, product)
        job += 1
        for piece, first, count, start in (
            (2, 0, MERGED, 0),
            (3, query_width, HEAD_SIZE, MERGED),
            (4, query_width + key_width, HEAD_SIZE, MERGED + HEAD_SIZE),
        ):
            copy = spread(
                at,
                device,
                piece,
                wh.at[block, pl.ds(start, count)],
                own_heads.at[:, shard_columns(first, place.index, count)],
            )
            copy.start()
            heads_copies.append(copy)
    scatter_b.relay()
    scatter_b.pair(0)
    input_back(scatter_b, inputs, gains_ref, gains, result, None)
    result_save = pltpu.make_async_copy(result, out_result, save_sem.at[10])
    result_save.start()

    gain_copies = []
    gains[...] += first_gains[0]
    head_gain[...] += first_head_gain[0]
    per_row = PLANE // 2
    count = 2 * HEAD_SIZE // PLANE
    for shard in range(PLANE):
        part = slice(shard * depth, (shard + 1) * depth)
        lanes = slice(shard % per_row * count, (shard % per_row + 1) * count)
        row = shard // per_row
        gain_out[shard] = jnp.zeros_like(gain_out[shard])
        gain_out[shard, :, :depth] = gains[0:1, part]
        gain_out[shard, :, depth : 2 * depth] = gains[1:2, part]
        gain_out[shard, :, 2 * depth : 2 * depth + count] = head_gain[row : row + 1, lanes]
    for at, device in others:
        copy = spread(at, device, 5, gain_out.at[device], gain_in.at[place.index])
        copy.start()
        gain_copies.append(copy)

    def first_load(at, device):
        block = pl.ds(pl.multiple_of(device * depth, depth), depth)
        into = wide.at[pl.ds(at % 2 * depth, depth), pl.ds(0, 2 * hidden_width)]
        return pltpu.make_async_copy(first_sum.at[block], into, load_sem.at[14 + at % 2])

    for at, device in others[:2]:
        first_load(at, device).start()
    for copy in joined_reps:
        copy.wait_recv()
    expand_copies = []
    for at, device in others:
        block = pl.ds(at * depth, depth)
        first_load(at, device).wait()
        before = pl.ds(at % 2 * depth, depth)

        def product(tile, columns):
            value = wide[before, columns].astype(jnp.float32)
            value += mm(tile[...], narrow[:, columns])
            we[block, columns] = value.astype(jnp.bfloat16)

        run_job(job, narrow.shape[1], product)
        job += 1
        if at + 2 < PLANE:
            first_load(*others[at + 2]).start()
        for piece in range(2):
            copy = spread(
                at,
                device,
                piece,
                we.at[block, pl.ds(piece * hidden_width, hidden_width)],
                own_expand.at[:, shard_columns(piece * FF, place.index, hidden_width)],
            )
            copy.start()
            expand_copies.append(copy)
        if at == 3:
            for copy in heads_copies[:21]:
                copy.wait_recv()
            for copy in heads_copies[21:]:
                copy.wait()
            heads_rep = rep_copy(8, own_heads, other_heads)
            heads_rep.start()
            for copy in gain_copies[:7]:
                copy.wait_recv()
            gain_copies[7].wait()
            total = gain_in[0]
            for shard in range(1, PLANE):
                total += gain_in[shard]
            gain_sum[...] = total
            gain_rep = rep_copy(9, gain_sum, gain_other)
            gain_rep.start()
    gain_rep.wait()
    out_gain[...] = gain_sum[...] + gain_other[...]
    gather_b.finish()
    for copy in expand_copies[:14]:
        copy.wait_recv()
    for copy in expand_copies[14:] + own_saves + [result_save, merge_save]:
        copy.wait()
    for copy in expand_copies[:14] + heads_copies[:21] + gain_copies[:7] + joined_reps:
        copy.wait_send()
    for copy in rep_copies + [merge_rep, heads_rep]:
        copy.wait()


def sems(*counts):
    return [pltpu.SemaphoreType.DMA((count,)) for count in counts]


def vmem(*shapes):
    return [pltpu.VMEM(shape, dtype) for *shape, dtype in shapes]


def any_specs(count):
    return [pl.BlockSpec(memory_space=pl.ANY)] * count


def vmem_specs(count):
    return [pl.BlockSpec(memory_space=pltpu.VMEM)] * count


def kernel_params(collective_id):
    return pltpu.CompilerParams(
        collective_id=collective_id, has_side_effects=True, vmem_limit_bytes=VMEM_BYTES
    )


def weight_buffers(width, hidden_width):
    b16 = jnp.bfloat16
    return vmem(
        (width, JOINT, b16),
        (MERGED, width, b16),
        (width, 2 * hidden_width, b16),
        (hidden_width, width, b16),
    )


def table_buffers(length):
    return vmem(
        (length, HEAD_SIZE, jnp.float32),
        (length, HEAD_SIZE, jnp.float32),
        (length, 1, jnp.int32),
    )


def attention_buffers(length):
    return vmem(
        (length, MERGED, jnp.float32),
        (length, HEAD_SIZE, jnp.float32),
        (length, HEAD_SIZE, jnp.float32),
    )


def scatter_buffers(rows, width):
    half, b16 = rows // 2, jnp.bfloat16
    return vmem(
        (4, rows, width, jnp.float32),
        (4, rows, width, b16),
        (4, rows, width, b16),
        *(((3, half, width, b16),) * 4),
    )


def run_layers(own, gain_row, tables, weights):
    micro, rows, width = own.shape
    length = tables[0].shape[1]
    hidden_width, depth = weights[3].shape[0], weights[0].shape[0]
    f32, b16 = jnp.float32, jnp.bfloat16
    shape = jax.ShapeDtypeStruct
    stashes = (
        (rows, width, b16),
        (length, width, b16),
        (length, JOINT, f32),
        (length, JOINT, b16),
        (length, MERGED, b16),
        (rows, width, f32),
        (length, width, b16),
        (length, 2 * hidden_width, f32),
        (length, hidden_width, b16),
        (length, width, b16),
        (length, width, b16),
        (length, JOINT, b16),
    )
    out = pl.pallas_call(
        functools.partial(layers_kernel, rows),
        out_shape=(
            shape((micro, rows, width), f32),
            *(shape((micro, *size), dtype) for *size, dtype in stashes),
            shape((rows, width), b16),
            shape((length, 2 * hidden_width), b16),
            shape((length, 2 * hidden_width), b16),
            shape((width, 2 * hidden_width), b16),
            shape((micro, length, width), b16),
            shape((width, JOINT), b16),
            shape((width, 2 * hidden_width), b16),
            shape((2, width), f32),
            shape((2, HEAD_SIZE), f32),
            shape((micro, 2, width), f32),
            shape((micro, 2, HEAD_SIZE), f32),
        ),
        in_specs=vmem_specs(2) + any_specs(7),
        out_specs=any_specs(20) + vmem_specs(4),
        scratch_shapes=vmem((PLANE, *gain_row.shape, f32))
        + weight_buffers(width, hidden_width)
        + vmem(
            (micro, rows, width, b16),
            (rows, width, b16),
            (rows, width, b16),
            (rows, width, f32),
            (rows, width, b16),
            (length, width, b16),
            (length, width, b16),
            (length, JOINT, f32),
            (length, JOINT, b16),
            (length, MERGED, b16),
            (2, 2 * rows, 2 * hidden_width, f32),
            (2 * length, 2 * hidden_width, b16),
            (length, JOINT, b16),
        )
        + table_buffers(length)
        + attention_buffers(length)
        + scatter_buffers(rows, width)
        + vmem(
            (2, 2 * length, depth, b16),
            (2, depth, 2 * length, b16),
            (2, depth, 2 * hidden_width, b16),
        )
        + sems(10)
        + [pltpu.SemaphoreType.DMA((6, PLANE - 1))] * 2
        + [pltpu.SemaphoreType.DMA((2, 2))] * 2
        + [pltpu.SemaphoreType.DMA((2, 2))]
        + sems(4, 4, 4, 4, 4)
        + sems(10, 7, 2, 4, micro, micro, 2, *((10,) * 8)),
        compiler_params=kernel_params(1),
    )(own, gain_row, *tables, *weights)
    return Layers(out[0], Saved(*out[1:13]), *out[13:])


def run_gradients(layers, tables, merge_w, reduce_w):
    saved = layers.saved
    micro, rows, width = saved.inputs.shape
    length = tables[0].shape[1]
    hidden_width, depth = reduce_w.shape[0], merge_w.shape[0]
    f32, b16 = jnp.float32, jnp.bfloat16
    shape = jax.ShapeDtypeStruct
    heads_term, merge_term = (depth, PLANE * JOINT), (depth, width)
    expand_term, reduce_term = (depth, 2 * FF), (hidden_width, width)
    terms = (heads_term,) * 2 + (merge_term,) * 2 + (expand_term,) + (reduce_term,) * 2
    gain_width = -(-(2 * depth + 2 * HEAD_SIZE // PLANE) // 128) * 128

    def flat(array):
        return array.reshape(micro * length, -1)

    return pl.pallas_call(
        functools.partial(gradient_kernel, rows),
        out_shape=(shape((rows, width), f32),)
        + tuple(shape(term, b16) for term in terms)
        + (shape((1, gain_width), f32),),
        in_specs=vmem_specs(4) + any_specs(22),
        out_specs=any_specs(8) + vmem_specs(1),
        scratch_shapes=weight_buffers(width, hidden_width)
        + vmem(
            (rows, width, b16),
            (rows, width, b16),
            (rows, width, f32),
            (length, width, b16),
            (length, width, b16),
            (length, JOINT, f32),
            (length, JOINT, b16),
            (length, MERGED, b16),
            (2, 2 * rows, 2 * hidden_width, f32),
            (length, JOINT, b16),
        )
        + table_buffers(length)
        + attention_buffers(length)
        + scatter_buffers(rows, width)
        + vmem(
            (2, micro * length, depth, b16),
            (2, depth, micro * length, b16),
            (length, width, b16),
            (2 * length, 2 * hidden_width, b16),
            (length, JOINT, b16),
            (2, width, f32),
            (2, HEAD_SIZE, f32),
            (PLANE, 1, gain_width, f32),
            (PLANE, 1, gain_width, f32),
            (1, gain_width, f32),
            (1, gain_width, f32),
        )
        + sems(18)
        + [pltpu.SemaphoreType.DMA((2, 2))]
        + sems(2, 11, *((10,) * 8))
        + [pltpu.SemaphoreType.DMA((6, PLANE - 1))] * 2
        + sems(10, 10),
        compiler_params=kernel_params(2),
    )(
        layers.gains,
        layers.head_gain,
        layers.gain_terms,
        layers.head_terms,
        *tables,
        layers.heads_w,
        merge_w,
        layers.expand_w,
        reduce_w,
        layers.handed,
        saved.inputs,
        saved.projected,
        saved.heads,
        saved.middle,
        saved.joined,
        flat(saved.hidden),
        saved.upstream,
        saved.normal_b,
        layers.other_normal,
        flat(saved.mixed),
        saved.grad_middle,
        flat(saved.normal_a),
        saved.grad_projected,
        layers.first_sum,
    )


def position_tables(lengths, length):
    document_index, positions = places(lengths, length)
    half_width = HEAD_SIZE // 2
    frequency = jnp.exp(
        jnp.arange(half_width, dtype=jnp.float32) * (-2.0 * math.log(ROPE_BASE) / HEAD_SIZE)
    )
    angles = positions.astype(jnp.float32)[:, None] * frequency[None, :]
    cosine, sine = jnp.cos(angles), jnp.sin(angles)
    first_key = jnp.arange(length, dtype=jnp.int32) - positions
    return (
        jnp.concatenate([cosine, cosine], axis=-1),
        jnp.concatenate([-sine, sine], axis=-1),
        first_key[:, None],
    )


def tensor_parallel_body(
    section_inputs,
    doc_lengths,
    mixer_gain,
    heads_weight,
    merge_weight,
    head_gain,
    feed_gain,
    expand_weight,
    reduce_weight,
):
    shards = lax.axis_size("fsdp")
    own = section_inputs[0, :, 0]
    micro, rows, width = own.shape
    length = rows * shards
    depth = heads_weight.shape[1]
    hidden_width = reduce_weight.shape[1]
    query_width = QUERY_HEADS * HEAD_SIZE

    gain_row = jnp.concatenate([mixer_gain[0], feed_gain[0], head_gain[0]]).astype(jnp.float32)
    gain_row = jnp.pad(gain_row, (0, -gain_row.shape[0] % 128))[None]
    tables = [position_tables(doc_lengths[at, 0], length) for at in range(micro)]
    cosine, sine, first_key = (jnp.stack(entry) for entry in zip(*tables))

    table_rows = (cosine, sine, first_key)
    layers = run_layers(
        own,
        gain_row,
        table_rows,
        (heads_weight[0], merge_weight[0], expand_weight[0], reduce_weight[0]),
    )
    last_rows, *terms, gain_sums = run_gradients(
        layers, table_rows, merge_weight[0], reduce_weight[0]
    )
    own_heads, other_heads, own_merge, other_merge, own_expand, own_reduce, other_reduce = terms
    grad_expand = own_expand.astype(jnp.float32)[None]
    grad_heads, grad_merge, grad_reduce = (
        (mine.astype(jnp.float32) + theirs.astype(jnp.float32))[None]
        for mine, theirs in (
            (own_heads, other_heads),
            (own_merge, other_merge),
            (own_reduce, other_reduce),
        )
    )
    head_count = head_gain.shape[1]
    head = lax.axis_index("section") == 0
    last_rows = jnp.where(head, last_rows, layers.rows[-1])
    return (
        jnp.concatenate([layers.rows[:-1], last_rows[None]])[None, :, None],
        gain_sums[:, :depth],
        grad_heads,
        grad_merge,
        gain_sums[:, 2 * depth : 2 * depth + head_count],
        gain_sums[:, depth : 2 * depth],
        grad_expand,
        grad_reduce,
    )


def solution(mesh):
    plane = mesh.shape["fsdp"] == PLANE
    return jax.shard_map(
        tensor_parallel_body if plane else body,
        mesh=mesh,
        in_specs=(
            P("section", None, "rep", "fsdp", None),
            P(None, "rep", None),
            P("section", "fsdp"),
            P("section", "fsdp", None),
            P("section", "fsdp", None),
            P("section", "fsdp"),
            P("section", "fsdp"),
            P("section", "fsdp", None),
            P("section", "fsdp", None),
        ),
        out_specs=(
            P("section", None, "rep", "fsdp", None),
            P("section", "fsdp"),
            P("section", "fsdp", None),
            P("section", "fsdp", None),
            P("section", "fsdp"),
            P("section", "fsdp"),
            P("section", "fsdp", None),
            P("section", "fsdp", None),
        ),
        check_vma=False,
    )
```

```python
import functools
import math
import types
import typing

import jax
import jax.numpy as jnp
from jax import lax
from jax.experimental import pallas as pl
from jax.experimental.pallas import tpu as pltpu
from jax.sharding import PartitionSpec as P

FF = 6144
QUERY_HEADS = 16
KEY_VALUE_HEADS = 8
HEAD_SIZE = 128


NORM_EPS = 1e-06
ROPE_BASE = 1000000.0
MASKED_SCORE = -1e30
PLANE = 8


def from_behind(array, axis, by):
    count = lax.axis_size(axis)
    pairs = [(i, i + by) for i in range(count) if 0 <= i + by < count]
    return lax.ppermute(array, axis, pairs)


def normed(values):
    return values * lax.rsqrt(jnp.mean(values * values, axis=-1, keepdims=True) + NORM_EPS)


def scaled(values, gain_row):
    return normed(values) * gain_row


def rotate(values, positions):
    half_width = values.shape[-1] // 2
    frequency = jnp.exp(
        jnp.arange(half_width, dtype=jnp.float32) * (-2.0 * math.log(ROPE_BASE) / values.shape[-1])
    )
    angles = positions.astype(jnp.float32)[:, None] * frequency[None, :]
    cosine = jnp.cos(angles)[:, None, :]
    sine_part = jnp.sin(angles)[:, None, :]
    lower_half = values[..., :half_width]
    upper_half = values[..., half_width:]
    return jnp.concatenate(
        [
            lower_half * cosine - upper_half * sine_part,
            upper_half * cosine + lower_half * sine_part,
        ],
        axis=-1,
    )


def places(doc_lengths, sequence_length):
    doc_ends = jnp.cumsum(doc_lengths)
    token_index = jnp.arange(sequence_length, dtype=jnp.int32)
    passed_ends = (token_index[:, None] >= doc_ends[None, :]).astype(jnp.int32)
    document_index = jnp.sum(passed_ends, axis=1)
    doc_start = jnp.sum(passed_ends * doc_lengths[None, :], axis=1)
    return (document_index, token_index - doc_start)


def heads_of(projected_output, head_gain, positions):
    count_of_tokens = projected_output.shape[0]
    query_rows = projected_output[:, : QUERY_HEADS * HEAD_SIZE].reshape(
        count_of_tokens, QUERY_HEADS, HEAD_SIZE
    )
    heads_of_keys = projected_output[
        :, QUERY_HEADS * HEAD_SIZE : (QUERY_HEADS + KEY_VALUE_HEADS) * HEAD_SIZE
    ].reshape(count_of_tokens, KEY_VALUE_HEADS, HEAD_SIZE)
    heads_of_values = projected_output[:, (QUERY_HEADS + KEY_VALUE_HEADS) * HEAD_SIZE :]
    return (
        rotate(scaled(query_rows, head_gain[:HEAD_SIZE]), positions),
        rotate(scaled(heads_of_keys, head_gain[HEAD_SIZE:]), positions),
        heads_of_values,
    )


def gated_unit(joined):
    return jax.nn.silu(joined[:, :FF]) * joined[:, FF:]


def times_transposed(left_side, right_side):
    return lax.dot_general(
        left_side, right_side, (((1,), (1,)), ((), ())), preferred_element_type=jnp.float32
    )


def allowed_mask(doc_rows, row_start, document_index):
    row_index = row_start + jnp.arange(doc_rows.shape[0], dtype=jnp.int32)
    key_index = jnp.arange(document_index.shape[0], dtype=jnp.int32)
    return (doc_rows[:, None] == document_index[None, :]) & (
        row_index[:, None] >= key_index[None, :]
    )


def raw_scores(query_rows_second, rows_of_keys, allowed):
    grouped_heads = query_rows_second.reshape(
        query_rows_second.shape[0], KEY_VALUE_HEADS, QUERY_HEADS // KEY_VALUE_HEADS, HEAD_SIZE
    )
    heads_of_keys = rows_of_keys.reshape(rows_of_keys.shape[0], KEY_VALUE_HEADS, HEAD_SIZE)
    scores = jnp.einsum(
        "rkgd,tkd->rkgt", grouped_heads, heads_of_keys, preferred_element_type=jnp.float32
    ) * HEAD_SIZE ** (-0.5)
    return jnp.where(allowed[:, None, None, :], scores, MASKED_SCORE)


def attend_rows(query_rows_second, rows_of_keys, rows_of_values, allowed):
    scores = raw_scores(query_rows_second, rows_of_keys, allowed)
    row_max = jnp.max(scores, axis=-1, keepdims=True)
    exp_scores = jnp.exp(scores - row_max)
    row_totals = jnp.sum(exp_scores, axis=-1, keepdims=True)
    attn_probs = (exp_scores / row_totals).astype(jnp.bfloat16)
    heads_of_values = rows_of_values.reshape(rows_of_values.shape[0], KEY_VALUE_HEADS, HEAD_SIZE)
    heads_mixed = jnp.einsum(
        "rkgt,tkd->rkgd", attn_probs, heads_of_values, preferred_element_type=jnp.float32
    )
    return (
        heads_mixed.reshape(query_rows_second.shape[0], QUERY_HEADS * HEAD_SIZE),
        row_max + jnp.log(row_totals),
    )


def attend_back(
    query_rows_second, rows_of_keys, rows_of_values, allowed, log_totals, mixed_gradient_second
):
    count_of_rows = query_rows_second.shape[0]
    count_of_keys = rows_of_keys.shape[0]
    grouped_heads = query_rows_second.reshape(
        count_of_rows, KEY_VALUE_HEADS, QUERY_HEADS // KEY_VALUE_HEADS, HEAD_SIZE
    )
    heads_of_keys = rows_of_keys.reshape(count_of_keys, KEY_VALUE_HEADS, HEAD_SIZE)
    heads_of_values = rows_of_values.reshape(count_of_keys, KEY_VALUE_HEADS, HEAD_SIZE)
    heads_gradient = mixed_gradient_second.reshape(
        count_of_rows, KEY_VALUE_HEADS, QUERY_HEADS // KEY_VALUE_HEADS, HEAD_SIZE
    )
    attn_probs = jnp.exp(raw_scores(query_rows_second, rows_of_keys, allowed) - log_totals)
    grad_probs = jnp.einsum(
        "rkgd,tkd->rkgt", heads_gradient, heads_of_values, preferred_element_type=jnp.float32
    )
    grad_scores = (
        attn_probs * (grad_probs - jnp.sum(grad_probs * attn_probs, axis=-1, keepdims=True))
    ).astype(jnp.bfloat16)
    queries_gradient = jnp.einsum(
        "rkgt,tkd->rkgd", grad_scores, heads_of_keys, preferred_element_type=jnp.float32
    ) * HEAD_SIZE ** (-0.5)
    keys_gradient = jnp.einsum(
        "rkgt,rkgd->tkd", grad_scores, grouped_heads, preferred_element_type=jnp.float32
    ) * HEAD_SIZE ** (-0.5)
    values_gradient = jnp.einsum(
        "rkgt,rkgd->tkd",
        attn_probs.astype(jnp.bfloat16),
        heads_gradient,
        preferred_element_type=jnp.float32,
    )
    return (
        queries_gradient.reshape(count_of_rows, QUERY_HEADS, HEAD_SIZE),
        keys_gradient.reshape(count_of_keys, KEY_VALUE_HEADS * HEAD_SIZE),
        values_gradient.reshape(count_of_keys, KEY_VALUE_HEADS * HEAD_SIZE),
    )


def layer_forward(inputs, layer_full, positions, allowed):
    mixer_gain, heads_weight, merge_weight, head_gain, feed_gain, expand_weight, reduce_weight = (
        layer_full
    )
    count_of_rows = inputs.shape[0]
    normal_a = scaled(inputs, mixer_gain).astype(jnp.bfloat16)
    projected_output = jnp.dot(normal_a, heads_weight, preferred_element_type=jnp.float32)
    query_rows, heads_of_keys, heads_of_values = heads_of(projected_output, head_gain, positions)
    rows_of_keys, rows_of_values = (
        lax.all_gather(
            heads_of_keys.reshape(count_of_rows, KEY_VALUE_HEADS * HEAD_SIZE).astype(jnp.bfloat16),
            "fsdp",
            axis=0,
            tiled=True,
        ),
        lax.all_gather(heads_of_values.astype(jnp.bfloat16), "fsdp", axis=0, tiled=True),
    )
    heads_mixed, log_totals = attend_rows(
        query_rows.astype(jnp.bfloat16), rows_of_keys, rows_of_values, allowed
    )
    mixed_b = heads_mixed.astype(jnp.bfloat16)
    middle = inputs + jnp.dot(mixed_b, merge_weight, preferred_element_type=jnp.float32)
    normal_b = scaled(middle, feed_gain).astype(jnp.bfloat16)
    joined = jnp.dot(normal_b, expand_weight, preferred_element_type=jnp.float32)
    hidden = gated_unit(joined).astype(jnp.bfloat16)
    result = middle + jnp.dot(hidden, reduce_weight, preferred_element_type=jnp.float32)
    return (
        result,
        (
            inputs,
            normal_a,
            projected_output,
            rows_of_keys,
            rows_of_values,
            log_totals,
            mixed_b,
            middle,
            normal_b,
            joined,
            hidden,
        ),
    )


def layer_backward(upstream, layer_full, saved, positions, allowed):
    mixer_gain, heads_weight, merge_weight, head_gain, feed_gain, expand_weight, reduce_weight = (
        layer_full
    )
    (
        inputs,
        normal_a,
        projected_output,
        rows_of_keys,
        rows_of_values,
        log_totals,
        mixed_b,
        middle,
        normal_b,
        joined,
        hidden,
    ) = saved
    count_of_rows = inputs.shape[0]
    upstream_b = upstream.astype(jnp.bfloat16)
    grad_hidden = times_transposed(upstream_b, reduce_weight)
    unused_joined, gated_back = jax.vjp(gated_unit, joined)
    grad_joined = gated_back(grad_hidden)[0].astype(jnp.bfloat16)
    unused_feed, feed_back = jax.vjp(scaled, middle, feed_gain)
    grad_middle_part, grad_feed = feed_back(times_transposed(grad_joined, expand_weight))
    grad_middle = upstream + grad_middle_part
    grad_middle_b = grad_middle.astype(jnp.bfloat16)
    grad_mixed = times_transposed(grad_middle_b, merge_weight).astype(jnp.bfloat16)
    head_values, heads_back = jax.vjp(
        lambda projected_rows, gain_rows: heads_of(projected_rows, gain_rows, positions),
        projected_output,
        head_gain,
    )
    queries_gradient, grad_keys_all, grad_values_all = attend_back(
        head_values[0].astype(jnp.bfloat16),
        rows_of_keys,
        rows_of_values,
        allowed,
        log_totals,
        grad_mixed,
    )
    keys_gradient, values_gradient = (
        lax.psum_scatter(
            grad_keys_all.astype(jnp.bfloat16), "fsdp", scatter_dimension=0, tiled=True
        ).astype(jnp.float32),
        lax.psum_scatter(
            grad_values_all.astype(jnp.bfloat16), "fsdp", scatter_dimension=0, tiled=True
        ).astype(jnp.float32),
    )
    grad_projected, grad_head = heads_back(
        (
            queries_gradient,
            keys_gradient.reshape(count_of_rows, KEY_VALUE_HEADS, HEAD_SIZE),
            values_gradient,
        )
    )
    grad_projected_b = grad_projected.astype(jnp.bfloat16)
    unused_mixer, mixer_back = jax.vjp(scaled, inputs, mixer_gain)
    grad_inputs_part, grad_mixer = mixer_back(times_transposed(grad_projected_b, heads_weight))
    operands = (
        normal_a,
        grad_projected_b,
        mixed_b,
        grad_middle_b,
        normal_b,
        grad_joined,
        hidden,
        upstream_b,
    )
    return (grad_middle + grad_inputs_part, operands, (grad_mixer, grad_feed, grad_head))


def product_term(left_side, right_side):
    return lax.dot_general(
        left_side, right_side, (((0,), (0,)), ((), ())), preferred_element_type=jnp.float32
    )


def reduce_grads(operands, gain_terms):
    (
        normal_a,
        grad_projected_b,
        mixed_b,
        grad_middle_b,
        normal_b,
        grad_joined,
        hidden,
        upstream_b,
    ) = operands
    heads_gradient = lax.psum_scatter(
        product_term(normal_a, grad_projected_b).astype(jnp.bfloat16),
        "fsdp",
        scatter_dimension=0,
        tiled=True,
    )
    grad_merge = lax.psum_scatter(
        product_term(mixed_b, grad_middle_b).astype(jnp.bfloat16),
        "fsdp",
        scatter_dimension=0,
        tiled=True,
    )
    grad_expand = lax.psum_scatter(
        product_term(normal_b, grad_joined).astype(jnp.bfloat16),
        "fsdp",
        scatter_dimension=0,
        tiled=True,
    )
    grad_reduce = lax.psum_scatter(
        product_term(hidden, upstream_b).astype(jnp.bfloat16),
        "fsdp",
        scatter_dimension=0,
        tiled=True,
    )
    grad_mixer, grad_feed, grad_head = (
        lax.psum_scatter(gain_terms[0], "fsdp", scatter_dimension=0, tiled=True),
        lax.psum_scatter(gain_terms[1], "fsdp", scatter_dimension=0, tiled=True),
        lax.psum_scatter(gain_terms[2], "fsdp", scatter_dimension=0, tiled=True),
    )
    return (
        lax.psum(grad_mixer.astype(jnp.bfloat16), "rep").astype(jnp.float32),
        lax.psum(heads_gradient, "rep").astype(jnp.float32),
        lax.psum(grad_merge, "rep").astype(jnp.float32),
        lax.psum(grad_head.astype(jnp.bfloat16), "rep").astype(jnp.float32),
        lax.psum(grad_feed.astype(jnp.bfloat16), "rep").astype(jnp.float32),
        lax.psum(grad_expand, "rep").astype(jnp.float32),
        lax.psum(grad_reduce, "rep").astype(jnp.float32),
    )


def body(
    section_inputs,
    doc_lengths,
    mixer_gain,
    heads_weight,
    merge_weight,
    head_gain,
    feed_gain,
    expand_weight,
    reduce_weight,
):
    section_index = lax.axis_index("section")
    head_section = section_index == 0
    shard_index = lax.axis_index("fsdp")
    count_of_rows = section_inputs.shape[3]
    sequence_length = count_of_rows * lax.axis_size("fsdp")
    own_rows = section_inputs[0, :, 0]
    micro_count = own_rows.shape[0]
    mixer_part = (
        lax.all_gather(mixer_gain, "fsdp", axis=1, tiled=True),
        lax.all_gather(heads_weight, "fsdp", axis=1, tiled=True),
        lax.all_gather(merge_weight, "fsdp", axis=1, tiled=True),
        lax.all_gather(head_gain, "fsdp", axis=1, tiled=True),
    )
    feed_part = (
        lax.all_gather(feed_gain, "fsdp", axis=1, tiled=True),
        lax.all_gather(expand_weight, "fsdp", axis=1, tiled=True),
        lax.all_gather(reduce_weight, "fsdp", axis=1, tiled=True),
    )
    layer_full = (
        mixer_part[0][0].astype(jnp.float32),
        mixer_part[1][0],
        mixer_part[2][0],
        mixer_part[3][0].astype(jnp.float32),
        feed_part[0][0].astype(jnp.float32),
        feed_part[1][0],
        feed_part[2][0],
    )

    def layout(micro_slot):
        document_index, positions = places(doc_lengths[micro_slot, 0], sequence_length)
        row_start = shard_index * count_of_rows
        doc_rows = lax.dynamic_slice_in_dim(document_index, row_start, count_of_rows)
        own_positions = lax.dynamic_slice_in_dim(positions, row_start, count_of_rows)
        return (own_positions, allowed_mask(doc_rows, row_start, document_index))

    results = jnp.zeros((micro_count, count_of_rows, own_rows.shape[2]), jnp.float32)
    saved_acts = None
    arrived = jnp.zeros((count_of_rows, own_rows.shape[2]), jnp.bfloat16)
    for step_index in range(micro_count + 1):
        slot_raw = step_index - section_index
        is_live = (slot_raw >= 0) & (slot_raw < micro_count)
        micro_slot = jnp.clip(slot_raw, 0, micro_count - 1)
        inputs = jnp.where(
            head_section, own_rows[min(step_index, micro_count - 1)], arrived
        ).astype(jnp.float32)
        positions, allowed = layout(micro_slot)
        result, saved = layer_forward(inputs, layer_full, positions, allowed)
        if saved_acts is None:
            saved_acts = tuple(
                (jnp.zeros((micro_count,) + current.shape, current.dtype) for current in saved)
            )
        saved_acts = tuple(
            (
                jnp.where(is_live, buffer.at[micro_slot].set(current), buffer)
                for buffer, current in zip(saved_acts, saved)
            )
        )
        results = jnp.where(
            is_live & jnp.logical_not(head_section), results.at[micro_slot].set(result), results
        )
        if step_index < micro_count:
            arrived = from_behind(result.astype(jnp.bfloat16), "section", 1)
    gradients = None
    stashed = None
    gain_sums = None
    from_next = jnp.zeros((count_of_rows, own_rows.shape[2]), jnp.bfloat16)
    for step_index in range(micro_count + 1):
        slot_raw = step_index - 1 + section_index
        is_live = (slot_raw >= 0) & (slot_raw < micro_count)
        micro_slot = jnp.clip(slot_raw, 0, micro_count - 1)
        upstream = jnp.where(
            head_section, from_next, own_rows[min(step_index, micro_count - 1)]
        ).astype(jnp.float32)
        upstream = jnp.where(is_live, upstream, 0.0)
        positions, allowed = layout(micro_slot)
        saved = tuple((buffer[micro_slot] for buffer in saved_acts))
        grad_inputs, operands, gain_terms = layer_backward(
            upstream, layer_full, saved, positions, allowed
        )
        results = jnp.where(
            is_live & head_section, results.at[micro_slot].set(grad_inputs), results
        )
        if step_index < micro_count:
            from_next = from_behind(grad_inputs.astype(jnp.bfloat16), "section", -1)
        if stashed is None:
            stashed = tuple(
                (jnp.zeros((micro_count,) + current.shape, current.dtype) for current in operands)
            )
            gain_sums = tuple((jnp.zeros_like(current) for current in gain_terms))
        stashed = tuple(
            (
                jnp.where(is_live, buffer.at[micro_slot].set(current), buffer)
                for buffer, current in zip(stashed, operands)
            )
        )
        gain_sums = tuple(
            (total_so_far + current for total_so_far, current in zip(gain_sums, gain_terms))
        )
    merged = tuple(
        (buffer.reshape((micro_count * count_of_rows,) + buffer.shape[2:]) for buffer in stashed)
    )
    gradients = reduce_grads(merged, gain_sums)
    grad_mixer, heads_gradient, grad_merge, grad_head, grad_feed, grad_expand, grad_reduce = (
        gradients
    )
    return (
        results[None, :, None],
        grad_mixer[None],
        heads_gradient[None],
        grad_merge[None],
        grad_head[None],
        grad_feed[None],
        grad_expand[None],
        grad_reduce[None],
    )


MESH = pl.DeviceIdType.MESH
MERGED = QUERY_HEADS // KEY_VALUE_HEADS * HEAD_SIZE
JOINT = MERGED + 2 * HEAD_SIZE
VMEM_BYTES = 63 * 2**20


def mm(left, right):
    return jnp.dot(left, right, preferred_element_type=jnp.float32)


def mm_t(left, right):
    return lax.dot_general(
        left, right, (((1,), (1,)), ((), ())), preferred_element_type=jnp.float32
    )


def t_mm(left, right):
    return lax.dot_general(
        left, right, (((0,), (0,)), ((), ())), preferred_element_type=jnp.float32
    )


def remote(src, dst, send, recv, device):
    return pltpu.make_async_remote_copy(
        src_ref=src,
        dst_ref=dst,
        send_sem=send,
        recv_sem=recv,
        device_id=device,
        device_id_type=MESH,
    )


class Place:
    def __init__(self):
        self.index = lax.axis_index("fsdp")
        self.core = lax.rem(self.index, 2)
        self.chip = lax.div(self.index, 2)
        self.x = lax.rem(self.chip, 2)
        self.y = lax.div(self.chip, 2)
        self.x_peer = {"fsdp": self.index + 2 - 4 * self.x}
        self.y_peer = {"fsdp": self.index + 4 - 8 * self.y}
        self.core_peer = {"fsdp": self.index + 1 - 2 * self.core}
        self.section = lax.axis_index("section")
        self.section_peer = {"section": 1 - self.section}
        self.replica = lax.axis_index("rep")
        self.rep_peer = {"rep": 1 - self.replica}

    def chip_at(self, rel):
        x, y = self.x, self.y
        if rel in (1, 3):
            x = 1 - x
        if rel in (2, 3):
            y = 1 - y
        return 2 * y + x

    def others(self):
        order = ((3, 0), (3, 1), (1, 0), (1, 1), (2, 0), (2, 1), (0, 1), (0, 0))
        return [
            (at, 2 * self.chip_at(rel) + (1 - self.core if other else self.core))
            for at, (rel, other) in enumerate(order)
        ]

    def greet(self, peers):
        barrier = pltpu.get_barrier_semaphore()
        for peer in peers:
            pl.semaphore_signal(barrier, inc=1, device_id=peer, device_id_type=MESH)
        pl.semaphore_wait(barrier, len(peers))


class Gather:
    def __init__(self, place, full, send, recv, rows):
        half = rows // 2

        def span(rel, part=None):
            first = (2 * place.chip_at(rel) + place.core) * rows
            if part is None:
                return pl.ds(pl.multiple_of(first, rows), rows)
            return pl.ds(pl.multiple_of(first + part * half, half), half)

        def copy(at, piece, peer):
            block = full.at[piece]
            return remote(block, block, send.at[at], recv.at[at], peer)

        self.copies = [
            copy(0, span(0, 1), place.x_peer),
            copy(1, span(0, 0), place.x_peer),
            copy(2, span(0, 0), place.y_peer),
            copy(3, span(0, 1), place.y_peer),
            copy(4, span(0), place.core_peer),
            copy(5, span(1, 1), place.y_peer),
            copy(6, span(2, 0), place.x_peer),
            copy(7, span(1), place.core_peer),
            copy(8, span(2), place.core_peer),
            copy(9, span(3), place.core_peer),
        ]

    def start(self):
        for at in (0, 2, 4, 1, 3):
            self.copies[at].start()

    def relay(self):
        self.copies[0].wait_recv()
        self.copies[5].start()
        self.copies[2].wait_recv()
        self.copies[6].start()

    def near(self):
        self.copies[1].wait_recv()
        self.copies[7].start()
        self.copies[3].wait_recv()
        self.copies[8].start()

    def far(self):
        self.copies[5].wait_recv()
        self.copies[6].wait_recv()
        self.copies[9].start()

    def wait(self, at):
        self.copies[at].wait_recv()

    def finish(self):
        for entry in self.copies:
            entry.wait_send()

    def over_blocks(self, block, between=lambda: None, early=lambda at: None):
        self.start()
        early(0)
        self.wait(4)
        block(0)
        early(1)
        self.relay()
        early(2)
        self.near()
        self.wait(7)
        block(1)
        early(3)
        self.wait(8)
        block(2)
        early(4)
        between()
        self.far()
        self.wait(9)
        block(3)


class Scatter:
    def __init__(self, place, held, to_core, from_core, to_x, to_y, from_x, from_y, send, recv, rows):
        self.place, self.held, self.to_core, self.from_core = place, held, to_core, from_core
        self.to_x, self.to_y, self.from_x, self.from_y = to_x, to_y, from_x, from_y
        self.rows, self.half = rows, rows // 2

        def copy(at, src, dst, peer):
            return remote(src, dst, send.at[at], recv.at[at], peer)

        self.copies = [
            copy(rel, to_core.at[rel], from_core.at[rel], place.core_peer) for rel in range(4)
        ] + [
            copy(4, to_x.at[0], from_x.at[0], place.x_peer),
            copy(5, to_y.at[0], from_y.at[0], place.y_peer),
            copy(6, to_x.at[1], from_x.at[1], place.x_peer),
            copy(7, to_y.at[1], from_y.at[1], place.y_peer),
            copy(8, to_y.at[2], from_y.at[2], place.y_peer),
            copy(9, to_x.at[2], from_x.at[2], place.x_peer),
        ]

    def put(self, rel, product, width):
        step, rows, mine = 512, self.rows, self.place.core == 0

        @pl.loop(0, width // step)
        def _(at):
            columns = pl.ds(pl.multiple_of(at * step, step), step)
            value = product(columns)
            low, high = value[:rows], value[rows:]
            self.held[rel, :, columns] = jnp.where(mine, low, high)
            self.to_core[rel, :, columns] = jnp.where(mine, high, low).astype(jnp.bfloat16)

        self.copies[rel].start()

    def pair(self, rel):
        self.copies[rel].wait_recv()
        half, held = self.half, self.held

        @pl.loop(0, self.rows // 16)
        def _(at):
            span = pl.ds(pl.multiple_of(at * 16, 16), 16)
            held[rel, span, :] += self.from_core[rel, span, :].astype(jnp.float32)

        if rel == 3:
            self.to_x[0] = held[3, :half].astype(jnp.bfloat16)
            self.copies[4].start()
            self.to_y[0] = held[3, half:].astype(jnp.bfloat16)
            self.copies[5].start()
        if rel == 1:
            self.to_x[1] = held[1, :half].astype(jnp.bfloat16)
            self.copies[6].start()
        if rel == 2:
            self.to_y[1] = held[2, half:].astype(jnp.bfloat16)
            self.copies[7].start()

    def relay(self):
        half, held = self.half, self.held
        self.copies[4].wait_recv()
        self.to_y[2] = (held[2, :half] + self.from_x[0].astype(jnp.float32)).astype(jnp.bfloat16)
        self.copies[8].start()
        self.copies[5].wait_recv()
        self.to_x[2] = (held[1, half:] + self.from_y[0].astype(jnp.float32)).astype(jnp.bfloat16)
        self.copies[9].start()

    def total(self, add):
        for at in (6, 7, 8, 9):
            self.copies[at].wait_recv()
        count = self.half // 16

        @pl.loop(0, count)
        def _(at):
            span = pl.ds(pl.multiple_of(at * 16, 16), 16)
            low = self.held[0, span, :] + self.from_x[1, span, :].astype(jnp.float32)
            add(span, low + self.from_y[2, span, :].astype(jnp.float32))

        @pl.loop(0, count)
        def _(at):
            span = pl.ds(pl.multiple_of(at * 16, 16), 16)
            below = pl.ds(pl.multiple_of(self.half + at * 16, 16), 16)
            high = self.held[0, below, :] + self.from_y[1, span, :].astype(jnp.float32)
            add(below, high + self.from_x[2, span, :].astype(jnp.float32))

        for entry in self.copies:
            entry.wait_send()


def turn_tile(tile, turned, first, last):
    for at in range(last - first):
        span = pl.ds(pl.multiple_of((first + at) * 256, 256), 256)
        turned[:, span] = tile[span, :].T


def product_and_turn(width, product, tile, turned):
    parts = 4 if width >= 1024 else 2
    step, share = width // parts, turned.shape[1] // (256 * parts)

    @pl.loop(0, parts)
    def _(chunk):
        product(pl.ds(pl.multiple_of(chunk * step, 128), step))
        for at in range(share):
            span = pl.ds(pl.multiple_of((chunk * share + at) * 256, 256), 256)
            turned[:, span] = tile[span, :].T


def by_rows(count, body):
    @pl.loop(0, count // 16)
    def _(at):
        body(pl.ds(pl.multiple_of(at * 16, 16), 16))


def inverse_size(values):
    return lax.rsqrt(jnp.mean(values * values, axis=-1, keepdims=True) + NORM_EPS)


def norm_back(values, gain, upstream):
    size = inverse_size(values)
    scaled_up = upstream * gain
    back = size * scaled_up - values * (
        size * size * size * jnp.mean(values * scaled_up, axis=-1, keepdims=True)
    )
    return back, upstream * values * size


def turn(values, cosine, sine):
    return values * cosine + pltpu.roll(values, HEAD_SIZE // 2, 1) * sine


def turn_back(values, cosine, sine):
    return values * cosine + pltpu.roll(values * sine, HEAD_SIZE // 2, 1)


def probabilities(queries, keys, first_keys, first_row):
    scores = mm_t(queries, keys) * HEAD_SIZE ** (-0.5)
    key_index = lax.broadcasted_iota(jnp.int32, scores.shape, 1)
    row_index = first_row + lax.broadcasted_iota(jnp.int32, scores.shape, 0)
    allowed = (key_index >= first_keys) & (key_index <= row_index)
    scores = jnp.where(allowed, scores, MASKED_SCORE)
    powers = jnp.exp(scores - jnp.max(scores, axis=-1, keepdims=True))
    return powers / jnp.sum(powers, axis=-1, keepdims=True)


def block_rows(place, rel, rows):
    return pl.ds(pl.multiple_of(place.chip_at(rel) * 2 * rows, 2 * rows), 2 * rows)


def shard_columns(first, device, count):
    return pl.ds(pl.multiple_of(first + device * count, 128), count)


def layer_forward_step(place, rows, refs, buffers, slot, step, hooks):
    (wh, wm, we, wr), gains_ref, head_gain_ref = refs.weights, refs.gains, refs.head_gain
    current, middle, result, result_b = (
        buffers.current,
        buffers.middle,
        buffers.result,
        buffers.result_b,
    )
    full_a, full_b = buffers.full_a, buffers.full_b
    projected, heads, mixed = buffers.projected, buffers.heads, buffers.mixed
    joined = buffers.joined
    chip_rows, width, hidden_width = 2 * rows, current.shape[1], wr.shape[0]
    save_sem = buffers.save_sem
    tables = [
        pltpu.make_async_copy(src.at[slot], dst, buffers.table_sem.at[at])
        for at, (src, dst) in enumerate(zip(refs.tables, buffers.tables))
    ]
    cosine, sine, first_key = buffers.tables
    for table in tables:
        table.start()

    def save(at, src, dst):
        copy = pltpu.make_async_copy(src, dst.at[slot], save_sem.at[at])
        copy.start()
        return copy

    saves = [save(0, current, refs.inputs)]

    def enter(span):
        values = current[span, :].astype(jnp.float32)
        base = pl.multiple_of(place.index * rows + span.start, 16)
        full_a[pl.ds(base, 16), :] = (
            values * inverse_size(values) * gains_ref[0:1, :]
        ).astype(jnp.bfloat16)

    by_rows(rows, enter)
    for table in tables:
        table.wait()
    gather = Gather(place, full_a, *buffers.gather_a, rows)

    def heads_block(rel):
        span = block_rows(place, rel, rows)
        if rel == 0:
            hooks.heads()
        values = mm(full_a[span, :], wh[...])
        projected[span, :] = values
        for at in range(3):
            columns = pl.ds(at * HEAD_SIZE, HEAD_SIZE)
            one = values[:, at * HEAD_SIZE : (at + 1) * HEAD_SIZE]
            gain = head_gain_ref[0:1, :] if at < 2 else head_gain_ref[1:2, :]
            heads[span, columns] = turn(
                one * inverse_size(one) * gain, cosine[span, :], sine[span, :]
            ).astype(jnp.bfloat16)
        heads[span, 3 * HEAD_SIZE :] = values[:, 3 * HEAD_SIZE :].astype(jnp.bfloat16)

    gather.over_blocks(heads_block)
    hooks.service()
    saves += [
        save(1, full_a, refs.normal_a),
        save(2, projected, refs.projected),
        save(3, heads, refs.heads),
    ]
    scatter = Scatter(place, *buffers.scatter, *buffers.scatter_a, rows)

    def attend_block(rel):
        first_row = place.chip_at(rel) * chip_rows
        span = block_rows(place, rel, rows)
        for at in range(2):
            columns = pl.ds(at * HEAD_SIZE, HEAD_SIZE)
            probs = probabilities(
                heads[span, columns],
                heads[:, 2 * HEAD_SIZE : 3 * HEAD_SIZE],
                first_key[span, :],
                first_row,
            )
            mixed[span, columns] = mm(
                probs.astype(jnp.bfloat16), heads[:, 3 * HEAD_SIZE :]
            ).astype(jnp.bfloat16)
        scatter.put(rel, lambda columns: mm(mixed[span, :], wm[:, columns]), width)

    attend_block(3)
    scatter.pair(3)
    attend_block(2)
    scatter.pair(2)
    attend_block(1)
    scatter.pair(1)
    attend_block(0)
    saves.append(save(4, mixed, refs.mixed))
    scatter.relay()
    scatter.pair(0)

    def residual(span, value):
        values = value + current[span, :].astype(jnp.float32)
        middle[span, :] = values
        base = pl.multiple_of(place.index * rows + span.start, 16)
        full_b[pl.ds(base, 16), :] = (
            values * inverse_size(values) * gains_ref[1:2, :]
        ).astype(jnp.bfloat16)

    scatter.total(residual)
    gather.finish()
    saves.append(save(5, middle, refs.middle))
    for copy in saves[:5]:
        copy.wait()
    gather_b = Gather(place, full_b, *buffers.gather_b, rows)
    scatter_b = Scatter(place, *buffers.scatter, *buffers.scatter_b, rows)
    joined_copies, hidden_copies = {}, []

    def feed_block(rel):
        span = block_rows(place, rel, rows)
        stage = joined.at[rel % 2]
        hidden = buffers.blocks.at[rel // 2, :, pl.ds(rel % 2 * hidden_width, hidden_width)]
        if rel == 0:
            hooks.feed()
        if rel >= 2:
            joined_copies[rel - 2].wait()

        @pl.loop(0, hidden_width // 256)
        def _(at):
            columns = pl.ds(pl.multiple_of(at * 256, 256), 256)
            later = pl.ds(pl.multiple_of(hidden_width + at * 256, 256), 256)
            gate = mm(full_b[span, :], we[:, columns])
            up = mm(full_b[span, :], we[:, later])
            stage[:, columns] = gate
            stage[:, later] = up
            hidden[:, columns] = (gate * jax.nn.sigmoid(gate) * up).astype(jnp.bfloat16)

        copy = pltpu.make_async_copy(
            stage, refs.joined.at[slot, span], save_sem.at[8 + rel % 2]
        )
        copy.start()
        joined_copies[rel] = copy
        copy = pltpu.make_async_copy(
            hidden, refs.hidden.at[slot, span], buffers.hidden_sem.at[rel]
        )
        copy.start()
        hidden_copies.append(copy)
        scatter_b.put(rel, lambda columns: mm(hidden[...], wr[:, columns]), width)
        if rel in (1, 2):
            scatter_b.pair(rel - 1)

    gather_b.over_blocks(feed_block, lambda: scatter_b.pair(2))
    later_saves = [save(6, full_b, refs.normal_b)] + hidden_copies
    scatter_b.pair(3)
    scatter_b.relay()
    hooks.finish()
    saves[5].wait()

    def finish(span, value):
        values = value + middle[span, :]
        result[span, :] = values
        result_b[span, :] = values.astype(jnp.bfloat16)

    scatter_b.total(finish)
    hooks.hand()
    gather_b.finish()
    for copy in later_saves + [joined_copies[2], joined_copies[3]]:
        copy.wait()
    hooks.after()


def feed_back(place, rows, gather, scatter, full, weights, joined, joined_load, out_of, done):
    wm, we, wr = weights
    hidden_width, width = wr.shape

    def feed_block(rel):
        span = block_rows(place, rel, rows)
        stage, out = joined.at[rel % 2], out_of(rel)
        joined_load(rel).wait()

        @pl.loop(0, hidden_width // 256)
        def _(at):
            columns = pl.ds(pl.multiple_of(at * 256, 256), 256)
            later = pl.ds(pl.multiple_of(hidden_width + at * 256, 256), 256)
            grad = mm_t(full[span, :], wr[columns, :])
            gate, up = stage[:, columns], stage[:, later]
            sigmoid = jax.nn.sigmoid(gate)
            unit = gate * sigmoid
            out[:, columns] = (grad * up * (sigmoid + unit * (1.0 - sigmoid))).astype(jnp.bfloat16)
            out[:, later] = (grad * unit).astype(jnp.bfloat16)

        if rel < 2:
            joined_load(rel + 2).start()
        done(rel, out)
        scatter.put(rel, lambda columns: mm_t(out[...], we[columns, :]), width)
        if rel in (1, 2):
            scatter.pair(rel - 1)

    gather.over_blocks(feed_block, lambda: scatter.pair(2))
    scatter.pair(3)


def feed_input_back(place, rows, scatter, middle, gains_ref, out_gains, current, result, full_b):
    out_gains[1:2, :] = jnp.zeros_like(out_gains[1:2, :])

    def feed_norm(span, value):
        back, gain_term = norm_back(middle[span, :], gains_ref[1:2, :], value)
        out_gains[1:2, :] += jnp.sum(gain_term, axis=0, keepdims=True)
        total = back + current[span, :].astype(jnp.float32)
        result[span, :] = total
        base = pl.multiple_of(place.index * rows + span.start, 16)
        full_b[pl.ds(base, 16), :] = total.astype(jnp.bfloat16)

    scatter.total(feed_norm)


def kept_probs(held, joined, at, block, chip_rows):
    rows, seen = chip_rows // 2, (block + 1) * chip_rows
    if at == 0:
        first, columns = ((2, 2 * chip_rows), (2, 0), (0, 4 * chip_rows), (0, 0))[block]
        return held.at[pl.ds(first, 2), pl.ds(0, rows), pl.ds(columns, seen)]
    first, columns = ((1, 3 * chip_rows), (0, 4 * chip_rows), (1, 0), (0, 0))[block]
    return joined.at[first, pl.ds(0, chip_rows), pl.ds(columns, seen)]


def attention_probs(held, joined, heads, first_key, chip_rows):
    for block in range(heads.shape[0] // chip_rows):
        span = pl.ds(block * chip_rows, chip_rows)
        seen = (block + 1) * chip_rows
        keys = heads[:seen, 2 * HEAD_SIZE : 3 * HEAD_SIZE]
        for at in range(2):
            queries = heads[span, pl.ds(at * HEAD_SIZE, HEAD_SIZE)]
            probs = probabilities(queries, keys, first_key[span, :], block * chip_rows)
            kept = kept_probs(held, joined, at, block, chip_rows)
            kept[...] = probs.reshape(kept.shape)


def attention_back(
    held, joined, heads, grad_mixed, grad_queries, grad_keys, grad_values, chip_rows
):
    grad_keys[...] = jnp.zeros_like(grad_keys)
    grad_values[...] = jnp.zeros_like(grad_values)
    for block in range(heads.shape[0] // chip_rows):
        span = pl.ds(block * chip_rows, chip_rows)
        seen = (block + 1) * chip_rows
        keys = heads[:seen, 2 * HEAD_SIZE : 3 * HEAD_SIZE]
        values = heads[:seen, 3 * HEAD_SIZE :]
        for at in range(2):
            columns = pl.ds(at * HEAD_SIZE, HEAD_SIZE)
            queries = heads[span, columns]
            grad = grad_mixed[span, columns]
            probs = kept_probs(held, joined, at, block, chip_rows)[...]
            probs = probs.reshape(chip_rows, seen)
            grad_probs = mm_t(grad, values)
            grad_scores = (
                probs * (grad_probs - jnp.sum(probs * grad_probs, axis=-1, keepdims=True))
            ).astype(jnp.bfloat16)
            grad_queries[span, columns] = mm(grad_scores, keys) * HEAD_SIZE ** (-0.5)
            grad_keys[:seen, :] += t_mm(grad_scores, queries) * HEAD_SIZE ** (-0.5)
            grad_values[:seen, :] += t_mm(probs.astype(jnp.bfloat16), grad)


def project_back(
    place, rows, scatter, buffers, head_gain_ref, out_head_gain, wh
):
    projected, grad_projected = buffers.projected, buffers.grad_projected
    grad_queries, grad_keys, grad_values = buffers.attention_grads
    cosine, sine, _ = buffers.tables
    out_head_gain[...] = jnp.zeros_like(out_head_gain)

    def project_block(rel):
        span = block_rows(place, rel, rows)
        for at in range(3):
            columns = pl.ds(at * HEAD_SIZE, HEAD_SIZE)
            which = 0 if at < 2 else 1
            upstream = grad_queries[span, columns] if at < 2 else grad_keys[span, :]
            back, gain_term = norm_back(
                projected[span, columns],
                head_gain_ref[which : which + 1, :],
                turn_back(upstream, cosine[span, :], sine[span, :]),
            )
            out_head_gain[which : which + 1, :] += jnp.sum(gain_term, axis=0, keepdims=True)
            grad_projected[span, columns] = back.astype(jnp.bfloat16)
        grad_projected[span, 3 * HEAD_SIZE :] = grad_values[span, :].astype(jnp.bfloat16)
        scatter.put(rel, lambda columns: mm_t(grad_projected[span, :], wh[columns, :]), wh.shape[0])

    project_block(3)
    scatter.pair(3)
    project_block(2)
    scatter.pair(2)
    project_block(1)
    scatter.pair(1)
    project_block(0)


def input_back(scatter, inputs, gains_ref, out_gains, result, result_b):
    out_gains[0:1, :] = jnp.zeros_like(out_gains[0:1, :])

    def mixer_norm(span, value):
        back, gain_term = norm_back(inputs[span, :].astype(jnp.float32), gains_ref[0:1, :], value)
        out_gains[0:1, :] += jnp.sum(gain_term, axis=0, keepdims=True)
        total = back + result[span, :]
        result[span, :] = total
        if result_b is not None:
            result_b[span, :] = total.astype(jnp.bfloat16)

    scatter.total(mixer_norm)


def layer_backward_step(place, rows, refs, buffers, slot, hooks):
    (wh, wm, we, wr), gains_ref = refs.weights, refs.gains
    current, middle, result, result_b, inputs = (
        buffers.current,
        buffers.middle,
        buffers.result,
        buffers.result_b,
        buffers.inputs,
    )
    full_a, full_b, joined = buffers.full_a, buffers.full_b, buffers.joined
    save_sem, grad_joined = buffers.save_sem, buffers.grad_joined
    tables = [
        pltpu.make_async_copy(src.at[slot], dst, buffers.table_sem.at[at])
        for at, (src, dst) in enumerate(
            [
                *zip(refs.tables, buffers.tables),
                (refs.middle, middle),
                (refs.projected, buffers.projected),
                (refs.heads, buffers.heads),
                (refs.inputs, inputs),
            ]
        )
    ]
    for table in tables:
        table.start()

    def joined_load(rel):
        return pltpu.make_async_copy(
            refs.joined.at[slot, block_rows(place, rel, rows)],
            joined.at[rel % 2],
            buffers.joined_sem.at[rel % 2],
        )

    joined_load(0).start()
    joined_load(1).start()
    own_rows = pl.ds(pl.multiple_of(place.index * rows, rows), rows)
    full_a[own_rows, :] = current[...]

    def save(at, src, dst):
        copy = pltpu.make_async_copy(src, dst.at[slot], save_sem.at[at])
        copy.start()
        return copy

    gather = Gather(place, full_a, *buffers.gather_a, rows)
    scatter = Scatter(place, *buffers.scatter, *buffers.scatter_a, rows)
    length = full_a.shape[0]

    def out_of(rel):
        first = place.replica * length + place.chip_at(rel) * 2 * rows
        return grad_joined.at[pl.ds(pl.multiple_of(first, 2 * rows), 2 * rows)]

    feed_back(
        place,
        rows,
        gather,
        scatter,
        full_a,
        (wm, we, wr),
        joined,
        joined_load,
        out_of,
        hooks.done,
    )
    upstream_save = save(0, full_a, refs.upstream)
    scatter.relay()
    for table in tables:
        table.wait()
    out_gains = refs.out_gains.at[slot]
    feed_input_back(place, rows, scatter, middle, gains_ref, out_gains, current, result, full_b)
    gather.finish()
    upstream_save.wait()
    for rel in range(4):
        hooks.settled(rel, out_of(rel))
    gather_b = Gather(place, full_b, *buffers.gather_b, rows)
    scatter_b = Scatter(place, *buffers.scatter, *buffers.scatter_b, rows)
    grad_mixed = buffers.mixed

    def mixed_block(rel):
        span = block_rows(place, rel, rows)
        grad_mixed[span, :] = mm_t(full_b[span, :], wm[...]).astype(jnp.bfloat16)

    held, heads = buffers.scatter[0], buffers.heads

    def early(at):
        hooks.early(at)
        if at == 0:
            attention_probs(held, joined, heads, buffers.tables[2], 2 * rows)

    gather_b.over_blocks(mixed_block, early=early)
    middle_save = save(1, full_b, refs.grad_middle)
    attention_back(held, joined, heads, grad_mixed, *buffers.attention_grads, 2 * rows)
    project_back(
        place, rows, scatter_b, buffers, refs.head_gain, refs.out_head_gain.at[slot], wh
    )
    projected_save = save(2, buffers.grad_projected, refs.grad_projected)
    hooks.early(5)
    scatter_b.relay()
    scatter_b.pair(0)
    hooks.early(6)
    hooks.finish()
    input_back(scatter_b, inputs, gains_ref, out_gains, result, result_b)
    hooks.hand()
    gather_b.finish()
    for copy in (middle_save, projected_save):
        copy.wait()
    hooks.after()


class Saved(typing.NamedTuple):
    inputs: typing.Any
    normal_a: typing.Any
    projected: typing.Any
    heads: typing.Any
    mixed: typing.Any
    middle: typing.Any
    normal_b: typing.Any
    joined: typing.Any
    hidden: typing.Any
    upstream: typing.Any
    grad_middle: typing.Any
    grad_projected: typing.Any


class Layers(typing.NamedTuple):
    rows: typing.Any
    saved: Saved
    handed: typing.Any
    own_joined: typing.Any
    other_joined: typing.Any
    first_sum: typing.Any
    other_normal: typing.Any
    other_normal_a: typing.Any
    other_projected: typing.Any
    heads_w: typing.Any
    expand_w: typing.Any
    gains: typing.Any
    head_gain: typing.Any
    gain_terms: typing.Any
    head_terms: typing.Any


class LayerBuffers(typing.NamedTuple):
    current: typing.Any
    inputs: typing.Any
    result: typing.Any
    result_b: typing.Any
    full_a: typing.Any
    full_b: typing.Any
    projected: typing.Any
    heads: typing.Any
    mixed: typing.Any
    joined: typing.Any
    grad_joined: typing.Any
    grad_projected: typing.Any


class GradientBuffers(typing.NamedTuple):
    current: typing.Any
    result: typing.Any
    full_a: typing.Any
    full_b: typing.Any
    projected: typing.Any
    heads: typing.Any
    mixed: typing.Any
    joined: typing.Any


def layers_kernel(rows, *refs):
    refs = list(refs)

    def some(count):
        taken = refs[:count]
        del refs[:count]
        return taken

    own_ref, gain_ref = some(2)
    table_refs = some(3)
    heads_w, merge_w, expand_w, reduce_w = some(4)
    (out_rows,) = some(1)
    saved = types.SimpleNamespace(**Saved(*some(12))._asdict())
    out_handed, own_joined, other_joined, first_sum, other_normal = some(5)
    other_normal_a, other_projected = some(2)
    out_heads_w, out_expand_w = some(2)
    gains_ref, head_gain_ref, out_gains, out_head_gain = some(4)
    all_gains, wh, wm, we, wr, arrived = some(6)
    buffers = types.SimpleNamespace(**LayerBuffers(*some(12))._asdict())
    buffers.middle = buffers.result
    buffers.tables = some(3)
    buffers.attention_grads = some(3)
    buffers.scatter = some(7)
    first_tiles, first_turned, first_stage = some(3)
    buffers.blocks = first_stage
    load_sem, spread_send, spread_recv = some(3)
    share_send, share_recv = some(2)
    tile_sem, first_sem, first_send, first_recv, normal_send, normal_recv = some(6)
    projected_send, projected_recv = some(2)
    buffers.save_sem, buffers.table_sem, buffers.joined_sem, buffers.hidden_sem = some(4)
    hand_send, hand_recv, out_sem = some(3)
    buffers.gather_a, buffers.scatter_a = some(2), some(2)
    buffers.gather_b, buffers.scatter_b = some(2), some(2)
    saved.weights, saved.tables = (wh, wm, we, wr), table_refs
    saved.gains, saved.head_gain = gains_ref, head_gain_ref
    saved.out_gains, saved.out_head_gain = out_gains, out_head_gain
    place = Place()
    head = place.section == 0
    rest = jnp.logical_not(head)
    hidden_width = wr.shape[0]
    depth = heads_w.shape[0]
    query_width, key_width = QUERY_HEADS * HEAD_SIZE, KEY_VALUE_HEADS * HEAD_SIZE
    loads = [
        pltpu.make_async_copy(src, dst, load_sem.at[at])
        for at, (src, dst) in enumerate(((merge_w, wm), (reduce_w, wr)))
    ]
    for load in loads:
        load.start()
    shard_rows = pl.ds(pl.multiple_of(place.index * depth, depth), depth)

    def spread(at, device, piece, src, dst):
        if at < 7:
            return remote(
                src, dst, spread_send.at[piece, at], spread_recv.at[piece, at], {"fsdp": device}
            )
        return pltpu.make_async_copy(src, dst, load_sem.at[2 + piece])

    gain_copies = [
        spread(at, device, 0, gain_ref, all_gains.at[place.index])
        for at, device in place.others()
    ]
    heads_copies, expand_copies = [], []
    for at, device in place.others():
        for piece, first, count, into in (
            (1, 0, MERGED, 0),
            (2, query_width, HEAD_SIZE, MERGED),
            (3, query_width + key_width, HEAD_SIZE, MERGED + HEAD_SIZE),
        ):
            src = heads_w.at[:, shard_columns(first, device, count)]
            heads_copies.append(
                spread(at, device, piece, src, wh.at[shard_rows, pl.ds(into, count)])
            )
        for piece in range(2):
            src = expand_w.at[:, shard_columns(piece * FF, device, hidden_width)]
            dst = we.at[shard_rows, pl.ds(piece * hidden_width, hidden_width)]
            expand_copies.append(spread(at, device, 4 + piece, src, dst))

    def arrive(copies, pieces):
        for copy in copies[:-pieces]:
            copy.wait_recv()
        for copy in copies[-pieces:]:
            copy.wait()

    heads_out = pltpu.make_async_copy(wh, out_heads_w, load_sem.at[8])
    expand_out = pltpu.make_async_copy(we, out_expand_w, load_sem.at[9])

    def share(at, device, kind, weight):
        block = weight.at[pl.ds(pl.multiple_of(device * depth, depth), depth)]
        return remote(
            block, block, share_send.at[kind, at], share_recv.at[kind, at], place.rep_peer
        )

    def start_all(copies, pieces, shared, first=0, last=PLANE):
        for at, device in place.others()[first:last]:
            mine = copies[at * pieces : (at + 1) * pieces]

            def begin():
                for copy in mine:
                    copy.start()

            if at < shared:
                pl.when(place.replica == at % 2)(begin)
            else:
                begin()

    def pass_on(copies, pieces, kind, weight, first, last):
        for at, device in place.others()[first:last]:
            mine = copies[at * pieces : (at + 1) * pieces]

            @pl.when(place.replica == at % 2)
            def _():
                for copy in mine:
                    copy.wait_recv()
                share(at, device, kind, weight).start()

    def take_shared(kind, weight, shared):
        for at, device in place.others()[:shared]:

            @pl.when(place.replica != at % 2)
            def _():
                share(at, device, kind, weight).wait_recv()

    def sent(copies, pieces, kind, weight, shared):
        for at, device in place.others()[:7]:
            mine = copies[at * pieces : (at + 1) * pieces]

            def settle():
                for copy in mine:
                    copy.wait_send()
                if at < shared:
                    share(at, device, kind, weight).wait_send()

            if at < shared:
                pl.when(place.replica == at % 2)(settle)
            else:
                settle()

    place.greet(
        [{"fsdp": device} for _, device in place.others()[:7]]
        + [place.section_peer, place.rep_peer]
    )
    for copy in gain_copies:
        copy.start()
    start_all(heads_copies, 3, 2)

    arrive(gain_copies, 1)
    for shard in range(PLANE):
        part = slice(shard * depth, (shard + 1) * depth)
        gains_ref[0:1, part] = all_gains[shard][:, :depth]
        gains_ref[1:2, part] = all_gains[shard][:, depth : 2 * depth]
    per_row = PLANE // 2
    count = 2 * HEAD_SIZE // PLANE
    for row in range(2):
        head_gain_ref[row : row + 1, :] = jnp.concatenate(
            [
                all_gains[row * per_row + at][:, 2 * depth : 2 * depth + count]
                for at in range(per_row)
            ],
            axis=1,
        )

    current, result, result_b = buffers.current, buffers.result, buffers.result_b
    length = buffers.full_a.shape[0]

    def joined_save(rel, out):
        return pltpu.make_async_copy(
            out, own_joined.at[block_rows(place, rel, rows)], first_sem.at[rel]
        )

    def joined_copy(rel, out):
        return remote(
            out,
            other_joined.at[block_rows(place, rel, rows)],
            first_send.at[rel],
            first_recv.at[rel],
            place.rep_peer,
        )

    def saved_block(rel):
        return own_joined.at[block_rows(place, rel, rows)]

    half = length // 2
    half_rows = pl.ds(pl.multiple_of(place.core * half, half), half)

    def normal_copy(slot, kind=0):
        src, dst = ((saved.normal_b, other_normal), (saved.normal_a, other_normal_a))[kind]
        return remote(
            src.at[slot, half_rows],
            dst.at[slot, half_rows],
            normal_send.at[kind, slot],
            normal_recv.at[kind, slot],
            place.rep_peer,
        )

    def normal_pass(slot, kind=0):
        block = (other_normal, other_normal_a)[kind].at[slot, half_rows]
        return remote(
            block,
            block,
            normal_send.at[kind, 2 + slot],
            normal_recv.at[kind, 2 + slot],
            place.core_peer,
        )

    projected_copy = remote(
        saved.grad_projected.at[0],
        other_projected,
        projected_send.at[0],
        projected_recv.at[0],
        place.rep_peer,
    )

    def token_rows(replica):
        return pl.ds(pl.multiple_of(replica * length, length), length)

    def first_loads(at):
        columns = pl.ds(pl.multiple_of(at * depth, depth), depth)
        parts = (
            (saved.normal_b.at[0, :, columns], place.replica),
            (other_normal.at[0, :, columns], 1 - place.replica),
        )
        into = lax.rem(at, 2)
        return [
            pltpu.make_async_copy(
                src, first_tiles.at[into, token_rows(replica)], tile_sem.at[into, part]
            )
            for part, (src, replica) in enumerate(parts)
        ]

    def first_save(at):
        rows_at = pl.ds(pl.multiple_of(at * depth, depth), depth)
        return pltpu.make_async_copy(
            first_stage.at[lax.rem(at, 2)], first_sum.at[rows_at], first_sem.at[lax.rem(at, 2)]
        )

    def whole_load(part):
        src, replica = ((own_joined, place.replica), (other_joined, 1 - place.replica))[part]
        return pltpu.make_async_copy(
            src, buffers.grad_joined.at[token_rows(replica)], first_sem.at[2 + part]
        )

    def first_begin():
        normal_copy(0).wait_recv()
        normal_pass(0).start()
        for rel in range(4):
            joined_copy(rel, saved_block(rel)).wait()
        for part in range(2):
            whole_load(part).start()
        normal_pass(0).wait_recv()
        for at in range(2):
            for copy in first_loads(jnp.int32(at)):
                copy.start()

    def first_turn():
        for part in range(2):
            whole_load(part).wait()
        for copy in first_loads(jnp.int32(0)):
            copy.wait()
        turn_tile(first_tiles.at[0], first_turned.at[0], 0, 2 * length // 256)
        for copy in first_loads(jnp.int32(2)):
            copy.start()

    def first_job(at):
        into, later = lax.rem(at, 2), lax.rem(at + 1, 2)

        @pl.when(at + 1 < PLANE)
        def _():
            for copy in first_loads(at + 1):
                copy.wait()

        @pl.when(at >= 2)
        def _():
            first_save(at - 2).wait()

        def product(columns):
            first_stage[into, :, columns] = mm(
                first_turned[into], buffers.grad_joined[:, columns]
            ).astype(jnp.bfloat16)

        product_and_turn(
            2 * hidden_width, product, first_tiles.at[later], first_turned.at[later]
        )
        first_save(at).start()

        @pl.when(at + 3 < PLANE)
        def _():
            for copy in first_loads(at + 3):
                copy.start()

    def first_jobs(first, last):
        @pl.loop(first, last)
        def _(at):
            first_job(at)

    def first_end():
        for at in (PLANE - 2, PLANE - 1):
            first_save(jnp.int32(at)).wait()

    def hand(slot):
        return remote(
            result_b, arrived.at[slot], hand_send.at[slot], hand_recv.at[slot], place.section_peer
        )

    def rows_copy(slot):
        return pltpu.make_async_copy(result, out_rows.at[slot], out_sem.at[0])

    def save_rows(slot):
        copy = rows_copy(slot)
        copy.start()
        copy.wait()

    def heads_ready():
        pass_on(heads_copies, 3, 0, wh, 0, 2)
        arrive(heads_copies[6:], 3)
        take_shared(0, wh, 2)
        heads_out.start()
        start_all(expand_copies, 2, 2, 0, 2)

    def expand_service():
        pass_on(expand_copies, 2, 1, we, 0, 2)
        start_all(expand_copies, 2, 2, 2)

    def feed_ready():
        arrive(expand_copies[4:], 2)
        take_shared(1, we, 2)
        expand_out.start()

    @pl.when(rest)
    def _():
        heads_ready()
        expand_service()
        feed_ready()

    for load in loads:
        load.wait()

    @pl.loop(0, 5)
    def _(step):
        forward = (head & (step <= 1)) | (rest & ((step == 1) | (step == 3)))
        backward = (step == 4) | (rest & (step == 2))

        @pl.when(forward)
        def _():
            slot = jnp.where(head, step, lax.div(step - 1, 2))

            @pl.when(head)
            def _():
                current[...] = own_ref[slot]

            @pl.when(rest)
            def _():
                hand(slot).wait_recv()
                current[...] = arrived[slot]

            def first(body):
                return lambda: pl.when(head & (slot == 0))(body)


            def finish():
                @pl.when(slot == 1)
                def _():
                    hand(0).wait_send()

            def handing():
                @pl.when(head)
                def _():
                    hand(slot).start()

                @pl.when(rest)
                def _():
                    save_rows(slot)

            def after():
                normal_copy(slot).start()
                normal_copy(slot, 1).start()

            layer_forward_step(
                place,
                rows,
                saved,
                buffers,
                slot,
                step,
                types.SimpleNamespace(
                    heads=first(heads_ready),
                    feed=first(feed_ready),
                    service=first(expand_service),
                    finish=finish,
                    hand=handing,
                    after=after,
                ),
            )

        @pl.when(backward)
        def _():
            slot = jnp.where(head, 0, lax.div(step - 2, 2))

            @pl.when(head)
            def _():
                hand(0).wait_recv()
                current[...] = arrived[0]

            @pl.when(rest)
            def _():
                current[...] = own_ref[slot]

            def finish():
                @pl.when(head)
                def _():
                    hand(1).wait_send()

            def handing():
                @pl.when(rest)
                def _():
                    hand(slot).start()

                @pl.when(rest & (slot == 0))
                def _():
                    for rel in range(4):
                        joined_copy(rel, saved_block(rel)).start()

                @pl.when(head)
                def _():
                    rows_copy(slot).start()

            def done(rel, out):
                @pl.when(slot == 0)
                def _():
                    joined_save(rel, out).start()

                @pl.when(head)
                def _():
                    joined_copy(rel, out).start()

            def settled(rel, out):
                pl.when(slot == 0)(lambda: joined_save(rel, out).wait())

            def early(at):
                @pl.when(rest & (slot == 1))
                def _():
                    if at == 0:
                        first_begin()
                    elif at == 2:
                        first_turn()
                    elif at == 3:
                        first_jobs(0, 2)
                    elif at == 6:
                        first_jobs(2, 5)

            def after():
                pl.when(slot == 0)(projected_copy.start)

            hooks = types.SimpleNamespace(
                finish=finish,
                hand=handing,
                done=done,
                settled=settled,
                early=early,
                after=after,
            )
            layer_backward_step(place, rows, saved, buffers, slot, hooks)

    @pl.when(head)
    def _():
        first_begin()
        first_turn()
        first_jobs(0, 5)

    first_jobs(5, PLANE)

    first_end()
    normal_copy(1).wait_recv()
    normal_pass(1).start()
    for slot in range(2):
        normal_copy(slot, 1).wait_recv()
        normal_pass(slot, 1).start()

    @pl.when(head)
    def _():
        hand(1).wait_recv()
        current[...] = arrived[1]

    @pl.when(rest)
    def _():
        hand(1).wait_send()
        current[...] = own_ref[1]

    handed = pltpu.make_async_copy(current, out_handed, out_sem.at[1])
    handed.start()
    normal_pass(1).wait_recv()
    for slot in range(2):
        normal_pass(slot, 1).wait_recv()
    projected_copy.wait()
    heads_out.wait()
    expand_out.wait()
    for copy in gain_copies[:7]:
        copy.wait_send()
    sent(heads_copies, 3, 0, wh, 2)
    sent(expand_copies, 2, 1, we, 2)
    for slot in range(2):
        for kind in range(2):
            normal_copy(slot, kind).wait_send()
            normal_pass(slot, kind).wait_send()
    handed.wait()
    pl.when(head)(lambda: rows_copy(0).wait())


def gradient_kernel(rows, *refs):
    refs = list(refs)

    def some(count):
        taken = refs[:count]
        del refs[:count]
        return taken

    gains_ref, head_gain_ref, first_gains, first_head_gain = some(4)
    table_refs = some(3)
    heads_w, merge_w, expand_w, reduce_w = some(4)
    in_handed, in_inputs, in_projected, in_heads, in_middle, in_joined = some(6)
    hidden_all, upstream_all, normal_b_all, other_normal = some(4)
    mixed_all, grad_middle_all, normal_a_all, other_normal_a = some(4)
    grad_projected_all, other_projected, first_sum, out_result = some(4)
    own_heads, own_merge, other_merge = some(3)
    own_expand, own_reduce, other_reduce = some(3)
    (out_gain,) = some(1)
    wh, wm, we, wr = some(4)
    buffers = types.SimpleNamespace(**GradientBuffers(*some(8))._asdict())
    buffers.tables = some(3)
    buffers.attention_grads = some(3)
    buffers.scatter = some(7)
    tiles, turned, wide, narrow, first_projected, last_projected = some(6)
    gains, head_gain, gain_out, gain_in, gain_sum, gain_other = some(6)
    load_sem, tile_sem, joined_sem, save_sem = some(4)
    buffers.gather_a, buffers.scatter_a = some(2), some(2)
    buffers.gather_b, buffers.scatter_b = some(2), some(2)
    spread_send, spread_recv, rep_send, rep_recv = some(4)
    current, result = buffers.current, buffers.result
    full_a, full_b, grad_mixed = buffers.full_a, buffers.full_b, buffers.mixed
    joined = buffers.joined

    place = Place()
    length, width = full_a.shape
    depth = wm.shape[0]
    hidden_width = wr.shape[0]
    last = in_inputs.shape[0] - 1
    tokens = narrow.shape[0]
    query_width, key_width = QUERY_HEADS * HEAD_SIZE, KEY_VALUE_HEADS * HEAD_SIZE
    others = place.others()

    def load(at, src, dst):
        copy = pltpu.make_async_copy(src, dst, load_sem.at[at])
        copy.start()
        return copy

    upstream_load = load(0, in_handed, current)
    reduce_load = load(1, reduce_w, wr)

    def joined_load(rel):
        return pltpu.make_async_copy(
            in_joined.at[last, block_rows(place, rel, rows)],
            joined.at[rel % 2],
            joined_sem.at[rel % 2],
        )

    joined_load(0).start()
    joined_load(1).start()
    expand_load = load(2, expand_w, we)
    middle_load = load(3, in_middle.at[last], result)
    wide_load = load(4, upstream_all.at[0], wide)
    def token_rows(replica):
        return pl.ds(pl.multiple_of(replica * length, length), length)

    buffers.grad_projected = last_projected.at[token_rows(place.replica)]
    jobs = [((hidden_all, None), at) for at in range(hidden_width // depth)]
    pair = (normal_b_all.at[last], other_normal.at[last])
    jobs += [(pair, device) for _, device in others]
    jobs += [((mixed_all, None), 0)]
    for slot in (0, last):
        pair = (normal_a_all.at[slot], other_normal_a.at[slot])
        jobs += [(pair, device) for _, device in others]
    job_count = len(jobs)

    def tile_loads(job):
        (mine, theirs), at = jobs[job]
        columns = pl.ds(pl.multiple_of(at * depth, depth), depth)
        if theirs is None:
            return [
                pltpu.make_async_copy(
                    mine.at[:, columns], tiles.at[job % 2], tile_sem.at[job % 2, 0]
                )
            ]
        parts = ((mine, place.replica), (theirs, 1 - place.replica))
        return [
            pltpu.make_async_copy(
                src.at[:, columns],
                tiles.at[job % 2, token_rows(replica)],
                tile_sem.at[job % 2, part],
            )
            for part, (src, replica) in enumerate(parts)
        ]

    def tile_start(job):
        for copy in tile_loads(job):
            copy.start()

    def run_job(job, width, product):
        now, later = turned.at[job % 2], (job + 1) % 2
        if job + 1 < job_count:
            for copy in tile_loads(job + 1):
                copy.wait()
        product_and_turn(
            width, lambda columns: product(now, columns), tiles.at[later], turned.at[later]
        )
        if job + 3 < job_count:
            tile_start(job + 3)

    tile_start(0)
    tile_start(1)
    projected_loads = [
        load(
            at, src, first_projected.at[token_rows(replica)]
        )
        for at, (src, replica) in (
            (5, (grad_projected_all.at[0], place.replica)),
            (16, (other_projected, 1 - place.replica)),
        )
    ]
    loads = [
        load(at + 6, src, dst)
        for at, (src, dst) in enumerate(
            [(merge_w, wm), (heads_w, wh)]
            + [(src.at[last], dst) for src, dst in zip(table_refs, buffers.tables)]
            + [
                (in_projected.at[last], buffers.projected),
                (in_heads.at[last], buffers.heads),
            ]
        )
    ]
    place.greet([{"fsdp": device} for _, device in others[:7]] + [place.rep_peer])

    def rep_copy(at, src, dst):
        return remote(src, dst, rep_send.at[at], rep_recv.at[at], place.rep_peer)

    def spread(at, device, piece, src, dst):
        if at < 7:
            return remote(
                src, dst, spread_send.at[piece, at], spread_recv.at[piece, at], {"fsdp": device}
            )
        return pltpu.make_async_copy(src, dst, save_sem.at[4 + piece])

    upstream_load.wait()
    own_rows = pl.ds(pl.multiple_of(place.index * rows, rows), rows)
    full_a[own_rows, :] = current[...]
    gather = Gather(place, full_a, *buffers.gather_a, rows)
    scatter = Scatter(place, *buffers.scatter, *buffers.scatter_a, rows)

    joined_reps = []

    def out_of(rel):
        if rel == 0:
            reduce_load.wait()
            expand_load.wait()
        first = place.replica * length + place.chip_at(rel) * 2 * rows
        return narrow.at[pl.ds(pl.multiple_of(first, 2 * rows), 2 * rows)]

    def done(rel, out):
        copy = rep_copy(4 + rel, out, out)
        copy.start()
        joined_reps.append(copy)

    feed_back(
        place,
        rows,
        gather,
        scatter,
        full_a,
        (wm, we, wr),
        joined,
        joined_load,
        out_of,
        done,
    )
    wide_load.wait()
    for copy in tile_loads(0):
        copy.wait()
    turn_tile(tiles.at[0], turned.at[0], 0, tokens // 256)
    tile_start(2)
    own_saves, rep_copies = [], []
    for at in range(hidden_width // depth):
        span = pl.ds(at * depth, depth)

        def product(tile, columns):
            value = mm(tile[:, :length], wide[:, columns])
            value += mm(tile[:, length:], full_a[:, columns])
            wr[span, columns] = value.astype(jnp.bfloat16)

        run_job(at, width, product)
        rep_copies.append(rep_copy(at, wr.at[span], other_reduce.at[span]))
        if at == 0:
            rep_copies[at].start()
        copy = pltpu.make_async_copy(wr.at[span], own_reduce.at[span], save_sem.at[at])
        copy.start()
        own_saves.append(copy)
        if at == 1:
            scatter.relay()
    middle_load.wait()
    feed_input_back(place, rows, scatter, result, gains_ref, gains, current, result, full_b)
    inputs_load = load(13, in_inputs.at[last], current)
    gather.finish()
    gather_b = Gather(place, full_b, *buffers.gather_b, rows)
    scatter_b = Scatter(place, *buffers.scatter, *buffers.scatter_b, rows)
    gather_b.start()
    for copy in loads:
        copy.wait()
    held = buffers.scatter[0]
    attention_probs(held, joined, buffers.heads, buffers.tables[2], 2 * rows)
    gather_b.relay()
    gather_b.near()
    gather_b.far()
    for rel, at in ((0, 4), (1, 7), (2, 8), (3, 9)):
        gather_b.wait(at)
        span = block_rows(place, rel, rows)
        grad_mixed[span, :] = mm_t(full_b[span, :], wm[...]).astype(jnp.bfloat16)
    attention_back(
        held, joined, buffers.heads, grad_mixed, *buffers.attention_grads, 2 * rows
    )
    project_back(place, rows, scatter_b, buffers, head_gain_ref, head_gain, wh)
    projected_rep = rep_copy(8, buffers.grad_projected, buffers.grad_projected)
    projected_rep.start()
    job = hidden_width // depth

    def first_load(at, device):
        block = pl.ds(pl.multiple_of(device * depth, depth), depth)
        into = wide.at[pl.ds(at % 2 * depth, depth), pl.ds(0, 2 * hidden_width)]
        return pltpu.make_async_copy(first_sum.at[block], into, load_sem.at[14 + at % 2])

    for at, device in others[:2]:
        first_load(at, device).start()
    for copy in joined_reps:
        copy.wait_recv()
    expand_copies = []
    for at, device in others:
        block = pl.ds(at * depth, depth)
        first_load(at, device).wait()
        before = pl.ds(at % 2 * depth, depth)

        def product(tile, columns):
            value = wide[before, columns].astype(jnp.float32)
            value += mm(tile[...], narrow[:, columns])
            we[block, columns] = value.astype(jnp.bfloat16)

        run_job(job, narrow.shape[1], product)
        job += 1
        if at + 2 < PLANE:
            first_load(*others[at + 2]).start()
        for piece in range(2):
            copy = spread(
                at,
                device,
                piece,
                we.at[block, pl.ds(piece * hidden_width, hidden_width)],
                own_expand.at[:, shard_columns(piece * FF, place.index, hidden_width)],
            )
            copy.start()
            expand_copies.append(copy)
    grad_middle_load = load(4, grad_middle_all.at[0], wide)
    rep_copies[1].start()
    grad_middle_load.wait()

    def merge_product(tile, columns):
        value = mm(tile[:, :length], wide[:, columns])
        value += mm(tile[:, length:], full_b[:, columns])
        wm[:, columns] = value.astype(jnp.bfloat16)

    run_job(job, width, merge_product)
    job += 1
    rep_copies[2].start()
    merge_rep = rep_copy(3, wm, other_merge)
    merge_rep.start()
    merge_save = pltpu.make_async_copy(wm, own_merge, save_sem.at[3])
    merge_save.start()
    for copy in projected_loads:
        copy.wait()
    for at, device in others:
        block = pl.ds(at * depth, depth)

        def product(tile, columns):
            wh[block, columns] = mm(tile[...], first_projected[:, columns]).astype(jnp.bfloat16)

        run_job(job, JOINT, product)
        job += 1
    projected_rep.wait_recv()
    heads_copies = []
    for at, device in others:
        block = pl.ds(at * depth, depth)

        def product(tile, columns):
            value = wh[block, columns].astype(jnp.float32)
            value += mm(tile[...], last_projected[:, columns])
            wh[block, columns] = value.astype(jnp.bfloat16)

        run_job(job, JOINT, product)
        job += 1
        for piece, first, count, start in (
            (2, 0, MERGED, 0),
            (3, query_width, HEAD_SIZE, MERGED),
            (4, query_width + key_width, HEAD_SIZE, MERGED + HEAD_SIZE),
        ):
            copy = spread(
                at,
                device,
                piece,
                wh.at[block, pl.ds(start, count)],
                own_heads.at[:, shard_columns(first, place.index, count)],
            )
            copy.start()
            heads_copies.append(copy)
    scatter_b.relay()
    scatter_b.pair(0)
    inputs_load.wait()
    input_back(scatter_b, current, gains_ref, gains, result, None)
    result_save = pltpu.make_async_copy(result, out_result, save_sem.at[10])
    result_save.start()

    gain_copies = []
    gains[...] += first_gains[0]
    head_gain[...] += first_head_gain[0]
    per_row = PLANE // 2
    count = 2 * HEAD_SIZE // PLANE
    for shard in range(PLANE):
        part = slice(shard * depth, (shard + 1) * depth)
        lanes = slice(shard % per_row * count, (shard % per_row + 1) * count)
        row = shard // per_row
        gain_out[shard] = jnp.zeros_like(gain_out[shard])
        gain_out[shard, :, :depth] = gains[0:1, part]
        gain_out[shard, :, depth : 2 * depth] = gains[1:2, part]
        gain_out[shard, :, 2 * depth : 2 * depth + count] = head_gain[row : row + 1, lanes]
    for at, device in others:
        copy = spread(at, device, 5, gain_out.at[device], gain_in.at[place.index])
        copy.start()
        gain_copies.append(copy)

    for copy in gain_copies[:7]:
        copy.wait_recv()
    gain_copies[7].wait()
    total = gain_in[0]
    for shard in range(1, PLANE):
        total += gain_in[shard]
    gain_sum[...] = total
    gain_rep = rep_copy(9, gain_sum, gain_other)
    gain_rep.start()
    for copy in heads_copies[:21]:
        copy.wait_recv()
    for copy in heads_copies[21:]:
        copy.wait()
    gain_rep.wait()
    out_gain[...] = gain_sum[...] + gain_other[...]
    gather_b.finish()
    for copy in expand_copies[:14]:
        copy.wait_recv()
    for copy in expand_copies[14:] + own_saves + [result_save, merge_save]:
        copy.wait()
    for copy in expand_copies[:14] + heads_copies[:21] + gain_copies[:7] + joined_reps:
        copy.wait_send()
    projected_rep.wait_send()
    for copy in rep_copies + [merge_rep]:
        copy.wait()


def sems(*counts):
    return [pltpu.SemaphoreType.DMA((count,)) for count in counts]


def vmem(*shapes):
    return [pltpu.VMEM(shape, dtype) for *shape, dtype in shapes]


def any_specs(count):
    return [pl.BlockSpec(memory_space=pl.ANY)] * count


def vmem_specs(count):
    return [pl.BlockSpec(memory_space=pltpu.VMEM)] * count


def kernel_params(collective_id):
    return pltpu.CompilerParams(
        collective_id=collective_id, has_side_effects=True, vmem_limit_bytes=VMEM_BYTES
    )


def weight_buffers(width, hidden_width):
    b16 = jnp.bfloat16
    return vmem(
        (width, JOINT, b16),
        (MERGED, width, b16),
        (width, 2 * hidden_width, b16),
        (hidden_width, width, b16),
    )


def table_buffers(length):
    return vmem(
        (length, HEAD_SIZE, jnp.float32),
        (length, HEAD_SIZE, jnp.float32),
        (length, 1, jnp.int32),
    )


def attention_buffers(length):
    return vmem(
        (length, MERGED, jnp.float32),
        (length, HEAD_SIZE, jnp.float32),
        (length, HEAD_SIZE, jnp.float32),
    )


def scatter_buffers(rows, width):
    half, b16 = rows // 2, jnp.bfloat16
    return vmem(
        (4, rows, width, jnp.float32),
        (4, rows, width, b16),
        (4, rows, width, b16),
        *(((3, half, width, b16),) * 4),
    )


def run_layers(own, gain_row, tables, weights):
    micro, rows, width = own.shape
    length = tables[0].shape[1]
    hidden_width, depth = weights[3].shape[0], weights[0].shape[0]
    f32, b16 = jnp.float32, jnp.bfloat16
    shape = jax.ShapeDtypeStruct
    stashes = (
        (rows, width, b16),
        (length, width, b16),
        (length, JOINT, f32),
        (length, JOINT, b16),
        (length, MERGED, b16),
        (rows, width, f32),
        (length, width, b16),
        (length, 2 * hidden_width, f32),
        (length, hidden_width, b16),
        (length, width, b16),
        (length, width, b16),
        (length, JOINT, b16),
    )
    out = pl.pallas_call(
        functools.partial(layers_kernel, rows),
        out_shape=(
            shape((micro, rows, width), f32),
            *(shape((micro, *size), dtype) for *size, dtype in stashes),
            shape((rows, width), b16),
            shape((length, 2 * hidden_width), b16),
            shape((length, 2 * hidden_width), b16),
            shape((width, 2 * hidden_width), b16),
            shape((micro, length, width), b16),
            shape((micro, length, width), b16),
            shape((length, JOINT), b16),
            shape((width, JOINT), b16),
            shape((width, 2 * hidden_width), b16),
            shape((2, width), f32),
            shape((2, HEAD_SIZE), f32),
            shape((micro, 2, width), f32),
            shape((micro, 2, HEAD_SIZE), f32),
        ),
        in_specs=vmem_specs(2) + any_specs(7),
        out_specs=any_specs(22) + vmem_specs(4),
        scratch_shapes=vmem((PLANE, *gain_row.shape, f32))
        + weight_buffers(width, hidden_width)
        + vmem(
            (micro, rows, width, b16),
            (rows, width, b16),
            (rows, width, b16),
            (rows, width, f32),
            (rows, width, b16),
            (length, width, b16),
            (length, width, b16),
            (length, JOINT, f32),
            (length, JOINT, b16),
            (length, MERGED, b16),
            (2, 2 * rows, 2 * hidden_width, f32),
            (2 * length, 2 * hidden_width, b16),
            (length, JOINT, b16),
        )
        + table_buffers(length)
        + attention_buffers(length)
        + scatter_buffers(rows, width)
        + vmem(
            (2, 2 * length, depth, b16),
            (2, depth, 2 * length, b16),
            (2, depth, 2 * hidden_width, b16),
        )
        + sems(10)
        + [pltpu.SemaphoreType.DMA((6, PLANE - 1))] * 2
        + [pltpu.SemaphoreType.DMA((2, 2))] * 2
        + [pltpu.SemaphoreType.DMA((2, 2))]
        + sems(4, 4, 4)
        + [pltpu.SemaphoreType.DMA((2, 4))] * 2
        + sems(1, 1)
        + sems(10, 7, 2, 4, micro, micro, 2, *((10,) * 8)),
        compiler_params=kernel_params(1),
    )(own, gain_row, *tables, *weights)
    return Layers(out[0], Saved(*out[1:13]), *out[13:])


def run_gradients(layers, tables, merge_w, reduce_w):
    saved = layers.saved
    micro, rows, width = saved.inputs.shape
    length = tables[0].shape[1]
    hidden_width, depth = reduce_w.shape[0], merge_w.shape[0]
    f32, b16 = jnp.float32, jnp.bfloat16
    shape = jax.ShapeDtypeStruct
    heads_term, merge_term = (depth, PLANE * JOINT), (depth, width)
    expand_term, reduce_term = (depth, 2 * FF), (hidden_width, width)
    terms = (heads_term,) + (merge_term,) * 2 + (expand_term,) + (reduce_term,) * 2
    gain_width = -(-(2 * depth + 2 * HEAD_SIZE // PLANE) // 128) * 128

    def flat(array):
        return array.reshape(micro * length, -1)

    return pl.pallas_call(
        functools.partial(gradient_kernel, rows),
        out_shape=(shape((rows, width), f32),)
        + tuple(shape(term, b16) for term in terms)
        + (shape((1, gain_width), f32),),
        in_specs=vmem_specs(4) + any_specs(24),
        out_specs=any_specs(7) + vmem_specs(1),
        scratch_shapes=weight_buffers(width, hidden_width)
        + vmem(
            (rows, width, b16),
            (rows, width, f32),
            (length, width, b16),
            (length, width, b16),
            (length, JOINT, f32),
            (length, JOINT, b16),
            (length, MERGED, b16),
            (2, 2 * rows, 2 * hidden_width, f32),
        )
        + table_buffers(length)
        + attention_buffers(length)
        + scatter_buffers(rows, width)
        + vmem(
            (2, micro * length, depth, b16),
            (2, depth, micro * length, b16),
            (length, width, b16),
            (2 * length, 2 * hidden_width, b16),
            (2 * length, JOINT, b16),
            (2 * length, JOINT, b16),
            (2, width, f32),
            (2, HEAD_SIZE, f32),
            (PLANE, 1, gain_width, f32),
            (PLANE, 1, gain_width, f32),
            (1, gain_width, f32),
            (1, gain_width, f32),
        )
        + sems(18)
        + [pltpu.SemaphoreType.DMA((2, 2))]
        + sems(2, 11, *((10,) * 8))
        + [pltpu.SemaphoreType.DMA((6, PLANE - 1))] * 2
        + sems(10, 10),
        compiler_params=kernel_params(2),
    )(
        layers.gains,
        layers.head_gain,
        layers.gain_terms,
        layers.head_terms,
        *tables,
        layers.heads_w,
        merge_w,
        layers.expand_w,
        reduce_w,
        layers.handed,
        saved.inputs,
        saved.projected,
        saved.heads,
        saved.middle,
        saved.joined,
        flat(saved.hidden),
        saved.upstream,
        saved.normal_b,
        layers.other_normal,
        flat(saved.mixed),
        saved.grad_middle,
        saved.normal_a,
        layers.other_normal_a,
        saved.grad_projected,
        layers.other_projected,
        layers.first_sum,
    )


def position_tables(lengths, length):
    document_index, positions = places(lengths, length)
    half_width = HEAD_SIZE // 2
    frequency = jnp.exp(
        jnp.arange(half_width, dtype=jnp.float32) * (-2.0 * math.log(ROPE_BASE) / HEAD_SIZE)
    )
    angles = positions.astype(jnp.float32)[:, None] * frequency[None, :]
    cosine, sine = jnp.cos(angles), jnp.sin(angles)
    first_key = jnp.arange(length, dtype=jnp.int32) - positions
    return (
        jnp.concatenate([cosine, cosine], axis=-1),
        jnp.concatenate([-sine, sine], axis=-1),
        first_key[:, None],
    )


def tensor_parallel_body(
    section_inputs,
    doc_lengths,
    mixer_gain,
    heads_weight,
    merge_weight,
    head_gain,
    feed_gain,
    expand_weight,
    reduce_weight,
):
    shards = lax.axis_size("fsdp")
    own = section_inputs[0, :, 0]
    micro, rows, width = own.shape
    length = rows * shards
    depth = heads_weight.shape[1]
    hidden_width = reduce_weight.shape[1]
    query_width = QUERY_HEADS * HEAD_SIZE

    gain_row = jnp.concatenate([mixer_gain[0], feed_gain[0], head_gain[0]]).astype(jnp.float32)
    gain_row = jnp.pad(gain_row, (0, -gain_row.shape[0] % 128))[None]
    tables = [position_tables(doc_lengths[at, 0], length) for at in range(micro)]
    cosine, sine, first_key = (jnp.stack(entry) for entry in zip(*tables))

    table_rows = (cosine, sine, first_key)
    layers = run_layers(
        own,
        gain_row,
        table_rows,
        (heads_weight[0], merge_weight[0], expand_weight[0], reduce_weight[0]),
    )
    last_rows, *terms, gain_sums = run_gradients(
        layers, table_rows, merge_weight[0], reduce_weight[0]
    )
    own_heads, own_merge, other_merge, own_expand, own_reduce, other_reduce = terms
    grad_heads = own_heads.astype(jnp.float32)[None]
    grad_expand = own_expand.astype(jnp.float32)[None]
    grad_merge, grad_reduce = (
        (mine.astype(jnp.float32) + theirs.astype(jnp.float32))[None]
        for mine, theirs in ((own_merge, other_merge), (own_reduce, other_reduce))
    )
    head_count = head_gain.shape[1]
    head = lax.axis_index("section") == 0
    last_rows = jnp.where(head, last_rows, layers.rows[-1])
    return (
        jnp.concatenate([layers.rows[:-1], last_rows[None]])[None, :, None],
        gain_sums[:, :depth],
        grad_heads,
        grad_merge,
        gain_sums[:, 2 * depth : 2 * depth + head_count],
        gain_sums[:, depth : 2 * depth],
        grad_expand,
        grad_reduce,
    )


def solution(mesh):
    plane = mesh.shape["fsdp"] == PLANE
    return jax.shard_map(
        tensor_parallel_body if plane else body,
        mesh=mesh,
        in_specs=(
            P("section", None, "rep", "fsdp", None),
            P(None, "rep", None),
            P("section", "fsdp"),
            P("section", "fsdp", None),
            P("section", "fsdp", None),
            P("section", "fsdp"),
            P("section", "fsdp"),
            P("section", "fsdp", None),
            P("section", "fsdp", None),
        ),
        out_specs=(
            P("section", None, "rep", "fsdp", None),
            P("section", "fsdp"),
            P("section", "fsdp", None),
            P("section", "fsdp", None),
            P("section", "fsdp"),
            P("section", "fsdp"),
            P("section", "fsdp", None),
            P("section", "fsdp", None),
        ),
        check_vma=False,
    )
```

```python
import functools
import math
import types
import typing

import jax
import jax.numpy as jnp
from jax import lax
from jax.experimental import pallas as pl
from jax.experimental.pallas import tpu as pltpu
from jax.sharding import PartitionSpec as P

FF = 6144
QUERY_HEADS = 16
KEY_VALUE_HEADS = 8
HEAD_SIZE = 128


NORM_EPS = 1e-06
ROPE_BASE = 1000000.0
MASKED_SCORE = -1e30
PLANE = 8


def from_behind(array, axis, by):
    count = lax.axis_size(axis)
    pairs = [(i, i + by) for i in range(count) if 0 <= i + by < count]
    return lax.ppermute(array, axis, pairs)


def normed(values):
    return values * lax.rsqrt(jnp.mean(values * values, axis=-1, keepdims=True) + NORM_EPS)


def scaled(values, gain_row):
    return normed(values) * gain_row


def rotate(values, positions):
    half_width = values.shape[-1] // 2
    frequency = jnp.exp(
        jnp.arange(half_width, dtype=jnp.float32) * (-2.0 * math.log(ROPE_BASE) / values.shape[-1])
    )
    angles = positions.astype(jnp.float32)[:, None] * frequency[None, :]
    cosine = jnp.cos(angles)[:, None, :]
    sine_part = jnp.sin(angles)[:, None, :]
    lower_half = values[..., :half_width]
    upper_half = values[..., half_width:]
    return jnp.concatenate(
        [
            lower_half * cosine - upper_half * sine_part,
            upper_half * cosine + lower_half * sine_part,
        ],
        axis=-1,
    )


def places(doc_lengths, sequence_length):
    doc_ends = jnp.cumsum(doc_lengths)
    token_index = jnp.arange(sequence_length, dtype=jnp.int32)
    passed_ends = (token_index[:, None] >= doc_ends[None, :]).astype(jnp.int32)
    document_index = jnp.sum(passed_ends, axis=1)
    doc_start = jnp.sum(passed_ends * doc_lengths[None, :], axis=1)
    return (document_index, token_index - doc_start)


def heads_of(projected_output, head_gain, positions):
    count_of_tokens = projected_output.shape[0]
    query_rows = projected_output[:, : QUERY_HEADS * HEAD_SIZE].reshape(
        count_of_tokens, QUERY_HEADS, HEAD_SIZE
    )
    heads_of_keys = projected_output[
        :, QUERY_HEADS * HEAD_SIZE : (QUERY_HEADS + KEY_VALUE_HEADS) * HEAD_SIZE
    ].reshape(count_of_tokens, KEY_VALUE_HEADS, HEAD_SIZE)
    heads_of_values = projected_output[:, (QUERY_HEADS + KEY_VALUE_HEADS) * HEAD_SIZE :]
    return (
        rotate(scaled(query_rows, head_gain[:HEAD_SIZE]), positions),
        rotate(scaled(heads_of_keys, head_gain[HEAD_SIZE:]), positions),
        heads_of_values,
    )


def gated_unit(joined):
    return jax.nn.silu(joined[:, :FF]) * joined[:, FF:]


def times_transposed(left_side, right_side):
    return lax.dot_general(
        left_side, right_side, (((1,), (1,)), ((), ())), preferred_element_type=jnp.float32
    )


def allowed_mask(doc_rows, row_start, document_index):
    row_index = row_start + jnp.arange(doc_rows.shape[0], dtype=jnp.int32)
    key_index = jnp.arange(document_index.shape[0], dtype=jnp.int32)
    return (doc_rows[:, None] == document_index[None, :]) & (
        row_index[:, None] >= key_index[None, :]
    )


def raw_scores(query_rows_second, rows_of_keys, allowed):
    grouped_heads = query_rows_second.reshape(
        query_rows_second.shape[0], KEY_VALUE_HEADS, QUERY_HEADS // KEY_VALUE_HEADS, HEAD_SIZE
    )
    heads_of_keys = rows_of_keys.reshape(rows_of_keys.shape[0], KEY_VALUE_HEADS, HEAD_SIZE)
    scores = jnp.einsum(
        "rkgd,tkd->rkgt", grouped_heads, heads_of_keys, preferred_element_type=jnp.float32
    ) * HEAD_SIZE ** (-0.5)
    return jnp.where(allowed[:, None, None, :], scores, MASKED_SCORE)


def attend_rows(query_rows_second, rows_of_keys, rows_of_values, allowed):
    scores = raw_scores(query_rows_second, rows_of_keys, allowed)
    row_max = jnp.max(scores, axis=-1, keepdims=True)
    exp_scores = jnp.exp(scores - row_max)
    row_totals = jnp.sum(exp_scores, axis=-1, keepdims=True)
    attn_probs = (exp_scores / row_totals).astype(jnp.bfloat16)
    heads_of_values = rows_of_values.reshape(rows_of_values.shape[0], KEY_VALUE_HEADS, HEAD_SIZE)
    heads_mixed = jnp.einsum(
        "rkgt,tkd->rkgd", attn_probs, heads_of_values, preferred_element_type=jnp.float32
    )
    return (
        heads_mixed.reshape(query_rows_second.shape[0], QUERY_HEADS * HEAD_SIZE),
        row_max + jnp.log(row_totals),
    )


def attend_back(
    query_rows_second, rows_of_keys, rows_of_values, allowed, log_totals, mixed_gradient_second
):
    count_of_rows = query_rows_second.shape[0]
    count_of_keys = rows_of_keys.shape[0]
    grouped_heads = query_rows_second.reshape(
        count_of_rows, KEY_VALUE_HEADS, QUERY_HEADS // KEY_VALUE_HEADS, HEAD_SIZE
    )
    heads_of_keys = rows_of_keys.reshape(count_of_keys, KEY_VALUE_HEADS, HEAD_SIZE)
    heads_of_values = rows_of_values.reshape(count_of_keys, KEY_VALUE_HEADS, HEAD_SIZE)
    heads_gradient = mixed_gradient_second.reshape(
        count_of_rows, KEY_VALUE_HEADS, QUERY_HEADS // KEY_VALUE_HEADS, HEAD_SIZE
    )
    attn_probs = jnp.exp(raw_scores(query_rows_second, rows_of_keys, allowed) - log_totals)
    grad_probs = jnp.einsum(
        "rkgd,tkd->rkgt", heads_gradient, heads_of_values, preferred_element_type=jnp.float32
    )
    grad_scores = (
        attn_probs * (grad_probs - jnp.sum(grad_probs * attn_probs, axis=-1, keepdims=True))
    ).astype(jnp.bfloat16)
    queries_gradient = jnp.einsum(
        "rkgt,tkd->rkgd", grad_scores, heads_of_keys, preferred_element_type=jnp.float32
    ) * HEAD_SIZE ** (-0.5)
    keys_gradient = jnp.einsum(
        "rkgt,rkgd->tkd", grad_scores, grouped_heads, preferred_element_type=jnp.float32
    ) * HEAD_SIZE ** (-0.5)
    values_gradient = jnp.einsum(
        "rkgt,rkgd->tkd",
        attn_probs.astype(jnp.bfloat16),
        heads_gradient,
        preferred_element_type=jnp.float32,
    )
    return (
        queries_gradient.reshape(count_of_rows, QUERY_HEADS, HEAD_SIZE),
        keys_gradient.reshape(count_of_keys, KEY_VALUE_HEADS * HEAD_SIZE),
        values_gradient.reshape(count_of_keys, KEY_VALUE_HEADS * HEAD_SIZE),
    )


def layer_forward(inputs, layer_full, positions, allowed):
    mixer_gain, heads_weight, merge_weight, head_gain, feed_gain, expand_weight, reduce_weight = (
        layer_full
    )
    count_of_rows = inputs.shape[0]
    normal_a = scaled(inputs, mixer_gain).astype(jnp.bfloat16)
    projected_output = jnp.dot(normal_a, heads_weight, preferred_element_type=jnp.float32)
    query_rows, heads_of_keys, heads_of_values = heads_of(projected_output, head_gain, positions)
    rows_of_keys, rows_of_values = (
        lax.all_gather(
            heads_of_keys.reshape(count_of_rows, KEY_VALUE_HEADS * HEAD_SIZE).astype(jnp.bfloat16),
            "fsdp",
            axis=0,
            tiled=True,
        ),
        lax.all_gather(heads_of_values.astype(jnp.bfloat16), "fsdp", axis=0, tiled=True),
    )
    heads_mixed, log_totals = attend_rows(
        query_rows.astype(jnp.bfloat16), rows_of_keys, rows_of_values, allowed
    )
    mixed_b = heads_mixed.astype(jnp.bfloat16)
    middle = inputs + jnp.dot(mixed_b, merge_weight, preferred_element_type=jnp.float32)
    normal_b = scaled(middle, feed_gain).astype(jnp.bfloat16)
    joined = jnp.dot(normal_b, expand_weight, preferred_element_type=jnp.float32)
    hidden = gated_unit(joined).astype(jnp.bfloat16)
    result = middle + jnp.dot(hidden, reduce_weight, preferred_element_type=jnp.float32)
    return (
        result,
        (
            inputs,
            normal_a,
            projected_output,
            rows_of_keys,
            rows_of_values,
            log_totals,
            mixed_b,
            middle,
            normal_b,
            joined,
            hidden,
        ),
    )


def layer_backward(upstream, layer_full, saved, positions, allowed):
    mixer_gain, heads_weight, merge_weight, head_gain, feed_gain, expand_weight, reduce_weight = (
        layer_full
    )
    (
        inputs,
        normal_a,
        projected_output,
        rows_of_keys,
        rows_of_values,
        log_totals,
        mixed_b,
        middle,
        normal_b,
        joined,
        hidden,
    ) = saved
    count_of_rows = inputs.shape[0]
    upstream_b = upstream.astype(jnp.bfloat16)
    grad_hidden = times_transposed(upstream_b, reduce_weight)
    unused_joined, gated_back = jax.vjp(gated_unit, joined)
    grad_joined = gated_back(grad_hidden)[0].astype(jnp.bfloat16)
    unused_feed, feed_back = jax.vjp(scaled, middle, feed_gain)
    grad_middle_part, grad_feed = feed_back(times_transposed(grad_joined, expand_weight))
    grad_middle = upstream + grad_middle_part
    grad_middle_b = grad_middle.astype(jnp.bfloat16)
    grad_mixed = times_transposed(grad_middle_b, merge_weight).astype(jnp.bfloat16)
    head_values, heads_back = jax.vjp(
        lambda projected_rows, gain_rows: heads_of(projected_rows, gain_rows, positions),
        projected_output,
        head_gain,
    )
    queries_gradient, grad_keys_all, grad_values_all = attend_back(
        head_values[0].astype(jnp.bfloat16),
        rows_of_keys,
        rows_of_values,
        allowed,
        log_totals,
        grad_mixed,
    )
    keys_gradient, values_gradient = (
        lax.psum_scatter(
            grad_keys_all.astype(jnp.bfloat16), "fsdp", scatter_dimension=0, tiled=True
        ).astype(jnp.float32),
        lax.psum_scatter(
            grad_values_all.astype(jnp.bfloat16), "fsdp", scatter_dimension=0, tiled=True
        ).astype(jnp.float32),
    )
    grad_projected, grad_head = heads_back(
        (
            queries_gradient,
            keys_gradient.reshape(count_of_rows, KEY_VALUE_HEADS, HEAD_SIZE),
            values_gradient,
        )
    )
    grad_projected_b = grad_projected.astype(jnp.bfloat16)
    unused_mixer, mixer_back = jax.vjp(scaled, inputs, mixer_gain)
    grad_inputs_part, grad_mixer = mixer_back(times_transposed(grad_projected_b, heads_weight))
    operands = (
        normal_a,
        grad_projected_b,
        mixed_b,
        grad_middle_b,
        normal_b,
        grad_joined,
        hidden,
        upstream_b,
    )
    return (grad_middle + grad_inputs_part, operands, (grad_mixer, grad_feed, grad_head))


def product_term(left_side, right_side):
    return lax.dot_general(
        left_side, right_side, (((0,), (0,)), ((), ())), preferred_element_type=jnp.float32
    )


def reduce_grads(operands, gain_terms):
    (
        normal_a,
        grad_projected_b,
        mixed_b,
        grad_middle_b,
        normal_b,
        grad_joined,
        hidden,
        upstream_b,
    ) = operands
    heads_gradient = lax.psum_scatter(
        product_term(normal_a, grad_projected_b).astype(jnp.bfloat16),
        "fsdp",
        scatter_dimension=0,
        tiled=True,
    )
    grad_merge = lax.psum_scatter(
        product_term(mixed_b, grad_middle_b).astype(jnp.bfloat16),
        "fsdp",
        scatter_dimension=0,
        tiled=True,
    )
    grad_expand = lax.psum_scatter(
        product_term(normal_b, grad_joined).astype(jnp.bfloat16),
        "fsdp",
        scatter_dimension=0,
        tiled=True,
    )
    grad_reduce = lax.psum_scatter(
        product_term(hidden, upstream_b).astype(jnp.bfloat16),
        "fsdp",
        scatter_dimension=0,
        tiled=True,
    )
    grad_mixer, grad_feed, grad_head = (
        lax.psum_scatter(gain_terms[0], "fsdp", scatter_dimension=0, tiled=True),
        lax.psum_scatter(gain_terms[1], "fsdp", scatter_dimension=0, tiled=True),
        lax.psum_scatter(gain_terms[2], "fsdp", scatter_dimension=0, tiled=True),
    )
    return (
        lax.psum(grad_mixer.astype(jnp.bfloat16), "rep").astype(jnp.float32),
        lax.psum(heads_gradient, "rep").astype(jnp.float32),
        lax.psum(grad_merge, "rep").astype(jnp.float32),
        lax.psum(grad_head.astype(jnp.bfloat16), "rep").astype(jnp.float32),
        lax.psum(grad_feed.astype(jnp.bfloat16), "rep").astype(jnp.float32),
        lax.psum(grad_expand, "rep").astype(jnp.float32),
        lax.psum(grad_reduce, "rep").astype(jnp.float32),
    )


def body(
    section_inputs,
    doc_lengths,
    mixer_gain,
    heads_weight,
    merge_weight,
    head_gain,
    feed_gain,
    expand_weight,
    reduce_weight,
):
    section_index = lax.axis_index("section")
    head_section = section_index == 0
    shard_index = lax.axis_index("fsdp")
    count_of_rows = section_inputs.shape[3]
    sequence_length = count_of_rows * lax.axis_size("fsdp")
    own_rows = section_inputs[0, :, 0]
    micro_count = own_rows.shape[0]
    mixer_part = (
        lax.all_gather(mixer_gain, "fsdp", axis=1, tiled=True),
        lax.all_gather(heads_weight, "fsdp", axis=1, tiled=True),
        lax.all_gather(merge_weight, "fsdp", axis=1, tiled=True),
        lax.all_gather(head_gain, "fsdp", axis=1, tiled=True),
    )
    feed_part = (
        lax.all_gather(feed_gain, "fsdp", axis=1, tiled=True),
        lax.all_gather(expand_weight, "fsdp", axis=1, tiled=True),
        lax.all_gather(reduce_weight, "fsdp", axis=1, tiled=True),
    )
    layer_full = (
        mixer_part[0][0].astype(jnp.float32),
        mixer_part[1][0],
        mixer_part[2][0],
        mixer_part[3][0].astype(jnp.float32),
        feed_part[0][0].astype(jnp.float32),
        feed_part[1][0],
        feed_part[2][0],
    )

    def layout(micro_slot):
        document_index, positions = places(doc_lengths[micro_slot, 0], sequence_length)
        row_start = shard_index * count_of_rows
        doc_rows = lax.dynamic_slice_in_dim(document_index, row_start, count_of_rows)
        own_positions = lax.dynamic_slice_in_dim(positions, row_start, count_of_rows)
        return (own_positions, allowed_mask(doc_rows, row_start, document_index))

    results = jnp.zeros((micro_count, count_of_rows, own_rows.shape[2]), jnp.float32)
    saved_acts = None
    arrived = jnp.zeros((count_of_rows, own_rows.shape[2]), jnp.bfloat16)
    for step_index in range(micro_count + 1):
        slot_raw = step_index - section_index
        is_live = (slot_raw >= 0) & (slot_raw < micro_count)
        micro_slot = jnp.clip(slot_raw, 0, micro_count - 1)
        inputs = jnp.where(
            head_section, own_rows[min(step_index, micro_count - 1)], arrived
        ).astype(jnp.float32)
        positions, allowed = layout(micro_slot)
        result, saved = layer_forward(inputs, layer_full, positions, allowed)
        if saved_acts is None:
            saved_acts = tuple(
                (jnp.zeros((micro_count,) + current.shape, current.dtype) for current in saved)
            )
        saved_acts = tuple(
            (
                jnp.where(is_live, buffer.at[micro_slot].set(current), buffer)
                for buffer, current in zip(saved_acts, saved)
            )
        )
        results = jnp.where(
            is_live & jnp.logical_not(head_section), results.at[micro_slot].set(result), results
        )
        if step_index < micro_count:
            arrived = from_behind(result.astype(jnp.bfloat16), "section", 1)
    gradients = None
    stashed = None
    gain_sums = None
    from_next = jnp.zeros((count_of_rows, own_rows.shape[2]), jnp.bfloat16)
    for step_index in range(micro_count + 1):
        slot_raw = step_index - 1 + section_index
        is_live = (slot_raw >= 0) & (slot_raw < micro_count)
        micro_slot = jnp.clip(slot_raw, 0, micro_count - 1)
        upstream = jnp.where(
            head_section, from_next, own_rows[min(step_index, micro_count - 1)]
        ).astype(jnp.float32)
        upstream = jnp.where(is_live, upstream, 0.0)
        positions, allowed = layout(micro_slot)
        saved = tuple((buffer[micro_slot] for buffer in saved_acts))
        grad_inputs, operands, gain_terms = layer_backward(
            upstream, layer_full, saved, positions, allowed
        )
        results = jnp.where(
            is_live & head_section, results.at[micro_slot].set(grad_inputs), results
        )
        if step_index < micro_count:
            from_next = from_behind(grad_inputs.astype(jnp.bfloat16), "section", -1)
        if stashed is None:
            stashed = tuple(
                (jnp.zeros((micro_count,) + current.shape, current.dtype) for current in operands)
            )
            gain_sums = tuple((jnp.zeros_like(current) for current in gain_terms))
        stashed = tuple(
            (
                jnp.where(is_live, buffer.at[micro_slot].set(current), buffer)
                for buffer, current in zip(stashed, operands)
            )
        )
        gain_sums = tuple(
            (total_so_far + current for total_so_far, current in zip(gain_sums, gain_terms))
        )
    merged = tuple(
        (buffer.reshape((micro_count * count_of_rows,) + buffer.shape[2:]) for buffer in stashed)
    )
    gradients = reduce_grads(merged, gain_sums)
    grad_mixer, heads_gradient, grad_merge, grad_head, grad_feed, grad_expand, grad_reduce = (
        gradients
    )
    return (
        results[None, :, None],
        grad_mixer[None],
        heads_gradient[None],
        grad_merge[None],
        grad_head[None],
        grad_feed[None],
        grad_expand[None],
        grad_reduce[None],
    )


MESH = pl.DeviceIdType.MESH
MERGED = QUERY_HEADS // KEY_VALUE_HEADS * HEAD_SIZE
JOINT = MERGED + 2 * HEAD_SIZE
VMEM_BYTES = 63 * 2**20


def mm(left, right):
    return jnp.dot(left, right, preferred_element_type=jnp.float32)


def mm_t(left, right):
    return lax.dot_general(
        left, right, (((1,), (1,)), ((), ())), preferred_element_type=jnp.float32
    )


def t_mm(left, right):
    return lax.dot_general(
        left, right, (((0,), (0,)), ((), ())), preferred_element_type=jnp.float32
    )


def remote(src, dst, send, recv, device):
    return pltpu.make_async_remote_copy(
        src_ref=src,
        dst_ref=dst,
        send_sem=send,
        recv_sem=recv,
        device_id=device,
        device_id_type=MESH,
    )


class Place:
    def __init__(self):
        self.index = lax.axis_index("fsdp")
        self.core = lax.rem(self.index, 2)
        self.chip = lax.div(self.index, 2)
        self.x = lax.rem(self.chip, 2)
        self.y = lax.div(self.chip, 2)
        self.x_peer = {"fsdp": self.index + 2 - 4 * self.x}
        self.y_peer = {"fsdp": self.index + 4 - 8 * self.y}
        self.core_peer = {"fsdp": self.index + 1 - 2 * self.core}
        self.section = lax.axis_index("section")
        self.section_peer = {"section": 1 - self.section}
        self.replica = lax.axis_index("rep")
        self.rep_peer = {"rep": 1 - self.replica}

    def chip_at(self, rel):
        x, y = self.x, self.y
        if rel in (1, 3):
            x = 1 - x
        if rel in (2, 3):
            y = 1 - y
        return 2 * y + x

    def others(self):
        order = ((3, 0), (3, 1), (1, 0), (1, 1), (2, 0), (2, 1), (0, 1), (0, 0))
        return [
            (at, 2 * self.chip_at(rel) + (1 - self.core if other else self.core))
            for at, (rel, other) in enumerate(order)
        ]

    def greet(self, peers):
        barrier = pltpu.get_barrier_semaphore()
        for peer in peers:
            pl.semaphore_signal(barrier, inc=1, device_id=peer, device_id_type=MESH)
        pl.semaphore_wait(barrier, len(peers))


class Gather:
    def __init__(self, place, full, send, recv, rows):
        half = rows // 2

        def span(rel, part=None):
            first = (2 * place.chip_at(rel) + place.core) * rows
            if part is None:
                return pl.ds(pl.multiple_of(first, rows), rows)
            return pl.ds(pl.multiple_of(first + part * half, half), half)

        def copy(at, piece, peer):
            block = full.at[piece]
            return remote(block, block, send.at[at], recv.at[at], peer)

        self.copies = [
            copy(0, span(0, 1), place.x_peer),
            copy(1, span(0, 0), place.x_peer),
            copy(2, span(0, 0), place.y_peer),
            copy(3, span(0, 1), place.y_peer),
            copy(4, span(0), place.core_peer),
            copy(5, span(1, 1), place.y_peer),
            copy(6, span(2, 0), place.x_peer),
            copy(7, span(1), place.core_peer),
            copy(8, span(2), place.core_peer),
            copy(9, span(3), place.core_peer),
        ]

    def start(self):
        for at in (0, 2, 4, 1, 3):
            self.copies[at].start()

    def relay(self):
        self.copies[0].wait_recv()
        self.copies[5].start()
        self.copies[2].wait_recv()
        self.copies[6].start()

    def near(self):
        self.copies[1].wait_recv()
        self.copies[7].start()
        self.copies[3].wait_recv()
        self.copies[8].start()

    def far(self):
        self.copies[5].wait_recv()
        self.copies[6].wait_recv()
        self.copies[9].start()

    def wait(self, at):
        self.copies[at].wait_recv()

    def finish(self):
        for entry in self.copies:
            entry.wait_send()

    def over_blocks(self, block, between=lambda: None, early=lambda at: None):
        self.start()
        early(0)
        self.wait(4)
        block(0)
        early(1)
        self.relay()
        early(2)
        self.near()
        self.wait(7)
        block(1)
        early(3)
        self.wait(8)
        block(2)
        early(4)
        between()
        self.far()
        self.wait(9)
        block(3)


class Scatter:
    def __init__(self, place, held, to_core, from_core, to_x, to_y, from_x, from_y, send, recv, rows):
        self.place, self.held, self.to_core, self.from_core = place, held, to_core, from_core
        self.to_x, self.to_y, self.from_x, self.from_y = to_x, to_y, from_x, from_y
        self.rows, self.half = rows, rows // 2

        def copy(at, src, dst, peer):
            return remote(src, dst, send.at[at], recv.at[at], peer)

        self.copies = [
            copy(rel, to_core.at[rel], from_core.at[rel], place.core_peer) for rel in range(4)
        ] + [
            copy(4, to_x.at[0], from_x.at[0], place.x_peer),
            copy(5, to_y.at[0], from_y.at[0], place.y_peer),
            copy(6, to_x.at[1], from_x.at[1], place.x_peer),
            copy(7, to_y.at[1], from_y.at[1], place.y_peer),
            copy(8, to_y.at[2], from_y.at[2], place.y_peer),
            copy(9, to_x.at[2], from_x.at[2], place.x_peer),
        ]

    def put(self, rel, product, width):
        step, rows, mine = 512, self.rows, self.place.core == 0

        @pl.loop(0, width // step)
        def _(at):
            columns = pl.ds(pl.multiple_of(at * step, step), step)
            value = product(columns)
            low, high = value[:rows], value[rows:]
            self.held[rel, :, columns] = jnp.where(mine, low, high)
            self.to_core[rel, :, columns] = jnp.where(mine, high, low).astype(jnp.bfloat16)

        self.copies[rel].start()

    def pair(self, rel):
        self.copies[rel].wait_recv()
        half, held = self.half, self.held

        @pl.loop(0, self.rows // 16)
        def _(at):
            span = pl.ds(pl.multiple_of(at * 16, 16), 16)
            held[rel, span, :] += self.from_core[rel, span, :].astype(jnp.float32)

        if rel == 3:
            self.to_x[0] = held[3, :half].astype(jnp.bfloat16)
            self.copies[4].start()
            self.to_y[0] = held[3, half:].astype(jnp.bfloat16)
            self.copies[5].start()
        if rel == 1:
            self.to_x[1] = held[1, :half].astype(jnp.bfloat16)
            self.copies[6].start()
        if rel == 2:
            self.to_y[1] = held[2, half:].astype(jnp.bfloat16)
            self.copies[7].start()

    def relay(self):
        half, held = self.half, self.held
        self.copies[4].wait_recv()
        self.to_y[2] = (held[2, :half] + self.from_x[0].astype(jnp.float32)).astype(jnp.bfloat16)
        self.copies[8].start()
        self.copies[5].wait_recv()
        self.to_x[2] = (held[1, half:] + self.from_y[0].astype(jnp.float32)).astype(jnp.bfloat16)
        self.copies[9].start()

    def total(self, add):
        for at in (6, 7, 8, 9):
            self.copies[at].wait_recv()
        count = self.half // 16

        @pl.loop(0, count)
        def _(at):
            span = pl.ds(pl.multiple_of(at * 16, 16), 16)
            low = self.held[0, span, :] + self.from_x[1, span, :].astype(jnp.float32)
            add(span, low + self.from_y[2, span, :].astype(jnp.float32))

        @pl.loop(0, count)
        def _(at):
            span = pl.ds(pl.multiple_of(at * 16, 16), 16)
            below = pl.ds(pl.multiple_of(self.half + at * 16, 16), 16)
            high = self.held[0, below, :] + self.from_y[1, span, :].astype(jnp.float32)
            add(below, high + self.from_x[2, span, :].astype(jnp.float32))

        for entry in self.copies:
            entry.wait_send()


def turn_tile(tile, turned, first, last):
    for at in range(last - first):
        span = pl.ds(pl.multiple_of((first + at) * 256, 256), 256)
        turned[:, span] = tile[span, :].T


def product_and_turn(width, product, tile, turned):
    parts = 4 if width >= 1024 else 2
    step, share = width // parts, turned.shape[1] // (256 * parts)

    @pl.loop(0, parts)
    def _(chunk):
        product(pl.ds(pl.multiple_of(chunk * step, 128), step))
        for at in range(share):
            span = pl.ds(pl.multiple_of((chunk * share + at) * 256, 256), 256)
            turned[:, span] = tile[span, :].T


def by_rows(count, body):
    @pl.loop(0, count // 16)
    def _(at):
        body(pl.ds(pl.multiple_of(at * 16, 16), 16))


def inverse_size(values):
    return lax.rsqrt(jnp.mean(values * values, axis=-1, keepdims=True) + NORM_EPS)


def norm_back(values, gain, upstream):
    size = inverse_size(values)
    scaled_up = upstream * gain
    back = size * scaled_up - values * (
        size * size * size * jnp.mean(values * scaled_up, axis=-1, keepdims=True)
    )
    return back, upstream * values * size


def turn(values, cosine, sine):
    return values * cosine + pltpu.roll(values, HEAD_SIZE // 2, 1) * sine


def turn_back(values, cosine, sine):
    return values * cosine + pltpu.roll(values * sine, HEAD_SIZE // 2, 1)


def probabilities(queries, keys, first_keys, first_row):
    scores = mm_t(queries, keys) * HEAD_SIZE ** (-0.5)
    key_index = lax.broadcasted_iota(jnp.int32, scores.shape, 1)
    row_index = first_row + lax.broadcasted_iota(jnp.int32, scores.shape, 0)
    allowed = (key_index >= first_keys) & (key_index <= row_index)
    scores = jnp.where(allowed, scores, MASKED_SCORE)
    powers = jnp.exp(scores - jnp.max(scores, axis=-1, keepdims=True))
    return powers / jnp.sum(powers, axis=-1, keepdims=True)


def block_rows(place, rel, rows):
    return pl.ds(pl.multiple_of(place.chip_at(rel) * 2 * rows, 2 * rows), 2 * rows)


def shard_columns(first, device, count):
    return pl.ds(pl.multiple_of(first + device * count, 128), count)


def layer_forward_step(place, rows, refs, buffers, slot, step, hooks):
    (wh, wm, we, wr), gains_ref, head_gain_ref = refs.weights, refs.gains, refs.head_gain
    current, middle, result, result_b = (
        buffers.current,
        buffers.middle,
        buffers.result,
        buffers.result_b,
    )
    full_a, full_b = buffers.full_a, buffers.full_b
    projected, heads, mixed = buffers.projected, buffers.heads, buffers.mixed
    joined = buffers.joined
    chip_rows, width, hidden_width = 2 * rows, current.shape[1], wr.shape[0]
    save_sem = buffers.save_sem
    tables = [
        pltpu.make_async_copy(src.at[slot], dst, buffers.table_sem.at[at])
        for at, (src, dst) in enumerate(zip(refs.tables, buffers.tables))
    ]
    cosine, sine, first_key = buffers.tables
    for table in tables:
        table.start()

    def save(at, src, dst):
        copy = pltpu.make_async_copy(src, dst.at[slot], save_sem.at[at])
        copy.start()
        return copy

    saves = [save(0, current, refs.inputs)]

    def enter(span):
        values = current[span, :].astype(jnp.float32)
        base = pl.multiple_of(place.index * rows + span.start, 16)
        full_a[pl.ds(base, 16), :] = (
            values * inverse_size(values) * gains_ref[0:1, :]
        ).astype(jnp.bfloat16)

    by_rows(rows, enter)
    for table in tables:
        table.wait()
    gather = Gather(place, full_a, *buffers.gather_a, rows)

    def heads_block(rel):
        span = block_rows(place, rel, rows)
        if rel == 0:
            hooks.heads()
        values = mm(full_a[span, :], wh[...])
        projected[span, :] = values
        for at in range(3):
            columns = pl.ds(at * HEAD_SIZE, HEAD_SIZE)
            one = values[:, at * HEAD_SIZE : (at + 1) * HEAD_SIZE]
            gain = head_gain_ref[0:1, :] if at < 2 else head_gain_ref[1:2, :]
            heads[span, columns] = turn(
                one * inverse_size(one) * gain, cosine[span, :], sine[span, :]
            ).astype(jnp.bfloat16)
        heads[span, 3 * HEAD_SIZE :] = values[:, 3 * HEAD_SIZE :].astype(jnp.bfloat16)

    gather.over_blocks(heads_block)
    hooks.service()
    saves += [
        save(1, full_a, refs.normal_a),
        save(2, projected, refs.projected),
        save(3, heads, refs.heads),
    ]
    scatter = Scatter(place, *buffers.scatter, *buffers.scatter_a, rows)

    def attend_block(rel):
        first_row = place.chip_at(rel) * chip_rows
        span = block_rows(place, rel, rows)
        for at in range(2):
            columns = pl.ds(at * HEAD_SIZE, HEAD_SIZE)
            probs = probabilities(
                heads[span, columns],
                heads[:, 2 * HEAD_SIZE : 3 * HEAD_SIZE],
                first_key[span, :],
                first_row,
            )
            mixed[span, columns] = mm(
                probs.astype(jnp.bfloat16), heads[:, 3 * HEAD_SIZE :]
            ).astype(jnp.bfloat16)
        scatter.put(rel, lambda columns: mm(mixed[span, :], wm[:, columns]), width)

    attend_block(3)
    scatter.pair(3)
    attend_block(2)
    scatter.pair(2)
    attend_block(1)
    scatter.pair(1)
    attend_block(0)
    saves.append(save(4, mixed, refs.mixed))
    scatter.relay()
    scatter.pair(0)

    def residual(span, value):
        values = value + current[span, :].astype(jnp.float32)
        middle[span, :] = values
        base = pl.multiple_of(place.index * rows + span.start, 16)
        full_b[pl.ds(base, 16), :] = (
            values * inverse_size(values) * gains_ref[1:2, :]
        ).astype(jnp.bfloat16)

    scatter.total(residual)
    gather.finish()
    saves.append(save(5, middle, refs.middle))
    for copy in saves[:5]:
        copy.wait()
    hooks.kept()
    gather_b = Gather(place, full_b, *buffers.gather_b, rows)
    scatter_b = Scatter(place, *buffers.scatter, *buffers.scatter_b, rows)
    joined_copies, hidden_copies = {}, []

    def feed_block(rel):
        span = block_rows(place, rel, rows)
        stage = joined.at[rel % 2]
        hidden = buffers.blocks.at[rel // 2, :, pl.ds(rel % 2 * hidden_width, hidden_width)]
        if rel == 0:
            hooks.feed()
        if rel >= 2:
            joined_copies[rel - 2].wait()

        @pl.loop(0, hidden_width // 256)
        def _(at):
            columns = pl.ds(pl.multiple_of(at * 256, 256), 256)
            later = pl.ds(pl.multiple_of(hidden_width + at * 256, 256), 256)
            gate = mm(full_b[span, :], we[:, columns])
            up = mm(full_b[span, :], we[:, later])
            stage[:, columns] = gate
            stage[:, later] = up
            hidden[:, columns] = (gate * jax.nn.sigmoid(gate) * up).astype(jnp.bfloat16)

        copy = pltpu.make_async_copy(
            stage, refs.joined.at[slot, span], save_sem.at[8 + rel % 2]
        )
        copy.start()
        joined_copies[rel] = copy
        copy = pltpu.make_async_copy(
            hidden, refs.hidden.at[slot, span], buffers.hidden_sem.at[rel]
        )
        copy.start()
        hidden_copies.append(copy)
        scatter_b.put(rel, lambda columns: mm(hidden[...], wr[:, columns]), width)
        if rel in (1, 2):
            scatter_b.pair(rel - 1)

    gather_b.over_blocks(feed_block, lambda: scatter_b.pair(2))
    later_saves = [save(6, full_b, refs.normal_b)] + hidden_copies
    scatter_b.pair(3)
    scatter_b.relay()
    hooks.finish()
    saves[5].wait()

    def finish(span, value):
        values = value + middle[span, :]
        result[span, :] = values
        result_b[span, :] = values.astype(jnp.bfloat16)

    scatter_b.total(finish)
    hooks.hand()
    gather_b.finish()
    for copy in later_saves + [joined_copies[2], joined_copies[3]]:
        copy.wait()
    hooks.after()


def feed_back(place, rows, gather, scatter, full, weights, joined, joined_load, out_of, done):
    wm, we, wr = weights
    hidden_width, width = wr.shape

    def feed_block(rel):
        span = block_rows(place, rel, rows)
        stage, out = joined.at[rel % 2], out_of(rel)
        joined_load(rel).wait()

        @pl.loop(0, hidden_width // 256)
        def _(at):
            columns = pl.ds(pl.multiple_of(at * 256, 256), 256)
            later = pl.ds(pl.multiple_of(hidden_width + at * 256, 256), 256)
            grad = mm_t(full[span, :], wr[columns, :])
            gate, up = stage[:, columns], stage[:, later]
            sigmoid = jax.nn.sigmoid(gate)
            unit = gate * sigmoid
            out[:, columns] = (grad * up * (sigmoid + unit * (1.0 - sigmoid))).astype(jnp.bfloat16)
            out[:, later] = (grad * unit).astype(jnp.bfloat16)

        if rel < 2:
            joined_load(rel + 2).start()
        done(rel, out)
        scatter.put(rel, lambda columns: mm_t(out[...], we[columns, :]), width)
        if rel in (1, 2):
            scatter.pair(rel - 1)

    gather.over_blocks(feed_block, lambda: scatter.pair(2))
    scatter.pair(3)


def feed_input_back(place, rows, scatter, middle, gains_ref, out_gains, current, result, full_b):
    out_gains[1:2, :] = jnp.zeros_like(out_gains[1:2, :])

    def feed_norm(span, value):
        back, gain_term = norm_back(middle[span, :], gains_ref[1:2, :], value)
        out_gains[1:2, :] += jnp.sum(gain_term, axis=0, keepdims=True)
        total = back + current[span, :].astype(jnp.float32)
        result[span, :] = total
        base = pl.multiple_of(place.index * rows + span.start, 16)
        full_b[pl.ds(base, 16), :] = total.astype(jnp.bfloat16)

    scatter.total(feed_norm)


def kept_probs(held, joined, at, block, chip_rows):
    rows, seen = chip_rows // 2, (block + 1) * chip_rows
    if at == 0:
        first, columns = ((2, 2 * chip_rows), (2, 0), (0, 4 * chip_rows), (0, 0))[block]
        return held.at[pl.ds(first, 2), pl.ds(0, rows), pl.ds(columns, seen)]
    first, columns = ((1, 3 * chip_rows), (0, 4 * chip_rows), (1, 0), (0, 0))[block]
    return joined.at[first, pl.ds(0, chip_rows), pl.ds(columns, seen)]


def attention_probs(held, joined, heads, first_key, chip_rows):
    for block in range(heads.shape[0] // chip_rows):
        span = pl.ds(block * chip_rows, chip_rows)
        seen = (block + 1) * chip_rows
        keys = heads[:seen, 2 * HEAD_SIZE : 3 * HEAD_SIZE]
        for at in range(2):
            queries = heads[span, pl.ds(at * HEAD_SIZE, HEAD_SIZE)]
            probs = probabilities(queries, keys, first_key[span, :], block * chip_rows)
            kept = kept_probs(held, joined, at, block, chip_rows)
            kept[...] = probs.reshape(kept.shape)


def attention_back(
    held, joined, heads, grad_mixed, grad_queries, grad_keys, grad_values, chip_rows
):
    grad_keys[...] = jnp.zeros_like(grad_keys)
    grad_values[...] = jnp.zeros_like(grad_values)
    for block in range(heads.shape[0] // chip_rows):
        span = pl.ds(block * chip_rows, chip_rows)
        seen = (block + 1) * chip_rows
        keys = heads[:seen, 2 * HEAD_SIZE : 3 * HEAD_SIZE]
        values = heads[:seen, 3 * HEAD_SIZE :]
        for at in range(2):
            columns = pl.ds(at * HEAD_SIZE, HEAD_SIZE)
            queries = heads[span, columns]
            grad = grad_mixed[span, columns]
            probs = kept_probs(held, joined, at, block, chip_rows)[...]
            probs = probs.reshape(chip_rows, seen)
            grad_probs = mm_t(grad, values)
            grad_scores = (
                probs * (grad_probs - jnp.sum(probs * grad_probs, axis=-1, keepdims=True))
            ).astype(jnp.bfloat16)
            grad_queries[span, columns] = mm(grad_scores, keys) * HEAD_SIZE ** (-0.5)
            grad_keys[:seen, :] += t_mm(grad_scores, queries) * HEAD_SIZE ** (-0.5)
            grad_values[:seen, :] += t_mm(probs.astype(jnp.bfloat16), grad)


def project_back(
    place, rows, scatter, buffers, head_gain_ref, out_head_gain, wh
):
    projected, grad_projected = buffers.projected, buffers.grad_projected
    grad_queries, grad_keys, grad_values = buffers.attention_grads
    cosine, sine, _ = buffers.tables
    out_head_gain[...] = jnp.zeros_like(out_head_gain)

    def project_block(rel):
        span = block_rows(place, rel, rows)
        for at in range(3):
            columns = pl.ds(at * HEAD_SIZE, HEAD_SIZE)
            which = 0 if at < 2 else 1
            upstream = grad_queries[span, columns] if at < 2 else grad_keys[span, :]
            back, gain_term = norm_back(
                projected[span, columns],
                head_gain_ref[which : which + 1, :],
                turn_back(upstream, cosine[span, :], sine[span, :]),
            )
            out_head_gain[which : which + 1, :] += jnp.sum(gain_term, axis=0, keepdims=True)
            grad_projected[span, columns] = back.astype(jnp.bfloat16)
        grad_projected[span, 3 * HEAD_SIZE :] = grad_values[span, :].astype(jnp.bfloat16)
        scatter.put(rel, lambda columns: mm_t(grad_projected[span, :], wh[columns, :]), wh.shape[0])

    project_block(3)
    scatter.pair(3)
    project_block(2)
    scatter.pair(2)
    project_block(1)
    scatter.pair(1)
    project_block(0)


def input_back(scatter, inputs, gains_ref, out_gains, result, result_b):
    out_gains[0:1, :] = jnp.zeros_like(out_gains[0:1, :])

    def mixer_norm(span, value):
        back, gain_term = norm_back(inputs[span, :].astype(jnp.float32), gains_ref[0:1, :], value)
        out_gains[0:1, :] += jnp.sum(gain_term, axis=0, keepdims=True)
        total = back + result[span, :]
        result[span, :] = total
        if result_b is not None:
            result_b[span, :] = total.astype(jnp.bfloat16)

    scatter.total(mixer_norm)


def layer_backward_step(place, rows, refs, buffers, slot, hooks):
    (wh, wm, we, wr), gains_ref = refs.weights, refs.gains
    current, middle, result, result_b, inputs = (
        buffers.current,
        buffers.middle,
        buffers.result,
        buffers.result_b,
        buffers.inputs,
    )
    full_a, full_b, joined = buffers.full_a, buffers.full_b, buffers.joined
    save_sem, grad_joined = buffers.save_sem, buffers.grad_joined
    tables = [
        pltpu.make_async_copy(src.at[slot], dst, buffers.table_sem.at[at])
        for at, (src, dst) in enumerate(
            [
                *zip(refs.tables, buffers.tables),
                (refs.middle, middle),
                (refs.projected, buffers.projected),
                (refs.heads, buffers.heads),
                (refs.inputs, inputs),
            ]
        )
    ]
    for table in tables:
        table.start()

    def joined_load(rel):
        return pltpu.make_async_copy(
            refs.joined.at[slot, block_rows(place, rel, rows)],
            joined.at[rel % 2],
            buffers.joined_sem.at[rel % 2],
        )

    joined_load(0).start()
    joined_load(1).start()
    own_rows = pl.ds(pl.multiple_of(place.index * rows, rows), rows)
    full_a[own_rows, :] = current[...]

    def save(at, src, dst):
        copy = pltpu.make_async_copy(src, dst.at[slot], save_sem.at[at])
        copy.start()
        return copy

    gather = Gather(place, full_a, *buffers.gather_a, rows)
    scatter = Scatter(place, *buffers.scatter, *buffers.scatter_a, rows)
    length = full_a.shape[0]

    def out_of(rel):
        first = place.replica * length + place.chip_at(rel) * 2 * rows
        return grad_joined.at[pl.ds(pl.multiple_of(first, 2 * rows), 2 * rows)]

    feed_back(
        place,
        rows,
        gather,
        scatter,
        full_a,
        (wm, we, wr),
        joined,
        joined_load,
        out_of,
        hooks.done,
    )
    upstream_save = save(0, full_a, refs.upstream)
    scatter.relay()
    for table in tables:
        table.wait()
    out_gains = refs.out_gains.at[slot]
    feed_input_back(place, rows, scatter, middle, gains_ref, out_gains, current, result, full_b)
    gather.finish()
    upstream_save.wait()
    for rel in range(4):
        hooks.settled(rel, out_of(rel))
    gather_b = Gather(place, full_b, *buffers.gather_b, rows)
    scatter_b = Scatter(place, *buffers.scatter, *buffers.scatter_b, rows)
    grad_mixed = buffers.mixed

    def mixed_block(rel):
        span = block_rows(place, rel, rows)
        grad_mixed[span, :] = mm_t(full_b[span, :], wm[...]).astype(jnp.bfloat16)

    held, heads = buffers.scatter[0], buffers.heads

    def early(at):
        hooks.early(at)
        if at == 0:
            attention_probs(held, joined, heads, buffers.tables[2], 2 * rows)

    gather_b.over_blocks(mixed_block, early=early)
    middle_save = save(1, full_b, refs.grad_middle)
    attention_back(held, joined, heads, grad_mixed, *buffers.attention_grads, 2 * rows)
    project_back(
        place, rows, scatter_b, buffers, refs.head_gain, refs.out_head_gain.at[slot], wh
    )
    projected_save = save(2, buffers.grad_projected, refs.grad_projected)
    hooks.early(5)
    scatter_b.relay()
    scatter_b.pair(0)
    hooks.early(6)
    hooks.finish()
    input_back(scatter_b, inputs, gains_ref, out_gains, result, result_b)
    hooks.hand()
    gather_b.finish()
    for copy in (middle_save, projected_save):
        copy.wait()
    hooks.after()


class Saved(typing.NamedTuple):
    inputs: typing.Any
    normal_a: typing.Any
    projected: typing.Any
    heads: typing.Any
    mixed: typing.Any
    middle: typing.Any
    normal_b: typing.Any
    joined: typing.Any
    hidden: typing.Any
    upstream: typing.Any
    grad_middle: typing.Any
    grad_projected: typing.Any


class Layers(typing.NamedTuple):
    rows: typing.Any
    saved: Saved
    handed: typing.Any
    own_joined: typing.Any
    other_joined: typing.Any
    first_sum: typing.Any
    other_normal: typing.Any
    other_normal_a: typing.Any
    other_projected: typing.Any
    heads_w: typing.Any
    expand_w: typing.Any
    gains: typing.Any
    head_gain: typing.Any
    gain_terms: typing.Any
    head_terms: typing.Any


class LayerBuffers(typing.NamedTuple):
    current: typing.Any
    inputs: typing.Any
    result: typing.Any
    result_b: typing.Any
    full_a: typing.Any
    full_b: typing.Any
    projected: typing.Any
    heads: typing.Any
    mixed: typing.Any
    joined: typing.Any
    grad_joined: typing.Any
    grad_projected: typing.Any


class GradientBuffers(typing.NamedTuple):
    current: typing.Any
    result: typing.Any
    full_a: typing.Any
    full_b: typing.Any
    projected: typing.Any
    heads: typing.Any
    mixed: typing.Any
    joined: typing.Any


def layers_kernel(rows, *refs):
    refs = list(refs)

    def some(count):
        taken = refs[:count]
        del refs[:count]
        return taken

    own_ref, gain_ref = some(2)
    table_refs = some(3)
    heads_w, merge_w, expand_w, reduce_w = some(4)
    (out_rows,) = some(1)
    saved = types.SimpleNamespace(**Saved(*some(12))._asdict())
    out_handed, own_joined, other_joined, first_sum, other_normal = some(5)
    other_normal_a, other_projected = some(2)
    out_heads_w, out_expand_w = some(2)
    gains_ref, head_gain_ref, out_gains, out_head_gain = some(4)
    all_gains, wh, wm, we, wr, arrived = some(6)
    buffers = types.SimpleNamespace(**LayerBuffers(*some(12))._asdict())
    buffers.middle = buffers.result
    buffers.tables = some(3)
    buffers.attention_grads = some(3)
    buffers.scatter = some(7)
    first_tiles, first_turned, first_stage = some(3)
    buffers.blocks = first_stage
    load_sem, spread_send, spread_recv = some(3)
    share_send, share_recv = some(2)
    tile_sem, first_sem, first_send, first_recv, normal_send, normal_recv = some(6)
    projected_send, projected_recv = some(2)
    buffers.save_sem, buffers.table_sem, buffers.joined_sem, buffers.hidden_sem = some(4)
    hand_send, hand_recv, out_sem = some(3)
    buffers.gather_a, buffers.scatter_a = some(2), some(2)
    buffers.gather_b, buffers.scatter_b = some(2), some(2)
    saved.weights, saved.tables = (wh, wm, we, wr), table_refs
    saved.gains, saved.head_gain = gains_ref, head_gain_ref
    saved.out_gains, saved.out_head_gain = out_gains, out_head_gain
    place = Place()
    head = place.section == 0
    rest = jnp.logical_not(head)
    hidden_width = wr.shape[0]
    depth = heads_w.shape[0]
    query_width, key_width = QUERY_HEADS * HEAD_SIZE, KEY_VALUE_HEADS * HEAD_SIZE
    loads = [
        pltpu.make_async_copy(src, dst, load_sem.at[at])
        for at, (src, dst) in enumerate(((merge_w, wm), (reduce_w, wr)))
    ]
    for load in loads:
        load.start()
    shard_rows = pl.ds(pl.multiple_of(place.index * depth, depth), depth)

    def spread(at, device, piece, src, dst):
        if at < 7:
            return remote(
                src, dst, spread_send.at[piece, at], spread_recv.at[piece, at], {"fsdp": device}
            )
        return pltpu.make_async_copy(src, dst, load_sem.at[2 + piece])

    gain_copies = [
        spread(at, device, 0, gain_ref, all_gains.at[place.index])
        for at, device in place.others()
    ]
    heads_copies, expand_copies = [], []
    for at, device in place.others():
        for piece, first, count, into in (
            (1, 0, MERGED, 0),
            (2, query_width, HEAD_SIZE, MERGED),
            (3, query_width + key_width, HEAD_SIZE, MERGED + HEAD_SIZE),
        ):
            src = heads_w.at[:, shard_columns(first, device, count)]
            heads_copies.append(
                spread(at, device, piece, src, wh.at[shard_rows, pl.ds(into, count)])
            )
        for piece in range(2):
            src = expand_w.at[:, shard_columns(piece * FF, device, hidden_width)]
            dst = we.at[shard_rows, pl.ds(piece * hidden_width, hidden_width)]
            expand_copies.append(spread(at, device, 4 + piece, src, dst))

    def arrive(copies, pieces):
        for copy in copies[:-pieces]:
            copy.wait_recv()
        for copy in copies[-pieces:]:
            copy.wait()

    heads_out = pltpu.make_async_copy(wh, out_heads_w, load_sem.at[8])
    expand_out = pltpu.make_async_copy(we, out_expand_w, load_sem.at[9])

    def share(at, device, kind, weight):
        block = weight.at[pl.ds(pl.multiple_of(device * depth, depth), depth)]
        return remote(
            block, block, share_send.at[kind, at], share_recv.at[kind, at], place.rep_peer
        )

    def start_all(copies, pieces, shared, first=0, last=PLANE):
        for at, device in place.others()[first:last]:
            mine = copies[at * pieces : (at + 1) * pieces]

            def begin():
                for copy in mine:
                    copy.start()

            if at < shared:
                pl.when(place.replica == at % 2)(begin)
            else:
                begin()

    def pass_on(copies, pieces, kind, weight, first, last):
        for at, device in place.others()[first:last]:
            mine = copies[at * pieces : (at + 1) * pieces]

            @pl.when(place.replica == at % 2)
            def _():
                for copy in mine:
                    copy.wait_recv()
                share(at, device, kind, weight).start()

    def take_shared(kind, weight, shared):
        for at, device in place.others()[:shared]:

            @pl.when(place.replica != at % 2)
            def _():
                share(at, device, kind, weight).wait_recv()

    def sent(copies, pieces, kind, weight, shared):
        for at, device in place.others()[:7]:
            mine = copies[at * pieces : (at + 1) * pieces]

            def settle():
                for copy in mine:
                    copy.wait_send()
                if at < shared:
                    share(at, device, kind, weight).wait_send()

            if at < shared:
                pl.when(place.replica == at % 2)(settle)
            else:
                settle()

    place.greet(
        [{"fsdp": device} for _, device in place.others()[:7]]
        + [place.section_peer, place.rep_peer]
    )
    for copy in gain_copies:
        copy.start()
    start_all(heads_copies, 3, 2)

    arrive(gain_copies, 1)
    for shard in range(PLANE):
        part = slice(shard * depth, (shard + 1) * depth)
        gains_ref[0:1, part] = all_gains[shard][:, :depth]
        gains_ref[1:2, part] = all_gains[shard][:, depth : 2 * depth]
    per_row = PLANE // 2
    count = 2 * HEAD_SIZE // PLANE
    for row in range(2):
        head_gain_ref[row : row + 1, :] = jnp.concatenate(
            [
                all_gains[row * per_row + at][:, 2 * depth : 2 * depth + count]
                for at in range(per_row)
            ],
            axis=1,
        )

    current, result, result_b = buffers.current, buffers.result, buffers.result_b
    length = buffers.full_a.shape[0]

    def joined_save(rel, out):
        return pltpu.make_async_copy(
            out, own_joined.at[block_rows(place, rel, rows)], first_sem.at[rel]
        )

    def joined_copy(rel, out):
        return remote(
            out,
            other_joined.at[block_rows(place, rel, rows)],
            first_send.at[rel],
            first_recv.at[rel],
            place.rep_peer,
        )

    def saved_block(rel):
        return own_joined.at[block_rows(place, rel, rows)]

    half = length // 2
    half_rows = pl.ds(pl.multiple_of(place.core * half, half), half)

    def normal_copy(slot, kind=0):
        src, dst = ((saved.normal_b, other_normal), (saved.normal_a, other_normal_a))[kind]
        return remote(
            src.at[slot, half_rows],
            dst.at[slot, half_rows],
            normal_send.at[kind, slot],
            normal_recv.at[kind, slot],
            place.rep_peer,
        )

    def normal_pass(slot, kind=0):
        block = (other_normal, other_normal_a)[kind].at[slot, half_rows]
        return remote(
            block,
            block,
            normal_send.at[kind, 2 + slot],
            normal_recv.at[kind, 2 + slot],
            place.core_peer,
        )

    projected_copy = remote(
        saved.grad_projected.at[0],
        other_projected,
        projected_send.at[0],
        projected_recv.at[0],
        place.rep_peer,
    )

    def token_rows(replica):
        return pl.ds(pl.multiple_of(replica * length, length), length)

    def first_loads(at):
        columns = pl.ds(pl.multiple_of(at * depth, depth), depth)
        parts = (
            (saved.normal_b.at[0, :, columns], place.replica),
            (other_normal.at[0, :, columns], 1 - place.replica),
        )
        into = lax.rem(at, 2)
        return [
            pltpu.make_async_copy(
                src, first_tiles.at[into, token_rows(replica)], tile_sem.at[into, part]
            )
            for part, (src, replica) in enumerate(parts)
        ]

    def first_save(at):
        rows_at = pl.ds(pl.multiple_of(at * depth, depth), depth)
        return pltpu.make_async_copy(
            first_stage.at[lax.rem(at, 2)], first_sum.at[rows_at], first_sem.at[lax.rem(at, 2)]
        )

    def whole_load(part):
        src, replica = ((own_joined, place.replica), (other_joined, 1 - place.replica))[part]
        return pltpu.make_async_copy(
            src, buffers.grad_joined.at[token_rows(replica)], first_sem.at[2 + part]
        )

    def first_begin():
        normal_copy(0).wait_recv()
        normal_pass(0).start()
        for rel in range(4):
            joined_copy(rel, saved_block(rel)).wait()
        for part in range(2):
            whole_load(part).start()
        normal_pass(0).wait_recv()
        for at in range(2):
            for copy in first_loads(jnp.int32(at)):
                copy.start()

    def first_turn():
        for part in range(2):
            whole_load(part).wait()
        for copy in first_loads(jnp.int32(0)):
            copy.wait()
        turn_tile(first_tiles.at[0], first_turned.at[0], 0, 2 * length // 256)
        for copy in first_loads(jnp.int32(2)):
            copy.start()

    def first_job(at):
        into, later = lax.rem(at, 2), lax.rem(at + 1, 2)

        @pl.when(at + 1 < PLANE)
        def _():
            for copy in first_loads(at + 1):
                copy.wait()

        @pl.when(at >= 2)
        def _():
            first_save(at - 2).wait()

        def product(columns):
            first_stage[into, :, columns] = mm(
                first_turned[into], buffers.grad_joined[:, columns]
            ).astype(jnp.bfloat16)

        product_and_turn(
            2 * hidden_width, product, first_tiles.at[later], first_turned.at[later]
        )
        first_save(at).start()

        @pl.when(at + 3 < PLANE)
        def _():
            for copy in first_loads(at + 3):
                copy.start()

    def first_jobs(first, last):
        @pl.loop(first, last)
        def _(at):
            first_job(at)

    def first_end():
        for at in (PLANE - 2, PLANE - 1):
            first_save(jnp.int32(at)).wait()

    def hand(slot):
        return remote(
            result_b, arrived.at[slot], hand_send.at[slot], hand_recv.at[slot], place.section_peer
        )

    def rows_copy(slot):
        return pltpu.make_async_copy(result, out_rows.at[slot], out_sem.at[0])

    def save_rows(slot):
        copy = rows_copy(slot)
        copy.start()
        copy.wait()

    def heads_ready():
        pass_on(heads_copies, 3, 0, wh, 0, 2)
        arrive(heads_copies[6:], 3)
        take_shared(0, wh, 2)
        heads_out.start()
        start_all(expand_copies, 2, 2, 0, 2)

    def expand_service():
        pass_on(expand_copies, 2, 1, we, 0, 2)
        start_all(expand_copies, 2, 2, 2)

    def feed_ready():
        arrive(expand_copies[4:], 2)
        take_shared(1, we, 2)
        expand_out.start()

    @pl.when(rest)
    def _():
        heads_ready()
        expand_service()
        feed_ready()

    for load in loads:
        load.wait()

    @pl.loop(0, 5)
    def _(step):
        forward = (head & (step <= 1)) | (rest & ((step == 1) | (step == 3)))
        backward = (step == 4) | (rest & (step == 2))

        @pl.when(forward)
        def _():
            slot = jnp.where(head, step, lax.div(step - 1, 2))

            @pl.when(head)
            def _():
                current[...] = own_ref[slot]

            @pl.when(rest)
            def _():
                hand(slot).wait_recv()
                current[...] = arrived[slot]

            def first(body):
                return lambda: pl.when(head & (slot == 0))(body)


            def finish():
                @pl.when(slot == 1)
                def _():
                    hand(0).wait_send()

            def handing():
                @pl.when(head)
                def _():
                    hand(slot).start()

                @pl.when(rest)
                def _():
                    save_rows(slot)

            def after():
                normal_copy(slot).start()
                pl.when(head)(normal_copy(slot, 1).start)

            def kept():
                pl.when(rest)(normal_copy(slot, 1).start)

            layer_forward_step(
                place,
                rows,
                saved,
                buffers,
                slot,
                step,
                types.SimpleNamespace(
                    heads=first(heads_ready),
                    feed=first(feed_ready),
                    service=first(expand_service),
                    finish=finish,
                    hand=handing,
                    kept=kept,
                    after=after,
                ),
            )

        @pl.when(backward)
        def _():
            slot = jnp.where(head, 0, lax.div(step - 2, 2))

            @pl.when(head)
            def _():
                hand(0).wait_recv()
                current[...] = arrived[0]

            @pl.when(rest)
            def _():
                current[...] = own_ref[slot]

            def finish():
                @pl.when(head)
                def _():
                    hand(1).wait_send()

            def handing():
                @pl.when(rest)
                def _():
                    hand(slot).start()

                @pl.when(rest & (slot == 0))
                def _():
                    for rel in range(4):
                        joined_copy(rel, saved_block(rel)).start()

                @pl.when(head)
                def _():
                    rows_copy(slot).start()

            def done(rel, out):
                @pl.when(slot == 0)
                def _():
                    joined_save(rel, out).start()

                @pl.when(head)
                def _():
                    joined_copy(rel, out).start()

            def settled(rel, out):
                pl.when(slot == 0)(lambda: joined_save(rel, out).wait())

            def early(at):
                @pl.when(rest & (slot == 1))
                def _():
                    if at == 0:
                        first_begin()
                    elif at == 2:
                        first_turn()
                    elif at == 3:
                        first_jobs(0, 2)
                    elif at == 6:
                        first_jobs(2, 5)

            def after():
                pl.when(slot == 0)(projected_copy.start)

            hooks = types.SimpleNamespace(
                finish=finish,
                hand=handing,
                done=done,
                settled=settled,
                early=early,
                after=after,
            )
            layer_backward_step(place, rows, saved, buffers, slot, hooks)

    @pl.when(head)
    def _():
        first_begin()
        first_turn()
        first_jobs(0, 5)

    first_jobs(5, PLANE)

    first_end()
    normal_copy(1).wait_recv()
    normal_pass(1).start()
    for slot in range(2):
        normal_copy(slot, 1).wait_recv()
        normal_pass(slot, 1).start()

    @pl.when(head)
    def _():
        hand(1).wait_recv()
        current[...] = arrived[1]

    @pl.when(rest)
    def _():
        hand(1).wait_send()
        current[...] = own_ref[1]

    handed = pltpu.make_async_copy(current, out_handed, out_sem.at[1])
    handed.start()
    normal_pass(1).wait_recv()
    for slot in range(2):
        normal_pass(slot, 1).wait_recv()
    projected_copy.wait()
    heads_out.wait()
    expand_out.wait()
    for copy in gain_copies[:7]:
        copy.wait_send()
    sent(heads_copies, 3, 0, wh, 2)
    sent(expand_copies, 2, 1, we, 2)
    for slot in range(2):
        for kind in range(2):
            normal_copy(slot, kind).wait_send()
            normal_pass(slot, kind).wait_send()
    handed.wait()
    pl.when(head)(lambda: rows_copy(0).wait())


def gradient_kernel(rows, *refs):
    refs = list(refs)

    def some(count):
        taken = refs[:count]
        del refs[:count]
        return taken

    gains_ref, head_gain_ref, first_gains, first_head_gain = some(4)
    table_refs = some(3)
    heads_w, merge_w, expand_w, reduce_w = some(4)
    in_handed, in_inputs, in_projected, in_heads, in_middle, in_joined = some(6)
    hidden_all, upstream_all, normal_b_all, other_normal = some(4)
    mixed_all, grad_middle_all, normal_a_all, other_normal_a = some(4)
    grad_projected_all, other_projected, first_sum, out_result = some(4)
    own_heads, own_merge, other_merge = some(3)
    own_expand, own_reduce, other_reduce = some(3)
    (out_gain,) = some(1)
    wh, wm, we, wr = some(4)
    buffers = types.SimpleNamespace(**GradientBuffers(*some(8))._asdict())
    buffers.tables = some(3)
    buffers.attention_grads = some(3)
    buffers.scatter = some(7)
    tiles, turned, wide, narrow, first_projected, last_projected = some(6)
    gains, head_gain, gain_out, gain_in, gain_sum, gain_other = some(6)
    load_sem, tile_sem, joined_sem, save_sem = some(4)
    buffers.gather_a, buffers.scatter_a = some(2), some(2)
    buffers.gather_b, buffers.scatter_b = some(2), some(2)
    spread_send, spread_recv, rep_send, rep_recv = some(4)
    current, result = buffers.current, buffers.result
    full_a, full_b, grad_mixed = buffers.full_a, buffers.full_b, buffers.mixed
    joined = buffers.joined

    place = Place()
    length, width = full_a.shape
    depth = wm.shape[0]
    hidden_width = wr.shape[0]
    last = in_inputs.shape[0] - 1
    tokens = narrow.shape[0]
    query_width, key_width = QUERY_HEADS * HEAD_SIZE, KEY_VALUE_HEADS * HEAD_SIZE
    others = place.others()

    def load(at, src, dst):
        copy = pltpu.make_async_copy(src, dst, load_sem.at[at])
        copy.start()
        return copy

    upstream_load = load(0, in_handed, current)
    reduce_load = load(1, reduce_w, wr)

    def joined_load(rel):
        return pltpu.make_async_copy(
            in_joined.at[last, block_rows(place, rel, rows)],
            joined.at[rel % 2],
            joined_sem.at[rel % 2],
        )

    joined_load(0).start()
    joined_load(1).start()
    expand_load = load(2, expand_w, we)
    middle_load = load(3, in_middle.at[last], result)
    wide_load = load(4, upstream_all.at[0], wide)
    def token_rows(replica):
        return pl.ds(pl.multiple_of(replica * length, length), length)

    buffers.grad_projected = last_projected.at[token_rows(place.replica)]
    jobs = [((hidden_all, None), at) for at in range(hidden_width // depth)]
    pair = (normal_b_all.at[last], other_normal.at[last])
    jobs += [(pair, device) for _, device in others]
    jobs += [((mixed_all, None), 0)]
    for slot in (0, last):
        pair = (normal_a_all.at[slot], other_normal_a.at[slot])
        jobs += [(pair, device) for _, device in others]
    job_count = len(jobs)

    def tile_loads(job):
        (mine, theirs), at = jobs[job]
        columns = pl.ds(pl.multiple_of(at * depth, depth), depth)
        if theirs is None:
            return [
                pltpu.make_async_copy(
                    mine.at[:, columns], tiles.at[job % 2], tile_sem.at[job % 2, 0]
                )
            ]
        parts = ((mine, place.replica), (theirs, 1 - place.replica))
        return [
            pltpu.make_async_copy(
                src.at[:, columns],
                tiles.at[job % 2, token_rows(replica)],
                tile_sem.at[job % 2, part],
            )
            for part, (src, replica) in enumerate(parts)
        ]

    def tile_start(job):
        for copy in tile_loads(job):
            copy.start()

    def run_job(job, width, product):
        now, later = turned.at[job % 2], (job + 1) % 2
        if job + 1 < job_count:
            for copy in tile_loads(job + 1):
                copy.wait()
        product_and_turn(
            width, lambda columns: product(now, columns), tiles.at[later], turned.at[later]
        )
        if job + 3 < job_count:
            tile_start(job + 3)

    tile_start(0)
    tile_start(1)
    projected_loads = [
        load(
            at, src, first_projected.at[token_rows(replica)]
        )
        for at, (src, replica) in (
            (5, (grad_projected_all.at[0], place.replica)),
            (16, (other_projected, 1 - place.replica)),
        )
    ]
    loads = [
        load(at + 6, src, dst)
        for at, (src, dst) in enumerate(
            [(merge_w, wm), (heads_w, wh)]
            + [(src.at[last], dst) for src, dst in zip(table_refs, buffers.tables)]
            + [
                (in_projected.at[last], buffers.projected),
                (in_heads.at[last], buffers.heads),
            ]
        )
    ]
    place.greet([{"fsdp": device} for _, device in others[:7]] + [place.rep_peer])

    def rep_copy(at, src, dst):
        return remote(src, dst, rep_send.at[at], rep_recv.at[at], place.rep_peer)

    def spread(at, device, piece, src, dst):
        if at < 7:
            return remote(
                src, dst, spread_send.at[piece, at], spread_recv.at[piece, at], {"fsdp": device}
            )
        return pltpu.make_async_copy(src, dst, save_sem.at[4 + piece])

    upstream_load.wait()
    own_rows = pl.ds(pl.multiple_of(place.index * rows, rows), rows)
    full_a[own_rows, :] = current[...]
    gather = Gather(place, full_a, *buffers.gather_a, rows)
    scatter = Scatter(place, *buffers.scatter, *buffers.scatter_a, rows)

    joined_reps = []

    def out_of(rel):
        if rel == 0:
            reduce_load.wait()
            expand_load.wait()
        first = place.replica * length + place.chip_at(rel) * 2 * rows
        return narrow.at[pl.ds(pl.multiple_of(first, 2 * rows), 2 * rows)]

    def done(rel, out):
        copy = rep_copy(4 + rel, out, out)
        copy.start()
        joined_reps.append(copy)

    feed_back(
        place,
        rows,
        gather,
        scatter,
        full_a,
        (wm, we, wr),
        joined,
        joined_load,
        out_of,
        done,
    )
    wide_load.wait()
    for copy in tile_loads(0):
        copy.wait()
    turn_tile(tiles.at[0], turned.at[0], 0, tokens // 256)
    tile_start(2)
    own_saves, rep_copies = [], []
    for at in range(hidden_width // depth):
        span = pl.ds(at * depth, depth)

        def product(tile, columns):
            value = mm(tile[:, :length], wide[:, columns])
            value += mm(tile[:, length:], full_a[:, columns])
            wr[span, columns] = value.astype(jnp.bfloat16)

        run_job(at, width, product)
        rep_copies.append(rep_copy(at, wr.at[span], other_reduce.at[span]))
        if at == 0:
            rep_copies[at].start()
        copy = pltpu.make_async_copy(wr.at[span], own_reduce.at[span], save_sem.at[at])
        copy.start()
        own_saves.append(copy)
        if at == 1:
            scatter.relay()
    middle_load.wait()
    feed_input_back(place, rows, scatter, result, gains_ref, gains, current, result, full_b)
    inputs_load = load(13, in_inputs.at[last], current)
    gather.finish()
    gather_b = Gather(place, full_b, *buffers.gather_b, rows)
    scatter_b = Scatter(place, *buffers.scatter, *buffers.scatter_b, rows)
    gather_b.start()
    for copy in loads:
        copy.wait()
    held = buffers.scatter[0]
    attention_probs(held, joined, buffers.heads, buffers.tables[2], 2 * rows)
    gather_b.relay()
    gather_b.near()
    gather_b.far()
    for rel, at in ((0, 4), (1, 7), (2, 8), (3, 9)):
        gather_b.wait(at)
        span = block_rows(place, rel, rows)
        grad_mixed[span, :] = mm_t(full_b[span, :], wm[...]).astype(jnp.bfloat16)
    attention_back(
        held, joined, buffers.heads, grad_mixed, *buffers.attention_grads, 2 * rows
    )
    project_back(place, rows, scatter_b, buffers, head_gain_ref, head_gain, wh)
    projected_rep = rep_copy(8, buffers.grad_projected, buffers.grad_projected)
    projected_rep.start()
    job = hidden_width // depth

    def first_load(at, device):
        block = pl.ds(pl.multiple_of(device * depth, depth), depth)
        into = wide.at[pl.ds(at % 2 * depth, depth), pl.ds(0, 2 * hidden_width)]
        return pltpu.make_async_copy(first_sum.at[block], into, load_sem.at[14 + at % 2])

    for at, device in others[:2]:
        first_load(at, device).start()
    for copy in joined_reps:
        copy.wait_recv()
    expand_copies = []
    for at, device in others:
        block = pl.ds(at * depth, depth)
        first_load(at, device).wait()
        before = pl.ds(at % 2 * depth, depth)

        def product(tile, columns):
            value = wide[before, columns].astype(jnp.float32)
            value += mm(tile[...], narrow[:, columns])
            we[block, columns] = value.astype(jnp.bfloat16)

        run_job(job, narrow.shape[1], product)
        job += 1
        if at + 2 < PLANE:
            first_load(*others[at + 2]).start()
        for piece in range(2):
            copy = spread(
                at,
                device,
                piece,
                we.at[block, pl.ds(piece * hidden_width, hidden_width)],
                own_expand.at[:, shard_columns(piece * FF, place.index, hidden_width)],
            )
            copy.start()
            expand_copies.append(copy)
    grad_middle_load = load(4, grad_middle_all.at[0], wide)
    rep_copies[1].start()
    grad_middle_load.wait()

    def merge_product(tile, columns):
        value = mm(tile[:, :length], wide[:, columns])
        value += mm(tile[:, length:], full_b[:, columns])
        wm[:, columns] = value.astype(jnp.bfloat16)

    run_job(job, width, merge_product)
    job += 1
    rep_copies[2].start()
    merge_rep = rep_copy(3, wm, other_merge)
    merge_rep.start()
    merge_save = pltpu.make_async_copy(wm, own_merge, save_sem.at[3])
    merge_save.start()
    for copy in projected_loads:
        copy.wait()
    for at, device in others:
        block = pl.ds(at * depth, depth)

        def product(tile, columns):
            wh[block, columns] = mm(tile[...], first_projected[:, columns]).astype(jnp.bfloat16)

        run_job(job, JOINT, product)
        job += 1
    projected_rep.wait_recv()
    heads_copies = []
    for at, device in others:
        block = pl.ds(at * depth, depth)

        def product(tile, columns):
            value = wh[block, columns].astype(jnp.float32)
            value += mm(tile[...], last_projected[:, columns])
            wh[block, columns] = value.astype(jnp.bfloat16)

        run_job(job, JOINT, product)
        job += 1
        for piece, first, count, start in (
            (2, 0, MERGED, 0),
            (3, query_width, HEAD_SIZE, MERGED),
            (4, query_width + key_width, HEAD_SIZE, MERGED + HEAD_SIZE),
        ):
            copy = spread(
                at,
                device,
                piece,
                wh.at[block, pl.ds(start, count)],
                own_heads.at[:, shard_columns(first, place.index, count)],
            )
            copy.start()
            heads_copies.append(copy)
    scatter_b.relay()
    scatter_b.pair(0)
    inputs_load.wait()
    input_back(scatter_b, current, gains_ref, gains, result, None)
    result_save = pltpu.make_async_copy(result, out_result, save_sem.at[10])
    result_save.start()

    gain_copies = []
    gains[...] += first_gains[0]
    head_gain[...] += first_head_gain[0]
    per_row = PLANE // 2
    count = 2 * HEAD_SIZE // PLANE
    for shard in range(PLANE):
        part = slice(shard * depth, (shard + 1) * depth)
        lanes = slice(shard % per_row * count, (shard % per_row + 1) * count)
        row = shard // per_row
        gain_out[shard] = jnp.zeros_like(gain_out[shard])
        gain_out[shard, :, :depth] = gains[0:1, part]
        gain_out[shard, :, depth : 2 * depth] = gains[1:2, part]
        gain_out[shard, :, 2 * depth : 2 * depth + count] = head_gain[row : row + 1, lanes]
    for at, device in others:
        copy = spread(at, device, 5, gain_out.at[device], gain_in.at[place.index])
        copy.start()
        gain_copies.append(copy)

    for copy in gain_copies[:7]:
        copy.wait_recv()
    gain_copies[7].wait()
    total = gain_in[0]
    for shard in range(1, PLANE):
        total += gain_in[shard]
    gain_sum[...] = total
    gain_rep = rep_copy(9, gain_sum, gain_other)
    gain_rep.start()
    for copy in heads_copies[:21]:
        copy.wait_recv()
    for copy in heads_copies[21:]:
        copy.wait()
    gain_rep.wait()
    out_gain[...] = gain_sum[...] + gain_other[...]
    gather_b.finish()
    for copy in expand_copies[:14]:
        copy.wait_recv()
    for copy in expand_copies[14:] + own_saves + [result_save, merge_save]:
        copy.wait()
    for copy in expand_copies[:14] + heads_copies[:21] + gain_copies[:7] + joined_reps:
        copy.wait_send()
    projected_rep.wait_send()
    for copy in rep_copies + [merge_rep]:
        copy.wait()


def sems(*counts):
    return [pltpu.SemaphoreType.DMA((count,)) for count in counts]


def vmem(*shapes):
    return [pltpu.VMEM(shape, dtype) for *shape, dtype in shapes]


def any_specs(count):
    return [pl.BlockSpec(memory_space=pl.ANY)] * count


def vmem_specs(count):
    return [pl.BlockSpec(memory_space=pltpu.VMEM)] * count


def kernel_params(collective_id):
    return pltpu.CompilerParams(
        collective_id=collective_id, has_side_effects=True, vmem_limit_bytes=VMEM_BYTES
    )


def weight_buffers(width, hidden_width):
    b16 = jnp.bfloat16
    return vmem(
        (width, JOINT, b16),
        (MERGED, width, b16),
        (width, 2 * hidden_width, b16),
        (hidden_width, width, b16),
    )


def table_buffers(length):
    return vmem(
        (length, HEAD_SIZE, jnp.float32),
        (length, HEAD_SIZE, jnp.float32),
        (length, 1, jnp.int32),
    )


def attention_buffers(length):
    return vmem(
        (length, MERGED, jnp.float32),
        (length, HEAD_SIZE, jnp.float32),
        (length, HEAD_SIZE, jnp.float32),
    )


def scatter_buffers(rows, width):
    half, b16 = rows // 2, jnp.bfloat16
    return vmem(
        (4, rows, width, jnp.float32),
        (4, rows, width, b16),
        (4, rows, width, b16),
        *(((3, half, width, b16),) * 4),
    )


def run_layers(own, gain_row, tables, weights):
    micro, rows, width = own.shape
    length = tables[0].shape[1]
    hidden_width, depth = weights[3].shape[0], weights[0].shape[0]
    f32, b16 = jnp.float32, jnp.bfloat16
    shape = jax.ShapeDtypeStruct
    stashes = (
        (rows, width, b16),
        (length, width, b16),
        (length, JOINT, f32),
        (length, JOINT, b16),
        (length, MERGED, b16),
        (rows, width, f32),
        (length, width, b16),
        (length, 2 * hidden_width, f32),
        (length, hidden_width, b16),
        (length, width, b16),
        (length, width, b16),
        (length, JOINT, b16),
    )
    out = pl.pallas_call(
        functools.partial(layers_kernel, rows),
        out_shape=(
            shape((micro, rows, width), f32),
            *(shape((micro, *size), dtype) for *size, dtype in stashes),
            shape((rows, width), b16),
            shape((length, 2 * hidden_width), b16),
            shape((length, 2 * hidden_width), b16),
            shape((width, 2 * hidden_width), b16),
            shape((micro, length, width), b16),
            shape((micro, length, width), b16),
            shape((length, JOINT), b16),
            shape((width, JOINT), b16),
            shape((width, 2 * hidden_width), b16),
            shape((2, width), f32),
            shape((2, HEAD_SIZE), f32),
            shape((micro, 2, width), f32),
            shape((micro, 2, HEAD_SIZE), f32),
        ),
        in_specs=vmem_specs(2) + any_specs(7),
        out_specs=any_specs(22) + vmem_specs(4),
        scratch_shapes=vmem((PLANE, *gain_row.shape, f32))
        + weight_buffers(width, hidden_width)
        + vmem(
            (micro, rows, width, b16),
            (rows, width, b16),
            (rows, width, b16),
            (rows, width, f32),
            (rows, width, b16),
            (length, width, b16),
            (length, width, b16),
            (length, JOINT, f32),
            (length, JOINT, b16),
            (length, MERGED, b16),
            (2, 2 * rows, 2 * hidden_width, f32),
            (2 * length, 2 * hidden_width, b16),
            (length, JOINT, b16),
        )
        + table_buffers(length)
        + attention_buffers(length)
        + scatter_buffers(rows, width)
        + vmem(
            (2, 2 * length, depth, b16),
            (2, depth, 2 * length, b16),
            (2, depth, 2 * hidden_width, b16),
        )
        + sems(10)
        + [pltpu.SemaphoreType.DMA((6, PLANE - 1))] * 2
        + [pltpu.SemaphoreType.DMA((2, 2))] * 2
        + [pltpu.SemaphoreType.DMA((2, 2))]
        + sems(4, 4, 4)
        + [pltpu.SemaphoreType.DMA((2, 4))] * 2
        + sems(1, 1)
        + sems(10, 7, 2, 4, micro, micro, 2, *((10,) * 8)),
        compiler_params=kernel_params(1),
    )(own, gain_row, *tables, *weights)
    return Layers(out[0], Saved(*out[1:13]), *out[13:])


def run_gradients(layers, tables, merge_w, reduce_w):
    saved = layers.saved
    micro, rows, width = saved.inputs.shape
    length = tables[0].shape[1]
    hidden_width, depth = reduce_w.shape[0], merge_w.shape[0]
    f32, b16 = jnp.float32, jnp.bfloat16
    shape = jax.ShapeDtypeStruct
    heads_term, merge_term = (depth, PLANE * JOINT), (depth, width)
    expand_term, reduce_term = (depth, 2 * FF), (hidden_width, width)
    terms = (heads_term,) + (merge_term,) * 2 + (expand_term,) + (reduce_term,) * 2
    gain_width = -(-(2 * depth + 2 * HEAD_SIZE // PLANE) // 128) * 128

    def flat(array):
        return array.reshape(micro * length, -1)

    return pl.pallas_call(
        functools.partial(gradient_kernel, rows),
        out_shape=(shape((rows, width), f32),)
        + tuple(shape(term, b16) for term in terms)
        + (shape((1, gain_width), f32),),
        in_specs=vmem_specs(4) + any_specs(24),
        out_specs=any_specs(7) + vmem_specs(1),
        scratch_shapes=weight_buffers(width, hidden_width)
        + vmem(
            (rows, width, b16),
            (rows, width, f32),
            (length, width, b16),
            (length, width, b16),
            (length, JOINT, f32),
            (length, JOINT, b16),
            (length, MERGED, b16),
            (2, 2 * rows, 2 * hidden_width, f32),
        )
        + table_buffers(length)
        + attention_buffers(length)
        + scatter_buffers(rows, width)
        + vmem(
            (2, micro * length, depth, b16),
            (2, depth, micro * length, b16),
            (length, width, b16),
            (2 * length, 2 * hidden_width, b16),
            (2 * length, JOINT, b16),
            (2 * length, JOINT, b16),
            (2, width, f32),
            (2, HEAD_SIZE, f32),
            (PLANE, 1, gain_width, f32),
            (PLANE, 1, gain_width, f32),
            (1, gain_width, f32),
            (1, gain_width, f32),
        )
        + sems(18)
        + [pltpu.SemaphoreType.DMA((2, 2))]
        + sems(2, 11, *((10,) * 8))
        + [pltpu.SemaphoreType.DMA((6, PLANE - 1))] * 2
        + sems(10, 10),
        compiler_params=kernel_params(2),
    )(
        layers.gains,
        layers.head_gain,
        layers.gain_terms,
        layers.head_terms,
        *tables,
        layers.heads_w,
        merge_w,
        layers.expand_w,
        reduce_w,
        layers.handed,
        saved.inputs,
        saved.projected,
        saved.heads,
        saved.middle,
        saved.joined,
        flat(saved.hidden),
        saved.upstream,
        saved.normal_b,
        layers.other_normal,
        flat(saved.mixed),
        saved.grad_middle,
        saved.normal_a,
        layers.other_normal_a,
        saved.grad_projected,
        layers.other_projected,
        layers.first_sum,
    )


def position_tables(lengths, length):
    token = jnp.arange(length, dtype=jnp.int32)[None, :, None]
    first_key = jnp.zeros((lengths.shape[0], length, 1), jnp.int32)
    doc_end = jnp.zeros((lengths.shape[0], 1, 1), jnp.int32)
    for at in range(lengths.shape[1]):
        one = lengths[:, at][:, None, None]
        doc_end = doc_end + one
        first_key = first_key + jnp.where(token >= doc_end, one, 0)
    half_width = HEAD_SIZE // 2
    lane = jnp.arange(HEAD_SIZE, dtype=jnp.int32)
    frequency = jnp.exp(
        (lane % half_width).astype(jnp.float32) * (-2.0 * math.log(ROPE_BASE) / HEAD_SIZE)
    )
    angles = (token - first_key).astype(jnp.float32) * frequency[None, None, :]
    sign = jnp.where(lane < half_width, -1.0, 1.0)
    return jnp.cos(angles), jnp.sin(angles) * sign, first_key


def tensor_parallel_body(
    section_inputs,
    doc_lengths,
    mixer_gain,
    heads_weight,
    merge_weight,
    head_gain,
    feed_gain,
    expand_weight,
    reduce_weight,
):
    shards = lax.axis_size("fsdp")
    own = section_inputs[0, :, 0]
    micro, rows, width = own.shape
    length = rows * shards
    depth = heads_weight.shape[1]
    hidden_width = reduce_weight.shape[1]
    query_width = QUERY_HEADS * HEAD_SIZE

    gain_row = jnp.concatenate([mixer_gain[0], feed_gain[0], head_gain[0]]).astype(jnp.float32)
    gain_row = jnp.pad(gain_row, (0, -gain_row.shape[0] % 128))[None]
    cosine, sine, first_key = position_tables(doc_lengths[:, 0], length)

    table_rows = (cosine, sine, first_key)
    layers = run_layers(
        own,
        gain_row,
        table_rows,
        (heads_weight[0], merge_weight[0], expand_weight[0], reduce_weight[0]),
    )
    last_rows, *terms, gain_sums = run_gradients(
        layers, table_rows, merge_weight[0], reduce_weight[0]
    )
    own_heads, own_merge, other_merge, own_expand, own_reduce, other_reduce = terms
    grad_heads = own_heads.astype(jnp.float32)[None]
    grad_expand = own_expand.astype(jnp.float32)[None]
    grad_merge, grad_reduce = (
        (mine.astype(jnp.float32) + theirs.astype(jnp.float32))[None]
        for mine, theirs in ((own_merge, other_merge), (own_reduce, other_reduce))
    )
    head_count = head_gain.shape[1]
    head = lax.axis_index("section") == 0
    last_rows = jnp.where(head, last_rows, layers.rows[-1])
    return (
        jnp.concatenate([layers.rows[:-1], last_rows[None]])[None, :, None],
        gain_sums[:, :depth],
        grad_heads,
        grad_merge,
        gain_sums[:, 2 * depth : 2 * depth + head_count],
        gain_sums[:, depth : 2 * depth],
        grad_expand,
        grad_reduce,
    )


def solution(mesh):
    plane = mesh.shape["fsdp"] == PLANE
    return jax.shard_map(
        tensor_parallel_body if plane else body,
        mesh=mesh,
        in_specs=(
            P("section", None, "rep", "fsdp", None),
            P(None, "rep", None),
            P("section", "fsdp"),
            P("section", "fsdp", None),
            P("section", "fsdp", None),
            P("section", "fsdp"),
            P("section", "fsdp"),
            P("section", "fsdp", None),
            P("section", "fsdp", None),
        ),
        out_specs=(
            P("section", None, "rep", "fsdp", None),
            P("section", "fsdp"),
            P("section", "fsdp", None),
            P("section", "fsdp", None),
            P("section", "fsdp"),
            P("section", "fsdp"),
            P("section", "fsdp", None),
            P("section", "fsdp", None),
        ),
        check_vma=False,
    )
```
